32 devices in a mesh: wide: 8 (over z, x), narrow: 4 (over y, core).
Axes of the slice: x: 2, y: 2, z: 4, core: 2. Of those that a mesh axis runs over, the one named last changes fastest.
Arguments:
- tokens: bfloat16 [4, 2048, 2048], P('narrow', 'wide'), may hold values from -6 to 6
- starts: int32 [4, 4], P('narrow'), may hold values from 0 to 2044, as said below
- init_state: float32 [4, 4, 2560], P('narrow'), may hold values from -4 to 4
- init_conv: bfloat16 [4, 4, 3, 2560], P('narrow'), may hold values from -6 to 6
- w_y: bfloat16 [2048, 2560], P(('wide', 'narrow')), may hold values from -0.125 to 0.125
- w_x: bfloat16 [2048, 2560], P(('wide', 'narrow')), may hold values from -0.125 to 0.125
- gate_a: bfloat16 [2560, 160], P(('wide', 'narrow')), may hold values from -0.5 to 0.5
- gate_i: bfloat16 [2560, 160], P(('wide', 'narrow')), may hold values from -0.5 to 0.5
- w_out: bfloat16 [2560, 2048], P(('wide', 'narrow')), may hold values from -0.3125 to 0.3125
- norm1_gain: bfloat16 [2048], P(('wide', 'narrow')), may hold values from 0.5 to 1.5
- conv_kernel: bfloat16 [4, 2560], P(None, ('wide', 'narrow')), may hold values from -3 to 3
- conv_bias: bfloat16 [2560], P(('wide', 'narrow')), may hold values from -3 to 3
- bias_a: bfloat16 [2560], P(('wide', 'narrow')), may hold values from -4 to 4
- bias_i: bfloat16 [2560], P(('wide', 'narrow')), may hold values from -4 to 4
- decay_param: bfloat16 [2560], P(('wide', 'narrow')), may hold values from -14 to -2
- w_gate: bfloat16 [2048, 6144], P(('wide', 'narrow')), may hold values from -0.125 to 0.125
- w_up: bfloat16 [2048, 6144], P(('wide', 'narrow')), may hold values from -0.125 to 0.125
- w_down: bfloat16 [6144, 2048], P(('wide', 'narrow')), may hold values from -0.15625 to 0.15625
- norm2_gain: bfloat16 [2048], P(('wide', 'narrow')), may hold values from 0.5 to 1.5
- cotangent: bfloat16 [4, 2048, 2048], P('narrow', 'wide'), may hold values from -6 to 6
Outputs:
- mixed: bfloat16 [4, 2048, 2048], P('narrow', 'wide')
- input_grad: bfloat16 [4, 2048, 2048], P('narrow', 'wide')
- final_state: float32 [4, 4, 2560], P('narrow')
- final_conv: bfloat16 [4, 4, 3, 2560], P('narrow')
- grad_w_y: float32 [2048, 2560], P(('wide', 'narrow'))
- grad_w_x: float32 [2048, 2560], P(('wide', 'narrow'))
- grad_gate_a: float32 [2560, 160], P(('wide', 'narrow'))
- grad_gate_i: float32 [2560, 160], P(('wide', 'narrow'))
- grad_w_out: float32 [2560, 2048], P(('wide', 'narrow'))
- grad_norm1_gain: float32 [2048], P(('wide', 'narrow'))
- grad_conv_kernel: float32 [4, 2560], P(None, ('wide', 'narrow'))
- grad_conv_bias: float32 [2560], P(('wide', 'narrow'))
- grad_bias_a: float32 [2560], P(('wide', 'narrow'))
- grad_bias_i: float32 [2560], P(('wide', 'narrow'))
- grad_decay_param: float32 [2560], P(('wide', 'narrow'))
- grad_w_gate: float32 [2048, 6144], P(('wide', 'narrow'))
- grad_w_up: float32 [2048, 6144], P(('wide', 'narrow'))
- grad_w_down: float32 [6144, 2048], P(('wide', 'narrow'))
- grad_norm2_gain: float32 [2048], P(('wide', 'narrow'))
The draws below stay inside these ranges and needn't reach their ends.
Inputs may be any that keep to these rules, and one draw needn't show every extreme that they name: `starts`: in each stream the 4 offsets increase, the first is 0, and every sequence holds 4 tokens or more of the 2048 tokens.
All inputs are finite; a program needn't handle non-finite values.
Results may differ from the reference program's by a relative error of at most 0.012.
Values may be sent and summed in bfloat16 or wider, within the bound.
A program may use at most 448 MiB of HBM per device.

```python
import jax
import jax.numpy as jnp
from jax import lax

D = 2048
HEAD_W = 160
F = 6144
CONV = 4
NSEQ = 4
TOK_DEV = 256
R = 2560
STREAM_LEN = 2048
STREAMS = 4


def draw_starts(key, part):
    key = jax.random.fold_in(key, 11)
    keys = jax.random.split(key, 9)
    count = STREAM_LEN // TOK_DEV
    first = jax.random.randint(keys[0], (STREAMS,), 4, TOK_DEV // 2 + 1)
    second = jax.random.randint(keys[1], (STREAMS,), STREAM_LEN - TOK_DEV // 2, STREAM_LEN - 7)
    third = jax.random.randint(keys[2], (STREAMS,), second + 4, STREAM_LEN - 3)
    edge_dev = jax.random.randint(keys[3], (STREAMS,), 1, count // 3 + 1)
    past_dev = jax.random.randint(keys[4], (STREAMS,), edge_dev + 1, count - 2)
    inner_dev = jax.random.randint(keys[5], (STREAMS,), past_dev + 1, count - 1)
    edge_start = edge_dev * TOK_DEV
    past_start = past_dev * TOK_DEV + jax.random.randint(keys[6], (STREAMS,), 1, 4)
    inner_start = inner_dev * TOK_DEV + jax.random.randint(keys[7], (STREAMS,), TOK_DEV // 4, 3 * TOK_DEV // 4 + 1)
    zeros = jnp.zeros((STREAMS,), jnp.int32)
    spanning = jnp.stack([zeros, first, second, third], axis=1)
    spread_out = jnp.stack([zeros, edge_start, past_start, inner_start], axis=1)
    leader = jax.random.randint(keys[8], (), 0, STREAMS)
    chosen = (jnp.arange(STREAMS, dtype=jnp.int32) == leader)[:, None]
    return jnp.where(chosen, spanning, spread_out).astype(jnp.int32)


def shard_levels(key, extent, cuts, smallest, high):
    loudness = 1.0
    for dim, shards_of in cuts:
        heights = jax.random.uniform(jax.random.fold_in(jax.random.fold_in(key, 6), dim), (shards_of,), jnp.float32, smallest / len(cuts), high / len(cuts))
        loudness = loudness * jnp.repeat(jnp.exp(heights), extent[dim] // shards_of).reshape((-1,) + (1,) * (len(extent) - 1 - dim))
    return loudness


def scatter_about(stream_key, shape, width, reach, shards=(), kind=jnp.bfloat16):
    array = jax.random.normal(stream_key, shape, jnp.float32) * width
    if len(shards) > 0:
        array = shard_levels(stream_key, shape, shards, -0.22, 0.18) * array
    return jnp.clip(array, min=-reach, max=reach).astype(kind)


def setup_inputs(seed: int = 0) -> dict:
    key_list = jax.random.split(jax.random.key(seed), 21)
    return {
        "tokens": scatter_about(key_list[0], (STREAMS, STREAM_LEN, D), 1.0, 6.0, ((0, 4), (1, 8))),
        "starts": draw_starts(jax.random.fold_in(key_list[20], 71), 0),
        "init_state": scatter_about(key_list[2], (STREAMS, NSEQ, R), 0.5, 4.0, ((0, 4),), jnp.float32),
        "init_conv": scatter_about(key_list[3], (STREAMS, NSEQ, CONV - 1, R), 1.0, 6.0, ((0, 4),)),
        "w_y": scatter_about(key_list[4], (D, R), D ** -0.5, 0.125, ((0, 32),)),
        "w_x": scatter_about(key_list[5], (D, R), D ** -0.5, 0.125, ((0, 32),)),
        "gate_a": scatter_about(key_list[6], (R, HEAD_W), HEAD_W ** -0.5, 0.5, ((0, 32),)),
        "gate_i": scatter_about(key_list[7], (R, HEAD_W), HEAD_W ** -0.5, 0.5, ((0, 32),)),
        "w_out": scatter_about(key_list[8], (R, D), (R // 8) ** -0.5, 0.3125, ((0, 32),)),
        "norm1_gain": jnp.clip(1.0 + 0.1 * jax.random.normal(key_list[9], (D,), jnp.float32), 0.5, 1.5).astype(jnp.bfloat16),
        "conv_kernel": scatter_about(key_list[10], (CONV, R), 0.5, 3.0, ((1, 32),)),
        "conv_bias": scatter_about(key_list[11], (R,), 0.5, 3.0, ((0, 32),)),
        "bias_a": scatter_about(key_list[12], (R,), 1.0, 4.0, ((0, 32),)),
        "bias_i": scatter_about(key_list[13], (R,), 1.0, 4.0, ((0, 32),)),
        "decay_param": jnp.clip(-14.0 + 12.0 * jax.random.uniform(key_list[14], (R,), jnp.float32) ** shard_levels(key_list[14], (R,), ((0, 32),), -0.2, 0.2), -14.0, -2.0).astype(jnp.bfloat16),
        "w_gate": scatter_about(key_list[15], (D, F), D ** -0.5, 0.125, ((0, 32),)),
        "w_up": scatter_about(key_list[16], (D, F), D ** -0.5, 0.125, ((0, 32),)),
        "w_down": scatter_about(key_list[17], (F, D), (F // 4) ** -0.5, 0.15625, ((0, 32),)),
        "norm2_gain": jnp.clip(1.0 + 0.1 * jax.random.normal(key_list[18], (D,), jnp.float32), 0.5, 1.5).astype(jnp.bfloat16),
        "cotangent": scatter_about(key_list[19], (STREAMS, STREAM_LEN, D), 1.0, 6.0, ((0, 4), (1, 8))),
    }


EPS = 1e-06
FLOOR = 0.001
HIGH = lax.Precision.HIGHEST

@jax.custom_vjp
def low(v):
    return lax.optimization_barrier(v.astype(jnp.bfloat16)).astype(jnp.float32)

@jax.custom_vjp
def low_back(v):
    return v

def low_keep(v):
    return (low(v), None)

def low_pass(kept, grad):
    return (grad,)

def back_keep(v):
    return (v, None)

def back_low(kept, grad):
    return (low(grad),)
low.defvjp(low_keep, low_pass)
low_back.defvjp(back_keep, back_low)

def matmul(left, right):
    return jnp.dot(left, right, precision=HIGH)

def link(earlier, later):
    return (earlier[0] * later[0], later[0] * earlier[1] + later[1])

def stream_block(params, stream, offsets, state_init, conv_init):
    w_y, w_x, gate_a, gate_i, w_out, gain_one, kernel, conv_bias, bias_a, bias_i, decay, w_gate, w_up, w_down, gain_two = params
    length = stream.shape[0]
    back = kernel.shape[0] - 1
    head_w = gate_a.shape[1]
    heads = gate_a.shape[0] // head_w
    position = jnp.arange(length, dtype=jnp.int32)
    segment = lax.optimization_barrier(jnp.sum((position[:, None] >= offsets[None, :]).astype(jnp.int32), axis=1)) - 1
    begin = offsets[segment]
    opening = (position == begin)[:, None]
    scale_one = lax.rsqrt(lax.optimization_barrier(jnp.mean(stream * stream, axis=-1, keepdims=True)) + EPS)
    normed = low(stream * scale_one * gain_one)
    gate_in = low_back(matmul(normed, w_y))
    linear = low_back(low(matmul(normed, w_x)))
    conv = conv_bias + kernel[0] * linear
    for shift_by in range(1, back + 1):
        earlier = jnp.concatenate([jnp.zeros((shift_by, linear.shape[1]), linear.dtype), linear[:-shift_by]], 0)
        offset = position - shift_by - begin
        stored = conv_init[segment, jnp.clip(offset + back, 0, back - 1)]
        conv = conv + kernel[shift_by] * jnp.where((offset >= 0)[:, None], earlier, stored)
    conv = low_back(low(conv))
    blocks = conv.reshape(length, heads, head_w)
    rate = low_back(jnp.einsum('thi,hij->thj', blocks, gate_a.reshape(heads, head_w, head_w), precision=HIGH).reshape(length, -1) + bias_a)
    inflow = low_back(jnp.einsum('thi,hij->thj', blocks, gate_i.reshape(heads, head_w, head_w), precision=HIGH).reshape(length, -1) + bias_i)
    retain = jax.nn.sigmoid(rate)
    admit = jax.nn.sigmoid(inflow)
    log_a = -8.0 * retain * jax.nn.softplus(decay)
    decay_now = jnp.exp(log_a)
    mult = jnp.sqrt(jnp.maximum(-jnp.expm1(2.0 * log_a), FLOOR))
    drive = mult * admit * conv
    state_rows = state_init[segment]
    a_used = jnp.where(opening, 0.0, decay_now)
    b_used = jnp.where(opening, decay_now * state_rows + drive, drive)
    carried = lax.associative_scan(link, (a_used, b_used), axis=0)
    hidden = carried[1]
    mixed_in = low(hidden * jax.nn.gelu(gate_in))
    resid = stream + low_back(matmul(mixed_in, w_out))
    scale_two = lax.rsqrt(lax.optimization_barrier(jnp.mean(resid * resid, axis=-1, keepdims=True)) + EPS)
    normed_two = low(resid * scale_two * gain_two)
    gate = low_back(matmul(normed_two, w_gate))
    upward = low_back(matmul(normed_two, w_up))
    inner = low(jax.nn.gelu(gate) * upward)
    result = resid + low_back(matmul(inner, w_down))
    ends = jnp.concatenate([offsets[1:], jnp.full((1,), length, jnp.int32)]) - 1
    final_h = hidden[ends]
    final_c = linear[ends[:, None] - back + 1 + jnp.arange(back, dtype=jnp.int32)[None, :]]
    return (result, final_h, final_c)

def reference(tokens, starts, init_state, init_conv, w_y, w_x, gate_a, gate_i, w_out, norm1_gain, conv_kernel, conv_bias, bias_a, bias_i, decay_param, w_gate, w_up, w_down, norm2_gain, cotangent):
    params = tuple((v.astype(jnp.float32) for v in (w_y, w_x, gate_a, gate_i, w_out, norm1_gain, conv_kernel, conv_bias, bias_a, bias_i, decay_param, w_gate, w_up, w_down, norm2_gain)))
    inputs = tokens.astype(jnp.float32)
    conv_start = init_conv.astype(jnp.float32)

    def forward(weights, values):

        def single(items):
            return stream_block(weights, items[0], items[1], items[2], items[3])
        result, final_h, final_c = lax.map(jax.checkpoint(single), (values, starts, init_state, conv_start))
        return (result, (final_h, final_c))
    result, pull, finals = jax.vjp(forward, params, inputs, has_aux=True)
    grads, input_grad = pull(cotangent.astype(jnp.float32))
    return (result.astype(jnp.bfloat16), input_grad.astype(jnp.bfloat16), finals[0], finals[1].astype(jnp.bfloat16), grads[0], grads[1], grads[2], grads[3], grads[4], grads[5], grads[6], grads[7], grads[8], grads[9], grads[10], grads[11], grads[12], grads[13], grads[14])
```

```python
import functools

import jax
import jax.numpy as jnp
from jax import lax
from jax.experimental import pallas as pl
from jax.experimental.pallas import tpu as pltpu
from jax.sharding import Mesh
from jax.sharding import PartitionSpec as P

EPS = 1e-06
FLOOR = 0.001
BF = jnp.bfloat16
F32 = jnp.float32


def tdot(left, right):
    return lax.dot_general(left, right, (((0,), (0,)), ((), ())), preferred_element_type=F32)


def ndot(left, right):
    return lax.dot_general(left, right, (((1,), (1,)), ((), ())), preferred_element_type=F32)


def mdot(left, right):
    return jnp.dot(left, right, preferred_element_type=F32)


def pick(stacked, index, axis=0):
    return lax.dynamic_index_in_dim(stacked, index, axis, keepdims=False)


def swap_c(value):
    return lax.ppermute(value, "c", [(0, 1), (1, 0)])


def xor_u(value, k):
    size = lax.axis_size("b") * lax.axis_size("n")
    return lax.ppermute(value, ("b", "n"), [(i, i ^ k) for i in range(size)])


def xor_stream(value, k):
    size = lax.axis_size("n") * lax.axis_size("c")
    return lax.ppermute(value, ("n", "c"), [(i, i ^ k) for i in range(size)])


def shift_a(value, by):
    size = lax.axis_size("a")
    return lax.ppermute(value, "a", [(i, i + by) for i in range(size) if 0 <= i + by < size])


def cycle_a(value, by):
    size = lax.axis_size("a")
    return lax.ppermute(value, "a", [(i, (i + by) % size) for i in range(size)])


def chips():
    return lax.axis_size("b") * lax.axis_size("n")


def chip():
    return lax.axis_index("b") * lax.axis_size("n") + lax.axis_index("n")


def plane_gather(value):
    mine = jnp.stack([value] + [xor_u(value, k) for k in range(1, chips())])
    return jnp.concatenate([mine, swap_c(mine)])


def plane_scatter(parts):
    count = chips()
    parts = parts.reshape((2, count, -1) + parts.shape[1:])
    got = swap_c(parts[1].astype(BF))
    summed = parts[0].astype(F32) + got.astype(F32)
    low = summed.astype(BF)
    total = summed[0]
    for k in range(1, count):
        total = total + xor_u(low[k], k).astype(F32)
    return total


def exchange(pieces):
    c, u = lax.axis_index("c"), chip()
    both = jnp.stack([pick(pieces, c), swap_c(pick(pieces, 1 - c))])
    out = []
    for k in range(chips()):
        piece = pick(both, u ^ k, 1)
        out.append(piece if k == 0 else xor_u(piece, k))
    return jnp.stack(out, 1)


def by_owner(rel):
    c, u = lax.axis_index("c"), chip()
    rel = jnp.stack([pick(rel, c), pick(rel, 1 - c)])
    return jnp.stack([pick(rel, u ^ q, 1) for q in range(chips())], 1)


def scan_kernel(reverse, a_ref, b_ref, p_ref, s_ref):
    blocks, rows, width = a_ref.shape
    groups = rows // 8
    row = lax.broadcasted_iota(jnp.int32, (blocks, 8, width), 1)
    if reverse:
        row = 7 - row

    def step(i, carry):
        cp, cs = carry
        g = groups - 1 - i if reverse else i
        at = pl.ds(pl.multiple_of(g * 8, 8), 8)
        a, b = a_ref[:, at, :], b_ref[:, at, :]
        for d in (1, 2, 4):
            by = 8 - d if reverse else d
            inside = row >= d
            a_far = jnp.where(inside, pltpu.roll(a, by, 1), 1.0)
            b_far = jnp.where(inside, pltpu.roll(b, by, 1), 0.0)
            b = a * b_far + b
            a = a * a_far
        b = a * cs + b
        a = a * cp
        p_ref[:, at, :] = a
        s_ref[:, at, :] = b
        last = 0 if reverse else 7
        return a[:, last : last + 1], b[:, last : last + 1]

    start = (jnp.ones((blocks, 1, width), F32), jnp.zeros((blocks, 1, width), F32))
    lax.fori_loop(0, groups, step, start)


def scan(a, b, reverse):
    blocks, rows, width = a.shape
    per = 4
    spec = pl.BlockSpec((per, rows, width), lambda i: (i, 0, 0))
    return pl.pallas_call(
        functools.partial(scan_kernel, reverse),
        grid=(blocks // per,),
        in_specs=[spec, spec],
        out_specs=[spec, spec],
        out_shape=[jax.ShapeDtypeStruct(a.shape, F32)] * 2,
        compiler_params=pltpu.CompilerParams(vmem_limit_bytes=48 * 1024 * 1024),
        name="scan",
    )(a, b)


def on_device(
    tokens,
    starts,
    init_state,
    init_conv,
    w_y,
    w_x,
    gate_a,
    gate_i,
    w_out,
    norm1_gain,
    conv_kernel,
    conv_bias,
    bias_a,
    bias_i,
    decay_param,
    w_gate,
    w_up,
    w_down,
    norm2_gain,
    cotangent,
):
    planes, count = lax.axis_size("a"), chips()
    a, b, n, c = (lax.axis_index(name) for name in ("a", "b", "n", "c"))
    u = chip()
    nn = count // 2
    rows, d_model = tokens.shape[1], tokens.shape[2]
    nseq = starts.shape[1]
    width = w_y.shape[1]
    head_w = gate_a.shape[1]
    half = gate_a.shape[0]
    taps = conv_kernel.shape[0]
    back = taps - 1
    heads_here = planes // 2
    wide_here = heads_here * head_w
    hid = w_down.shape[0]
    drows = w_y.shape[0]
    nblocks = 2 * count

    def head_pieces(w):
        w = w.reshape(w.shape[0], 2, heads_here, count, head_w)
        return w.transpose(1, 3, 0, 2, 4).reshape(2, count, w.shape[0], wide_here)

    def from_head_pieces(pieces):
        r = pieces.shape[2]
        pieces = pieces.reshape(2, count, r, heads_here, head_w)
        return pieces.transpose(2, 0, 3, 1, 4).reshape(r, width)

    def hidden_pieces(w):
        w = w.reshape(w.shape[0], planes, count, 2, hid)
        return w.transpose(3, 2, 0, 1, 4).reshape(2, count, w.shape[0], planes * hid)

    def from_hidden_pieces(pieces):
        r = pieces.shape[2]
        pieces = pieces.reshape(2, count, r, planes, hid)
        return pieces.transpose(2, 3, 1, 0, 4).reshape(r, planes * count * 2 * hid)

    def row_blocks(owned):
        return owned.swapaxes(0, 1).reshape((-1,) + owned.shape[3:])

    def to_owner_rows(full):
        return full.reshape((count, 2, -1) + full.shape[1:]).swapaxes(0, 1)

    def gather_a(value):
        return lax.all_gather(value, "a", axis=0, tiled=True)

    def scatter_a(value):
        return lax.psum_scatter(value, "a", scatter_dimension=0, tiled=True)

    packed = jnp.concatenate([head_pieces(w_y), head_pieces(w_x)], -1)
    w_yx = gather_a(row_blocks(by_owner(exchange(packed))))

    def join_halves(mine_all):
        away = swap_c(lax.dynamic_slice_in_dim(mine_all, (1 - c) * heads_here, heads_here, 0))
        own = lax.dynamic_slice_in_dim(mine_all, c * heads_here, heads_here, 0)
        first = jnp.where(c == 0, own, away)
        second = jnp.where(c == 0, away, own)
        return jnp.stack([first, second], 1).reshape((wide_here,) + mine_all.shape[2:])

    def part_halves(full):
        full = full.reshape((heads_here, 2, half) + full.shape[1:])
        own, away = pick(full, c, 1), swap_c(pick(full, 1 - c, 1))
        first = jnp.where(c == 0, own, away)
        second = jnp.where(c == 0, away, own)
        return jnp.concatenate([first, second], 0).reshape((planes * half,) + full.shape[3:])

    mixer_rows = jnp.concatenate([w_out, gate_a, gate_i], 1)
    mixer_rows = join_halves(gather_a(mixer_rows).reshape(planes, half, -1))
    w_o = mixer_rows[:, :d_model]

    def block_diagonal(m):
        m = m.reshape(heads_here, head_w, head_w)
        eye = jnp.eye(heads_here, dtype=m.dtype)
        return (m[:, :, None, :] * eye[:, None, :, None]).reshape(wide_here, wide_here)

    w_gates = jnp.concatenate(
        [
            block_diagonal(mixer_rows[:, d_model : d_model + head_w]),
            block_diagonal(mixer_rows[:, d_model + head_w :]),
        ],
        1,
    )

    packed = jnp.concatenate([hidden_pieces(w_gate), hidden_pieces(w_up)], -1)
    w_gu = gather_a(row_blocks(by_owner(exchange(packed))))
    w_d = gather_a(w_down)
    f_here = planes * hid

    vectors = jnp.concatenate(
        [conv_kernel, conv_bias[None], bias_a[None], bias_i[None], decay_param[None]], 0
    ).reshape(-1)
    small = jnp.concatenate([vectors, norm1_gain, norm2_gain])
    small = jnp.stack([small] + [xor_u(small, k) for k in range(1, count)])
    small = jnp.stack([small, swap_c(small)])
    small = jnp.stack([small] + [cycle_a(small, d) for d in range(1, planes)])
    small = small.reshape(planes * nblocks, -1)
    rel = jnp.arange(planes * nblocks, dtype=jnp.int32)
    r_a, r_c, r_u = rel // nblocks, (rel // count) % 2, rel % count
    owner = ((a - r_a + planes) % planes) * nblocks + (u ^ r_u) * 2 + (c ^ r_c)
    order = (rel[:, None] == owner[None, :]).astype(BF)
    canon = mdot(order, small)
    nvec = (taps + 4) * half
    gain_one = canon[:, nvec : nvec + drows].reshape(-1)
    gain_two = canon[:, nvec + drows :].reshape(-1)
    mine = pick(canon[:, :nvec].reshape(2, heads_here, count, 2, taps + 4, half), c)
    mine = pick(mine, u, 1).transpose(2, 0, 1, 3).reshape(taps + 4, wide_here)
    kernel, cbias, abias, ibias, decay_f = (
        mine[:taps], mine[taps], mine[taps + 1], mine[taps + 2], mine[taps + 3]
    )
    gate_bias = jnp.concatenate([abias, ibias])

    def my_channels(v):
        lead = v.shape[:-1]
        v = v.reshape(lead + (2, heads_here, count, head_w))
        v = pick(v, c, len(lead))
        return pick(v, u, len(lead) + 1).reshape(lead + (wide_here,))

    streams = 2 * nn
    at_start = jnp.concatenate([init_state[0][:, None], init_conv[0].astype(F32)], 1)
    at_start = jnp.concatenate([at_start.reshape(-1), starts[0].astype(F32)])
    rel_streams = [at_start] + [xor_stream(at_start, k) for k in range(1, streams)]
    at_start = jnp.stack([rel_streams[kn * 2 + kc] for kc in range(2) for kn in range(nn)])
    offsets = at_start[:, -nseq:].astype(jnp.int32)
    at_start = my_channels(at_start[:, :-nseq].reshape(streams, nseq, taps, width))
    state_0 = at_start[:, :, 0]
    conv_0 = at_start[:, :, 1:].reshape(streams, nseq * back, wide_here).astype(BF)

    def per_block(v):
        v = v.reshape((2, 1, nn) + v.shape[1:])
        return jnp.broadcast_to(v, (2, 2, nn) + v.shape[3:]).reshape((nblocks,) + v.shape[3:])

    block_b = (jnp.arange(nblocks, dtype=jnp.int32) // nn) % 2
    first_row = (a * 2 + (b ^ block_b)) * rows
    position = first_row[:, None] + jnp.arange(rows, dtype=jnp.int32)[None]
    off_b = per_block(offsets)

    def segment_of(where_at):
        return jnp.sum((where_at[:, :, None] >= off_b[:, None, :]).astype(jnp.int32), 2) - 1

    segment = segment_of(position)
    member = segment[:, :, None] == jnp.arange(nseq, dtype=jnp.int32)
    begin = jnp.sum(jnp.where(member, off_b[:, None, :], 0), 2)
    opening = position == begin

    def norm(value, gain):
        factor = lax.rsqrt(jnp.mean(value * value, axis=-1, keepdims=True) + EPS)
        return factor, (value * factor * gain).astype(BF)

    inputs = tokens[0].astype(F32)
    normed = norm(plane_gather(tokens[0]).reshape(nblocks * rows, d_model).astype(F32), gain_one)[1]
    prod = mdot(normed, w_yx)
    gate_in = prod[:, :wide_here].reshape(nblocks, rows, wide_here)
    linear = prod[:, wide_here:].astype(BF).reshape(nblocks, rows, wide_here)

    def two(v):
        return v.reshape((2, 2, nn) + v.shape[1:])

    def flip(v):
        v = two(v)
        return jnp.stack([v[:, 1], v[:, 0]], 1).reshape((nblocks,) + v.shape[3:])

    def of_stream(v, which):
        v = two(v)
        return jnp.where(b == which, v[:, 0], v[:, 1]).reshape((streams,) + v.shape[3:])

    def second_half(shape):
        return ((b ^ block_b) == 1).reshape((nblocks,) + (1,) * (len(shape) - 1))

    tail = linear[:, rows - back :]
    rim = per_block(shift_a(of_stream(tail, 1), 1))
    rim = jnp.where(second_half(rim.shape), flip(tail), rim)
    extended = jnp.concatenate([rim, linear], 1)
    conv_0b = per_block(conv_0)
    slots = jnp.arange(back, dtype=jnp.int32)
    by_tap = [linear.astype(F32)]
    for k in range(1, taps):
        offset = position - k - begin
        hot = member[:, :, :, None] & ((offset + back)[:, :, None, None] == slots)
        hot = hot.reshape(nblocks, rows, nseq * back).astype(BF)
        stored = lax.dot_general(
            hot, conv_0b, (((2,), (1,)), ((0,), (0,))), preferred_element_type=F32
        )
        earlier = extended[:, back - k : back - k + rows].astype(F32)
        by_tap.append(jnp.where((offset >= 0)[:, :, None], earlier, stored))
    conv_sum = cbias
    for k in range(taps):
        conv_sum = conv_sum + kernel[k] * by_tap[k]
    conv_low = conv_sum.astype(BF)
    conv_val = conv_low.astype(F32)
    conv_flat = conv_low.reshape(-1, wide_here)
    gates = jax.nn.sigmoid(mdot(conv_flat, w_gates) + gate_bias)
    retain = gates[:, :wide_here].reshape(nblocks, rows, wide_here)
    admit = gates[:, wide_here:].reshape(nblocks, rows, wide_here)
    soft_decay = jax.nn.softplus(decay_f)
    log_a = -8.0 * retain * soft_decay
    decay_now = jnp.exp(log_a)
    spread = -jnp.expm1(2.0 * log_a)
    mult = jnp.sqrt(jnp.maximum(spread, FLOOR))
    drive = mult * admit * conv_val
    state_0b = per_block(state_0)
    state_rows = jnp.zeros_like(drive)
    for s in range(nseq):
        state_rows = jnp.where(member[:, :, s, None], state_0b[:, s, None], state_rows)
    open_3 = opening[:, :, None]
    a_used = jnp.where(open_3, 0.0, decay_now)
    b_used = jnp.where(open_3, decay_now * state_rows + drive, drive)
    carry_mul, carry_add = scan(a_used, b_used, False)

    def entering(mul, add, reverse):
        pair = jnp.stack([mul, add])
        near = of_stream(pair.swapaxes(0, 1), 1 if reverse else 0)
        far = of_stream(pair.swapaxes(0, 1), 0 if reverse else 1)
        whole = jnp.stack([near[:, 0] * far[:, 0], far[:, 0] * near[:, 1] + far[:, 1]])
        came = [shift_a(whole, -d if reverse else d) for d in range(1, planes)]
        value = came[-1][1]
        for part in came[-2::-1]:
            value = part[0] * value + part[1]
        to_far = near[:, 0] * value + near[:, 1]
        value, to_far = per_block(value), per_block(to_far)
        is_far = second_half(value.shape)
        return jnp.where(is_far != reverse, to_far, value)

    state_in = entering(carry_mul[:, -1], carry_add[:, -1], False)[:, None]
    hidden = carry_mul * state_in + carry_add
    gelu_y, gelu_y_back = jax.vjp(jax.nn.gelu, gate_in)
    mixed_in = (hidden * gelu_y).astype(BF).reshape(-1, wide_here)
    resid = inputs + plane_scatter(mdot(mixed_in, w_o))
    scale_two, normed_two = norm(resid, gain_two)
    normed_two = plane_gather(normed_two).reshape(nblocks * rows, d_model)
    grad_low = cotangent[0]
    grads = plane_gather(grad_low).reshape(nblocks * rows, d_model)

    pair = mdot(normed_two, w_gu)
    gate, upward = pair[:, :f_here], pair[:, f_here:]
    active, gate_back = jax.vjp(jax.nn.gelu, gate)
    inner = (active * upward).astype(BF)
    result = (resid + plane_scatter(mdot(inner, w_d))).astype(BF)
    d_inner = ndot(grads, w_d)
    grad_wd = scatter_a(tdot(inner, grads).astype(BF)).astype(F32)
    d_gate = gate_back(d_inner * upward)[0].astype(BF)
    d_up = (d_inner * active).astype(BF)
    d_pair = jnp.concatenate([d_gate, d_up], 1)
    d_normed_two = plane_scatter(ndot(d_pair, w_gu))
    sums = scatter_a(tdot(normed_two, d_pair).astype(BF))
    sums = by_owner(exchange(to_owner_rows(sums)))
    grad_wg = from_hidden_pieces(sums[..., :f_here]).astype(F32)
    grad_wu = from_hidden_pieces(sums[..., f_here:]).astype(F32)

    def norm_back(value, factor, gain, grad):
        weighted = grad * gain
        inner = jnp.mean(weighted * value, axis=-1, keepdims=True)
        return factor * weighted - value * factor * factor * factor * inner

    d_resid = grad_low.astype(F32) + norm_back(resid, scale_two, gain_two, d_normed_two)
    d_resid_low = plane_gather(d_resid.astype(BF)).reshape(nblocks * rows, d_model)

    d_mixed = ndot(d_resid_low, w_o).reshape(nblocks, rows, wide_here)
    sums_o = tdot(mixed_in, d_resid_low).astype(BF)
    grad_wo = scatter_a(part_halves(sums_o)).astype(F32)
    d_hidden = d_mixed * gelu_y
    d_gate_in = gelu_y_back(d_mixed * hidden)[0].astype(BF).reshape(-1, wide_here)
    forward_mul = jnp.concatenate([a_used[:, 1:], jnp.ones((nblocks, 1, wide_here), F32)], 1)
    back_mul, back_add = scan(forward_mul, d_hidden, True)
    grad_in = entering(a_used[:, 0] * back_mul[:, 0], a_used[:, 0] * back_add[:, 0], True)[:, None]
    total_grad = back_mul * grad_in + back_add
    previous = jnp.concatenate([state_in, hidden[:, :-1]], 1)
    previous = jnp.where(open_3, state_rows, previous)
    d_decay = total_grad * previous
    d_mult = total_grad * admit * conv_val
    d_admit = total_grad * mult * conv_val
    d_conv = total_grad * mult * admit
    d_spread = jnp.where(spread > FLOOR, d_mult * 0.5 / mult, 0.0)
    d_log = d_decay * decay_now - 2.0 * decay_now * decay_now * d_spread
    d_retain = d_log * (-8.0 * soft_decay)
    grad_decay = jnp.sum(d_log * (-8.0 * retain), axis=(0, 1)) * jax.nn.sigmoid(decay_f)
    d_rate = (d_retain * retain * (1.0 - retain)).astype(BF)
    d_inflow = (d_admit * admit * (1.0 - admit)).astype(BF)
    grad_abias = jnp.sum(d_rate.astype(F32), axis=(0, 1))
    grad_ibias = jnp.sum(d_inflow.astype(F32), axis=(0, 1))
    d_gates = jnp.concatenate([d_rate, d_inflow], 2).reshape(-1, 2 * wide_here)
    d_conv = d_conv + ndot(d_gates, w_gates).reshape(d_conv.shape)
    sums_gates = tdot(conv_flat, d_gates)

    def diagonal(m):
        m = m.reshape(heads_here, head_w, heads_here, head_w)
        return jnp.concatenate([m[h, :, h] for h in range(heads_here)], 0)

    grad_gates = jnp.concatenate(
        [diagonal(sums_gates[:, :wide_here]), diagonal(sums_gates[:, wide_here:])], 1
    )
    d_conv_low = d_conv.astype(BF)
    d_conv_val = d_conv_low.astype(F32)
    head = d_conv_low[:, :back]
    rim_back = per_block(shift_a(of_stream(head, 0), -1))
    rim_back = jnp.where(second_half(head.shape), rim_back, flip(head))
    ahead = jnp.concatenate([d_conv_low, rim_back], 1)
    d_linear = kernel[0] * d_conv_val
    kernel_grads = [jnp.sum(d_conv_val * by_tap[0], axis=(0, 1))]
    for k in range(1, taps):
        later_rows = ahead[:, k : k + rows].astype(F32)
        same = (segment_of(position + k) == segment)[:, :, None]
        d_linear = d_linear + kernel[k] * jnp.where(same, later_rows, 0.0)
        kernel_grads.append(jnp.sum(d_conv_val * by_tap[k], axis=(0, 1)))
    grad_cbias = jnp.sum(d_conv_val, axis=(0, 1))
    vec_grads = jnp.stack(kernel_grads + [grad_cbias, grad_abias, grad_ibias, grad_decay], 1)
    late = jnp.concatenate([grad_gates, vec_grads], 1).astype(BF)
    late = scatter_a(part_halves(late)).astype(F32)
    grad_wa, grad_wi = late[:, :head_w], late[:, head_w : 2 * head_w]
    vec_grads = late[:, 2 * head_w :].T

    d_linear_low = d_linear.astype(BF).reshape(-1, wide_here)
    d_both = jnp.concatenate([d_gate_in, d_linear_low], 1)
    d_normed = plane_scatter(ndot(d_both, w_yx))
    sums = scatter_a(tdot(normed, d_both).astype(BF))
    sums = by_owner(exchange(to_owner_rows(sums)))
    grad_wy = from_head_pieces(sums[..., :wide_here]).astype(F32)
    grad_wx = from_head_pieces(sums[..., wide_here:]).astype(F32)
    scale_one = lax.rsqrt(jnp.mean(inputs * inputs, axis=-1, keepdims=True) + EPS)
    input_grad = (d_resid + norm_back(inputs, scale_one, gain_one, d_normed)).astype(BF)

    def gain_grad(gain, *pairs):
        total = sum(jnp.sum(w.astype(F32) * g, axis=1) for w, g in pairs)
        return total / gain.astype(F32)

    grad_gain_one = gain_grad(norm1_gain, (w_y, grad_wy), (w_x, grad_wx))
    grad_gain_two = gain_grad(norm2_gain, (w_gate, grad_wg), (w_up, grad_wu))

    end = jnp.concatenate(
        [offsets[:, 1:], jnp.full((streams, 1), planes * 2 * rows, jnp.int32)], 1
    )
    end_b = per_block(end) - 1
    hot = (position[:, None, :] == end_b[:, :, None]).astype(BF)
    lasts = lax.dot_general(
        hot, hidden.astype(BF), (((2,), (1,)), ((0,), (0,))), preferred_element_type=F32
    )
    where_conv = (end_b[:, :, None] - back + 1 + slots).reshape(nblocks, nseq * back)
    hot = (position[:, None, :] == where_conv[:, :, None]).astype(BF)
    conv_lasts = lax.dot_general(
        hot, linear, (((2,), (1,)), ((0,), (0,))), preferred_element_type=F32
    )
    lasts = two(jnp.concatenate([lasts, conv_lasts], 1))
    lasts = (lasts[:, 0] + lasts[:, 1]).astype(BF)
    came = [cycle_a(lasts, d) for d in range(1, planes)]
    lasts = sum(part.astype(F32) for part in [lasts] + came).astype(BF)
    both = jnp.stack([lasts[0], swap_c(lasts[1])])
    found = jnp.stack(
        [both[:, k % nn] if k == 0 else xor_u(both[:, k % nn], k) for k in range(count)], 1
    )
    found = by_owner(found).reshape(2, count, nseq * taps, heads_here, head_w)
    found = found.transpose(2, 0, 3, 1, 4).reshape(nseq * taps, width)
    final_state = found[:nseq].astype(F32)
    final_conv = found[nseq:].reshape(nseq, back, width)

    return (
        result[None],
        input_grad[None],
        final_state[None],
        final_conv[None],
        grad_wy,
        grad_wx,
        grad_wa,
        grad_wi,
        grad_wo,
        grad_gain_one,
        vec_grads[:taps],
        vec_grads[taps],
        vec_grads[taps + 1],
        vec_grads[taps + 2],
        vec_grads[taps + 3],
        grad_wg,
        grad_wu,
        grad_wd,
        grad_gain_two,
    )


WIDE = ("a", "b")
EVERY = ("a", "b", "n", "c")
HIGH = lax.Precision.HIGHEST


def passed_along(value, axis, by):
    size = lax.axis_size(axis)
    pairs = [(i, i + by) for i in range(size) if 0 <= i + by < size]
    return lax.ppermute(value, axis, pairs)


def entering(value, axis, combine, identity, reverse):
    size, place = (lax.axis_size(axis), lax.axis_index(axis))
    everything = jax.tree.map(lambda part: lax.all_gather(part, axis), value)
    start = jax.tree.map(
        lambda part, zero: jnp.broadcast_to(jnp.asarray(zero, part.dtype), part.shape),
        value,
        identity,
    )

    def hop(k, before):
        at = size - 1 - k if reverse else k
        reached = at > place if reverse else at < place
        new = combine(before, jax.tree.map(lambda part: part[at], everything))
        return jax.tree.map(lambda a, b: jnp.where(reached, a, b), new, before)

    return lax.fori_loop(0, size, hop, start)


def merged_2(value, axis, combine):
    everything = jax.tree.map(
        lambda part, kind: lax.all_gather(part.astype(kind), axis),
        value,
        jax.tree.map(lambda a: jnp.bfloat16 if a.dtype == jnp.float32 else a.dtype, value),
    )

    def take(k):
        return jax.tree.map(lambda part, own: part[k].astype(own.dtype), everything, value)

    return lax.fori_loop(
        1, lax.axis_size(axis), lambda k, so_far: combine(so_far, take(k)), take(0)
    )


def link(earlier, later):
    return (earlier[0] * later[0], later[0] * earlier[1] + later[1])


def norm_back(value, factor, gain, grad):
    weighted = grad * gain
    inner = jnp.mean(weighted * value, axis=-1, keepdims=True)
    return (
        factor * weighted - value * factor * factor * factor * inner,
        jnp.sum(grad * value * factor, axis=0),
    )


def later_one(first, second):
    pick = first[0] > second[0]
    return (
        jnp.where(pick, first[0], second[0]),
        jnp.where(pick[:, None], first[1], second[1]),
        jnp.where(pick[:, None, None], first[2], second[2]),
    )


def on_device_any(
    tokens,
    starts,
    init_state,
    init_conv,
    w_y,
    w_x,
    gate_a,
    gate_i,
    w_out,
    norm1_gain,
    conv_kernel,
    conv_bias,
    bias_a,
    bias_i,
    decay_param,
    w_gate,
    w_up,
    w_down,
    norm2_gain,
    cotangent,
):
    inputs = tokens[0].astype(jnp.float32)
    offsets = starts[0]
    nseqs = offsets.shape[0]
    rows_here = inputs.shape[0]
    width = w_y.shape[1]
    head_w = gate_a.shape[1]
    heads = width // head_w
    place = lax.axis_index(WIDE)
    mixer = (
        lax.all_gather(w_y, EVERY, axis=0, tiled=True),
        lax.all_gather(w_x, EVERY, axis=0, tiled=True),
        lax.all_gather(gate_a, EVERY, axis=0, tiled=True),
        lax.all_gather(gate_i, EVERY, axis=0, tiled=True),
        lax.all_gather(w_out, EVERY, axis=0, tiled=True),
        lax.all_gather(norm1_gain, EVERY, axis=0, tiled=True),
        lax.all_gather(conv_kernel, EVERY, axis=1, tiled=True),
        lax.all_gather(conv_bias, EVERY, axis=0, tiled=True),
        lax.all_gather(bias_a, EVERY, axis=0, tiled=True),
        lax.all_gather(bias_i, EVERY, axis=0, tiled=True),
        lax.all_gather(decay_param, EVERY, axis=0, tiled=True),
    )
    wy_full, wx_full, wa_full, wi_full, wo_full, gain_one, kernel, cbias, abias, ibias, decay = (
        mixer
    )
    gain_one = gain_one.astype(jnp.float32)
    kernel = kernel.astype(jnp.float32)
    taps = kernel.shape[0]
    back = taps - 1
    position = place * rows_here + jnp.arange(rows_here, dtype=jnp.int32)

    def segment_of(where_at):
        return jnp.sum((where_at[:, None] >= offsets[None, :]).astype(jnp.int32), axis=1) - 1

    segment = segment_of(position)
    member = segment[:, None] == jnp.arange(nseqs, dtype=jnp.int32)[None, :]
    begin = jnp.sum(jnp.where(member, offsets[None, :], 0), axis=1)
    opening = (position == begin)[:, None]
    scale_one = lax.rsqrt(jnp.mean(inputs * inputs, axis=-1, keepdims=True) + EPS)
    normed = (inputs * scale_one * gain_one).astype(jnp.bfloat16)
    gate_in = mdot(normed, wy_full)
    linear = mdot(normed, wx_full).astype(jnp.bfloat16)
    rim_rows = passed_along(linear[rows_here - back :], WIDE, 1)
    extended = jnp.concatenate([rim_rows, linear], 0)
    stored = mdot(member.astype(jnp.bfloat16), init_conv[0].reshape(nseqs, back * width)).reshape(
        rows_here, back, width
    )
    inputs_by_tap = [linear.astype(jnp.float32)]
    for shift_by in range(1, taps):
        earlier = extended[back - shift_by : back - shift_by + rows_here].astype(jnp.float32)
        offset = position - shift_by - begin
        from_start = jnp.zeros((rows_here, width), jnp.float32)
        for slot in range(back):
            from_start = from_start + jnp.where(
                (offset + back == slot)[:, None], stored[:, slot], 0.0
            )
        inputs_by_tap.append(jnp.where((offset >= 0)[:, None], earlier, from_start))
    conv_sum = cbias.astype(jnp.float32)
    for shift_by in range(taps):
        conv_sum = conv_sum + kernel[shift_by] * inputs_by_tap[shift_by]
    conv_low = conv_sum.astype(jnp.bfloat16)
    conv_val = conv_low.astype(jnp.float32)
    blocks = conv_low.reshape(rows_here, heads, head_w)
    wa_heads = wa_full.reshape(heads, head_w, head_w)
    wi_heads = wi_full.reshape(heads, head_w, head_w)
    rate = jnp.einsum("thi,hij->thj", blocks, wa_heads, preferred_element_type=jnp.float32).reshape(
        rows_here, width
    ) + abias.astype(jnp.float32)
    inflow = jnp.einsum(
        "thi,hij->thj", blocks, wi_heads, preferred_element_type=jnp.float32
    ).reshape(rows_here, width) + ibias.astype(jnp.float32)
    retain = jax.nn.sigmoid(rate)
    admit = jax.nn.sigmoid(inflow)
    decay_f = decay.astype(jnp.float32)
    soft_decay = jax.nn.softplus(decay_f)
    log_a = -8.0 * retain * soft_decay
    decay_now = jnp.exp(log_a)
    spread = -jnp.expm1(2.0 * log_a)
    mult = jnp.sqrt(jnp.maximum(spread, FLOOR))
    drive = mult * admit * conv_val
    state_rows = jnp.dot(member.astype(jnp.float32), init_state[0], precision=HIGH)
    a_used = jnp.where(opening, 0.0, decay_now)
    b_used = jnp.where(opening, decay_now * state_rows + drive, drive)
    carry_mul, carry_add = lax.associative_scan(link, (a_used, b_used), axis=0)
    identity = (jnp.ones((width,), jnp.float32), jnp.zeros((width,), jnp.float32))
    state_in = entering(
        (carry_mul[rows_here - 1], carry_add[rows_here - 1]), WIDE, link, identity, False
    )[1]
    hidden = carry_mul * state_in + carry_add
    gelu_y, gelu_y_back = jax.vjp(jax.nn.gelu, gate_in)
    mixed_in = (hidden * gelu_y).astype(jnp.bfloat16)
    resid = inputs + mdot(mixed_in, wo_full)
    wg_full, wu_full, wd_full, gain_two = (
        lax.all_gather(w_gate, EVERY, axis=0, tiled=True),
        lax.all_gather(w_up, EVERY, axis=0, tiled=True),
        lax.all_gather(w_down, EVERY, axis=0, tiled=True),
        lax.all_gather(norm2_gain, EVERY, axis=0, tiled=True),
    )
    gain_two = gain_two.astype(jnp.float32)
    scale_two = lax.rsqrt(jnp.mean(resid * resid, axis=-1, keepdims=True) + EPS)
    normed_two = (resid * scale_two * gain_two).astype(jnp.bfloat16)
    gate = mdot(normed_two, wg_full)
    upward = mdot(normed_two, wu_full)
    active, gate_back = jax.vjp(jax.nn.gelu, gate)
    inner = (active * upward).astype(jnp.bfloat16)
    result = (resid + mdot(inner, wd_full)).astype(jnp.bfloat16)
    local_rows = jnp.arange(rows_here, dtype=jnp.int32)
    last_row = jnp.max(jnp.where(member, local_rows[:, None], -1), axis=0)
    present = last_row >= 0
    safe_row = jnp.maximum(last_row, 0)
    marker = jnp.where(present, (place * rows_here + last_row).astype(jnp.float32), -1.0)
    state_last = jnp.where(present[:, None], hidden[safe_row], 0.0)
    conv_rows = extended[safe_row[:, None] + 1 + jnp.arange(back, dtype=jnp.int32)[None, :]].astype(
        jnp.float32
    )
    conv_last = jnp.where(present[:, None, None], conv_rows, 0.0)
    merged = merged_2((marker, state_last, conv_last), WIDE, later_one)
    wg_back, wu_back, wd_back = (
        lax.all_gather(w_gate, EVERY, axis=0, tiled=True),
        lax.all_gather(w_up, EVERY, axis=0, tiled=True),
        lax.all_gather(w_down, EVERY, axis=0, tiled=True),
    )
    grad_low = cotangent[0]
    grad_out = grad_low.astype(jnp.float32)
    d_inner = ndot(grad_low, wd_back)
    grad_wd = tdot(inner, grad_low)
    d_gate = gate_back(d_inner * upward)[0].astype(jnp.bfloat16)
    d_up = (d_inner * active).astype(jnp.bfloat16)
    grad_wg = tdot(normed_two, d_gate)
    grad_wu = tdot(normed_two, d_up)
    d_normed_two = ndot(d_gate, wg_back) + ndot(d_up, wu_back)
    d_resid_norm, grad_gain_two = norm_back(resid, scale_two, gain_two, d_normed_two)
    d_resid = grad_out + d_resid_norm
    wy_back, wx_back, wa_back, wi_back, wo_back = (
        lax.all_gather(w_y, EVERY, axis=0, tiled=True),
        lax.all_gather(w_x, EVERY, axis=0, tiled=True),
        lax.all_gather(gate_a, EVERY, axis=0, tiled=True),
        lax.all_gather(gate_i, EVERY, axis=0, tiled=True),
        lax.all_gather(w_out, EVERY, axis=0, tiled=True),
    )
    d_resid_low = d_resid.astype(jnp.bfloat16)
    d_mixed = ndot(d_resid_low, wo_back)
    grad_wo = tdot(mixed_in, d_resid_low)
    d_hidden = d_mixed * gelu_y
    d_gate_in = gelu_y_back(d_mixed * hidden)[0].astype(jnp.bfloat16)
    forward_mul = jnp.concatenate([a_used[1:], jnp.ones((1, width), jnp.float32)], 0)
    back_mul, back_add = lax.associative_scan(link, (forward_mul, d_hidden), reverse=True, axis=0)
    head_map = (a_used[0] * back_mul[0], a_used[0] * back_add[0])
    grad_in = entering(head_map, WIDE, link, identity, True)[1]
    total_grad = back_mul * grad_in + back_add
    previous = jnp.concatenate([state_in[None], hidden[:-1]], 0)
    previous = jnp.where(opening, state_rows, previous)
    d_decay = total_grad * previous
    d_mult = total_grad * admit * conv_val
    d_admit = total_grad * mult * conv_val
    d_conv = total_grad * mult * admit
    d_spread = jnp.where(spread > FLOOR, d_mult * 0.5 / mult, 0.0)
    d_log = d_decay * decay_now - 2.0 * decay_now * decay_now * d_spread
    d_retain = d_log * (-8.0 * soft_decay)
    grad_decay = jnp.sum(d_log * (-8.0 * retain), axis=0) * jax.nn.sigmoid(decay_f)
    d_rate = (d_retain * retain * (1.0 - retain)).astype(jnp.bfloat16)
    d_inflow = (d_admit * admit * (1.0 - admit)).astype(jnp.bfloat16)
    grad_abias = jnp.sum(d_rate.astype(jnp.float32), axis=0)
    grad_ibias = jnp.sum(d_inflow.astype(jnp.float32), axis=0)
    rate_heads = d_rate.reshape(rows_here, heads, head_w)
    inflow_heads = d_inflow.reshape(rows_here, heads, head_w)
    grad_wa = jnp.einsum(
        "thi,thj->hij", blocks, rate_heads, preferred_element_type=jnp.float32
    ).reshape(width, head_w)
    grad_wi = jnp.einsum(
        "thi,thj->hij", blocks, inflow_heads, preferred_element_type=jnp.float32
    ).reshape(width, head_w)
    d_conv = d_conv + jnp.einsum(
        "thj,hij->thi",
        rate_heads,
        wa_back.reshape(heads, head_w, head_w),
        preferred_element_type=jnp.float32,
    ).reshape(rows_here, width)
    d_conv = d_conv + jnp.einsum(
        "thj,hij->thi",
        inflow_heads,
        wi_back.reshape(heads, head_w, head_w),
        preferred_element_type=jnp.float32,
    ).reshape(rows_here, width)
    d_conv_low = d_conv.astype(jnp.bfloat16)
    d_conv_val = d_conv_low.astype(jnp.float32)
    rim_back = passed_along(d_conv_low[:back], WIDE, -1)
    ahead = jnp.concatenate([d_conv_low, rim_back], 0)
    d_linear = kernel[0] * d_conv_val
    kernel_grads = [jnp.sum(d_conv_val * inputs_by_tap[0], axis=0)]
    for shift_by in range(1, taps):
        later_rows = ahead[shift_by : shift_by + rows_here].astype(jnp.float32)
        same = (segment_of(position + shift_by) == segment)[:, None]
        d_linear = d_linear + kernel[shift_by] * jnp.where(same, later_rows, 0.0)
        kernel_grads.append(jnp.sum(d_conv_val * inputs_by_tap[shift_by], axis=0))
    grad_kernel = jnp.stack(kernel_grads, 0)
    grad_cbias = jnp.sum(d_conv_val, axis=0)
    d_linear_low = d_linear.astype(jnp.bfloat16)
    d_normed = ndot(d_gate_in, wy_back) + ndot(d_linear_low, wx_back)
    grad_wy = tdot(normed, d_gate_in)
    grad_wx = tdot(normed, d_linear_low)
    d_input_norm, grad_gain_one = norm_back(inputs, scale_one, gain_one, d_normed)
    input_grad = (d_resid + d_input_norm).astype(jnp.bfloat16)
    every_sum = (
        lax.psum_scatter(grad_wy, EVERY, scatter_dimension=0, tiled=True),
        lax.psum_scatter(grad_wx, EVERY, scatter_dimension=0, tiled=True),
        lax.psum_scatter(grad_wa, EVERY, scatter_dimension=0, tiled=True),
        lax.psum_scatter(grad_wi, EVERY, scatter_dimension=0, tiled=True),
        lax.psum_scatter(grad_wo, EVERY, scatter_dimension=0, tiled=True),
        lax.psum_scatter(grad_gain_one, EVERY, scatter_dimension=0, tiled=True),
        lax.psum_scatter(grad_kernel, EVERY, scatter_dimension=1, tiled=True),
        lax.psum_scatter(grad_cbias, EVERY, scatter_dimension=0, tiled=True),
        lax.psum_scatter(grad_abias, EVERY, scatter_dimension=0, tiled=True),
        lax.psum_scatter(grad_ibias, EVERY, scatter_dimension=0, tiled=True),
        lax.psum_scatter(grad_decay, EVERY, scatter_dimension=0, tiled=True),
        lax.psum_scatter(grad_wg, EVERY, scatter_dimension=0, tiled=True),
        lax.psum_scatter(grad_wu, EVERY, scatter_dimension=0, tiled=True),
        lax.psum_scatter(grad_wd, EVERY, scatter_dimension=0, tiled=True),
        lax.psum_scatter(grad_gain_two, EVERY, scatter_dimension=0, tiled=True),
    )
    mixer_sums = every_sum[:11]
    mlp_sums = every_sum[11:]
    return (
        result[None],
        input_grad[None],
        merged[1][None],
        merged[2].astype(jnp.bfloat16)[None],
        mixer_sums[0],
        mixer_sums[1],
        mixer_sums[2],
        mixer_sums[3],
        mixer_sums[4],
        mixer_sums[5],
        mixer_sums[6],
        mixer_sums[7],
        mixer_sums[8],
        mixer_sums[9],
        mixer_sums[10],
        mlp_sums[0],
        mlp_sums[1],
        mlp_sums[2],
        mlp_sums[3],
    )


def solution(mesh):
    wide, narrow = mesh.shape["wide"], mesh.shape["narrow"]
    def plan(*args):
        fits = args[6].shape[0] * 2 == args[6].shape[1]
        return (on_device if fits else on_device_any)(*args)

    fine = Mesh(mesh.devices.reshape(wide // 2, 2, narrow // 2, 2), ("a", "b", "n", "c"))
    w, s = ("a", "b"), ("n", "c")
    everywhere = ("a", "b", "n", "c")
    acts, rows, vec = P(s, w, None), P(everywhere, None), P(everywhere)
    return jax.shard_map(
        plan,
        mesh=fine,
        in_specs=(
            acts,
            P(s, None),
            P(s, None, None),
            P(s, None, None, None),
            rows, rows, rows, rows, rows,
            vec,
            P(None, everywhere),
            vec, vec, vec, vec,
            rows, rows, rows,
            vec,
            acts,
        ),
        out_specs=(
            acts,
            acts,
            P(s, None, None),
            P(s, None, None, None),
            rows, rows, rows, rows, rows,
            vec,
            P(None, everywhere),
            vec, vec, vec, vec,
            rows, rows, rows,
            vec,
        ),
        check_vma=False,
    )
```

```python
import functools

import jax
import jax.numpy as jnp
from jax import lax
from jax.experimental import pallas as pl
from jax.experimental.pallas import tpu as pltpu
from jax.sharding import Mesh
from jax.sharding import PartitionSpec as P

EPS = 1e-06
FLOOR = 0.001
BF = jnp.bfloat16
F32 = jnp.float32


def tdot(left, right):
    return lax.dot_general(left, right, (((0,), (0,)), ((), ())), preferred_element_type=F32)


def ndot(left, right):
    return lax.dot_general(left, right, (((1,), (1,)), ((), ())), preferred_element_type=F32)


def mdot(left, right):
    return jnp.dot(left, right, preferred_element_type=F32)


def pick(stacked, index, axis=0):
    return lax.dynamic_index_in_dim(stacked, index, axis, keepdims=False)


def swap_c(value):
    return lax.ppermute(value, "c", [(0, 1), (1, 0)])


def xor_u(value, k):
    size = lax.axis_size("b") * lax.axis_size("n")
    return lax.ppermute(value, ("b", "n"), [(i, i ^ k) for i in range(size)])


def shift_a(value, by):
    size = lax.axis_size("a")
    return lax.ppermute(value, "a", [(i, i + by) for i in range(size) if 0 <= i + by < size])


def cycle_a(value, by):
    size = lax.axis_size("a")
    return lax.ppermute(value, "a", [(i, (i + by) % size) for i in range(size)])


def chips():
    return lax.axis_size("b") * lax.axis_size("n")


def chip():
    return lax.axis_index("b") * lax.axis_size("n") + lax.axis_index("n")


def plane_gather(value):
    mine = jnp.stack([value] + [xor_u(value, k) for k in range(1, chips())])
    return jnp.concatenate([mine, swap_c(mine)])


def exchange(pieces):
    c, u = lax.axis_index("c"), chip()
    both = jnp.stack([pick(pieces, c), swap_c(pick(pieces, 1 - c))])
    out = []
    for k in range(chips()):
        piece = pick(both, u ^ k, 1)
        out.append(piece if k == 0 else xor_u(piece, k))
    return jnp.stack(out, 1)


def by_owner(rel):
    c, u = lax.axis_index("c"), chip()
    rel = jnp.stack([pick(rel, c), pick(rel, 1 - c)])
    return jnp.stack([pick(rel, u ^ q, 1) for q in range(chips())], 1)


MESH = pl.DeviceIdType.MESH
VMEM_LIMIT = 60 * 1024 * 1024


def places():
    return tuple(lax.axis_index(name) for name in ("a", "b", "n", "c"))


def neighbours():
    a, b, n, c = places()
    return (a, 1 - b, n, c), (a, b, 1 - n, c), (a, b, n, 1 - c)


def greet(peers):
    barrier = pltpu.get_barrier_semaphore()
    for peer in peers:
        pl.semaphore_signal(barrier, inc=1, device_id=peer, device_id_type=MESH)
    pl.semaphore_wait(barrier, len(peers))


class Mover:
    def __init__(self, send, recv):
        self.send, self.recv, self.made = send, recv, {}
        self.names = []

    def copy(self, name, src, dst, peer):
        if name not in self.names:
            self.names.append(name)
        at = self.names.index(name)
        made = pltpu.make_async_remote_copy(
            src_ref=src,
            dst_ref=dst,
            send_sem=self.send.at[at],
            recv_sem=self.recv.at[at],
            device_id=peer,
            device_id_type=MESH,
        )
        self.made[name] = made
        return made

    def start(self, name, src, dst, peer):
        self.copy(name, src, dst, peer).start()

    def arrived(self, name):
        self.made[name].wait_recv()

    def sent(self):
        for made in self.made.values():
            made.wait_send()


def gather_plane_start(move, mine, everyone, h, half_rows):
    x, y, z = neighbours()
    at = pl.ds(h * half_rows, half_rows)
    move.start(f"gx{h}", mine.at[at], everyone.at[2, at], x)
    move.start(f"gy{h}", mine.at[at], everyone.at[1, at], y)
    move.start(f"gc{h}", mine.at[at], everyone.at[4, at], z)


def gather_plane_rest(move, everyone, half_rows, stage=None):
    x, y, z = neighbours()
    rows = [pl.ds(h * half_rows, half_rows) for h in range(2)]

    def on(name, k, h):
        move.start(name, everyone.at[k, rows[h]], everyone.at[4 + k, rows[h]], z)

    if stage in (None, 0):
        move.arrived("gx0")
        move.start("fy", everyone.at[2, rows[0]], everyone.at[3, rows[0]], y)
        on("cx0", 2, 0)
        move.arrived("gy1")
        move.start("fx", everyone.at[1, rows[1]], everyone.at[3, rows[1]], x)
        on("cy1", 1, 1)
    if stage in (None, 1):
        move.arrived("gx1")
        on("cx1", 2, 1)
        move.arrived("gy0")
        on("cy0", 1, 0)
    if stage in (None, 2):
        move.arrived("fy")
        on("cd0", 3, 0)
        move.arrived("fx")
        on("cd1", 3, 1)
        for name in ("gc0", "gc1", "cx0", "cx1", "cy0", "cy1", "cd0", "cd1"):
            move.arrived(name)


GATHER_COPIES = 14


def reduce_kernel(nt, post, waits, x_hbm, w_hbm, *refs):
    gain_ref, first_ref, second_ref = refs[:3]
    out_ref, refs = refs[3 + waits], refs[4 + waits :]
    if post == "last":
        everyone = mine = None
    else:
        everyone, refs = refs[0], refs[1:]
        mine, refs = refs[0], refs[1:]
    x_v, w_v, away_s, away_r, acc, out_b, in_b, local, send, recv = refs
    rows, d_model = acc.shape[1:]
    half = rows // 2
    tile = min(512, d_model)
    px, py, pc = neighbours()
    move = Mover(send, recv)

    w_copy = pltpu.make_async_copy(w_hbm, w_v, local.at[8])
    w_copy.start()
    loads = {}
    for i, (k, kc) in enumerate((k, kc) for k in (3, 2, 1, 0) for kc in (1, 0)):
        loads[kc, k] = pltpu.make_async_copy(x_hbm.at[kc, k], x_v.at[kc, k], local.at[i])
        loads[kc, k].start()
    greet((px, py, pc))
    w_copy.wait()

    def product(kc, k, t):
        at = pl.ds(pl.multiple_of(t * tile, tile), tile)
        if nt:
            return at, ndot(x_v[kc, k], w_v[at, :])
        return at, mdot(x_v[kc, k], w_v[:, at])

    step = min(32, half)

    def by_rows(h, body):
        @pl.loop(0, half // step)
        def _(i):
            body(pl.ds(pl.multiple_of(i * step, step), step),
                 pl.ds(pl.multiple_of(h * half + i * step, step), step))

    def hand_on(name, slot, k, h, peer, extra=None):
        def body(inner, outer):
            value = acc[k, outer, :]
            if extra is not None:
                value = value + in_b[extra, inner, :].astype(F32)
            out_b[slot, inner, :] = value.astype(BF)

        by_rows(h, body)
        move.start(name, out_b.at[slot], in_b.at[slot], peer)

    for k in (3, 2, 1, 0):
        loads[1, k].wait()

        @pl.loop(0, d_model // tile)
        def _(t):
            at, value = product(1, k, t)
            away_s[k, :, at] = value.astype(BF)

        move.start(f"away{k}", away_s.at[k], away_r.at[k], pc)
        loads[0, k].wait()

        @pl.loop(0, d_model // tile)
        def _(t):
            at, value = product(0, k, t)
            acc[k, :, at] = value

        move.arrived(f"away{k}")
        for h in range(2):
            def add(inner, outer):
                acc[k, outer, :] += away_r[k, outer, :].astype(F32)

            by_rows(h, add)
        if k == 3:
            hand_on("d0", 0, 3, 0, px)
            hand_on("d1", 1, 3, 1, py)
        elif k == 2:
            hand_on("x0", 2, 2, 0, px)
        elif k == 1:
            hand_on("y1", 5, 1, 1, py)
    move.arrived("d0")
    hand_on("y0", 4, 1, 0, py, 0)
    move.arrived("d1")
    hand_on("x1", 3, 2, 1, px, 1)

    for h in range(2):
        move.arrived(f"x{h}")
        move.arrived(f"y{h}")

        def body(inner, outer):
            total = acc[0, outer, :]
            total = total + in_b[2 + h, inner, :].astype(F32)
            total = total + in_b[4 + h, inner, :].astype(F32)
            gain = gain_ref[...]
            if post == "fwd":
                value = first_ref[outer, :].astype(F32) + total
                out_ref[outer, :] = value
                factor = lax.rsqrt(jnp.mean(value * value, axis=-1, keepdims=True) + EPS)
                mine[outer, :] = (value * factor * gain).astype(BF)
                return
            value = second_ref[outer, :] if post == "mid" else first_ref[outer, :].astype(F32)
            base = first_ref[outer, :].astype(F32) if post == "mid" else second_ref[outer, :]
            factor = lax.rsqrt(jnp.mean(value * value, axis=-1, keepdims=True) + EPS)
            weighted = total * gain
            inner_mean = jnp.mean(weighted * value, axis=-1, keepdims=True)
            grad = base + factor * weighted - value * (factor * factor * factor * inner_mean)
            if post == "mid":
                out_ref[outer, :] = grad
                mine[outer, :] = grad.astype(BF)
            else:
                out_ref[outer, :] = grad.astype(BF)

        by_rows(h, body)
        if everyone is not None:
            gather_plane_start(move, mine, everyone, h, half)
    if everyone is not None:
        own = pltpu.make_async_copy(mine, everyone.at[0], local.at[9])
        own.start()
        gather_plane_rest(move, everyone, half)
        own.wait()
    move.sent()


def plane_reduce(ident, post, nt, x, w, gain, first, second, done=()):
    rows, d_model = first.shape
    vmem = pl.BlockSpec(memory_space=pltpu.VMEM)
    hbm = pl.BlockSpec(memory_space=pl.ANY)
    out_type = BF if post == "last" else F32
    out_shape = [jax.ShapeDtypeStruct((rows, d_model), out_type)]
    out_specs = [vmem]
    scratch = []
    copies = 10
    if post != "last":
        out_shape.append(jax.ShapeDtypeStruct((8, rows, d_model), BF))
        out_specs.append(hbm)
        scratch.append(pltpu.VMEM((rows, d_model), BF))
        copies += GATHER_COPIES
    scratch += [
        pltpu.VMEM(x.shape, BF),
        pltpu.VMEM(w.shape, BF),
        pltpu.VMEM((4, rows, d_model), BF),
        pltpu.VMEM((4, rows, d_model), BF),
        pltpu.VMEM((4, rows, d_model), F32),
        pltpu.VMEM((6, rows // 2, d_model), BF),
        pltpu.VMEM((6, rows // 2, d_model), BF),
        pltpu.SemaphoreType.DMA((10,)),
        pltpu.SemaphoreType.DMA((copies,)),
        pltpu.SemaphoreType.DMA((copies,)),
    ]
    return pl.pallas_call(
        functools.partial(reduce_kernel, nt, post, len(done)),
        in_specs=[hbm, hbm, vmem, vmem, vmem] + [hbm] * len(done),
        out_specs=out_specs,
        out_shape=out_shape,
        scratch_shapes=scratch,
        compiler_params=pltpu.CompilerParams(
            collective_id=ident, has_side_effects=True, vmem_limit_bytes=VMEM_LIMIT
        ),
        cost_estimate=pl.CostEstimate(
            flops=2 * x.size * d_model, bytes_accessed=2 * (x.size + w.size), transcendentals=0
        ),
        name=f"plane_reduce_{post}",
    )(x, w, gain.reshape(1, -1), first, second, *done)


def start_kernel(
    tokens_ref, yx_ref, gu_ref, rows_ref, vec_ref, stream_ref,
    tok_out, yx_out, gu_out, rows_out, halves_out, vec_out, stream_out,
    local, send, recv,
):
    a, b, n, c = places()
    planes = yx_out.shape[0]
    u = b * 2 + n
    p = u * 2 + c
    px, py, pc = neighbours()
    plane_peers = {}
    for kc in range(2):
        for k in range(4):
            if (kc, k) != (0, 0):
                b2 = 1 - b if k & 2 else b
                n2 = 1 - n if k & 1 else n
                plane_peers[kc, k] = (a, b2, n2, 1 - c if kc else c)
    up, down = (a + 1, b, n, c), (a - 1, b, n, c)

    barrier = pltpu.get_barrier_semaphore()
    for peer in plane_peers.values():
        pl.semaphore_signal(barrier, inc=1, device_id=peer, device_id_type=MESH)

    @pl.when(a < planes - 1)
    def _():
        pl.semaphore_signal(barrier, inc=1, device_id=up, device_id_type=MESH)

    @pl.when(a > 0)
    def _():
        pl.semaphore_signal(barrier, inc=1, device_id=down, device_id_type=MESH)

    others = len(plane_peers) + jnp.minimum(planes - 1 - a, 1) + jnp.minimum(a, 1)
    pl.semaphore_wait(barrier, others)

    move = Mover(send, recv)
    half = tokens_ref.shape[0] // 2
    locals_ = []

    def keep(i, src, dst):
        made = pltpu.make_async_copy(src, dst, local.at[i])
        made.start()
        return made

    def to_owners(name, pieces, out):
        for (kc, k), peer in plane_peers.items():
            owner = (u ^ k) * 2 + (1 - c if kc else c)
            move.start(f"{name}{kc}{k}", pieces.at[owner], out.at[a, p], peer)

    chains = {}

    def chain_step(name, out, s):
        def up_copy(block):
            return move.copy(f"{name}u{s}", out.at[block], out.at[block], up)

        def down_copy(block):
            return move.copy(f"{name}d{s}", out.at[block], out.at[block], down)

        sends_up, sends_down = (a < planes - 1) & (a >= s), (a > 0) & (a + s < planes)

        @pl.when(sends_up)
        def _():
            up_copy(a - s).start()

        @pl.when(sends_down)
        def _():
            down_copy(a + s).start()

        chains[name, s] = (up_copy, down_copy, sends_up, sends_down)

    def chain_arrived(name, s):
        up_copy, down_copy, _, _ = chains[name, s]

        @pl.when(a - 1 >= s)
        def _():
            up_copy(a - 1 - s).wait_recv()

        @pl.when(a + 1 + s < planes)
        def _():
            down_copy(a + 1 + s).wait_recv()

    def chain_sent(name, s):
        up_copy, down_copy, sends_up, sends_down = chains[name, s]

        @pl.when(sends_up)
        def _():
            up_copy(a - s).wait_send()

        @pl.when(sends_down)
        def _():
            down_copy(a + s).wait_send()

    to_owners("yx", yx_ref, yx_out)
    for (kc, k), peer in plane_peers.items():
        move.start(f"vec{kc}{k}", vec_ref, vec_out.at[a, p], peer)
    own_yx = keep(1, yx_ref.at[p], yx_out.at[a, p])
    own_vec = keep(2, vec_ref, vec_out.at[a, p])
    own_rows = keep(0, rows_ref, rows_out.at[a])
    own_gu = keep(3, gu_ref.at[p], gu_out.at[p])
    own_tok = keep(4, tokens_ref, tok_out.at[0])
    own_stream = keep(5, stream_ref, stream_out.at[0, 0])
    own_yx.wait()
    own_vec.wait()
    for kc, k in plane_peers:
        move.arrived(f"yx{kc}{k}")
        move.arrived(f"vec{kc}{k}")
    own_rows.wait()
    outs = (("yx", yx_out), ("vec", vec_out), ("rows", rows_out))
    for name, out in outs:
        chain_step(name, out, 0)
    for h in range(2):
        gather_plane_start(move, tokens_ref, tok_out, h, half)
    gather_plane_rest(move, tok_out, half, 0)
    for kc in range(2):
        for kn in range(2):
            if (kc, kn) != (0, 0):
                move.start(f"st{kc}{kn}", stream_ref, stream_out.at[kc, kn], plane_peers[kc, kn])
    for name, out in outs:
        chain_arrived(name, 0)
        chain_step(name, out, 1)
    gather_plane_rest(move, tok_out, half, 1)
    for (kc, k), peer in plane_peers.items():
        owner = (u ^ k) * 2 + (1 - c if kc else c)
        move.start(f"gu{kc}{k}", gu_ref.at[owner], gu_out.at[p], peer)
    for s in range(1, planes - 1):
        for name, out in outs:
            chain_arrived(name, s)
            if s + 1 < planes - 1:
                chain_step(name, out, s + 1)
    gather_plane_rest(move, tok_out, half, 2)
    each = planes // 2
    swap = pltpu.make_async_remote_copy(
        src_ref=rows_out.at[pl.ds((1 - c) * each, each)],
        dst_ref=halves_out.at[:, c],
        send_sem=send.at[send.shape[0] - 1],
        recv_sem=recv.at[recv.shape[0] - 1],
        device_id=pc,
        device_id_type=MESH,
    )
    swap.start()
    own_halves = keep(6, rows_out.at[pl.ds(c * each, each)], halves_out.at[:, c])
    for kc, k in plane_peers:
        move.arrived(f"gu{kc}{k}")
    for kc in range(2):
        for kn in range(2):
            if (kc, kn) != (0, 0):
                move.arrived(f"st{kc}{kn}")
    for made in (own_gu, own_tok, own_stream, own_halves):
        made.wait()
    swap.wait()
    for name, s in chains:
        chain_sent(name, s)
    for name in [n for n in move.names if not any(n == f"{w}{d}{s}" for w, s in chains for d in "ud")]:
        move.made[name].wait_send()


def start_exchange(tokens, yx, gu, mixer_rows, vec, stream):
    planes = lax.axis_size("a")
    hbm = pl.BlockSpec(memory_space=pl.ANY)
    shapes = [
        ((8,) + tokens.shape, BF),
        ((planes,) + yx.shape, BF),
        (gu.shape, BF),
        ((planes,) + mixer_rows.shape, BF),
        ((planes // 2, 2) + mixer_rows.shape, BF),
        ((planes, 8) + vec.shape, F32),
        ((2, 2) + stream.shape, F32),
    ]
    copies = 7 * 3 + 3 + GATHER_COPIES + 6 * (planes - 1) + 1
    return pl.pallas_call(
        start_kernel,
        in_specs=[hbm] * 6,
        out_specs=[hbm] * 7,
        out_shape=[jax.ShapeDtypeStruct(*s) for s in shapes],
        scratch_shapes=[
            pltpu.SemaphoreType.DMA((7,)),
            pltpu.SemaphoreType.DMA((copies,)),
            pltpu.SemaphoreType.DMA((copies,)),
        ],
        compiler_params=pltpu.CompilerParams(
            collective_id=1, has_side_effects=True, vmem_limit_bytes=VMEM_LIMIT
        ),
        cost_estimate=pl.CostEstimate(flops=0, bytes_accessed=100 << 20, transcendentals=0),
        name="start_exchange",
    )(tokens, yx, gu, mixer_rows, vec, stream)


def norm_product_kernel(info, tok_ref, w_ref, gain_ref, n_ref, gate_ref, lin_ref):
    rows, d_model = tok_ref.shape[1:]
    step = min(64, rows)

    @pl.loop(0, rows // step)
    def _(i):
        at = pl.ds(pl.multiple_of(i * step, step), step)
        value = tok_ref[0, at, :].astype(F32)
        factor = lax.rsqrt(jnp.mean(value * value, axis=-1, keepdims=True) + EPS)
        n_ref[0, at, :] = (value * factor * gain_ref[...]).astype(BF)

    wide = gate_ref.shape[2]
    both = mdot(n_ref[0], w_ref[...])
    gate_ref[0] = both[:, :wide]
    lin_ref[0] = both[:, wide:].astype(BF)


def row_places(info, rows, nseq):
    i = pl.program_id(0)
    pos = info[i, 0] + lax.broadcasted_iota(jnp.int32, (rows, 1), 0)
    begin = jnp.zeros((rows, 1), jnp.int32) + info[i, 1]
    seg = jnp.zeros((rows, 1), jnp.int32)
    for s in range(1, nseq):
        begin = jnp.where(pos >= info[i, 1 + s], info[i, 1 + s], begin)
        seg = jnp.where(pos >= info[i, 1 + s], s, seg)
    return pos, begin, seg


def inputs_by_tap(ext, lin_ref, rim_ref, conv0_ref, begin_at, seg, taps):
    rows = lin_ref.shape[1]
    back = taps - 1
    ext[0:8, :] = rim_ref[0]
    ext[8 : 8 + rows, :] = lin_ref[0].astype(F32)
    slots = conv0_ref.shape[1]
    column = lax.broadcasted_iota(jnp.int32, (rows, slots), 1)
    found = [ext[8 : 8 + rows, :]]
    for k in range(1, taps):
        hot = (column == seg * back + begin_at - k + back) & (begin_at < k)
        stored = mdot(jnp.where(hot, 1.0, 0.0).astype(BF), conv0_ref[0])
        found.append(jnp.where(begin_at >= k, ext[8 - k : 8 - k + rows, :], stored))
    return found


def run_scan(a_s, b_s, p_ref, s_ref, rows, reverse):
    width = b_s.shape[1]
    groups = rows // 8
    row = lax.broadcasted_iota(jnp.int32, (8, width), 0)
    if reverse:
        row = 7 - row

    def step(i, carry):
        cp, cs = carry
        g = groups - 1 - i if reverse else i
        at = pl.ds(pl.multiple_of(g * 8, 8), 8)
        a, b = a_s[at, :], b_s[at, :]
        for d in (1, 2, 4):
            by = 8 - d if reverse else d
            inside = row >= d
            a_far = jnp.where(inside, pltpu.roll(a, by, 0), 1.0)
            b_far = jnp.where(inside, pltpu.roll(b, by, 0), 0.0)
            b = a * b_far + b
            a = a * a_far
        b = a * cs + b
        a = a * cp
        p_ref[0, at, :] = a
        s_ref[0, at, :] = b
        last = 0 if reverse else 7
        return a[last : last + 1], b[last : last + 1]

    start = (jnp.ones((1, width), F32), jnp.zeros((1, width), F32))
    lax.fori_loop(0, groups, step, start, unroll=4)


V_CBIAS, V_ABIAS, V_IBIAS, V_SOFT = 0, 1, 2, 3


def forward_kernel(
    nseq, taps, info, lin_ref, rim_ref, conv0_ref, state0_ref, wg_ref, vec_ref,
    conv_ref, retain_ref, admit_ref, p_ref, s_ref, ext, a_s, b_s,
):
    i = pl.program_id(0)
    rows, wide = lin_ref.shape[1:]
    pos, begin, seg = row_places(info, rows, nseq)
    at = pos - begin

    def vec(k):
        return vec_ref[k : k + 1, :]

    by_tap = inputs_by_tap(ext, lin_ref, rim_ref, conv0_ref, at, seg, taps)
    total = vec(taps + V_CBIAS)
    for k in range(taps):
        total = total + vec(k) * by_tap[k]
    low = total.astype(BF)
    conv_ref[0] = low
    conv = low.astype(F32)
    both = mdot(low, wg_ref[...])
    retain = jax.nn.sigmoid(both[:, :wide] + vec(taps + V_ABIAS))
    admit = jax.nn.sigmoid(both[:, wide:] + vec(taps + V_IBIAS))
    retain_ref[0] = retain
    admit_ref[0] = admit
    a = jnp.exp(-8.0 * retain * vec(taps + V_SOFT))
    mult = jnp.sqrt(jnp.maximum((1.0 - a) * (1.0 + a), FLOOR))
    drive = mult * admit * conv
    for s in range(nseq):
        drive = drive + jnp.where(pos == info[i, 1 + s], a * state0_ref[0, s : s + 1, :], 0.0)
    a_s[...] = jnp.where(at == 0, 0.0, a)
    b_s[...] = drive
    run_scan(a_s, b_s, p_ref, s_ref, rows, False)


def gelu_pair(x):
    root = 0.7978845608028654
    inner = root * (x + 0.044715 * (x * x * x))
    th = jnp.tanh(inner)
    cdf = 0.5 * (1.0 + th)
    slope = cdf + 0.5 * x * (1.0 - th * th) * (root * (1.0 + 3.0 * 0.044715 * (x * x)))
    return x * cdf, slope


def back_scan_kernel(
    nseq, taps, info, dres_ref, wo_ref, gate_ref, hidden_ref, retain_ref, vec_ref, *refs
):
    dgate_ref, p_ref, s_ref, head_ref, ext, a_s, b_s = refs[-7:]
    rows = gate_ref.shape[1]
    pos, begin, _ = row_places(info, rows, nseq)
    d_mixed = ndot(dres_ref[0], wo_ref[...])
    gelu, slope = gelu_pair(gate_ref[0])
    dgate_ref[0] = (d_mixed * hidden_ref[0] * slope).astype(BF)
    b_s[...] = d_mixed * gelu
    soft = vec_ref[taps + V_SOFT : taps + V_SOFT + 1, :]
    a = jnp.where(pos == begin, 0.0, jnp.exp(-8.0 * retain_ref[0] * soft))
    ext[0:rows, :] = a
    ext[rows : rows + 8, :] = jnp.ones((8, a.shape[1]), F32)
    head_ref[0] = ext[0:8, :]
    a_s[...] = ext[1 : rows + 1, :]
    run_scan(a_s, b_s, p_ref, s_ref, rows, True)


def back_kernel(
    nseq, taps, info, p_ref, s_ref, grad_in_ref, hidden_ref, state_in_ref, state0_ref, conv_ref,
    retain_ref, admit_ref, lin_ref, rim_ref, conv0_ref, wg_ref, vec_ref, *refs
):
    dconv_ref, wgrad_ref, vgrad_ref, ext = refs[-4:]
    i = pl.program_id(0)
    rows, wide = lin_ref.shape[1:]
    pos, begin, seg = row_places(info, rows, nseq)
    at = pos - begin
    conv_low = conv_ref[0]
    conv = conv_low.astype(F32)
    retain, admit = retain_ref[0], admit_ref[0]
    soft = vec_ref[taps + V_SOFT : taps + V_SOFT + 1, :]
    e = p_ref[0] * grad_in_ref[0, 0:1, :] + s_ref[0]
    ext[0:8, :] = jnp.broadcast_to(state_in_ref[0], (8, wide))
    ext[8 : 8 + rows, :] = hidden_ref[0]
    previous = ext[7 : 7 + rows, :]
    for s in range(nseq):
        previous = jnp.where(pos == info[i, 1 + s], state0_ref[0, s : s + 1, :], previous)
    a = jnp.exp(-8.0 * retain * soft)
    spread = (1.0 - a) * (1.0 + a)
    mult = jnp.sqrt(jnp.maximum(spread, FLOOR))
    d_mult = e * admit * conv
    d_spread = jnp.where(spread > FLOOR, d_mult * 0.5 / mult, 0.0)
    d_log = e * previous * a - 2.0 * a * a * d_spread
    d_rate = (d_log * (-8.0 * soft) * retain * (1.0 - retain)).astype(BF)
    d_inflow = (e * mult * conv * admit * (1.0 - admit)).astype(BF)
    d_gates = jnp.concatenate([d_rate, d_inflow], 1)
    d_conv = e * mult * admit + ndot(d_gates, wg_ref[...])
    low = d_conv.astype(BF)
    dconv_ref[0] = low
    low = low.astype(F32)

    @pl.when(i == 0)
    def _():
        wgrad_ref[...] = jnp.zeros_like(wgrad_ref)
        vgrad_ref[...] = jnp.zeros_like(vgrad_ref)

    wgrad_ref[...] += tdot(conv_low, d_gates)
    sums = [low * v for v in inputs_by_tap(ext, lin_ref, rim_ref, conv0_ref, at, seg, taps)]
    sums += [low, d_rate.astype(F32), d_inflow.astype(F32), d_log * (-8.0 * retain)]
    for k, value in enumerate(sums):
        vgrad_ref[k : k + 1, :] += jnp.sum(value, axis=0, keepdims=True)


def back_conv_kernel(nseq, taps, info, dconv_ref, rim_ref, dgate_ref, vec_ref, out_ref, ext):
    i = pl.program_id(0)
    rows, wide = dconv_ref.shape[1:]
    pos = info[i, 0] + lax.broadcasted_iota(jnp.int32, (rows, 1), 0)
    ext[0:rows, :] = dconv_ref[0].astype(F32)
    ext[rows : rows + 8, :] = rim_ref[0]
    total = vec_ref[0:1, :] * ext[0:rows, :]
    for k in range(1, taps):
        cut = jnp.zeros((rows, 1), jnp.int32)
        for s in range(nseq):
            start = info[i, 1 + s]
            cut = jnp.where((pos < start) & (pos + k >= start), 1, cut)
        total = total + vec_ref[k : k + 1, :] * jnp.where(cut == 0, ext[k : k + rows, :], 0.0)
    out_ref[0, :, :wide] = dgate_ref[0]
    out_ref[0, :, wide:] = total.astype(BF)


def by_block(body, info, ins, outs, scratch, done=(), name=None, cost=None):
    blocks = info.shape[0]

    def spec(shape, blocked):
        zeros = (0,) * (len(shape) - 1)
        if blocked:
            return pl.BlockSpec((1,) + tuple(shape[1:]), lambda i, *_: (i,) + zeros)
        return pl.BlockSpec(tuple(shape), lambda i, *_: (0,) + zeros)

    hbm = pl.BlockSpec(memory_space=pl.ANY)
    return pl.pallas_call(
        body,
        grid_spec=pltpu.PrefetchScalarGridSpec(
            num_scalar_prefetch=1,
            grid=(blocks,),
            in_specs=[spec(v.shape, blocked) for v, blocked in ins] + [hbm] * len(done),
            out_specs=[spec(shape, blocked) for shape, _, blocked in outs],
            scratch_shapes=[pltpu.VMEM(shape, F32) for shape in scratch],
        ),
        out_shape=[jax.ShapeDtypeStruct(shape, kind) for shape, kind, _ in outs],
        compiler_params=pltpu.CompilerParams(vmem_limit_bytes=VMEM_LIMIT),
        cost_estimate=cost,
        name=name,
    )(info, *[v for v, _ in ins], *done)


def on_device(
    tokens,
    starts,
    init_state,
    init_conv,
    w_y,
    w_x,
    gate_a,
    gate_i,
    w_out,
    norm1_gain,
    conv_kernel,
    conv_bias,
    bias_a,
    bias_i,
    decay_param,
    w_gate,
    w_up,
    w_down,
    norm2_gain,
    cotangent,
):
    planes, count = lax.axis_size("a"), chips()
    a, b, n, c = (lax.axis_index(name) for name in ("a", "b", "n", "c"))
    u = chip()
    nn = count // 2
    rows, d_model = tokens.shape[1], tokens.shape[2]
    nseq = starts.shape[1]
    width = w_y.shape[1]
    head_w = gate_a.shape[1]
    half = gate_a.shape[0]
    taps = conv_kernel.shape[0]
    back = taps - 1
    heads_here = planes // 2
    wide_here = heads_here * head_w
    wp = -(-wide_here // 128) * 128
    hid = w_down.shape[0]
    drows = w_y.shape[0]
    nblocks = 2 * count

    def head_pieces(w):
        w = w.reshape(w.shape[0], 2, heads_here, count, head_w)
        return w.transpose(1, 3, 0, 2, 4).reshape(2, count, w.shape[0], wide_here)

    def from_head_pieces(pieces):
        r = pieces.shape[2]
        pieces = pieces.reshape(2, count, r, heads_here, head_w)
        return pieces.transpose(2, 0, 3, 1, 4).reshape(r, width)

    def hidden_pieces(w):
        w = w.reshape(w.shape[0], planes, count, 2, hid)
        return w.transpose(3, 2, 0, 1, 4).reshape(2, count, w.shape[0], planes * hid)

    def from_hidden_pieces(pieces):
        r = pieces.shape[2]
        pieces = pieces.reshape(2, count, r, planes, hid)
        return pieces.transpose(2, 3, 1, 0, 4).reshape(r, planes * count * 2 * hid)

    def row_blocks(owned):
        return owned.swapaxes(0, 1).reshape((-1,) + owned.shape[3:])

    def to_owner_rows(full):
        return full.reshape((count, 2, -1) + full.shape[1:]).swapaxes(0, 1)

    def gather_a(value):
        return lax.all_gather(value, "a", axis=0, tiled=True)

    def scatter_a(value):
        return lax.psum_scatter(value, "a", scatter_dimension=0, tiled=True)

    def padded(v, axis=-1):
        pads = [(0, 0)] * v.ndim
        pads[axis] = (0, wp - wide_here)
        return jnp.pad(v, pads)

    def owners(pieces):
        return pieces.swapaxes(0, 1).reshape((nblocks,) + pieces.shape[2:])

    vectors = jnp.concatenate(
        [conv_kernel, conv_bias[None], bias_a[None], bias_i[None], decay_param[None]], 0
    ).reshape(-1)
    vectors = jnp.concatenate([vectors, norm1_gain, norm2_gain]).astype(F32)
    lanes = -(-vectors.shape[0] // 1024) * 128
    vectors = jnp.pad(vectors, (0, 8 * lanes - vectors.shape[0])).reshape(8, lanes)
    at_start = jnp.concatenate([init_state[0][:, None], init_conv[0].astype(F32)], 1)
    at_start = at_start.reshape(nseq * taps, width)
    at_start = jnp.pad(at_start, ((0, 8), (0, 0)))
    at_start = at_start.at[nseq * taps, :nseq].set(starts[0].astype(F32))
    all_tokens, w_yx, w_gu, _, gate_rows, canon, at_start = start_exchange(
        tokens[0],
        owners(jnp.concatenate([head_pieces(w_y), head_pieces(w_x)], -1)),
        owners(jnp.concatenate([hidden_pieces(w_gate), hidden_pieces(w_up)], -1)),
        jnp.concatenate([gate_a, gate_i], 1),
        vectors,
        at_start,
    )
    w_yx = w_yx.reshape(d_model, 2 * wide_here)
    w_yx = jnp.concatenate([padded(w_yx[:, :wide_here]), padded(w_yx[:, wide_here:])], 1)
    w_gu = gather_a(w_gu.reshape(-1, 2 * planes * hid))
    gate_rows = gate_rows.reshape(wide_here, -1)

    def join_halves(mine_all):
        away = swap_c(lax.dynamic_slice_in_dim(mine_all, (1 - c) * heads_here, heads_here, 0))
        own = lax.dynamic_slice_in_dim(mine_all, c * heads_here, heads_here, 0)
        first = jnp.where(c == 0, own, away)
        second = jnp.where(c == 0, away, own)
        return jnp.stack([first, second], 1).reshape((wide_here,) + mine_all.shape[2:])


    def part_halves(full):
        full = full.reshape((heads_here, 2, half) + full.shape[1:])
        own, away = pick(full, c, 1), swap_c(pick(full, 1 - c, 1))
        first = jnp.where(c == 0, own, away)
        second = jnp.where(c == 0, away, own)
        return jnp.concatenate([first, second], 0).reshape((planes * half,) + full.shape[3:])

    w_o = padded(join_halves(gather_a(w_out).reshape(planes, half, d_model)), 0)

    def block_diagonal(m):
        m = m.reshape(heads_here, head_w, head_w)
        eye = jnp.eye(heads_here, dtype=m.dtype)
        full = (m[:, :, None, :] * eye[:, None, :, None]).reshape(wide_here, wide_here)
        return padded(padded(full), 0)

    w_gates = jnp.concatenate(
        [
            block_diagonal(gate_rows[:, :head_w]),
            block_diagonal(gate_rows[:, head_w:]),
        ],
        1,
    )

    w_d = gather_a(w_down)
    f_here = planes * hid

    canon = canon.reshape(planes * nblocks, -1)
    nvec = (taps + 4) * half
    gain_one = canon[:, nvec : nvec + drows].reshape(-1)
    gain_two = canon[:, nvec + drows : nvec + 2 * drows].reshape(-1)
    mine = pick(canon[:, :nvec].reshape(2, heads_here, count, 2, taps + 4, half), c)
    mine = pick(mine, u, 1).transpose(2, 0, 1, 3).reshape(taps + 4, wide_here)
    decay_f = mine[taps + 3]
    vec = padded(jnp.concatenate([mine[: taps + 3], jax.nn.softplus(decay_f)[None]]))

    def my_channels(v):
        lead = v.shape[:-1]
        v = v.reshape(lead + (2, heads_here, count, head_w))
        v = pick(v, c, len(lead))
        return pick(v, u, len(lead) + 1).reshape(lead + (wide_here,))

    streams = 2 * nn
    at_start = at_start.reshape(streams, -1, width)
    offsets = at_start[:, nseq * taps, :nseq].astype(jnp.int32)
    at_start = my_channels(at_start[:, : nseq * taps].reshape(streams, nseq, taps, width))
    at_start = padded(at_start)
    state_0 = jnp.pad(at_start[:, :, 0], ((0, 0), (0, -nseq % 8), (0, 0)))
    conv_0 = at_start[:, :, 1:].reshape(streams, nseq * back, wp).astype(BF)
    conv_0 = jnp.pad(conv_0, ((0, 0), (0, -(nseq * back) % 16), (0, 0)))

    def per_block(v):
        v = v.reshape((2, 1, nn) + v.shape[1:])
        return jnp.broadcast_to(v, (2, 2, nn) + v.shape[3:]).reshape((nblocks,) + v.shape[3:])

    block_b = (jnp.arange(nblocks, dtype=jnp.int32) // nn) % 2
    first_row = (a * 2 + (b ^ block_b)) * rows
    position = first_row[:, None] + jnp.arange(rows, dtype=jnp.int32)[None]
    off_b = per_block(offsets)

    info = jnp.concatenate(
        [first_row[:, None], off_b, jnp.zeros((nblocks, -(nseq + 1) % 8), jnp.int32)], 1
    )

    grad_low = cotangent[0]
    grads = plane_gather(grad_low).reshape(nblocks * rows, d_model)

    normed, gate_in, linear = by_block(
        norm_product_kernel,
        info,
        [(all_tokens, True), (w_yx, False), (gain_one[None], False)],
        [
            ((nblocks, rows, d_model), BF, True),
            ((nblocks, rows, wp), F32, True),
            ((nblocks, rows, wp), BF, True),
        ],
        [],
        name="norm_product",
    )
    normed = normed.reshape(nblocks * rows, d_model)

    def two(v):
        return v.reshape((2, 2, nn) + v.shape[1:])

    def flip(v):
        v = two(v)
        return jnp.stack([v[:, 1], v[:, 0]], 1).reshape((nblocks,) + v.shape[3:])

    def of_stream(v, which):
        v = two(v)
        return jnp.where(b == which, v[:, 0], v[:, 1]).reshape((streams,) + v.shape[3:])

    def second_half(shape):
        return ((b ^ block_b) == 1).reshape((nblocks,) + (1,) * (len(shape) - 1))

    tail = linear[:, rows - back :]
    rim = per_block(shift_a(of_stream(tail, 1), 1))
    rim = jnp.where(second_half(rim.shape), flip(tail), rim)
    rim = jnp.pad(rim.astype(F32), ((0, 0), (8 - back, 0), (0, 0)))
    conv_0b, state_0b = per_block(conv_0), per_block(state_0)
    full = (nblocks, rows, wp)
    conv_low, retain, admit, carry_mul, carry_add = by_block(
        functools.partial(forward_kernel, nseq, taps),
        info,
        [
            (linear, True), (rim, True), (conv_0b, True), (state_0b, True),
            (w_gates, False), (vec, False),
        ],
        [
            (full, BF, True), (full, F32, True), (full, F32, True),
            (full, F32, True), (full, F32, True),
        ],
        [(rows + 8, wp), (rows, wp), (rows, wp)],
        name="mixer_forward",
    )

    def entering(mul, add, reverse):
        pair = jnp.stack([mul, add])
        near = of_stream(pair.swapaxes(0, 1), 1 if reverse else 0)
        far = of_stream(pair.swapaxes(0, 1), 0 if reverse else 1)
        whole = jnp.stack([near[:, 0] * far[:, 0], far[:, 0] * near[:, 1] + far[:, 1]])
        came = [shift_a(whole, -d if reverse else d) for d in range(1, planes)]
        value = came[-1][1]
        for part in came[-2::-1]:
            value = part[0] * value + part[1]
        to_far = near[:, 0] * value + near[:, 1]
        value, to_far = per_block(value), per_block(to_far)
        is_far = second_half(value.shape)
        return jnp.where(is_far != reverse, to_far, value)

    state_in = entering(carry_mul[:, -1], carry_add[:, -1], False)[:, None]
    hidden = carry_mul * state_in + carry_add
    mixed_in = (hidden * jax.nn.gelu(gate_in)).astype(BF).reshape(-1, wp)
    resid, normed_two = plane_reduce(
        2, "fwd", False, mixed_in.reshape(2, count, rows, -1), w_o, gain_two, tokens[0], tokens[0],
        (grads,),
    )
    normed_two = normed_two.reshape(nblocks * rows, d_model)

    pair = mdot(normed_two, w_gu)
    gate, upward = pair[:, :f_here], pair[:, f_here:]
    active, gate_back = jax.vjp(jax.nn.gelu, gate)
    inner = (active * upward).astype(BF)
    parts = inner.reshape(2, count * rows, f_here)
    away = swap_c(mdot(parts[1], w_d).astype(BF))
    low = (mdot(parts[0], w_d) + away.astype(F32)).astype(BF).reshape(count, rows, d_model)
    result = resid + low[0].astype(F32)
    for k in range(1, count):
        result = result + xor_u(low[k], k).astype(F32)
    result = result.astype(BF)
    d_inner = ndot(grads, w_d)
    sums_d = tdot(inner, grads).astype(BF)
    grad_wd = scatter_a(sums_d)
    d_gate = gate_back(d_inner * upward)[0].astype(BF)
    d_up = (d_inner * active).astype(BF)
    d_pair = jnp.concatenate([d_gate, d_up], 1)
    sums_gu = tdot(normed_two, d_pair).astype(BF)
    sums = scattered_gu = scatter_a(sums_gu)
    sums = by_owner(exchange(to_owner_rows(sums)))
    grad_wg = from_hidden_pieces(sums[..., :f_here]).astype(F32)
    grad_wu = from_hidden_pieces(sums[..., f_here:]).astype(F32)

    d_resid, d_resid_low = plane_reduce(
        3, "mid", True, d_pair.reshape(2, count, rows, -1), w_gu, gain_two, grad_low, resid,
        (sums_gu,),
    )
    d_resid_low = d_resid_low.reshape(nblocks * rows, d_model)

    d_gate_in, back_mul, back_add, first = by_block(
        functools.partial(back_scan_kernel, nseq, taps),
        info,
        [
            (d_resid_low.reshape(nblocks, rows, d_model), True), (w_o, False), (gate_in, True),
            (hidden, True), (retain, True), (vec, False),
        ],
        [(full, BF, True), (full, F32, True), (full, F32, True), ((nblocks, 8, wp), F32, True)],
        [(rows + 8, wp), (rows, wp), (rows, wp)],
        name="mixer_back_scan",
    )
    sums_o = tdot(mixed_in, d_resid_low)[:wide_here].astype(BF)
    grad_wo = scatter_a(part_halves(sums_o)).astype(F32)
    grad_in = entering(first[:, 0] * back_mul[:, 0], first[:, 0] * back_add[:, 0], True)[:, None]
    d_conv_low, sums_gates, vec_grads = by_block(
        functools.partial(back_kernel, nseq, taps),
        info,
        [
            (back_mul, True), (back_add, True), (grad_in, True), (hidden, True),
            (state_in, True), (state_0b, True), (conv_low, True), (retain, True),
            (admit, True), (linear, True), (rim, True), (conv_0b, True), (w_gates, False), (vec, False),
        ],
        [(full, BF, True), ((wp, 2 * wp), F32, False), ((taps + 4, wp), F32, False)],
        [(rows + 8, wp)],
        (scattered_gu,),
        name="mixer_back",
    )

    def diagonal(m):
        m = m.reshape(heads_here, head_w, heads_here, head_w)
        return jnp.concatenate([m[h, :, h] for h in range(heads_here)], 0)

    grad_gates = jnp.concatenate(
        [
            diagonal(sums_gates[:wide_here, :wide_here]),
            diagonal(sums_gates[:wide_here, wp : wp + wide_here]),
        ],
        1,
    )
    head = d_conv_low[:, :back]
    rim_back = per_block(shift_a(of_stream(head, 0), -1))
    rim_back = jnp.where(second_half(head.shape), rim_back, flip(head))
    rim_back = jnp.pad(rim_back.astype(F32), ((0, 0), (0, 8 - back), (0, 0)))
    d_both = by_block(
        functools.partial(back_conv_kernel, nseq, taps),
        info,
        [(d_conv_low, True), (rim_back, True), (d_gate_in, True), (vec, False)],
        [((nblocks, rows, 2 * wp), BF, True)],
        [(rows + 8, wp)],
        name="mixer_back_conv",
    )[0]
    vec_grads = vec_grads[:, :wide_here].T
    vec_grads = jnp.concatenate(
        [vec_grads[:, :-1], vec_grads[:, -1:] * jax.nn.sigmoid(decay_f)[:, None]], 1
    )
    late = jnp.concatenate([grad_gates, vec_grads], 1).astype(BF)
    late = scatter_a(part_halves(late)).astype(F32)
    grad_wa, grad_wi = late[:, :head_w], late[:, head_w : 2 * head_w]
    vec_grads = late[:, 2 * head_w :].T

    sums_yx = tdot(normed, d_both.reshape(nblocks * rows, 2 * wp)).astype(BF)
    sums_yx = jnp.concatenate([sums_yx[:, :wide_here], sums_yx[:, wp : wp + wide_here]], 1)
    input_grad = plane_reduce(
        4, "last", True, d_both.reshape(2, count, rows, -1), w_yx, gain_one, tokens[0], d_resid,
        (grad_wd, sums_yx, result),
    )[0]
    sums = scatter_a(sums_yx)
    sums = by_owner(exchange(to_owner_rows(sums)))
    grad_wy = from_head_pieces(sums[..., :wide_here]).astype(F32)
    grad_wx = from_head_pieces(sums[..., wide_here:]).astype(F32)
    def gain_grad(gain, *pairs):
        total = sum(jnp.sum(w.astype(F32) * g, axis=1) for w, g in pairs)
        return total / gain.astype(F32)

    grad_gain_one = gain_grad(norm1_gain, (w_y, grad_wy), (w_x, grad_wx))
    grad_gain_two = gain_grad(norm2_gain, (w_gate, grad_wg), (w_up, grad_wu))

    end = jnp.concatenate(
        [offsets[:, 1:], jnp.full((streams, 1), planes * 2 * rows, jnp.int32)], 1
    )
    end_b = per_block(end) - 1
    hot = (position[:, None, :] == end_b[:, :, None]).astype(BF)
    lasts = lax.dot_general(
        hot, hidden.astype(BF), (((2,), (1,)), ((0,), (0,))), preferred_element_type=F32
    )
    slots = jnp.arange(back, dtype=jnp.int32)
    where_conv = (end_b[:, :, None] - back + 1 + slots).reshape(nblocks, nseq * back)
    hot = (position[:, None, :] == where_conv[:, :, None]).astype(BF)
    conv_lasts = lax.dot_general(
        hot, linear, (((2,), (1,)), ((0,), (0,))), preferred_element_type=F32
    )
    lasts = two(jnp.concatenate([lasts, conv_lasts], 1)[..., :wide_here])
    lasts = (lasts[:, 0] + lasts[:, 1]).astype(BF)
    came = [cycle_a(lasts, d) for d in range(1, planes)]
    lasts = sum(part.astype(F32) for part in [lasts] + came).astype(BF)
    both = jnp.stack([lasts[0], swap_c(lasts[1])])
    found = jnp.stack(
        [both[:, k % nn] if k == 0 else xor_u(both[:, k % nn], k) for k in range(count)], 1
    )
    found = by_owner(found).reshape(2, count, nseq * taps, heads_here, head_w)
    found = found.transpose(2, 0, 3, 1, 4).reshape(nseq * taps, width)
    final_state = found[:nseq].astype(F32)
    final_conv = found[nseq:].reshape(nseq, back, width)

    return (
        result[None],
        input_grad[None],
        final_state[None],
        final_conv[None],
        grad_wy,
        grad_wx,
        grad_wa,
        grad_wi,
        grad_wo,
        grad_gain_one,
        vec_grads[:taps],
        vec_grads[taps],
        vec_grads[taps + 1],
        vec_grads[taps + 2],
        vec_grads[taps + 3],
        grad_wg,
        grad_wu,
        grad_wd.astype(F32),
        grad_gain_two,
    )


WIDE = ("a", "b")
EVERY = ("a", "b", "n", "c")
HIGH = lax.Precision.HIGHEST


def passed_along(value, axis, by):
    size = lax.axis_size(axis)
    pairs = [(i, i + by) for i in range(size) if 0 <= i + by < size]
    return lax.ppermute(value, axis, pairs)


def entering(value, axis, combine, identity, reverse):
    size, place = (lax.axis_size(axis), lax.axis_index(axis))
    everything = jax.tree.map(lambda part: lax.all_gather(part, axis), value)
    start = jax.tree.map(
        lambda part, zero: jnp.broadcast_to(jnp.asarray(zero, part.dtype), part.shape),
        value,
        identity,
    )

    def hop(k, before):
        at = size - 1 - k if reverse else k
        reached = at > place if reverse else at < place
        new = combine(before, jax.tree.map(lambda part: part[at], everything))
        return jax.tree.map(lambda a, b: jnp.where(reached, a, b), new, before)

    return lax.fori_loop(0, size, hop, start)


def merged_2(value, axis, combine):
    everything = jax.tree.map(
        lambda part, kind: lax.all_gather(part.astype(kind), axis),
        value,
        jax.tree.map(lambda a: jnp.bfloat16 if a.dtype == jnp.float32 else a.dtype, value),
    )

    def take(k):
        return jax.tree.map(lambda part, own: part[k].astype(own.dtype), everything, value)

    return lax.fori_loop(
        1, lax.axis_size(axis), lambda k, so_far: combine(so_far, take(k)), take(0)
    )


def link(earlier, later):
    return (earlier[0] * later[0], later[0] * earlier[1] + later[1])


def norm_back(value, factor, gain, grad):
    weighted = grad * gain
    inner = jnp.mean(weighted * value, axis=-1, keepdims=True)
    return (
        factor * weighted - value * factor * factor * factor * inner,
        jnp.sum(grad * value * factor, axis=0),
    )


def later_one(first, second):
    pick = first[0] > second[0]
    return (
        jnp.where(pick, first[0], second[0]),
        jnp.where(pick[:, None], first[1], second[1]),
        jnp.where(pick[:, None, None], first[2], second[2]),
    )


def on_device_any(
    tokens,
    starts,
    init_state,
    init_conv,
    w_y,
    w_x,
    gate_a,
    gate_i,
    w_out,
    norm1_gain,
    conv_kernel,
    conv_bias,
    bias_a,
    bias_i,
    decay_param,
    w_gate,
    w_up,
    w_down,
    norm2_gain,
    cotangent,
):
    inputs = tokens[0].astype(jnp.float32)
    offsets = starts[0]
    nseqs = offsets.shape[0]
    rows_here = inputs.shape[0]
    width = w_y.shape[1]
    head_w = gate_a.shape[1]
    heads = width // head_w
    place = lax.axis_index(WIDE)
    mixer = (
        lax.all_gather(w_y, EVERY, axis=0, tiled=True),
        lax.all_gather(w_x, EVERY, axis=0, tiled=True),
        lax.all_gather(gate_a, EVERY, axis=0, tiled=True),
        lax.all_gather(gate_i, EVERY, axis=0, tiled=True),
        lax.all_gather(w_out, EVERY, axis=0, tiled=True),
        lax.all_gather(norm1_gain, EVERY, axis=0, tiled=True),
        lax.all_gather(conv_kernel, EVERY, axis=1, tiled=True),
        lax.all_gather(conv_bias, EVERY, axis=0, tiled=True),
        lax.all_gather(bias_a, EVERY, axis=0, tiled=True),
        lax.all_gather(bias_i, EVERY, axis=0, tiled=True),
        lax.all_gather(decay_param, EVERY, axis=0, tiled=True),
    )
    wy_full, wx_full, wa_full, wi_full, wo_full, gain_one, kernel, cbias, abias, ibias, decay = (
        mixer
    )
    gain_one = gain_one.astype(jnp.float32)
    kernel = kernel.astype(jnp.float32)
    taps = kernel.shape[0]
    back = taps - 1
    position = place * rows_here + jnp.arange(rows_here, dtype=jnp.int32)

    def segment_of(where_at):
        return jnp.sum((where_at[:, None] >= offsets[None, :]).astype(jnp.int32), axis=1) - 1

    segment = segment_of(position)
    member = segment[:, None] == jnp.arange(nseqs, dtype=jnp.int32)[None, :]
    begin = jnp.sum(jnp.where(member, offsets[None, :], 0), axis=1)
    opening = (position == begin)[:, None]
    scale_one = lax.rsqrt(jnp.mean(inputs * inputs, axis=-1, keepdims=True) + EPS)
    normed = (inputs * scale_one * gain_one).astype(jnp.bfloat16)
    gate_in = mdot(normed, wy_full)
    linear = mdot(normed, wx_full).astype(jnp.bfloat16)
    rim_rows = passed_along(linear[rows_here - back :], WIDE, 1)
    extended = jnp.concatenate([rim_rows, linear], 0)
    stored = mdot(member.astype(jnp.bfloat16), init_conv[0].reshape(nseqs, back * width)).reshape(
        rows_here, back, width
    )
    inputs_by_tap = [linear.astype(jnp.float32)]
    for shift_by in range(1, taps):
        earlier = extended[back - shift_by : back - shift_by + rows_here].astype(jnp.float32)
        offset = position - shift_by - begin
        from_start = jnp.zeros((rows_here, width), jnp.float32)
        for slot in range(back):
            from_start = from_start + jnp.where(
                (offset + back == slot)[:, None], stored[:, slot], 0.0
            )
        inputs_by_tap.append(jnp.where((offset >= 0)[:, None], earlier, from_start))
    conv_sum = cbias.astype(jnp.float32)
    for shift_by in range(taps):
        conv_sum = conv_sum + kernel[shift_by] * inputs_by_tap[shift_by]
    conv_low = conv_sum.astype(jnp.bfloat16)
    conv_val = conv_low.astype(jnp.float32)
    blocks = conv_low.reshape(rows_here, heads, head_w)
    wa_heads = wa_full.reshape(heads, head_w, head_w)
    wi_heads = wi_full.reshape(heads, head_w, head_w)
    rate = jnp.einsum("thi,hij->thj", blocks, wa_heads, preferred_element_type=jnp.float32).reshape(
        rows_here, width
    ) + abias.astype(jnp.float32)
    inflow = jnp.einsum(
        "thi,hij->thj", blocks, wi_heads, preferred_element_type=jnp.float32
    ).reshape(rows_here, width) + ibias.astype(jnp.float32)
    retain = jax.nn.sigmoid(rate)
    admit = jax.nn.sigmoid(inflow)
    decay_f = decay.astype(jnp.float32)
    soft_decay = jax.nn.softplus(decay_f)
    log_a = -8.0 * retain * soft_decay
    decay_now = jnp.exp(log_a)
    spread = -jnp.expm1(2.0 * log_a)
    mult = jnp.sqrt(jnp.maximum(spread, FLOOR))
    drive = mult * admit * conv_val
    state_rows = jnp.dot(member.astype(jnp.float32), init_state[0], precision=HIGH)
    a_used = jnp.where(opening, 0.0, decay_now)
    b_used = jnp.where(opening, decay_now * state_rows + drive, drive)
    carry_mul, carry_add = lax.associative_scan(link, (a_used, b_used), axis=0)
    identity = (jnp.ones((width,), jnp.float32), jnp.zeros((width,), jnp.float32))
    state_in = entering(
        (carry_mul[rows_here - 1], carry_add[rows_here - 1]), WIDE, link, identity, False
    )[1]
    hidden = carry_mul * state_in + carry_add
    gelu_y, gelu_y_back = jax.vjp(jax.nn.gelu, gate_in)
    mixed_in = (hidden * gelu_y).astype(jnp.bfloat16)
    resid = inputs + mdot(mixed_in, wo_full)
    wg_full, wu_full, wd_full, gain_two = (
        lax.all_gather(w_gate, EVERY, axis=0, tiled=True),
        lax.all_gather(w_up, EVERY, axis=0, tiled=True),
        lax.all_gather(w_down, EVERY, axis=0, tiled=True),
        lax.all_gather(norm2_gain, EVERY, axis=0, tiled=True),
    )
    gain_two = gain_two.astype(jnp.float32)
    scale_two = lax.rsqrt(jnp.mean(resid * resid, axis=-1, keepdims=True) + EPS)
    normed_two = (resid * scale_two * gain_two).astype(jnp.bfloat16)
    gate = mdot(normed_two, wg_full)
    upward = mdot(normed_two, wu_full)
    active, gate_back = jax.vjp(jax.nn.gelu, gate)
    inner = (active * upward).astype(jnp.bfloat16)
    result = (resid + mdot(inner, wd_full)).astype(jnp.bfloat16)
    local_rows = jnp.arange(rows_here, dtype=jnp.int32)
    last_row = jnp.max(jnp.where(member, local_rows[:, None], -1), axis=0)
    present = last_row >= 0
    safe_row = jnp.maximum(last_row, 0)
    marker = jnp.where(present, (place * rows_here + last_row).astype(jnp.float32), -1.0)
    state_last = jnp.where(present[:, None], hidden[safe_row], 0.0)
    conv_rows = extended[safe_row[:, None] + 1 + jnp.arange(back, dtype=jnp.int32)[None, :]].astype(
        jnp.float32
    )
    conv_last = jnp.where(present[:, None, None], conv_rows, 0.0)
    merged = merged_2((marker, state_last, conv_last), WIDE, later_one)
    wg_back, wu_back, wd_back = (
        lax.all_gather(w_gate, EVERY, axis=0, tiled=True),
        lax.all_gather(w_up, EVERY, axis=0, tiled=True),
        lax.all_gather(w_down, EVERY, axis=0, tiled=True),
    )
    grad_low = cotangent[0]
    grad_out = grad_low.astype(jnp.float32)
    d_inner = ndot(grad_low, wd_back)
    grad_wd = tdot(inner, grad_low)
    d_gate = gate_back(d_inner * upward)[0].astype(jnp.bfloat16)
    d_up = (d_inner * active).astype(jnp.bfloat16)
    grad_wg = tdot(normed_two, d_gate)
    grad_wu = tdot(normed_two, d_up)
    d_normed_two = ndot(d_gate, wg_back) + ndot(d_up, wu_back)
    d_resid_norm, grad_gain_two = norm_back(resid, scale_two, gain_two, d_normed_two)
    d_resid = grad_out + d_resid_norm
    wy_back, wx_back, wa_back, wi_back, wo_back = (
        lax.all_gather(w_y, EVERY, axis=0, tiled=True),
        lax.all_gather(w_x, EVERY, axis=0, tiled=True),
        lax.all_gather(gate_a, EVERY, axis=0, tiled=True),
        lax.all_gather(gate_i, EVERY, axis=0, tiled=True),
        lax.all_gather(w_out, EVERY, axis=0, tiled=True),
    )
    d_resid_low = d_resid.astype(jnp.bfloat16)
    d_mixed = ndot(d_resid_low, wo_back)
    grad_wo = tdot(mixed_in, d_resid_low)
    d_hidden = d_mixed * gelu_y
    d_gate_in = gelu_y_back(d_mixed * hidden)[0].astype(jnp.bfloat16)
    forward_mul = jnp.concatenate([a_used[1:], jnp.ones((1, width), jnp.float32)], 0)
    back_mul, back_add = lax.associative_scan(link, (forward_mul, d_hidden), reverse=True, axis=0)
    head_map = (a_used[0] * back_mul[0], a_used[0] * back_add[0])
    grad_in = entering(head_map, WIDE, link, identity, True)[1]
    total_grad = back_mul * grad_in + back_add
    previous = jnp.concatenate([state_in[None], hidden[:-1]], 0)
    previous = jnp.where(opening, state_rows, previous)
    d_decay = total_grad * previous
    d_mult = total_grad * admit * conv_val
    d_admit = total_grad * mult * conv_val
    d_conv = total_grad * mult * admit
    d_spread = jnp.where(spread > FLOOR, d_mult * 0.5 / mult, 0.0)
    d_log = d_decay * decay_now - 2.0 * decay_now * decay_now * d_spread
    d_retain = d_log * (-8.0 * soft_decay)
    grad_decay = jnp.sum(d_log * (-8.0 * retain), axis=0) * jax.nn.sigmoid(decay_f)
    d_rate = (d_retain * retain * (1.0 - retain)).astype(jnp.bfloat16)
    d_inflow = (d_admit * admit * (1.0 - admit)).astype(jnp.bfloat16)
    grad_abias = jnp.sum(d_rate.astype(jnp.float32), axis=0)
    grad_ibias = jnp.sum(d_inflow.astype(jnp.float32), axis=0)
    rate_heads = d_rate.reshape(rows_here, heads, head_w)
    inflow_heads = d_inflow.reshape(rows_here, heads, head_w)
    grad_wa = jnp.einsum(
        "thi,thj->hij", blocks, rate_heads, preferred_element_type=jnp.float32
    ).reshape(width, head_w)
    grad_wi = jnp.einsum(
        "thi,thj->hij", blocks, inflow_heads, preferred_element_type=jnp.float32
    ).reshape(width, head_w)
    d_conv = d_conv + jnp.einsum(
        "thj,hij->thi",
        rate_heads,
        wa_back.reshape(heads, head_w, head_w),
        preferred_element_type=jnp.float32,
    ).reshape(rows_here, width)
    d_conv = d_conv + jnp.einsum(
        "thj,hij->thi",
        inflow_heads,
        wi_back.reshape(heads, head_w, head_w),
        preferred_element_type=jnp.float32,
    ).reshape(rows_here, width)
    d_conv_low = d_conv.astype(jnp.bfloat16)
    d_conv_val = d_conv_low.astype(jnp.float32)
    rim_back = passed_along(d_conv_low[:back], WIDE, -1)
    ahead = jnp.concatenate([d_conv_low, rim_back], 0)
    d_linear = kernel[0] * d_conv_val
    kernel_grads = [jnp.sum(d_conv_val * inputs_by_tap[0], axis=0)]
    for shift_by in range(1, taps):
        later_rows = ahead[shift_by : shift_by + rows_here].astype(jnp.float32)
        same = (segment_of(position + shift_by) == segment)[:, None]
        d_linear = d_linear + kernel[shift_by] * jnp.where(same, later_rows, 0.0)
        kernel_grads.append(jnp.sum(d_conv_val * inputs_by_tap[shift_by], axis=0))
    grad_kernel = jnp.stack(kernel_grads, 0)
    grad_cbias = jnp.sum(d_conv_val, axis=0)
    d_linear_low = d_linear.astype(jnp.bfloat16)
    d_normed = ndot(d_gate_in, wy_back) + ndot(d_linear_low, wx_back)
    grad_wy = tdot(normed, d_gate_in)
    grad_wx = tdot(normed, d_linear_low)
    d_input_norm, grad_gain_one = norm_back(inputs, scale_one, gain_one, d_normed)
    input_grad = (d_resid + d_input_norm).astype(jnp.bfloat16)
    every_sum = (
        lax.psum_scatter(grad_wy, EVERY, scatter_dimension=0, tiled=True),
        lax.psum_scatter(grad_wx, EVERY, scatter_dimension=0, tiled=True),
        lax.psum_scatter(grad_wa, EVERY, scatter_dimension=0, tiled=True),
        lax.psum_scatter(grad_wi, EVERY, scatter_dimension=0, tiled=True),
        lax.psum_scatter(grad_wo, EVERY, scatter_dimension=0, tiled=True),
        lax.psum_scatter(grad_gain_one, EVERY, scatter_dimension=0, tiled=True),
        lax.psum_scatter(grad_kernel, EVERY, scatter_dimension=1, tiled=True),
        lax.psum_scatter(grad_cbias, EVERY, scatter_dimension=0, tiled=True),
        lax.psum_scatter(grad_abias, EVERY, scatter_dimension=0, tiled=True),
        lax.psum_scatter(grad_ibias, EVERY, scatter_dimension=0, tiled=True),
        lax.psum_scatter(grad_decay, EVERY, scatter_dimension=0, tiled=True),
        lax.psum_scatter(grad_wg, EVERY, scatter_dimension=0, tiled=True),
        lax.psum_scatter(grad_wu, EVERY, scatter_dimension=0, tiled=True),
        lax.psum_scatter(grad_wd, EVERY, scatter_dimension=0, tiled=True),
        lax.psum_scatter(grad_gain_two, EVERY, scatter_dimension=0, tiled=True),
    )
    mixer_sums = every_sum[:11]
    mlp_sums = every_sum[11:]
    return (
        result[None],
        input_grad[None],
        merged[1][None],
        merged[2].astype(jnp.bfloat16)[None],
        mixer_sums[0],
        mixer_sums[1],
        mixer_sums[2],
        mixer_sums[3],
        mixer_sums[4],
        mixer_sums[5],
        mixer_sums[6],
        mixer_sums[7],
        mixer_sums[8],
        mixer_sums[9],
        mixer_sums[10],
        mlp_sums[0],
        mlp_sums[1],
        mlp_sums[2],
        mlp_sums[3],
    )


def solution(mesh):
    wide, narrow = mesh.shape["wide"], mesh.shape["narrow"]
    def plan(*args):
        fits = args[6].shape[0] * 2 == args[6].shape[1] and narrow == 4
        return (on_device if fits else on_device_any)(*args)

    fine = Mesh(mesh.devices.reshape(wide // 2, 2, narrow // 2, 2), ("a", "b", "n", "c"))
    w, s = ("a", "b"), ("n", "c")
    everywhere = ("a", "b", "n", "c")
    acts, rows, vec = P(s, w, None), P(everywhere, None), P(everywhere)
    return jax.shard_map(
        plan,
        mesh=fine,
        in_specs=(
            acts,
            P(s, None),
            P(s, None, None),
            P(s, None, None, None),
            rows, rows, rows, rows, rows,
            vec,
            P(None, everywhere),
            vec, vec, vec, vec,
            rows, rows, rows,
            vec,
            acts,
        ),
        out_specs=(
            acts,
            acts,
            P(s, None, None),
            P(s, None, None, None),
            rows, rows, rows, rows, rows,
            vec,
            P(None, everywhere),
            vec, vec, vec, vec,
            rows, rows, rows,
            vec,
        ),
        check_vma=False,
    )
```

```python
import functools

import jax
import jax.numpy as jnp
from jax import lax
from jax.experimental import pallas as pl
from jax.experimental.pallas import tpu as pltpu
from jax.sharding import Mesh
from jax.sharding import PartitionSpec as P

EPS = 1e-06
FLOOR = 0.001
BF = jnp.bfloat16
F32 = jnp.float32


def tdot(left, right):
    return lax.dot_general(left, right, (((0,), (0,)), ((), ())), preferred_element_type=F32)


def ndot(left, right):
    return lax.dot_general(left, right, (((1,), (1,)), ((), ())), preferred_element_type=F32)


def mdot(left, right):
    return jnp.dot(left, right, preferred_element_type=F32)


def pick(stacked, index, axis=0):
    return lax.dynamic_index_in_dim(stacked, index, axis, keepdims=False)


def swap_c(value):
    return lax.ppermute(value, "c", [(0, 1), (1, 0)])


def xor_u(value, k):
    size = lax.axis_size("b") * lax.axis_size("n")
    return lax.ppermute(value, ("b", "n"), [(i, i ^ k) for i in range(size)])


def shift_a(value, by):
    size = lax.axis_size("a")
    return lax.ppermute(value, "a", [(i, i + by) for i in range(size) if 0 <= i + by < size])


def chips():
    return lax.axis_size("b") * lax.axis_size("n")


def chip():
    return lax.axis_index("b") * lax.axis_size("n") + lax.axis_index("n")


MESH = pl.DeviceIdType.MESH
VMEM_LIMIT = 60 * 1024 * 1024


def places():
    return tuple(lax.axis_index(name) for name in ("a", "b", "n", "c"))


def neighbours():
    a, b, n, c = places()
    return (a, 1 - b, n, c), (a, b, 1 - n, c), (a, b, n, 1 - c)


def greet(peers):
    barrier = pltpu.get_barrier_semaphore()
    for peer in peers:
        pl.semaphore_signal(barrier, inc=1, device_id=peer, device_id_type=MESH)
    pl.semaphore_wait(barrier, len(peers))


class Mover:
    def __init__(self, send, recv):
        self.send, self.recv, self.made = send, recv, {}
        self.names = []

    def copy(self, name, src, dst, peer):
        if name not in self.names:
            self.names.append(name)
        at = self.names.index(name)
        made = pltpu.make_async_remote_copy(
            src_ref=src,
            dst_ref=dst,
            send_sem=self.send.at[at],
            recv_sem=self.recv.at[at],
            device_id=peer,
            device_id_type=MESH,
        )
        self.made[name] = made
        return made

    def start(self, name, src, dst, peer):
        self.copy(name, src, dst, peer).start()

    def arrived(self, name):
        self.made[name].wait_recv()

    def sent(self):
        for made in self.made.values():
            made.wait_send()


def gather_plane_start(move, mine, everyone, h, half_rows):
    x, y, z = neighbours()
    at = pl.ds(h * half_rows, half_rows)
    move.start(f"gx{h}", mine.at[at], everyone.at[2, at], x)
    move.start(f"gy{h}", mine.at[at], everyone.at[1, at], y)
    move.start(f"gc{h}", mine.at[at], everyone.at[4, at], z)


def gather_plane_rest(move, everyone, half_rows, stage=None):
    x, y, z = neighbours()
    rows = [pl.ds(h * half_rows, half_rows) for h in range(2)]

    def on(name, k, h):
        move.start(name, everyone.at[k, rows[h]], everyone.at[4 + k, rows[h]], z)

    if stage in (None, 0):
        move.arrived("gx0")
        move.start("fy", everyone.at[2, rows[0]], everyone.at[3, rows[0]], y)
        on("cx0", 2, 0)
        move.arrived("gy1")
        move.start("fx", everyone.at[1, rows[1]], everyone.at[3, rows[1]], x)
        on("cy1", 1, 1)
    if stage in (None, 1):
        move.arrived("gx1")
        on("cx1", 2, 1)
        move.arrived("gy0")
        on("cy0", 1, 0)
    if stage in (None, 2):
        move.arrived("fy")
        on("cd0", 3, 0)
        move.arrived("fx")
        on("cd1", 3, 1)
        for name in ("gc0", "gc1", "cx0", "cx1", "cy0", "cy1", "cd0", "cd1"):
            move.arrived(name)


GATHER_COPIES = 14


def plane_peers_of():
    a, b, n, c = places()
    peers = {}
    for kc in range(2):
        for k in range(4):
            if (kc, k) != (0, 0):
                there = (a, 1 - b if k & 2 else b, 1 - n if k & 1 else n, 1 - c if kc else c)
                peers[kc, k] = there
    return peers


def peer_owner(kc, k):
    _, b, n, c = places()
    return ((b * 2 + n) ^ k) * 2 + (1 - c if kc else c)


def set_side_by_side(pieces, order, width):
    group = 1
    while group * width % 128 and group < len(order):
        group += 1
    for i in range(0, len(order), group):
        runs = [pieces[p, :, o : o + width].astype(F32) for p, o in order[i : i + group]]
        yield slice(i * width, (i + len(runs)) * width), jnp.concatenate(runs, 1)


def reduce_kernel(nt, post, nx, extra, waits, hid, *refs):
    x_hbm, refs = refs[:nx], refs[nx:]
    w_hbm, gain_ref, first_ref, second_ref = refs[:4]
    extra_in, refs = refs[4 : 4 + extra], refs[4 + extra :]
    if post == "last":
        lasts_ref, refs = refs[0], refs[1:]
    refs = refs[waits:]
    out_ref, refs = refs[0], refs[1:]
    if post == "last":
        everyone = mine = None
        extra_out, lasts_out = refs[:extra], refs[extra]
        extra_buf, lasts_buf, lasts_mine, lasts_far, refs = *refs[extra + 1 : extra + 5], refs[extra + 5 :]
    else:
        everyone, refs = refs[0], refs[1:]
        if extra:
            extra_out, refs = refs[0], refs[1:]
        mine, refs = refs[0], refs[1:]
    x_v, w_v, away_s, away_r, acc, out_b, in_b, local, send, recv = refs
    rows, d_model = acc.shape[1:]
    half = rows // 2
    tile = min(512, d_model)
    px, py, pc = neighbours()
    move = Mover(send, recv)

    slots = iter(range(local.shape[0]))

    def keep(src, dst):
        made = pltpu.make_async_copy(src, dst, local.at[next(slots)])
        made.start()
        return made

    w_copy = keep(w_hbm, w_v)
    loads = {}
    each = x_v.shape[3] // nx
    for k in (3, 2, 1, 0):
        for kc in (1, 0):
            loads[kc, k] = [
                keep(x.at[kc, k], x_v.at[kc, k, :, pl.ds(i * each, each)])
                for i, x in enumerate(x_hbm)
            ]
    if post == "last":
        a, b, n, c = places()
        planes = lasts_far.shape[0] + 1
        columns = [(lax.rem(a + d, planes), b, n, c) for d in range(1, planes)]
        peers = plane_peers_of()
        greet([*peers.values(), *columns])
        for (kc, k), peer in peers.items():
            move.start(f"l{kc}{k}", lasts_ref.at[kc, k % 2], lasts_buf.at[kc, k], peer)
    else:
        greet((px, py, pc))
    w_copy.wait()

    def product(kc, k, t):
        at = pl.ds(pl.multiple_of(t * tile, tile), tile)
        if nt:
            return at, ndot(x_v[kc, k], w_v[at, :])
        return at, mdot(x_v[kc, k], w_v[:, at])

    step = min(32, half)

    def by_rows(h, body):
        @pl.loop(0, half // step)
        def _(i):
            body(pl.ds(pl.multiple_of(i * step, step), step),
                 pl.ds(pl.multiple_of(h * half + i * step, step), step))

    def hand_on(name, slot, k, h, peer, extra=None):
        def body(inner, outer):
            value = acc[k, outer, :]
            if extra is not None:
                value = value + in_b[extra, inner, :].astype(F32)
            out_b[slot, inner, :] = value.astype(BF)

        by_rows(h, body)
        move.start(name, out_b.at[slot], in_b.at[slot], peer)

    for k in (3, 2, 1, 0):
        for load in loads[1, k]:
            load.wait()

        @pl.loop(0, d_model // tile)
        def _(t):
            at, value = product(1, k, t)
            away_s[k, :, at] = value.astype(BF)

        move.start(f"away{k}", away_s.at[k], away_r.at[k], pc)
        for load in loads[0, k]:
            load.wait()

        @pl.loop(0, d_model // tile)
        def _(t):
            at, value = product(0, k, t)
            acc[k, :, at] = value

        move.arrived(f"away{k}")
        for h in range(2):
            def add(inner, outer):
                acc[k, outer, :] += away_r[k, outer, :].astype(F32)

            by_rows(h, add)
        if k == 3:
            hand_on("d0", 0, 3, 0, px)
            hand_on("d1", 1, 3, 1, py)
        elif k == 2:
            hand_on("x0", 2, 2, 0, px)
        elif k == 1:
            hand_on("y1", 5, 1, 1, py)
    kept = []
    if extra and post == "fwd":
        for k in range(4):
            kept.append(keep(extra_in[k], extra_out.at[k]))
            move.start(f"e{k}", extra_in[k], extra_out.at[4 + k], pc)
    move.arrived("d0")
    hand_on("y0", 4, 1, 0, py, 0)
    move.arrived("d1")
    hand_on("x1", 3, 2, 1, px, 1)
    if extra and post == "last":
        lasts_buf[0, 0] = lasts_ref[0, 0]
        for kc, k in peers:
            move.arrived(f"l{kc}{k}")
        u = b * 2 + n
        me = u * 2 + c
        for kc in range(2):
            for q in range(4):
                found = lasts_buf[kc, 0]
                for k in range(1, 4):
                    found = jnp.where((u ^ k) == q, lasts_buf[kc, k], found)
                lasts_mine[jnp.bitwise_xor(c, kc), q] = found
        for i, peer in enumerate(columns):
            move.start(f"z{i}", lasts_mine, lasts_far.at[i], peer)
        each_rows = extra_buf.shape[2]
        for i in range(extra):
            def part(owner, i=i):
                at = pl.multiple_of(owner * each_rows, each_rows)
                return extra_in[i].at[pl.ds(at, each_rows)]

            kept.append(keep(part(me), extra_buf.at[i, me]))
            for (kc, k), peer in plane_peers_of().items():
                move.start(f"e{i}{kc}{k}", part(peer_owner(kc, k)), extra_buf.at[i, me], peer)

    for h in range(2):
        move.arrived(f"x{h}")
        move.arrived(f"y{h}")

        def body(inner, outer):
            total = acc[0, outer, :]
            total = total + in_b[2 + h, inner, :].astype(F32)
            total = total + in_b[4 + h, inner, :].astype(F32)
            gain = gain_ref[...]
            if post == "fwd":
                value = first_ref[outer, :].astype(F32) + total
                out_ref[outer, :] = value
                factor = lax.rsqrt(jnp.mean(value * value, axis=-1, keepdims=True) + EPS)
                mine[outer, :] = (value * factor * gain).astype(BF)
                return
            value = second_ref[outer, :] if post == "mid" else first_ref[outer, :].astype(F32)
            base = first_ref[outer, :].astype(F32) if post == "mid" else second_ref[outer, :]
            factor = lax.rsqrt(jnp.mean(value * value, axis=-1, keepdims=True) + EPS)
            weighted = total * gain
            inner_mean = jnp.mean(weighted * value, axis=-1, keepdims=True)
            grad = base + factor * weighted - value * (factor * factor * factor * inner_mean)
            if post == "mid":
                out_ref[outer, :] = grad
                mine[outer, :] = grad.astype(BF)
            else:
                out_ref[outer, :] = grad.astype(BF)

        by_rows(h, body)
        if everyone is not None:
            gather_plane_start(move, mine, everyone, h, half)
    if everyone is not None:
        kept.append(keep(mine, everyone.at[0]))
        gather_plane_rest(move, everyone, half)
    if extra and post == "fwd":
        for k in range(4):
            move.arrived(f"e{k}")
    for made in kept:
        made.wait()
    if extra and post == "last":
        total = lasts_mine[...].astype(F32)
        for i in range(len(columns)):
            move.arrived(f"z{i}")
            total = total + lasts_far[i].astype(F32)
        lasts_out[...] = total.astype(BF)
        order = [(p, z * hid) for z in range(extra_buf.shape[3] // hid) for p in range(8)]
        for i in range(extra):
            for kc, k in plane_peers_of():
                move.arrived(f"e{i}{kc}{k}")
            for at, value in set_side_by_side(extra_buf.at[i], order, hid):
                extra_out[i][:, at] = value
    move.sent()


def plane_reduce(ident, post, nt, xs, w, gain, first, second, extra=(), done=(), hid=0, lasts=None):
    rows, d_model = first.shape
    vmem = pl.BlockSpec(memory_space=pltpu.VMEM)
    hbm = pl.BlockSpec(memory_space=pl.ANY)
    out_type = BF if post == "last" else F32
    out_shape = [jax.ShapeDtypeStruct((rows, d_model), out_type)]
    out_specs = [vmem]
    scratch = []
    copies = 10
    if post != "last":
        out_shape.append(jax.ShapeDtypeStruct((8, rows, d_model), BF))
        out_specs.append(hbm)
        copies += GATHER_COPIES
        if extra:
            out_shape.append(jax.ShapeDtypeStruct((8, rows, d_model), BF))
            out_specs.append(hbm)
            copies += 4
        scratch.append(pltpu.VMEM((rows, d_model), BF))
    else:
        each = extra[0].shape[0] // 8, extra[0].shape[1]
        for _ in extra:
            out_shape.append(jax.ShapeDtypeStruct((each[0], 8 * each[1]), F32))
            out_specs.append(vmem)
        planes = lax.axis_size("a")
        copies += 7 * len(extra) + 7 + planes - 1
        block = (2, 4) + lasts.shape[2:]
        out_shape.append(jax.ShapeDtypeStruct(block, BF))
        out_specs.append(vmem)
        scratch.append(pltpu.VMEM((len(extra), 8) + each, BF))
        scratch += [pltpu.VMEM(block, BF)] * 2 + [pltpu.VMEM((planes - 1,) + block, BF)]
    wide = sum(x.shape[3] for x in xs)
    scratch += [
        pltpu.VMEM((2, 4, rows, wide), BF),
        pltpu.VMEM(w.shape, BF),
        pltpu.VMEM((4, rows, d_model), BF),
        pltpu.VMEM((4, rows, d_model), BF),
        pltpu.VMEM((4, rows, d_model), F32),
        pltpu.VMEM((6, rows // 2, d_model), BF),
        pltpu.VMEM((6, rows // 2, d_model), BF),
        pltpu.SemaphoreType.DMA((2 + 8 * len(xs) + len(extra),)),
        pltpu.SemaphoreType.DMA((copies,)),
        pltpu.SemaphoreType.DMA((copies,)),
    ]
    return pl.pallas_call(
        functools.partial(reduce_kernel, nt, post, len(xs), len(extra), len(done), hid),
        in_specs=[hbm] * (len(xs) + 1)
        + [vmem] * 3
        + [hbm if post == "last" else vmem] * len(extra)
        + [vmem] * (lasts is not None)
        + [hbm] * len(done),
        out_specs=out_specs,
        out_shape=out_shape,
        scratch_shapes=scratch,
        compiler_params=pltpu.CompilerParams(
            collective_id=ident, has_side_effects=True, vmem_limit_bytes=VMEM_LIMIT
        ),
        cost_estimate=pl.CostEstimate(flops=0, bytes_accessed=8 << 20, transcendentals=0),
        name=f"plane_reduce_{post}",
    )(*xs, w, gain.reshape(1, -1), first, second, *extra, *([] if lasts is None else [lasts]), *done)


def start_kernel(
    head_w, hid, tokens_ref, wy_ref, wx_ref, wg_ref, wu_ref, rows_ref, vec_ref, stream_ref,
    tok_out, yx_out, gu_out, rows_out, halves_out, vec_out, stream_out,
    yx_ref, gu_ref, local, send, recv,
):
    a, b, n, c = places()
    planes = yx_out.shape[0]
    p = (b * 2 + n) * 2 + c
    pc = neighbours()[2]
    plane_peers = plane_peers_of()
    up, down = (a + 1, b, n, c), (a - 1, b, n, c)
    each = planes // 2

    def pack(out, sources, columns, width):
        for owner in range(8):
            runs = [w[:, o : o + width] for w in sources for o in columns(owner)]
            out[owner] = jnp.concatenate(runs, 1)

    barrier = pltpu.get_barrier_semaphore()
    for peer in plane_peers.values():
        pl.semaphore_signal(barrier, inc=1, device_id=peer, device_id_type=MESH)

    @pl.when(a < planes - 1)
    def _():
        pl.semaphore_signal(barrier, inc=1, device_id=up, device_id_type=MESH)

    @pl.when(a > 0)
    def _():
        pl.semaphore_signal(barrier, inc=1, device_id=down, device_id_type=MESH)

    def head_columns(owner):
        return [((owner % 2 * each + j) * 4 + owner // 2) * head_w for j in range(each)]

    pack(yx_ref, (wy_ref, wx_ref), head_columns, head_w)
    others = len(plane_peers) + jnp.minimum(planes - 1 - a, 1) + jnp.minimum(a, 1)
    pl.semaphore_wait(barrier, others)

    move = Mover(send, recv)
    half = tokens_ref.shape[0] // 2

    def keep(i, src, dst):
        made = pltpu.make_async_copy(src, dst, local.at[i])
        made.start()
        return made

    def to_owners(name, pieces, out):
        for (kc, k), peer in plane_peers.items():
            move.start(f"{name}{kc}{k}", pieces.at[peer_owner(kc, k)], out.at[a, p], peer)

    chains = {}

    def chain_step(name, out, s):
        def up_copy(block):
            return move.copy(f"{name}u{s}", out.at[block], out.at[block], up)

        def down_copy(block):
            return move.copy(f"{name}d{s}", out.at[block], out.at[block], down)

        sends_up, sends_down = (a < planes - 1) & (a >= s), (a > 0) & (a + s < planes)

        @pl.when(sends_up)
        def _():
            up_copy(a - s).start()

        @pl.when(sends_down)
        def _():
            down_copy(a + s).start()

        chains[name, s] = (up_copy, down_copy, sends_up, sends_down)

    def chain_arrived(name, s):
        up_copy, down_copy, _, _ = chains[name, s]

        @pl.when(a - 1 >= s)
        def _():
            up_copy(a - 1 - s).wait_recv()

        @pl.when(a + 1 + s < planes)
        def _():
            down_copy(a + 1 + s).wait_recv()

    def chain_sent(name, s):
        up_copy, down_copy, sends_up, sends_down = chains[name, s]

        @pl.when(sends_up)
        def _():
            up_copy(a - s).wait_send()

        @pl.when(sends_down)
        def _():
            down_copy(a + s).wait_send()

    to_owners("yx", yx_ref, yx_out)
    for (kc, k), peer in plane_peers.items():
        move.start(f"vec{kc}{k}", vec_ref, vec_out.at[a, p], peer)
    own_yx = keep(1, yx_ref.at[p], yx_out.at[a, p])
    own_vec = keep(2, vec_ref, vec_out.at[a, p])
    own_rows = keep(0, rows_ref, rows_out.at[a])
    own_tok = keep(4, tokens_ref, tok_out.at[0])
    own_stream = keep(5, stream_ref, stream_out.at[0, 0])
    own_yx.wait()
    own_vec.wait()
    for kc, k in plane_peers:
        move.arrived(f"yx{kc}{k}")
        move.arrived(f"vec{kc}{k}")
    own_rows.wait()
    outs = (("yx", yx_out), ("vec", vec_out), ("rows", rows_out))
    for name, out in outs:
        chain_step(name, out, 0)
    for h in range(2):
        gather_plane_start(move, tokens_ref, tok_out, h, half)
    pack(gu_ref, (wg_ref, wu_ref), lambda o: [(z * 8 + o) * hid for z in range(planes)], hid)
    own_gu = keep(3, gu_ref.at[p], gu_out.at[p])
    gather_plane_rest(move, tok_out, half, 0)
    for kc in range(2):
        for kn in range(2):
            if (kc, kn) != (0, 0):
                move.start(f"st{kc}{kn}", stream_ref, stream_out.at[kc, kn], plane_peers[kc, kn])
    for name, out in outs:
        chain_arrived(name, 0)
        chain_step(name, out, 1)
    gather_plane_rest(move, tok_out, half, 1)
    for (kc, k), peer in plane_peers.items():
        move.start(f"gu{kc}{k}", gu_ref.at[peer_owner(kc, k)], gu_out.at[p], peer)
    for s in range(1, planes - 1):
        for name, out in outs:
            chain_arrived(name, s)
            if s + 1 < planes - 1:
                chain_step(name, out, s + 1)
    gather_plane_rest(move, tok_out, half, 2)
    swap = pltpu.make_async_remote_copy(
        src_ref=rows_out.at[pl.ds((1 - c) * each, each)],
        dst_ref=halves_out.at[:, c],
        send_sem=send.at[send.shape[0] - 1],
        recv_sem=recv.at[recv.shape[0] - 1],
        device_id=pc,
        device_id_type=MESH,
    )
    swap.start()
    own_halves = keep(6, rows_out.at[pl.ds(c * each, each)], halves_out.at[:, c])
    for kc, k in plane_peers:
        move.arrived(f"gu{kc}{k}")
    for kc in range(2):
        for kn in range(2):
            if (kc, kn) != (0, 0):
                move.arrived(f"st{kc}{kn}")
    for made in (own_gu, own_tok, own_stream, own_halves):
        made.wait()
    swap.wait()
    for name, s in chains:
        chain_sent(name, s)
    for name in [n for n in move.names if not any(n == f"{w}{d}{s}" for w, s in chains for d in "ud")]:
        move.made[name].wait_send()


def start_exchange(tokens, w_y, w_x, w_gate, w_up, gate_rows, vec, stream):
    planes = lax.axis_size("a")
    head_w, hid = gate_rows.shape[1] // 2, w_gate.shape[1] // (planes * 8)
    vmem = pl.BlockSpec(memory_space=pltpu.VMEM)
    hbm = pl.BlockSpec(memory_space=pl.ANY)
    yx = (8, w_y.shape[0], 2 * w_y.shape[1] // 8)
    gu = (8, w_gate.shape[0], 2 * w_gate.shape[1] // 8)
    shapes = [
        ((8,) + tokens.shape, BF),
        ((planes,) + yx, BF),
        (gu, BF),
        ((planes,) + gate_rows.shape, BF),
        ((planes // 2, 2) + gate_rows.shape, BF),
        ((planes, 8) + vec.shape, F32),
        ((2, 2) + stream.shape, F32),
    ]
    copies = 7 * 3 + 3 + GATHER_COPIES + 6 * (planes - 1) + 1
    return pl.pallas_call(
        functools.partial(start_kernel, head_w, hid),
        in_specs=[vmem] * 8,
        out_specs=[hbm] * 7,
        out_shape=[jax.ShapeDtypeStruct(*shape) for shape in shapes],
        scratch_shapes=[
            pltpu.VMEM(yx, BF),
            pltpu.VMEM(gu, BF),
            pltpu.SemaphoreType.DMA((7,)),
            pltpu.SemaphoreType.DMA((copies,)),
            pltpu.SemaphoreType.DMA((copies,)),
        ],
        compiler_params=pltpu.CompilerParams(
            collective_id=1, has_side_effects=True, vmem_limit_bytes=VMEM_LIMIT
        ),
        cost_estimate=pl.CostEstimate(flops=0, bytes_accessed=8 << 20, transcendentals=0),
        name="start_exchange",
    )(tokens, w_y, w_x, w_gate, w_up, gate_rows, vec, stream)


def finish_kernel(head_w, sums_ref, y_ref, x_ref, buf, local, send, recv):
    _, b, n, c = places()
    me = (b * 2 + n) * 2 + c
    peers = plane_peers_of()
    greet(list(peers.values()))
    move = Mover(send, recv)
    each_rows = buf.shape[1]

    def part(owner):
        return sums_ref.at[pl.ds(pl.multiple_of(owner * each_rows, each_rows), each_rows)]

    for (kc, k), peer in peers.items():
        move.start(f"e{kc}{k}", part(peer_owner(kc, k)), buf.at[me], peer)
    own = pltpu.make_async_copy(part(me), buf.at[me], local.at[0])
    own.start()
    own.wait()
    for kc, k in peers:
        move.arrived(f"e{kc}{k}")
    wide = buf.shape[2] // 2
    each = wide // head_w
    order = [(q * 2 + i, j * head_w) for i in range(2) for j in range(each) for q in range(4)]
    for first, out in ((0, y_ref), (wide, x_ref)):
        for at, value in set_side_by_side(buf, [(p, o + first) for p, o in order], head_w):
            out[:, at] = value
    move.sent()


def finish(sums, head_w):
    each = sums.shape[0] // 8, sums.shape[1]
    vmem = pl.BlockSpec(memory_space=pltpu.VMEM)
    return pl.pallas_call(
        functools.partial(finish_kernel, head_w),
        in_specs=[pl.BlockSpec(memory_space=pl.ANY)],
        out_specs=[vmem, vmem],
        out_shape=[jax.ShapeDtypeStruct((each[0], 4 * each[1]), F32)] * 2,
        scratch_shapes=[
            pltpu.VMEM((8,) + each, BF),
            pltpu.SemaphoreType.DMA((1,)),
            pltpu.SemaphoreType.DMA((7,)),
            pltpu.SemaphoreType.DMA((7,)),
        ],
        compiler_params=pltpu.CompilerParams(
            collective_id=5, has_side_effects=True, vmem_limit_bytes=VMEM_LIMIT
        ),
        name="finish",
    )(sums)


def column_peers(planes):
    a, b, n, c = places()
    return [(lax.rem(a + d, planes), b, n, c) for d in range(1, planes)]


def earlier_blocks(ref, want, row=0, count=1):
    _, b, _, _ = places()
    return [
        jnp.where(
            b == want,
            ref[kc * 4 + kn, row : row + count, :],
            ref[kc * 4 + 2 + kn, row : row + count, :],
        )
        for kc in range(2)
        for kn in range(2)
    ]


def pass_state_kernel(reverse, mul_ref, add_ref, out_ref, whole, came, send, recv):
    a, b, n, c = places()
    planes = came.shape[0] + 1
    row = 0 if reverse else 7
    near_at, far_at = (1, 0) if reverse else (0, 1)
    came[...] = jnp.zeros_like(came)
    near_mul, near_add = earlier_blocks(mul_ref, near_at, row), earlier_blocks(add_ref, near_at, row)
    far_mul, far_add = earlier_blocks(mul_ref, far_at, row), earlier_blocks(add_ref, far_at, row)
    for i in range(4):
        whole[0, i : i + 1, :] = near_mul[i] * far_mul[i]
        whole[1, i : i + 1, :] = far_mul[i] * near_add[i] + far_add[i]
    greet(column_peers(planes))

    def copy(d):
        return pltpu.make_async_remote_copy(
            src_ref=whole,
            dst_ref=came.at[d - 1],
            send_sem=send.at[d - 1],
            recv_sem=recv.at[d - 1],
            device_id=(a - d if reverse else a + d, b, n, c),
            device_id_type=MESH,
        )

    def sends(d):
        return a >= d if reverse else a + d < planes

    def receives(d):
        return a + d < planes if reverse else a >= d

    for d in range(1, planes):
        @pl.when(sends(d))
        def _():
            copy(d).start()

    for d in range(1, planes):
        @pl.when(receives(d))
        def _():
            copy(d).wait_recv()

    for i in range(4):
        at = slice(i, i + 1)
        value = came[planes - 2, 1, at, :]
        for d in range(planes - 2, 0, -1):
            value = came[d - 1, 0, at, :] * value + came[d - 1, 1, at, :]
        to_far = near_mul[i] * value + near_add[i]
        for kb in range(2):
            is_far = (b if kb == 0 else 1 - b) == far_at
            at = (i // 2) * 4 + kb * 2 + i % 2
            out_ref[at] = jnp.where(is_far, to_far, value)

    for d in range(1, planes):
        @pl.when(sends(d))
        def _():
            copy(d).wait_send()


def pass_rows_kernel(reverse, edge_ref, out_ref, leaving, came, send, recv):
    a, b, n, c = places()
    planes = lax.axis_size("a")
    near_at, far_at = (1, 0) if reverse else (0, 1)
    came[...] = jnp.zeros_like(came)
    out_ref[...] = jnp.zeros_like(out_ref)
    first = 0 if reverse else 4
    for i, value in enumerate(earlier_blocks(edge_ref, far_at, first, 4)):
        leaving[i * 4 : i * 4 + 4, :] = value
    greet(column_peers(planes))
    copy = pltpu.make_async_remote_copy(
        src_ref=leaving,
        dst_ref=came,
        send_sem=send.at[0],
        recv_sem=recv.at[0],
        device_id=(a - 1 if reverse else a + 1, b, n, c),
        device_id_type=MESH,
    )
    sends = a >= 1 if reverse else a + 1 < planes
    receives = a + 1 < planes if reverse else a >= 1

    @pl.when(sends)
    def _():
        copy.start()

    @pl.when(receives)
    def _():
        copy.wait_recv()

    for i in range(4):
        for kb in range(2):
            is_far = (b if kb == 0 else 1 - b) == far_at
            at = (i // 2) * 4 + kb * 2 + i % 2
            other = (i // 2) * 4 + (1 - kb) * 2 + i % 2
            out_ref[at, first : first + 4, :] = jnp.where(
                is_far, edge_ref[other, first : first + 4, :], came[i * 4 : i * 4 + 4, :]
            )

    @pl.when(sends)
    def _():
        copy.wait_send()


def pass_along(ident, name, reverse, *edges):
    shape = edges[0].shape
    planes = lax.axis_size("a")
    vmem = pl.BlockSpec(memory_space=pltpu.VMEM)
    if len(edges) == 2:
        body, out = pass_state_kernel, (shape[0], 1, shape[2])
        buffers = [(2, 4) + shape[2:], (planes - 1, 2, 4) + shape[2:]]
    else:
        body, out = pass_rows_kernel, shape
        buffers = [(16,) + shape[2:]] * 2
    return pl.pallas_call(
        functools.partial(body, reverse),
        in_specs=[vmem] * len(edges),
        out_specs=vmem,
        out_shape=jax.ShapeDtypeStruct(out, F32),
        scratch_shapes=[pltpu.VMEM(shape, F32) for shape in buffers]
        + [pltpu.SemaphoreType.DMA((planes - 1,))] * 2,
        compiler_params=pltpu.CompilerParams(
            collective_id=ident, has_side_effects=True, vmem_limit_bytes=VMEM_LIMIT
        ),
        cost_estimate=pl.CostEstimate(flops=0, bytes_accessed=1 << 20, transcendentals=0),
        name=name,
    )(*edges)


def norm_product_kernel(info, tok_ref, w_ref, gain_ref, n_ref, gate_ref, lin_ref, tail_ref):
    rows, d_model = tok_ref.shape[1:]
    step = min(64, rows)

    @pl.loop(0, rows // step)
    def _(i):
        at = pl.ds(pl.multiple_of(i * step, step), step)
        value = tok_ref[0, at, :].astype(F32)
        factor = lax.rsqrt(jnp.mean(value * value, axis=-1, keepdims=True) + EPS)
        n_ref[0, at, :] = (value * factor * gain_ref[...]).astype(BF)

    wide = gate_ref.shape[2]
    both = mdot(n_ref[0], w_ref[...])
    used = both.shape[1] // 2
    pad = [jnp.zeros((rows, wide - used), F32)] if wide > used else []
    gate_ref[0] = jnp.concatenate([both[:, :used]] + pad, 1)
    low = jnp.concatenate([both[:, used:]] + pad, 1).astype(BF)
    lin_ref[0] = low
    tail_ref[0] = low.astype(F32)[rows - 8 :, :]


def row_places(info, rows, nseq):
    i = pl.program_id(0)
    pos = info[i, 0] + lax.broadcasted_iota(jnp.int32, (rows, 1), 0)
    begin = jnp.zeros((rows, 1), jnp.int32) + info[i, 1]
    seg = jnp.zeros((rows, 1), jnp.int32)
    for s in range(1, nseq):
        begin = jnp.where(pos >= info[i, 1 + s], info[i, 1 + s], begin)
        seg = jnp.where(pos >= info[i, 1 + s], s, seg)
    return pos, begin, seg


def inputs_by_tap(ext, lin_ref, rim_ref, conv0_ref, begin_at, seg, taps):
    rows = lin_ref.shape[1]
    back = taps - 1
    ext[0:8, :] = rim_ref[0]
    ext[8 : 8 + rows, :] = lin_ref[0].astype(F32)
    slots = conv0_ref.shape[1]
    column = lax.broadcasted_iota(jnp.int32, (rows, slots), 1)
    found = [ext[8 : 8 + rows, :]]
    for k in range(1, taps):
        hot = (column == seg * back + begin_at - k + back) & (begin_at < k)
        stored = mdot(jnp.where(hot, 1.0, 0.0).astype(BF), conv0_ref[0])
        found.append(jnp.where(begin_at >= k, ext[8 - k : 8 - k + rows, :], stored))
    return found


def run_scan(a_s, b_s, p_ref, s_ref, rows, reverse):
    width = b_s.shape[1]
    groups = rows // 8
    row = lax.broadcasted_iota(jnp.int32, (8, width), 0)
    if reverse:
        row = 7 - row

    def step(i, carry):
        cp, cs = carry
        g = groups - 1 - i if reverse else i
        at = pl.ds(pl.multiple_of(g * 8, 8), 8)
        a, b = a_s[at, :], b_s[at, :]
        for d in (1, 2, 4):
            by = 8 - d if reverse else d
            inside = row >= d
            a_far = jnp.where(inside, pltpu.roll(a, by, 0), 1.0)
            b_far = jnp.where(inside, pltpu.roll(b, by, 0), 0.0)
            b = a * b_far + b
            a = a * a_far
        b = a * cs + b
        a = a * cp
        p_ref[0, at, :] = a
        s_ref[0, at, :] = b
        last = 0 if reverse else 7
        return a[last : last + 1], b[last : last + 1]

    start = (jnp.ones((1, width), F32), jnp.zeros((1, width), F32))
    lax.fori_loop(0, groups, step, start, unroll=4)


V_CBIAS, V_ABIAS, V_IBIAS, V_SOFT = 0, 1, 2, 3


def forward_kernel(
    nseq, taps, info, lin_ref, rim_ref, conv0_ref, state0_ref, wg_ref, vec_ref,
    conv_ref, retain_ref, admit_ref, p_ref, s_ref, pe_ref, se_ref, ext, a_s, b_s,
):
    i = pl.program_id(0)
    rows, wide = lin_ref.shape[1:]
    pos, begin, seg = row_places(info, rows, nseq)
    at = pos - begin

    def vec(k):
        return vec_ref[k : k + 1, :]

    by_tap = inputs_by_tap(ext, lin_ref, rim_ref, conv0_ref, at, seg, taps)
    total = vec(taps + V_CBIAS)
    for k in range(taps):
        total = total + vec(k) * by_tap[k]
    low = total.astype(BF)
    conv_ref[0] = low
    conv = low.astype(F32)
    both = mdot(low, wg_ref[...])
    retain = jax.nn.sigmoid(both[:, :wide] + vec(taps + V_ABIAS))
    admit = jax.nn.sigmoid(both[:, wide:] + vec(taps + V_IBIAS))
    retain_ref[0] = retain
    admit_ref[0] = admit
    a = jnp.exp(-8.0 * retain * vec(taps + V_SOFT))
    mult = jnp.sqrt(jnp.maximum((1.0 - a) * (1.0 + a), FLOOR))
    drive = mult * admit * conv
    for s in range(nseq):
        drive = drive + jnp.where(pos == info[i, 1 + s], a * state0_ref[0, s : s + 1, :], 0.0)
    a_s[...] = jnp.where(at == 0, 0.0, a)
    b_s[...] = drive
    run_scan(a_s, b_s, p_ref, s_ref, rows, False)
    pe_ref[0] = p_ref[0, rows - 8 : rows, :]
    se_ref[0] = s_ref[0, rows - 8 : rows, :]


def gelu_pair(x):
    root = 0.7978845608028654
    inner = root * (x + 0.044715 * (x * x * x))
    th = jnp.tanh(inner)
    cdf = 0.5 * (1.0 + th)
    slope = cdf + 0.5 * x * (1.0 - th * th) * (root * (1.0 + 3.0 * 0.044715 * (x * x)))
    return x * cdf, slope


def back_scan_kernel(
    nseq, taps, info, dres_ref, wo_ref, gate_ref, hidden_ref, retain_ref, vec_ref, *refs
):
    dgate_ref, p_ref, s_ref, pe_ref, se_ref, ext, a_s, b_s = refs[-8:]
    rows = gate_ref.shape[1]
    pos, begin, _ = row_places(info, rows, nseq)
    d_mixed = ndot(dres_ref[0], wo_ref[...])
    gelu, slope = gelu_pair(gate_ref[0])
    dgate_ref[0] = (d_mixed * hidden_ref[0] * slope).astype(BF)
    b_s[...] = d_mixed * gelu
    soft = vec_ref[taps + V_SOFT : taps + V_SOFT + 1, :]
    a = jnp.where(pos == begin, 0.0, jnp.exp(-8.0 * retain_ref[0] * soft))
    ext[0:rows, :] = a
    ext[rows : rows + 8, :] = jnp.ones((8, a.shape[1]), F32)
    a_s[...] = ext[1 : rows + 1, :]
    run_scan(a_s, b_s, p_ref, s_ref, rows, True)
    pe_ref[0] = ext[0:8, :] * p_ref[0, 0:8, :]
    se_ref[0] = ext[0:8, :] * s_ref[0, 0:8, :]


def back_kernel(
    nseq, taps, info, p_ref, s_ref, grad_in_ref, hidden_ref, state_in_ref, state0_ref, conv_ref,
    retain_ref, admit_ref, lin_ref, rim_ref, conv0_ref, wg_ref, vec_ref, *refs
):
    dconv_ref, head_ref, wgrad_ref, vgrad_ref, ext = refs[-5:]
    i = pl.program_id(0)
    rows, wide = lin_ref.shape[1:]
    pos, begin, seg = row_places(info, rows, nseq)
    at = pos - begin
    conv_low = conv_ref[0]
    conv = conv_low.astype(F32)
    retain, admit = retain_ref[0], admit_ref[0]
    soft = vec_ref[taps + V_SOFT : taps + V_SOFT + 1, :]
    e = p_ref[0] * grad_in_ref[0, 0:1, :] + s_ref[0]
    ext[0:8, :] = jnp.broadcast_to(state_in_ref[0], (8, wide))
    ext[8 : 8 + rows, :] = hidden_ref[0]
    previous = ext[7 : 7 + rows, :]
    for s in range(nseq):
        previous = jnp.where(pos == info[i, 1 + s], state0_ref[0, s : s + 1, :], previous)
    a = jnp.exp(-8.0 * retain * soft)
    spread = (1.0 - a) * (1.0 + a)
    mult = jnp.sqrt(jnp.maximum(spread, FLOOR))
    d_mult = e * admit * conv
    d_spread = jnp.where(spread > FLOOR, d_mult * 0.5 / mult, 0.0)
    d_log = e * previous * a - 2.0 * a * a * d_spread
    d_rate = (d_log * (-8.0 * soft) * retain * (1.0 - retain)).astype(BF)
    d_inflow = (e * mult * conv * admit * (1.0 - admit)).astype(BF)
    d_gates = jnp.concatenate([d_rate, d_inflow], 1)
    d_conv = e * mult * admit + ndot(d_gates, wg_ref[...])
    low = d_conv.astype(BF)
    dconv_ref[0] = low
    low = low.astype(F32)
    head_ref[0] = low[0:8, :]

    @pl.when(i == 0)
    def _():
        wgrad_ref[...] = jnp.zeros_like(wgrad_ref)
        vgrad_ref[...] = jnp.zeros_like(vgrad_ref)

    wgrad_ref[...] += tdot(conv_low, d_gates)
    sums = [low * v for v in inputs_by_tap(ext, lin_ref, rim_ref, conv0_ref, at, seg, taps)]
    sums += [low, d_rate.astype(F32), d_inflow.astype(F32), d_log * (-8.0 * retain)]
    for k, value in enumerate(sums):
        vgrad_ref[k : k + 1, :] += jnp.sum(value, axis=0, keepdims=True)


def back_conv_kernel(nseq, taps, info, dconv_ref, rim_ref, dgate_ref, vec_ref, *refs):
    out_ref, ext = refs[-2:]
    i = pl.program_id(0)
    rows, wide = dconv_ref.shape[1:]
    pos = info[i, 0] + lax.broadcasted_iota(jnp.int32, (rows, 1), 0)
    ext[0:rows, :] = dconv_ref[0].astype(F32)
    ext[rows : rows + 8, :] = rim_ref[0]
    total = vec_ref[0:1, :] * ext[0:rows, :]
    for k in range(1, taps):
        cut = jnp.zeros((rows, 1), jnp.int32)
        for s in range(nseq):
            start = info[i, 1 + s]
            cut = jnp.where((pos < start) & (pos + k >= start), 1, cut)
        total = total + vec_ref[k : k + 1, :] * jnp.where(cut == 0, ext[k : k + rows, :], 0.0)
    used = out_ref.shape[2] // 2
    both = [dgate_ref[0].astype(F32)[:, :used], total[:, :used]]
    out_ref[0] = jnp.concatenate(both, 1).astype(BF)


def by_block(body, info, ins, outs, scratch, done=(), name=None):
    blocks = info.shape[0]

    def spec(shape, blocked):
        zeros = (0,) * (len(shape) - 1)
        if blocked:
            return pl.BlockSpec((1,) + tuple(shape[1:]), lambda i, *_: (i,) + zeros)
        return pl.BlockSpec(tuple(shape), lambda i, *_: (0,) + zeros)

    hbm = pl.BlockSpec(memory_space=pl.ANY)
    return pl.pallas_call(
        body,
        grid_spec=pltpu.PrefetchScalarGridSpec(
            num_scalar_prefetch=1,
            grid=(blocks,),
            in_specs=[spec(v.shape, blocked) for v, blocked in ins] + [hbm] * len(done),
            out_specs=[spec(shape, blocked) for shape, _, blocked in outs],
            scratch_shapes=[pltpu.VMEM(shape, F32) for shape in scratch],
        ),
        out_shape=[jax.ShapeDtypeStruct(shape, kind) for shape, kind, _ in outs],
        compiler_params=pltpu.CompilerParams(vmem_limit_bytes=VMEM_LIMIT),
        cost_estimate=pl.CostEstimate(flops=0, bytes_accessed=1 << 20, transcendentals=0),
        name=name,
    )(info, *[v for v, _ in ins], *done)


def on_device(
    tokens,
    starts,
    init_state,
    init_conv,
    w_y,
    w_x,
    gate_a,
    gate_i,
    w_out,
    norm1_gain,
    conv_kernel,
    conv_bias,
    bias_a,
    bias_i,
    decay_param,
    w_gate,
    w_up,
    w_down,
    norm2_gain,
    cotangent,
):
    planes, count = lax.axis_size("a"), chips()
    a, b, n, c = (lax.axis_index(name) for name in ("a", "b", "n", "c"))
    u = chip()
    nn = count // 2
    rows, d_model = tokens.shape[1], tokens.shape[2]
    nseq = starts.shape[1]
    width = w_y.shape[1]
    head_w = gate_a.shape[1]
    half = gate_a.shape[0]
    taps = conv_kernel.shape[0]
    back = taps - 1
    heads_here = planes // 2
    wide_here = heads_here * head_w
    wp = -(-wide_here // 128) * 128
    hid = w_down.shape[0]
    drows = w_y.shape[0]
    nblocks = 2 * count

    def gather_a(value):
        return lax.all_gather(value, "a", axis=0, tiled=True)

    def scatter_a(value):
        return lax.psum_scatter(value, "a", scatter_dimension=0, tiled=True)

    def padded(v, axis=-1):
        pads = [(0, 0)] * v.ndim
        pads[axis] = (0, wp - wide_here)
        return jnp.pad(v, pads)

    vectors = jnp.concatenate(
        [conv_kernel, conv_bias[None], bias_a[None], bias_i[None], decay_param[None]], 0
    ).reshape(-1)
    vectors = jnp.concatenate([vectors, norm1_gain, norm2_gain]).astype(F32)
    lanes = -(-vectors.shape[0] // 1024) * 128
    vectors = jnp.pad(vectors, (0, 8 * lanes - vectors.shape[0])).reshape(8, lanes)
    at_start = jnp.concatenate([init_state[0][:, None], init_conv[0].astype(F32)], 1)
    at_start = at_start.reshape(nseq * taps, width)
    at_start = jnp.pad(at_start, ((0, 8), (0, 0)))
    at_start = at_start.at[nseq * taps, :nseq].set(starts[0].astype(F32))
    all_tokens, w_yx, w_gu, _, gate_rows, canon, at_start = start_exchange(
        tokens[0],
        w_y,
        w_x,
        w_gate,
        w_up,
        jnp.concatenate([gate_a, gate_i], 1),
        vectors,
        at_start,
    )
    w_yx = w_yx.reshape(d_model, 2 * wide_here)
    w_gu = gather_a(w_gu.reshape(-1, 2 * planes * hid))
    gate_rows = gate_rows.reshape(wide_here, -1)

    def join_halves(mine_all):
        away = swap_c(lax.dynamic_slice_in_dim(mine_all, (1 - c) * heads_here, heads_here, 0))
        own = lax.dynamic_slice_in_dim(mine_all, c * heads_here, heads_here, 0)
        first = jnp.where(c == 0, own, away)
        second = jnp.where(c == 0, away, own)
        return jnp.stack([first, second], 1).reshape((wide_here,) + mine_all.shape[2:])


    def part_halves(full):
        full = full.reshape((heads_here, 2, half) + full.shape[1:])
        own, away = pick(full, c, 1), swap_c(pick(full, 1 - c, 1))
        first = jnp.where(c == 0, own, away)
        second = jnp.where(c == 0, away, own)
        return jnp.concatenate([first, second], 0).reshape((planes * half,) + full.shape[3:])

    w_o = padded(join_halves(gather_a(w_out).reshape(planes, half, d_model)), 0)

    def block_diagonal(m):
        m = m.reshape(heads_here, head_w, head_w)
        eye = jnp.eye(heads_here, dtype=m.dtype)
        full = (m[:, :, None, :] * eye[:, None, :, None]).reshape(wide_here, wide_here)
        return padded(padded(full), 0)

    w_gates = jnp.concatenate(
        [
            block_diagonal(gate_rows[:, :head_w]),
            block_diagonal(gate_rows[:, head_w:]),
        ],
        1,
    )

    w_d = gather_a(w_down)
    f_here = planes * hid

    canon = canon.reshape(planes * nblocks, -1)
    nvec = (taps + 4) * half
    gain_one = canon[:, nvec : nvec + drows].reshape(-1)
    gain_two = canon[:, nvec + drows : nvec + 2 * drows].reshape(-1)
    mine = pick(canon[:, :nvec].reshape(2, heads_here, count, 2, taps + 4, half), c)
    mine = pick(mine, u, 1).transpose(2, 0, 1, 3).reshape(taps + 4, wide_here)
    decay_f = mine[taps + 3]
    vec = padded(jnp.concatenate([mine[: taps + 3], jax.nn.softplus(decay_f)[None]]))

    def my_channels(v):
        lead = v.shape[:-1]
        v = v.reshape(lead + (2, heads_here, count, head_w))
        v = pick(v, c, len(lead))
        return pick(v, u, len(lead) + 1).reshape(lead + (wide_here,))

    streams = 2 * nn
    at_start = at_start.reshape(streams, -1, width)
    offsets = at_start[:, nseq * taps, :nseq].astype(jnp.int32)
    at_start = my_channels(at_start[:, : nseq * taps].reshape(streams, nseq, taps, width))
    at_start = padded(at_start)
    state_0 = jnp.pad(at_start[:, :, 0], ((0, 0), (0, -nseq % 8), (0, 0)))
    conv_0 = at_start[:, :, 1:].reshape(streams, nseq * back, wp).astype(BF)
    conv_0 = jnp.pad(conv_0, ((0, 0), (0, -(nseq * back) % 16), (0, 0)))

    def per_block(v):
        v = v.reshape((2, 1, nn) + v.shape[1:])
        return jnp.broadcast_to(v, (2, 2, nn) + v.shape[3:]).reshape((nblocks,) + v.shape[3:])

    block_b = (jnp.arange(nblocks, dtype=jnp.int32) // nn) % 2
    first_row = (a * 2 + (b ^ block_b)) * rows
    position = first_row[:, None] + jnp.arange(rows, dtype=jnp.int32)[None]
    off_b = per_block(offsets)

    info = jnp.concatenate(
        [first_row[:, None], off_b, jnp.zeros((nblocks, -(nseq + 1) % 8), jnp.int32)], 1
    )

    grad_low = cotangent[0]
    grads = [grad_low] + [xor_u(grad_low, k) for k in range(1, count)]

    edge = ((nblocks, 8, wp), F32, True)
    normed, gate_in, linear, tail = by_block(
        norm_product_kernel,
        info,
        [(all_tokens, True), (w_yx, False), (gain_one[None], False)],
        [
            ((nblocks, rows, d_model), BF, True),
            ((nblocks, rows, wp), F32, True),
            ((nblocks, rows, wp), BF, True),
            edge,
        ],
        [],
        name="norm_product",
    )
    normed = normed.reshape(nblocks * rows, d_model)

    def two(v):
        return v.reshape((2, 2, nn) + v.shape[1:])

    rim = pass_along(6, "pass_rows", False, tail)
    conv_0b, state_0b = per_block(conv_0), per_block(state_0)
    full = (nblocks, rows, wp)
    conv_low, retain, admit, carry_mul, carry_add, end_mul, end_add = by_block(
        functools.partial(forward_kernel, nseq, taps),
        info,
        [
            (linear, True), (rim, True), (conv_0b, True), (state_0b, True),
            (w_gates, False), (vec, False),
        ],
        [
            (full, BF, True), (full, F32, True), (full, F32, True),
            (full, F32, True), (full, F32, True), edge, edge,
        ],
        [(rows + 8, wp), (rows, wp), (rows, wp)],
        name="mixer_forward",
    )

    (end_mul, end_add), grads = lax.optimization_barrier(((end_mul, end_add), grads))
    state_in = pass_along(7, "pass_state", False, end_mul, end_add)
    hidden = carry_mul * state_in + carry_add
    mixed_in = (hidden * jax.nn.gelu(gate_in)).astype(BF).reshape(-1, wp)
    resid, normed_two, grads = plane_reduce(
        2, "fwd", False, (mixed_in.reshape(2, count, rows, -1),), w_o, gain_two, tokens[0],
        tokens[0], grads,
    )
    normed_two = normed_two.reshape(nblocks * rows, d_model)
    grads = grads.reshape(nblocks * rows, d_model)

    pair = mdot(normed_two, w_gu)
    gate, upward = pair[:, :f_here], pair[:, f_here:]
    active, gate_back = jax.vjp(jax.nn.gelu, gate)
    inner = (active * upward).astype(BF)
    sums_d = tdot(inner, grads).astype(BF)
    grad_wd = scatter_a(sums_d)
    grads, _ = lax.optimization_barrier((grads, sums_d))
    d_inner = ndot(grads, w_d)
    d_gate = gate_back(d_inner * upward)[0].astype(BF)
    d_up = (d_inner * active).astype(BF)
    sums_g = tdot(normed_two, d_gate).astype(BF)
    sums_u = tdot(normed_two, d_up).astype(BF)
    sent_g, sent_u = scatter_a(sums_g), scatter_a(sums_u)
    parts = inner.reshape(2, count * rows, f_here)
    away = swap_c(mdot(parts[1], w_d).astype(BF))
    d_resid, d_resid_low = plane_reduce(
        3, "mid", True, (d_gate.reshape(2, count, rows, -1), d_up.reshape(2, count, rows, -1)), w_gu,
        gain_two, grad_low, resid, (), (grad_wd, sums_g, sums_u, away),
    )
    d_resid_low = d_resid_low.reshape(nblocks * rows, d_model)

    sums_o = tdot(mixed_in, d_resid_low)[:wide_here].astype(BF)
    grad_wo = scatter_a(part_halves(sums_o))
    own, _ = lax.optimization_barrier((parts[0], sums_o))
    low = (mdot(own, w_d) + away.astype(F32)).astype(BF).reshape(count, rows, d_model)
    result = resid + low[0].astype(F32)
    for k in range(1, count):
        result = result + xor_u(low[k], k).astype(F32)
    result = result.astype(BF)

    d_gate_in, back_mul, back_add, end_mul, end_add = by_block(
        functools.partial(back_scan_kernel, nseq, taps),
        info,
        [
            (d_resid_low.reshape(nblocks, rows, d_model), True), (w_o, False), (gate_in, True),
            (hidden, True), (retain, True), (vec, False),
        ],
        [(full, BF, True), (full, F32, True), (full, F32, True), edge, edge],
        [(rows + 8, wp), (rows, wp), (rows, wp)],
        (low, sent_g),
        name="mixer_back_scan",
    )
    grad_in = pass_along(8, "pass_state_back", True, end_mul, end_add)
    d_conv_low, head, sums_gates, vec_grads = by_block(
        functools.partial(back_kernel, nseq, taps),
        info,
        [
            (back_mul, True), (back_add, True), (grad_in, True), (hidden, True),
            (state_in, True), (state_0b, True), (conv_low, True), (retain, True),
            (admit, True), (linear, True), (rim, True), (conv_0b, True), (w_gates, False), (vec, False),
        ],
        [(full, BF, True), edge, ((wp, 2 * wp), F32, False), ((taps + 4, wp), F32, False)],
        [(rows + 8, wp)],
        (result, sent_u),
        name="mixer_back",
    )

    def diagonal(m):
        m = m.reshape(heads_here, head_w, heads_here, head_w)
        return jnp.concatenate([m[h, :, h] for h in range(heads_here)], 0)

    grad_gates = jnp.concatenate(
        [
            diagonal(sums_gates[:wide_here, :wide_here]),
            diagonal(sums_gates[:wide_here, wp : wp + wide_here]),
        ],
        1,
    )
    rim_back = pass_along(9, "pass_rows_back", True, head)
    d_both = by_block(
        functools.partial(back_conv_kernel, nseq, taps),
        info,
        [(d_conv_low, True), (rim_back, True), (d_gate_in, True), (vec, False)],
        [((nblocks, rows, 2 * wide_here), BF, True)],
        [(rows + 8, wp)],
        (grad_wo,),
        name="mixer_back_conv",
    )[0]
    vec_grads = vec_grads[:, :wide_here].T
    vec_grads = jnp.concatenate(
        [vec_grads[:, :-1], vec_grads[:, -1:] * jax.nn.sigmoid(decay_f)[:, None]], 1
    )
    late = jnp.concatenate([grad_gates, vec_grads], 1).astype(BF)
    late = scatter_a(part_halves(late)).astype(F32)
    grad_wa, grad_wi = late[:, :head_w], late[:, head_w : 2 * head_w]
    vec_grads = late[:, 2 * head_w :].T

    sums_yx = tdot(normed, d_both.reshape(nblocks * rows, 2 * wide_here)).astype(BF)
    end = jnp.concatenate(
        [offsets[:, 1:], jnp.full((streams, 1), planes * 2 * rows, jnp.int32)], 1
    )
    end_b = per_block(end) - 1
    hot = (position[:, None, :] == end_b[:, :, None]).astype(BF)
    lasts = lax.dot_general(
        hot, hidden.astype(BF), (((2,), (1,)), ((0,), (0,))), preferred_element_type=F32
    )
    slots = jnp.arange(back, dtype=jnp.int32)
    where_conv = (end_b[:, :, None] - back + 1 + slots).reshape(nblocks, nseq * back)
    hot = (position[:, None, :] == where_conv[:, :, None]).astype(BF)
    conv_lasts = lax.dot_general(
        hot, linear, (((2,), (1,)), ((0,), (0,))), preferred_element_type=F32
    )
    lasts = two(jnp.concatenate([lasts, conv_lasts], 1)[..., :wide_here])
    lasts = (lasts[:, 0] + lasts[:, 1]).astype(BF)
    input_grad, grad_wg, grad_wu, found = plane_reduce(
        4, "last", True, (d_both.reshape(2, count, rows, -1),), w_yx, gain_one, tokens[0], d_resid,
        (sent_g, sent_u), (sums_yx, result), hid, lasts,
    )
    grad_wy, grad_wx = finish(scatter_a(sums_yx), head_w)

    def gain_grad(gain, *pairs):
        total = sum(jnp.sum(w.astype(F32) * g, axis=1) for w, g in pairs)
        return total / gain.astype(F32)

    grad_gain_one = gain_grad(norm1_gain, (w_y, grad_wy), (w_x, grad_wx))
    grad_gain_two = gain_grad(norm2_gain, (w_gate, grad_wg), (w_up, grad_wu))

    found = found.reshape(2, count, nseq * taps, heads_here, head_w)
    found = found.transpose(2, 0, 3, 1, 4).reshape(nseq * taps, width)
    final_state = found[:nseq].astype(F32)
    final_conv = found[nseq:].reshape(nseq, back, width)

    return (
        result[None],
        input_grad[None],
        final_state[None],
        final_conv[None],
        grad_wy,
        grad_wx,
        grad_wa,
        grad_wi,
        grad_wo.astype(F32),
        grad_gain_one,
        vec_grads[:taps],
        vec_grads[taps],
        vec_grads[taps + 1],
        vec_grads[taps + 2],
        vec_grads[taps + 3],
        grad_wg,
        grad_wu,
        grad_wd.astype(F32),
        grad_gain_two,
    )


WIDE = ("a", "b")
EVERY = ("a", "b", "n", "c")
HIGH = lax.Precision.HIGHEST


def passed_along(value, axis, by):
    size = lax.axis_size(axis)
    pairs = [(i, i + by) for i in range(size) if 0 <= i + by < size]
    return lax.ppermute(value, axis, pairs)


def entering(value, axis, combine, identity, reverse):
    size, place = (lax.axis_size(axis), lax.axis_index(axis))
    everything = jax.tree.map(lambda part: lax.all_gather(part, axis), value)
    start = jax.tree.map(
        lambda part, zero: jnp.broadcast_to(jnp.asarray(zero, part.dtype), part.shape),
        value,
        identity,
    )

    def hop(k, before):
        at = size - 1 - k if reverse else k
        reached = at > place if reverse else at < place
        new = combine(before, jax.tree.map(lambda part: part[at], everything))
        return jax.tree.map(lambda a, b: jnp.where(reached, a, b), new, before)

    return lax.fori_loop(0, size, hop, start)


def merged_2(value, axis, combine):
    everything = jax.tree.map(
        lambda part, kind: lax.all_gather(part.astype(kind), axis),
        value,
        jax.tree.map(lambda a: jnp.bfloat16 if a.dtype == jnp.float32 else a.dtype, value),
    )

    def take(k):
        return jax.tree.map(lambda part, own: part[k].astype(own.dtype), everything, value)

    return lax.fori_loop(
        1, lax.axis_size(axis), lambda k, so_far: combine(so_far, take(k)), take(0)
    )


def link(earlier, later):
    return (earlier[0] * later[0], later[0] * earlier[1] + later[1])


def norm_back(value, factor, gain, grad):
    weighted = grad * gain
    inner = jnp.mean(weighted * value, axis=-1, keepdims=True)
    return (
        factor * weighted - value * factor * factor * factor * inner,
        jnp.sum(grad * value * factor, axis=0),
    )


def later_one(first, second):
    pick = first[0] > second[0]
    return (
        jnp.where(pick, first[0], second[0]),
        jnp.where(pick[:, None], first[1], second[1]),
        jnp.where(pick[:, None, None], first[2], second[2]),
    )


def on_device_any(
    tokens,
    starts,
    init_state,
    init_conv,
    w_y,
    w_x,
    gate_a,
    gate_i,
    w_out,
    norm1_gain,
    conv_kernel,
    conv_bias,
    bias_a,
    bias_i,
    decay_param,
    w_gate,
    w_up,
    w_down,
    norm2_gain,
    cotangent,
):
    inputs = tokens[0].astype(jnp.float32)
    offsets = starts[0]
    nseqs = offsets.shape[0]
    rows_here = inputs.shape[0]
    width = w_y.shape[1]
    head_w = gate_a.shape[1]
    heads = width // head_w
    place = lax.axis_index(WIDE)
    mixer = (
        lax.all_gather(w_y, EVERY, axis=0, tiled=True),
        lax.all_gather(w_x, EVERY, axis=0, tiled=True),
        lax.all_gather(gate_a, EVERY, axis=0, tiled=True),
        lax.all_gather(gate_i, EVERY, axis=0, tiled=True),
        lax.all_gather(w_out, EVERY, axis=0, tiled=True),
        lax.all_gather(norm1_gain, EVERY, axis=0, tiled=True),
        lax.all_gather(conv_kernel, EVERY, axis=1, tiled=True),
        lax.all_gather(conv_bias, EVERY, axis=0, tiled=True),
        lax.all_gather(bias_a, EVERY, axis=0, tiled=True),
        lax.all_gather(bias_i, EVERY, axis=0, tiled=True),
        lax.all_gather(decay_param, EVERY, axis=0, tiled=True),
    )
    wy_full, wx_full, wa_full, wi_full, wo_full, gain_one, kernel, cbias, abias, ibias, decay = (
        mixer
    )
    gain_one = gain_one.astype(jnp.float32)
    kernel = kernel.astype(jnp.float32)
    taps = kernel.shape[0]
    back = taps - 1
    position = place * rows_here + jnp.arange(rows_here, dtype=jnp.int32)

    def segment_of(where_at):
        return jnp.sum((where_at[:, None] >= offsets[None, :]).astype(jnp.int32), axis=1) - 1

    segment = segment_of(position)
    member = segment[:, None] == jnp.arange(nseqs, dtype=jnp.int32)[None, :]
    begin = jnp.sum(jnp.where(member, offsets[None, :], 0), axis=1)
    opening = (position == begin)[:, None]
    scale_one = lax.rsqrt(jnp.mean(inputs * inputs, axis=-1, keepdims=True) + EPS)
    normed = (inputs * scale_one * gain_one).astype(jnp.bfloat16)
    gate_in = mdot(normed, wy_full)
    linear = mdot(normed, wx_full).astype(jnp.bfloat16)
    rim_rows = passed_along(linear[rows_here - back :], WIDE, 1)
    extended = jnp.concatenate([rim_rows, linear], 0)
    stored = mdot(member.astype(jnp.bfloat16), init_conv[0].reshape(nseqs, back * width)).reshape(
        rows_here, back, width
    )
    inputs_by_tap = [linear.astype(jnp.float32)]
    for shift_by in range(1, taps):
        earlier = extended[back - shift_by : back - shift_by + rows_here].astype(jnp.float32)
        offset = position - shift_by - begin
        from_start = jnp.zeros((rows_here, width), jnp.float32)
        for slot in range(back):
            from_start = from_start + jnp.where(
                (offset + back == slot)[:, None], stored[:, slot], 0.0
            )
        inputs_by_tap.append(jnp.where((offset >= 0)[:, None], earlier, from_start))
    conv_sum = cbias.astype(jnp.float32)
    for shift_by in range(taps):
        conv_sum = conv_sum + kernel[shift_by] * inputs_by_tap[shift_by]
    conv_low = conv_sum.astype(jnp.bfloat16)
    conv_val = conv_low.astype(jnp.float32)
    blocks = conv_low.reshape(rows_here, heads, head_w)
    wa_heads = wa_full.reshape(heads, head_w, head_w)
    wi_heads = wi_full.reshape(heads, head_w, head_w)
    rate = jnp.einsum("thi,hij->thj", blocks, wa_heads, preferred_element_type=jnp.float32).reshape(
        rows_here, width
    ) + abias.astype(jnp.float32)
    inflow = jnp.einsum(
        "thi,hij->thj", blocks, wi_heads, preferred_element_type=jnp.float32
    ).reshape(rows_here, width) + ibias.astype(jnp.float32)
    retain = jax.nn.sigmoid(rate)
    admit = jax.nn.sigmoid(inflow)
    decay_f = decay.astype(jnp.float32)
    soft_decay = jax.nn.softplus(decay_f)
    log_a = -8.0 * retain * soft_decay
    decay_now = jnp.exp(log_a)
    spread = -jnp.expm1(2.0 * log_a)
    mult = jnp.sqrt(jnp.maximum(spread, FLOOR))
    drive = mult * admit * conv_val
    state_rows = jnp.dot(member.astype(jnp.float32), init_state[0], precision=HIGH)
    a_used = jnp.where(opening, 0.0, decay_now)
    b_used = jnp.where(opening, decay_now * state_rows + drive, drive)
    carry_mul, carry_add = lax.associative_scan(link, (a_used, b_used), axis=0)
    identity = (jnp.ones((width,), jnp.float32), jnp.zeros((width,), jnp.float32))
    state_in = entering(
        (carry_mul[rows_here - 1], carry_add[rows_here - 1]), WIDE, link, identity, False
    )[1]
    hidden = carry_mul * state_in + carry_add
    gelu_y, gelu_y_back = jax.vjp(jax.nn.gelu, gate_in)
    mixed_in = (hidden * gelu_y).astype(jnp.bfloat16)
    resid = inputs + mdot(mixed_in, wo_full)
    wg_full, wu_full, wd_full, gain_two = (
        lax.all_gather(w_gate, EVERY, axis=0, tiled=True),
        lax.all_gather(w_up, EVERY, axis=0, tiled=True),
        lax.all_gather(w_down, EVERY, axis=0, tiled=True),
        lax.all_gather(norm2_gain, EVERY, axis=0, tiled=True),
    )
    gain_two = gain_two.astype(jnp.float32)
    scale_two = lax.rsqrt(jnp.mean(resid * resid, axis=-1, keepdims=True) + EPS)
    normed_two = (resid * scale_two * gain_two).astype(jnp.bfloat16)
    gate = mdot(normed_two, wg_full)
    upward = mdot(normed_two, wu_full)
    active, gate_back = jax.vjp(jax.nn.gelu, gate)
    inner = (active * upward).astype(jnp.bfloat16)
    result = (resid + mdot(inner, wd_full)).astype(jnp.bfloat16)
    local_rows = jnp.arange(rows_here, dtype=jnp.int32)
    last_row = jnp.max(jnp.where(member, local_rows[:, None], -1), axis=0)
    present = last_row >= 0
    safe_row = jnp.maximum(last_row, 0)
    marker = jnp.where(present, (place * rows_here + last_row).astype(jnp.float32), -1.0)
    state_last = jnp.where(present[:, None], hidden[safe_row], 0.0)
    conv_rows = extended[safe_row[:, None] + 1 + jnp.arange(back, dtype=jnp.int32)[None, :]].astype(
        jnp.float32
    )
    conv_last = jnp.where(present[:, None, None], conv_rows, 0.0)
    merged = merged_2((marker, state_last, conv_last), WIDE, later_one)
    wg_back, wu_back, wd_back = (
        lax.all_gather(w_gate, EVERY, axis=0, tiled=True),
        lax.all_gather(w_up, EVERY, axis=0, tiled=True),
        lax.all_gather(w_down, EVERY, axis=0, tiled=True),
    )
    grad_low = cotangent[0]
    grad_out = grad_low.astype(jnp.float32)
    d_inner = ndot(grad_low, wd_back)
    grad_wd = tdot(inner, grad_low)
    d_gate = gate_back(d_inner * upward)[0].astype(jnp.bfloat16)
    d_up = (d_inner * active).astype(jnp.bfloat16)
    grad_wg = tdot(normed_two, d_gate)
    grad_wu = tdot(normed_two, d_up)
    d_normed_two = ndot(d_gate, wg_back) + ndot(d_up, wu_back)
    d_resid_norm, grad_gain_two = norm_back(resid, scale_two, gain_two, d_normed_two)
    d_resid = grad_out + d_resid_norm
    wy_back, wx_back, wa_back, wi_back, wo_back = (
        lax.all_gather(w_y, EVERY, axis=0, tiled=True),
        lax.all_gather(w_x, EVERY, axis=0, tiled=True),
        lax.all_gather(gate_a, EVERY, axis=0, tiled=True),
        lax.all_gather(gate_i, EVERY, axis=0, tiled=True),
        lax.all_gather(w_out, EVERY, axis=0, tiled=True),
    )
    d_resid_low = d_resid.astype(jnp.bfloat16)
    d_mixed = ndot(d_resid_low, wo_back)
    grad_wo = tdot(mixed_in, d_resid_low)
    d_hidden = d_mixed * gelu_y
    d_gate_in = gelu_y_back(d_mixed * hidden)[0].astype(jnp.bfloat16)
    forward_mul = jnp.concatenate([a_used[1:], jnp.ones((1, width), jnp.float32)], 0)
    back_mul, back_add = lax.associative_scan(link, (forward_mul, d_hidden), reverse=True, axis=0)
    head_map = (a_used[0] * back_mul[0], a_used[0] * back_add[0])
    grad_in = entering(head_map, WIDE, link, identity, True)[1]
    total_grad = back_mul * grad_in + back_add
    previous = jnp.concatenate([state_in[None], hidden[:-1]], 0)
    previous = jnp.where(opening, state_rows, previous)
    d_decay = total_grad * previous
    d_mult = total_grad * admit * conv_val
    d_admit = total_grad * mult * conv_val
    d_conv = total_grad * mult * admit
    d_spread = jnp.where(spread > FLOOR, d_mult * 0.5 / mult, 0.0)
    d_log = d_decay * decay_now - 2.0 * decay_now * decay_now * d_spread
    d_retain = d_log * (-8.0 * soft_decay)
    grad_decay = jnp.sum(d_log * (-8.0 * retain), axis=0) * jax.nn.sigmoid(decay_f)
    d_rate = (d_retain * retain * (1.0 - retain)).astype(jnp.bfloat16)
    d_inflow = (d_admit * admit * (1.0 - admit)).astype(jnp.bfloat16)
    grad_abias = jnp.sum(d_rate.astype(jnp.float32), axis=0)
    grad_ibias = jnp.sum(d_inflow.astype(jnp.float32), axis=0)
    rate_heads = d_rate.reshape(rows_here, heads, head_w)
    inflow_heads = d_inflow.reshape(rows_here, heads, head_w)
    grad_wa = jnp.einsum(
        "thi,thj->hij", blocks, rate_heads, preferred_element_type=jnp.float32
    ).reshape(width, head_w)
    grad_wi = jnp.einsum(
        "thi,thj->hij", blocks, inflow_heads, preferred_element_type=jnp.float32
    ).reshape(width, head_w)
    d_conv = d_conv + jnp.einsum(
        "thj,hij->thi",
        rate_heads,
        wa_back.reshape(heads, head_w, head_w),
        preferred_element_type=jnp.float32,
    ).reshape(rows_here, width)
    d_conv = d_conv + jnp.einsum(
        "thj,hij->thi",
        inflow_heads,
        wi_back.reshape(heads, head_w, head_w),
        preferred_element_type=jnp.float32,
    ).reshape(rows_here, width)
    d_conv_low = d_conv.astype(jnp.bfloat16)
    d_conv_val = d_conv_low.astype(jnp.float32)
    rim_back = passed_along(d_conv_low[:back], WIDE, -1)
    ahead = jnp.concatenate([d_conv_low, rim_back], 0)
    d_linear = kernel[0] * d_conv_val
    kernel_grads = [jnp.sum(d_conv_val * inputs_by_tap[0], axis=0)]
    for shift_by in range(1, taps):
        later_rows = ahead[shift_by : shift_by + rows_here].astype(jnp.float32)
        same = (segment_of(position + shift_by) == segment)[:, None]
        d_linear = d_linear + kernel[shift_by] * jnp.where(same, later_rows, 0.0)
        kernel_grads.append(jnp.sum(d_conv_val * inputs_by_tap[shift_by], axis=0))
    grad_kernel = jnp.stack(kernel_grads, 0)
    grad_cbias = jnp.sum(d_conv_val, axis=0)
    d_linear_low = d_linear.astype(jnp.bfloat16)
    d_normed = ndot(d_gate_in, wy_back) + ndot(d_linear_low, wx_back)
    grad_wy = tdot(normed, d_gate_in)
    grad_wx = tdot(normed, d_linear_low)
    d_input_norm, grad_gain_one = norm_back(inputs, scale_one, gain_one, d_normed)
    input_grad = (d_resid + d_input_norm).astype(jnp.bfloat16)
    every_sum = (
        lax.psum_scatter(grad_wy, EVERY, scatter_dimension=0, tiled=True),
        lax.psum_scatter(grad_wx, EVERY, scatter_dimension=0, tiled=True),
        lax.psum_scatter(grad_wa, EVERY, scatter_dimension=0, tiled=True),
        lax.psum_scatter(grad_wi, EVERY, scatter_dimension=0, tiled=True),
        lax.psum_scatter(grad_wo, EVERY, scatter_dimension=0, tiled=True),
        lax.psum_scatter(grad_gain_one, EVERY, scatter_dimension=0, tiled=True),
        lax.psum_scatter(grad_kernel, EVERY, scatter_dimension=1, tiled=True),
        lax.psum_scatter(grad_cbias, EVERY, scatter_dimension=0, tiled=True),
        lax.psum_scatter(grad_abias, EVERY, scatter_dimension=0, tiled=True),
        lax.psum_scatter(grad_ibias, EVERY, scatter_dimension=0, tiled=True),
        lax.psum_scatter(grad_decay, EVERY, scatter_dimension=0, tiled=True),
        lax.psum_scatter(grad_wg, EVERY, scatter_dimension=0, tiled=True),
        lax.psum_scatter(grad_wu, EVERY, scatter_dimension=0, tiled=True),
        lax.psum_scatter(grad_wd, EVERY, scatter_dimension=0, tiled=True),
        lax.psum_scatter(grad_gain_two, EVERY, scatter_dimension=0, tiled=True),
    )
    mixer_sums = every_sum[:11]
    mlp_sums = every_sum[11:]
    return (
        result[None],
        input_grad[None],
        merged[1][None],
        merged[2].astype(jnp.bfloat16)[None],
        mixer_sums[0],
        mixer_sums[1],
        mixer_sums[2],
        mixer_sums[3],
        mixer_sums[4],
        mixer_sums[5],
        mixer_sums[6],
        mixer_sums[7],
        mixer_sums[8],
        mixer_sums[9],
        mixer_sums[10],
        mlp_sums[0],
        mlp_sums[1],
        mlp_sums[2],
        mlp_sums[3],
    )


def solution(mesh):
    wide, narrow = mesh.shape["wide"], mesh.shape["narrow"]
    def plan(*args):
        fits = args[6].shape[0] * 2 == args[6].shape[1] and narrow == 4
        return (on_device if fits else on_device_any)(*args)

    fine = Mesh(mesh.devices.reshape(wide // 2, 2, narrow // 2, 2), ("a", "b", "n", "c"))
    w, s = ("a", "b"), ("n", "c")
    everywhere = ("a", "b", "n", "c")
    acts, rows, vec = P(s, w, None), P(everywhere, None), P(everywhere)
    return jax.shard_map(
        plan,
        mesh=fine,
        in_specs=(
            acts,
            P(s, None),
            P(s, None, None),
            P(s, None, None, None),
            rows, rows, rows, rows, rows,
            vec,
            P(None, everywhere),
            vec, vec, vec, vec,
            rows, rows, rows,
            vec,
            acts,
        ),
        out_specs=(
            acts,
            acts,
            P(s, None, None),
            P(s, None, None, None),
            rows, rows, rows, rows, rows,
            vec,
            P(None, everywhere),
            vec, vec, vec, vec,
            rows, rows, rows,
            vec,
        ),
        check_vma=False,
    )
```

```python
import functools

import jax
import jax.numpy as jnp
from jax import lax
from jax.experimental import pallas as pl
from jax.experimental.pallas import tpu as pltpu
from jax.sharding import Mesh
from jax.sharding import PartitionSpec as P

EPS = 1e-06
FLOOR = 0.001
BF = jnp.bfloat16
F32 = jnp.float32


def tdot(left, right):
    return lax.dot_general(left, right, (((0,), (0,)), ((), ())), preferred_element_type=F32)


def ndot(left, right):
    return lax.dot_general(left, right, (((1,), (1,)), ((), ())), preferred_element_type=F32)


def mdot(left, right):
    return jnp.dot(left, right, preferred_element_type=F32)


def pick(stacked, index, axis=0):
    return lax.dynamic_index_in_dim(stacked, index, axis, keepdims=False)


def swap_c(value):
    return lax.ppermute(value, "c", [(0, 1), (1, 0)])


def xor_u(value, k):
    size = lax.axis_size("b") * lax.axis_size("n")
    return lax.ppermute(value, ("b", "n"), [(i, i ^ k) for i in range(size)])


def shift_a(value, by):
    size = lax.axis_size("a")
    return lax.ppermute(value, "a", [(i, i + by) for i in range(size) if 0 <= i + by < size])


def chips():
    return lax.axis_size("b") * lax.axis_size("n")


def chip():
    return lax.axis_index("b") * lax.axis_size("n") + lax.axis_index("n")


MESH = pl.DeviceIdType.MESH
VMEM_LIMIT = 60 * 1024 * 1024


def places():
    return tuple(lax.axis_index(name) for name in ("a", "b", "n", "c"))


def neighbours():
    a, b, n, c = places()
    return (a, 1 - b, n, c), (a, b, 1 - n, c), (a, b, n, 1 - c)


def greet(peers):
    barrier = pltpu.get_barrier_semaphore()
    for peer in peers:
        pl.semaphore_signal(barrier, inc=1, device_id=peer, device_id_type=MESH)
    pl.semaphore_wait(barrier, len(peers))


class Mover:
    def __init__(self, send, recv):
        self.send, self.recv, self.made = send, recv, {}
        self.names = []

    def copy(self, name, src, dst, peer):
        if name not in self.names:
            self.names.append(name)
        at = self.names.index(name)
        made = pltpu.make_async_remote_copy(
            src_ref=src,
            dst_ref=dst,
            send_sem=self.send.at[at],
            recv_sem=self.recv.at[at],
            device_id=peer,
            device_id_type=MESH,
        )
        self.made[name] = made
        return made

    def start(self, name, src, dst, peer):
        self.copy(name, src, dst, peer).start()

    def arrived(self, name):
        self.made[name].wait_recv()

    def sent(self):
        for made in self.made.values():
            made.wait_send()


def gather_plane_start(move, mine, everyone, h, half_rows):
    x, y, z = neighbours()
    at = pl.ds(h * half_rows, half_rows)
    move.start(f"gx{h}", mine.at[at], everyone.at[2, at], x)
    move.start(f"gy{h}", mine.at[at], everyone.at[1, at], y)
    move.start(f"gc{h}", mine.at[at], everyone.at[4, at], z)


def gather_plane_rest(move, everyone, half_rows, stage=None):
    x, y, z = neighbours()
    rows = [pl.ds(h * half_rows, half_rows) for h in range(2)]

    def on(name, k, h):
        move.start(name, everyone.at[k, rows[h]], everyone.at[4 + k, rows[h]], z)

    if stage in (None, 0):
        move.arrived("gx0")
        move.start("fy", everyone.at[2, rows[0]], everyone.at[3, rows[0]], y)
        on("cx0", 2, 0)
        move.arrived("gy1")
        move.start("fx", everyone.at[1, rows[1]], everyone.at[3, rows[1]], x)
        on("cy1", 1, 1)
    if stage in (None, 1):
        move.arrived("gx1")
        on("cx1", 2, 1)
        move.arrived("gy0")
        on("cy0", 1, 0)
    if stage in (None, 2):
        move.arrived("fy")
        on("cd0", 3, 0)
        move.arrived("fx")
        on("cd1", 3, 1)
        for name in ("gc0", "gc1", "cx0", "cx1", "cy0", "cy1", "cd0", "cd1"):
            move.arrived(name)


GATHER_COPIES = 14


def plane_peers_of():
    a, b, n, c = places()
    peers = {}
    for kc in range(2):
        for k in range(4):
            if (kc, k) != (0, 0):
                there = (a, 1 - b if k & 2 else b, 1 - n if k & 1 else n, 1 - c if kc else c)
                peers[kc, k] = there
    return peers


def peer_owner(kc, k):
    _, b, n, c = places()
    return ((b * 2 + n) ^ k) * 2 + (1 - c if kc else c)


def set_side_by_side(pieces, order, width):
    group = 1
    while group * width % 128 and group < len(order):
        group += 1
    for i in range(0, len(order), group):
        runs = [pieces[p, :, o : o + width].astype(F32) for p, o in order[i : i + group]]
        yield slice(i * width, (i + len(runs)) * width), jnp.concatenate(runs, 1)


def reduce_kernel(nt, post, nx, extra, waits, hid, *refs):
    x_hbm, refs = refs[:nx], refs[nx:]
    w_hbm, gain_ref, first_ref, second_ref = refs[:4]
    extra_in, refs = refs[4 : 4 + extra], refs[4 + extra :]
    if post == "last":
        lasts_ref, refs = refs[0], refs[1:]
    refs = refs[waits:]
    out_ref, refs = refs[0], refs[1:]
    if post == "last":
        everyone = mine = None
        extra_out, lasts_out = refs[:2], refs[2]
        extra_buf, lasts_buf, lasts_mine, lasts_far = refs[3:7]
        refs = refs[7:]
    else:
        everyone, refs = refs[0], refs[1:]
        if extra:
            extra_out, refs = refs[0], refs[1:]
        mine, refs = refs[0], refs[1:]
        if post == "mid":
            (side_x, side_w, side_s, side_r), refs = refs[:4], refs[4:]
    x_v, w_v, away_s, away_r, acc, out_b, in_b, local, send, recv = refs
    rows, d_model = acc.shape[1:]
    half = rows // 2
    tile = min(512, d_model)
    px, py, pc = neighbours()
    move = Mover(send, recv)

    slots = iter(range(local.shape[0]))

    def keep(src, dst):
        made = pltpu.make_async_copy(src, dst, local.at[next(slots)])
        made.start()
        return made

    w_copy = keep(w_hbm, w_v)
    loads = {}
    each = x_v.shape[3] // nx
    for k in (3, 2, 1, 0):
        for kc in (1, 0):
            loads[kc, k] = [
                keep(x.at[kc, k], x_v.at[kc, k, :, pl.ds(i * each, each)])
                for i, x in enumerate(x_hbm)
            ]
    if post == "mid":
        side_loads = [keep(extra_in[0], side_x), keep(extra_in[1], side_w)]
    if post == "last":
        a, b, n, c = places()
        planes = lasts_far.shape[0] + 1
        columns = [(lax.rem(a + d, planes), b, n, c) for d in range(1, planes)]
        peers = plane_peers_of()
        greet([*peers.values(), *columns])
        for (kc, k), peer in peers.items():
            move.start(f"l{kc}{k}", lasts_ref.at[kc, k % 2], lasts_buf.at[kc, k], peer)
    else:
        greet((px, py, pc))
    w_copy.wait()

    def product(kc, k, t):
        at = pl.ds(pl.multiple_of(t * tile, tile), tile)
        if nt:
            return at, ndot(x_v[kc, k], w_v[at, :])
        return at, mdot(x_v[kc, k], w_v[:, at])

    step = min(32, half)

    def by_rows(h, body):
        @pl.loop(0, half // step)
        def _(i):
            body(pl.ds(pl.multiple_of(i * step, step), step),
                 pl.ds(pl.multiple_of(h * half + i * step, step), step))

    def hand_on(name, slot, k, h, peer, extra=None):
        def body(inner, outer):
            value = acc[k, outer, :]
            if extra is not None:
                value = value + in_b[extra, inner, :].astype(F32)
            out_b[slot, inner, :] = value.astype(BF)

        by_rows(h, body)
        move.start(name, out_b.at[slot], in_b.at[slot], peer)

    for k in (3, 2, 1, 0):
        for load in loads[1, k]:
            load.wait()

        @pl.loop(0, d_model // tile)
        def _(t):
            at, value = product(1, k, t)
            away_s[k, :, at] = value.astype(BF)

        move.start(f"away{k}", away_s.at[k], away_r.at[k], pc)
        for load in loads[0, k]:
            load.wait()

        @pl.loop(0, d_model // tile)
        def _(t):
            at, value = product(0, k, t)
            acc[k, :, at] = value

        move.arrived(f"away{k}")
        for h in range(2):
            def add(inner, outer):
                acc[k, outer, :] += away_r[k, outer, :].astype(F32)

            by_rows(h, add)
        if k == 3:
            hand_on("d0", 0, 3, 0, px)
            hand_on("d1", 1, 3, 1, py)
        elif k == 2:
            hand_on("x0", 2, 2, 0, px)
        elif k == 1:
            hand_on("y1", 5, 1, 1, py)
    kept = []
    if extra and post == "fwd":
        for k in range(4):
            kept.append(keep(extra_in[k], extra_out.at[k]))
            move.start(f"e{k}", extra_in[k], extra_out.at[4 + k], pc)
    move.arrived("d0")
    hand_on("y0", 4, 1, 0, py, 0)
    move.arrived("d1")
    hand_on("x1", 3, 2, 1, px, 1)
    if post == "mid":
        for load in side_loads:
            load.wait()
        for k in range(4):

            @pl.loop(0, d_model // tile)
            def _(t):
                at = pl.ds(pl.multiple_of(t * tile, tile), tile)
                side_s[k, :, at] = mdot(side_x[1, k], side_w[:, at]).astype(BF)

            move.start(f"s{k}", side_s.at[k], side_r.at[k], pc)
        for k in range(4):
            move.arrived(f"s{k}")
            move.made.pop(f"s{k}").wait_send()

            @pl.loop(0, d_model // tile)
            def _(t):
                at = pl.ds(pl.multiple_of(t * tile, tile), tile)
                value = mdot(side_x[0, k], side_w[:, at]) + side_r[k, :, at].astype(F32)
                side_s[k, :, at] = value.astype(BF)

            kept.append(keep(side_s.at[k], extra_out.at[k]))
    if extra and post == "last":
        lasts_buf[0, 0] = lasts_ref[0, 0]
        for kc, k in peers:
            move.arrived(f"l{kc}{k}")
        u = b * 2 + n
        me = u * 2 + c
        for kc in range(2):
            for q in range(4):
                found = lasts_buf[kc, 0]
                for k in range(1, 4):
                    found = jnp.where((u ^ k) == q, lasts_buf[kc, k], found)
                lasts_mine[jnp.bitwise_xor(c, kc), q] = found
        for i, peer in enumerate(columns):
            move.start(f"z{i}", lasts_mine, lasts_far.at[i], peer)
        each_rows = extra_buf.shape[1]

        def part(owner):
            at = pl.multiple_of(owner * each_rows, each_rows)
            return extra_in[0].at[pl.ds(at, each_rows)]

        kept.append(keep(part(me), extra_buf.at[me]))
        for (kc, k), peer in peers.items():
            move.start(f"e{kc}{k}", part(peer_owner(kc, k)), extra_buf.at[me], peer)

    for h in range(2):
        move.arrived(f"x{h}")
        move.arrived(f"y{h}")

        def body(inner, outer):
            total = acc[0, outer, :]
            total = total + in_b[2 + h, inner, :].astype(F32)
            total = total + in_b[4 + h, inner, :].astype(F32)
            gain = gain_ref[...]
            if post == "fwd":
                value = first_ref[outer, :].astype(F32) + total
                out_ref[outer, :] = value
                factor = lax.rsqrt(jnp.mean(value * value, axis=-1, keepdims=True) + EPS)
                mine[outer, :] = (value * factor * gain).astype(BF)
                return
            value = second_ref[outer, :] if post == "mid" else first_ref[outer, :].astype(F32)
            base = first_ref[outer, :].astype(F32) if post == "mid" else second_ref[outer, :]
            factor = lax.rsqrt(jnp.mean(value * value, axis=-1, keepdims=True) + EPS)
            weighted = total * gain
            inner_mean = jnp.mean(weighted * value, axis=-1, keepdims=True)
            grad = base + factor * weighted - value * (factor * factor * factor * inner_mean)
            if post == "mid":
                out_ref[outer, :] = grad
                mine[outer, :] = grad.astype(BF)
            else:
                out_ref[outer, :] = grad.astype(BF)

        by_rows(h, body)
        if everyone is not None:
            gather_plane_start(move, mine, everyone, h, half)
    if everyone is not None:
        kept.append(keep(mine, everyone.at[0]))
        gather_plane_rest(move, everyone, half)
    if extra and post == "fwd":
        for k in range(4):
            move.arrived(f"e{k}")
    for made in kept:
        made.wait()
    if extra and post == "last":
        total = lasts_mine[...].astype(F32)
        for i in range(len(columns)):
            move.arrived(f"z{i}")
            total = total + lasts_far[i].astype(F32)
        lasts_out[...] = total.astype(BF)
        for kc, k in peers:
            move.arrived(f"e{kc}{k}")
        wide = extra_buf.shape[2] // 2
        for i in range(2):
            order = [(p, i * wide + z * hid) for z in range(wide // hid) for p in range(8)]
            for at, value in set_side_by_side(extra_buf, order, hid):
                extra_out[i][:, at] = value
    move.sent()


def plane_reduce(ident, post, nt, xs, w, gain, first, second, extra=(), done=(), hid=0, lasts=None):
    rows, d_model = first.shape
    vmem = pl.BlockSpec(memory_space=pltpu.VMEM)
    hbm = pl.BlockSpec(memory_space=pl.ANY)
    out_type = BF if post == "last" else F32
    out_shape = [jax.ShapeDtypeStruct((rows, d_model), out_type)]
    out_specs = [vmem]
    scratch = []
    copies = 10
    if post != "last":
        out_shape.append(jax.ShapeDtypeStruct((8, rows, d_model), BF))
        out_specs.append(hbm)
        copies += GATHER_COPIES
        if extra:
            blocks = 8 if post == "fwd" else 4
            out_shape.append(jax.ShapeDtypeStruct((blocks, rows, d_model), BF))
            out_specs.append(hbm)
            copies += 4
        scratch.append(pltpu.VMEM((rows, d_model), BF))
        if post == "mid":
            scratch += [pltpu.VMEM(v.shape, BF) for v in extra]
            scratch += [pltpu.VMEM((4, rows, d_model), BF)] * 2
    else:
        each = extra[0].shape[0] // 8, extra[0].shape[1]
        for _ in range(2):
            out_shape.append(jax.ShapeDtypeStruct((each[0], 4 * each[1]), F32))
            out_specs.append(vmem)
        planes = lax.axis_size("a")
        copies += 7 * len(extra) + 7 + planes - 1
        block = (2, 4) + lasts.shape[2:]
        out_shape.append(jax.ShapeDtypeStruct(block, BF))
        out_specs.append(vmem)
        scratch.append(pltpu.VMEM((8,) + each, BF))
        scratch += [pltpu.VMEM(block, BF)] * 2 + [pltpu.VMEM((planes - 1,) + block, BF)]
    wide = sum(x.shape[3] for x in xs)
    scratch += [
        pltpu.VMEM((2, 4, rows, wide), BF),
        pltpu.VMEM(w.shape, BF),
        pltpu.VMEM((4, rows, d_model), BF),
        pltpu.VMEM((4, rows, d_model), BF),
        pltpu.VMEM((4, rows, d_model), F32),
        pltpu.VMEM((6, rows // 2, d_model), BF),
        pltpu.VMEM((6, rows // 2, d_model), BF),
        pltpu.SemaphoreType.DMA((8 + 8 * len(xs),)),
        pltpu.SemaphoreType.DMA((copies,)),
        pltpu.SemaphoreType.DMA((copies,)),
    ]
    return pl.pallas_call(
        functools.partial(reduce_kernel, nt, post, len(xs), len(extra), len(done), hid),
        in_specs=[hbm] * (len(xs) + 1)
        + [vmem] * 3
        + [vmem if post == "fwd" else hbm] * len(extra)
        + [vmem] * (lasts is not None)
        + [hbm] * len(done),
        out_specs=out_specs,
        out_shape=out_shape,
        scratch_shapes=scratch,
        compiler_params=pltpu.CompilerParams(
            collective_id=ident, has_side_effects=True, vmem_limit_bytes=VMEM_LIMIT
        ),
        cost_estimate=pl.CostEstimate(flops=0, bytes_accessed=8 << 20, transcendentals=0),
        name=f"plane_reduce_{post}",
    )(*xs, w, gain.reshape(1, -1), first, second, *extra, *([] if lasts is None else [lasts]), *done)


def start_kernel(
    head_w, hid, tokens_ref, wy_ref, wx_ref, wg_ref, wu_ref, rows_ref, vec_ref, stream_ref,
    tok_out, yx_out, gu_out, rows_out, halves_out, vec_out, stream_out,
    yx_ref, gu_ref, local, send, recv,
):
    a, b, n, c = places()
    planes = yx_out.shape[0]
    p = (b * 2 + n) * 2 + c
    pc = neighbours()[2]
    plane_peers = plane_peers_of()
    up, down = (a + 1, b, n, c), (a - 1, b, n, c)
    each = planes // 2

    def pack(out, sources, columns, width):
        for owner in range(8):
            runs = [w[:, o : o + width] for w in sources for o in columns(owner)]
            out[owner] = jnp.concatenate(runs, 1)

    barrier = pltpu.get_barrier_semaphore()
    for peer in plane_peers.values():
        pl.semaphore_signal(barrier, inc=1, device_id=peer, device_id_type=MESH)

    @pl.when(a < planes - 1)
    def _():
        pl.semaphore_signal(barrier, inc=1, device_id=up, device_id_type=MESH)

    @pl.when(a > 0)
    def _():
        pl.semaphore_signal(barrier, inc=1, device_id=down, device_id_type=MESH)

    def head_columns(owner):
        return [((owner % 2 * each + j) * 4 + owner // 2) * head_w for j in range(each)]

    pack(yx_ref, (wy_ref, wx_ref), head_columns, head_w)
    others = len(plane_peers) + jnp.minimum(planes - 1 - a, 1) + jnp.minimum(a, 1)
    pl.semaphore_wait(barrier, others)

    move = Mover(send, recv)
    half = tokens_ref.shape[0] // 2

    def keep(i, src, dst):
        made = pltpu.make_async_copy(src, dst, local.at[i])
        made.start()
        return made

    def to_owners(name, pieces, out):
        for (kc, k), peer in plane_peers.items():
            move.start(f"{name}{kc}{k}", pieces.at[peer_owner(kc, k)], out.at[a, p], peer)

    chains = {}

    def chain_step(name, out, s):
        def up_copy(block):
            return move.copy(f"{name}u{s}", out.at[block], out.at[block], up)

        def down_copy(block):
            return move.copy(f"{name}d{s}", out.at[block], out.at[block], down)

        sends_up, sends_down = (a < planes - 1) & (a >= s), (a > 0) & (a + s < planes)

        @pl.when(sends_up)
        def _():
            up_copy(a - s).start()

        @pl.when(sends_down)
        def _():
            down_copy(a + s).start()

        chains[name, s] = (up_copy, down_copy, sends_up, sends_down)

    def chain_arrived(name, s):
        up_copy, down_copy, _, _ = chains[name, s]

        @pl.when(a - 1 >= s)
        def _():
            up_copy(a - 1 - s).wait_recv()

        @pl.when(a + 1 + s < planes)
        def _():
            down_copy(a + 1 + s).wait_recv()

    def chain_sent(name, s):
        up_copy, down_copy, sends_up, sends_down = chains[name, s]

        @pl.when(sends_up)
        def _():
            up_copy(a - s).wait_send()

        @pl.when(sends_down)
        def _():
            down_copy(a + s).wait_send()

    to_owners("yx", yx_ref, yx_out)
    for (kc, k), peer in plane_peers.items():
        move.start(f"vec{kc}{k}", vec_ref, vec_out.at[a, p], peer)
    own_yx = keep(1, yx_ref.at[p], yx_out.at[a, p])
    own_vec = keep(2, vec_ref, vec_out.at[a, p])
    own_rows = keep(0, rows_ref, rows_out.at[a])
    own_tok = keep(4, tokens_ref, tok_out.at[0])
    own_stream = keep(5, stream_ref, stream_out.at[0, 0])
    own_yx.wait()
    own_vec.wait()
    for kc, k in plane_peers:
        move.arrived(f"yx{kc}{k}")
        move.arrived(f"vec{kc}{k}")
    own_rows.wait()
    outs = (("yx", yx_out), ("vec", vec_out), ("rows", rows_out))
    for name, out in outs:
        chain_step(name, out, 0)
    for h in range(2):
        gather_plane_start(move, tokens_ref, tok_out, h, half)
    pack(gu_ref, (wg_ref, wu_ref), lambda o: [(z * 8 + o) * hid for z in range(planes)], hid)
    own_gu = keep(3, gu_ref.at[p], gu_out.at[p])
    gather_plane_rest(move, tok_out, half, 0)
    for kc in range(2):
        for kn in range(2):
            if (kc, kn) != (0, 0):
                move.start(f"st{kc}{kn}", stream_ref, stream_out.at[kc, kn], plane_peers[kc, kn])
    for name, out in outs:
        chain_arrived(name, 0)
        chain_step(name, out, 1)
    gather_plane_rest(move, tok_out, half, 1)
    for (kc, k), peer in plane_peers.items():
        move.start(f"gu{kc}{k}", gu_ref.at[peer_owner(kc, k)], gu_out.at[p], peer)
    for s in range(1, planes - 1):
        for name, out in outs:
            chain_arrived(name, s)
            if s + 1 < planes - 1:
                chain_step(name, out, s + 1)
    gather_plane_rest(move, tok_out, half, 2)
    swap = pltpu.make_async_remote_copy(
        src_ref=rows_out.at[pl.ds((1 - c) * each, each)],
        dst_ref=halves_out.at[:, c],
        send_sem=send.at[send.shape[0] - 1],
        recv_sem=recv.at[recv.shape[0] - 1],
        device_id=pc,
        device_id_type=MESH,
    )
    swap.start()
    own_halves = keep(6, rows_out.at[pl.ds(c * each, each)], halves_out.at[:, c])
    for kc, k in plane_peers:
        move.arrived(f"gu{kc}{k}")
    for kc in range(2):
        for kn in range(2):
            if (kc, kn) != (0, 0):
                move.arrived(f"st{kc}{kn}")
    for made in (own_gu, own_tok, own_stream, own_halves):
        made.wait()
    swap.wait()
    for name, s in chains:
        chain_sent(name, s)
    for name in [n for n in move.names if not any(n == f"{w}{d}{s}" for w, s in chains for d in "ud")]:
        move.made[name].wait_send()


def start_exchange(tokens, w_y, w_x, w_gate, w_up, gate_rows, vec, stream):
    planes = lax.axis_size("a")
    head_w, hid = gate_rows.shape[1] // 2, w_gate.shape[1] // (planes * 8)
    vmem = pl.BlockSpec(memory_space=pltpu.VMEM)
    hbm = pl.BlockSpec(memory_space=pl.ANY)
    yx = (8, w_y.shape[0], 2 * w_y.shape[1] // 8)
    gu = (8, w_gate.shape[0], 2 * w_gate.shape[1] // 8)
    shapes = [
        ((8,) + tokens.shape, BF),
        ((planes,) + yx, BF),
        (gu, BF),
        ((planes,) + gate_rows.shape, BF),
        ((planes // 2, 2) + gate_rows.shape, BF),
        ((planes, 8) + vec.shape, F32),
        ((2, 2) + stream.shape, F32),
    ]
    copies = 7 * 3 + 3 + GATHER_COPIES + 6 * (planes - 1) + 1
    return pl.pallas_call(
        functools.partial(start_kernel, head_w, hid),
        in_specs=[vmem] * 8,
        out_specs=[hbm] * 7,
        out_shape=[jax.ShapeDtypeStruct(*shape) for shape in shapes],
        scratch_shapes=[
            pltpu.VMEM(yx, BF),
            pltpu.VMEM(gu, BF),
            pltpu.SemaphoreType.DMA((7,)),
            pltpu.SemaphoreType.DMA((copies,)),
            pltpu.SemaphoreType.DMA((copies,)),
        ],
        compiler_params=pltpu.CompilerParams(
            collective_id=1, has_side_effects=True, vmem_limit_bytes=VMEM_LIMIT
        ),
        cost_estimate=pl.CostEstimate(flops=0, bytes_accessed=8 << 20, transcendentals=0),
        name="start_exchange",
    )(tokens, w_y, w_x, w_gate, w_up, gate_rows, vec, stream)


def finish_kernel(head_w, sums_ref, y_ref, x_ref, buf, local, send, recv):
    _, b, n, c = places()
    me = (b * 2 + n) * 2 + c
    peers = plane_peers_of()
    greet(list(peers.values()))
    move = Mover(send, recv)
    each_rows = buf.shape[1]

    def part(owner):
        return sums_ref.at[pl.ds(pl.multiple_of(owner * each_rows, each_rows), each_rows)]

    for (kc, k), peer in peers.items():
        move.start(f"e{kc}{k}", part(peer_owner(kc, k)), buf.at[me], peer)
    own = pltpu.make_async_copy(part(me), buf.at[me], local.at[0])
    own.start()
    own.wait()
    for kc, k in peers:
        move.arrived(f"e{kc}{k}")
    wide = buf.shape[2] // 2
    each = wide // head_w
    order = [(q * 2 + i, j * head_w) for i in range(2) for j in range(each) for q in range(4)]
    for first, out in ((0, y_ref), (wide, x_ref)):
        for at, value in set_side_by_side(buf, [(p, o + first) for p, o in order], head_w):
            out[:, at] = value
    move.sent()


def finish(sums, head_w):
    each = sums.shape[0] // 8, sums.shape[1]
    vmem = pl.BlockSpec(memory_space=pltpu.VMEM)
    return pl.pallas_call(
        functools.partial(finish_kernel, head_w),
        in_specs=[pl.BlockSpec(memory_space=pl.ANY)],
        out_specs=[vmem, vmem],
        out_shape=[jax.ShapeDtypeStruct((each[0], 4 * each[1]), F32)] * 2,
        scratch_shapes=[
            pltpu.VMEM((8,) + each, BF),
            pltpu.SemaphoreType.DMA((1,)),
            pltpu.SemaphoreType.DMA((7,)),
            pltpu.SemaphoreType.DMA((7,)),
        ],
        compiler_params=pltpu.CompilerParams(
            collective_id=5, has_side_effects=True, vmem_limit_bytes=VMEM_LIMIT
        ),
        name="finish",
    )(sums)


def column_peers(planes):
    a, b, n, c = places()
    return [(lax.rem(a + d, planes), b, n, c) for d in range(1, planes)]


def earlier_blocks(ref, want, row=0, count=1):
    _, b, _, _ = places()
    return [
        jnp.where(
            b == want,
            ref[kc * 4 + kn, row : row + count, :],
            ref[kc * 4 + 2 + kn, row : row + count, :],
        )
        for kc in range(2)
        for kn in range(2)
    ]


def pass_state_kernel(reverse, mul_ref, add_ref, out_ref, whole, came, send, recv):
    a, b, n, c = places()
    planes = came.shape[0] + 1
    row = 0 if reverse else 7
    near_at, far_at = (1, 0) if reverse else (0, 1)
    came[...] = jnp.zeros_like(came)
    near_mul, near_add = earlier_blocks(mul_ref, near_at, row), earlier_blocks(add_ref, near_at, row)
    far_mul, far_add = earlier_blocks(mul_ref, far_at, row), earlier_blocks(add_ref, far_at, row)
    for i in range(4):
        whole[0, i : i + 1, :] = near_mul[i] * far_mul[i]
        whole[1, i : i + 1, :] = far_mul[i] * near_add[i] + far_add[i]
    greet(column_peers(planes))

    def copy(d):
        return pltpu.make_async_remote_copy(
            src_ref=whole,
            dst_ref=came.at[d - 1],
            send_sem=send.at[d - 1],
            recv_sem=recv.at[d - 1],
            device_id=(a - d if reverse else a + d, b, n, c),
            device_id_type=MESH,
        )

    def sends(d):
        return a >= d if reverse else a + d < planes

    def receives(d):
        return a + d < planes if reverse else a >= d

    for d in range(1, planes):
        @pl.when(sends(d))
        def _():
            copy(d).start()

    for d in range(1, planes):
        @pl.when(receives(d))
        def _():
            copy(d).wait_recv()

    for i in range(4):
        at = slice(i, i + 1)
        value = came[planes - 2, 1, at, :]
        for d in range(planes - 2, 0, -1):
            value = came[d - 1, 0, at, :] * value + came[d - 1, 1, at, :]
        to_far = near_mul[i] * value + near_add[i]
        for kb in range(2):
            is_far = (b if kb == 0 else 1 - b) == far_at
            at = (i // 2) * 4 + kb * 2 + i % 2
            out_ref[at] = jnp.where(is_far, to_far, value)

    for d in range(1, planes):
        @pl.when(sends(d))
        def _():
            copy(d).wait_send()


def pass_rows_kernel(reverse, edge_ref, out_ref, leaving, came, send, recv):
    a, b, n, c = places()
    planes = lax.axis_size("a")
    near_at, far_at = (1, 0) if reverse else (0, 1)
    came[...] = jnp.zeros_like(came)
    out_ref[...] = jnp.zeros_like(out_ref)
    first = 0 if reverse else 4
    for i, value in enumerate(earlier_blocks(edge_ref, far_at, first, 4)):
        leaving[i * 4 : i * 4 + 4, :] = value
    greet(column_peers(planes))
    copy = pltpu.make_async_remote_copy(
        src_ref=leaving,
        dst_ref=came,
        send_sem=send.at[0],
        recv_sem=recv.at[0],
        device_id=(a - 1 if reverse else a + 1, b, n, c),
        device_id_type=MESH,
    )
    sends = a >= 1 if reverse else a + 1 < planes
    receives = a + 1 < planes if reverse else a >= 1

    @pl.when(sends)
    def _():
        copy.start()

    @pl.when(receives)
    def _():
        copy.wait_recv()

    for i in range(4):
        for kb in range(2):
            is_far = (b if kb == 0 else 1 - b) == far_at
            at = (i // 2) * 4 + kb * 2 + i % 2
            other = (i // 2) * 4 + (1 - kb) * 2 + i % 2
            out_ref[at, first : first + 4, :] = jnp.where(
                is_far, edge_ref[other, first : first + 4, :], came[i * 4 : i * 4 + 4, :]
            )

    @pl.when(sends)
    def _():
        copy.wait_send()


def pass_along(ident, name, reverse, *edges):
    shape = edges[0].shape
    planes = lax.axis_size("a")
    vmem = pl.BlockSpec(memory_space=pltpu.VMEM)
    if len(edges) == 2:
        body, out = pass_state_kernel, (shape[0], 1, shape[2])
        buffers = [(2, 4) + shape[2:], (planes - 1, 2, 4) + shape[2:]]
    else:
        body, out = pass_rows_kernel, shape
        buffers = [(16,) + shape[2:]] * 2
    return pl.pallas_call(
        functools.partial(body, reverse),
        in_specs=[vmem] * len(edges),
        out_specs=vmem,
        out_shape=jax.ShapeDtypeStruct(out, F32),
        scratch_shapes=[pltpu.VMEM(shape, F32) for shape in buffers]
        + [pltpu.SemaphoreType.DMA((planes - 1,))] * 2,
        compiler_params=pltpu.CompilerParams(
            collective_id=ident, has_side_effects=True, vmem_limit_bytes=VMEM_LIMIT
        ),
        cost_estimate=pl.CostEstimate(flops=0, bytes_accessed=1 << 20, transcendentals=0),
        name=name,
    )(*edges)


def norm_product_kernel(info, tok_ref, w_ref, gain_ref, n_ref, gate_ref, lin_ref, tail_ref):
    rows, d_model = tok_ref.shape[1:]
    step = min(64, rows)

    @pl.loop(0, rows // step)
    def _(i):
        at = pl.ds(pl.multiple_of(i * step, step), step)
        value = tok_ref[0, at, :].astype(F32)
        factor = lax.rsqrt(jnp.mean(value * value, axis=-1, keepdims=True) + EPS)
        n_ref[0, at, :] = (value * factor * gain_ref[...]).astype(BF)

    wide = gate_ref.shape[2]
    both = mdot(n_ref[0], w_ref[...])
    used = both.shape[1] // 2
    pad = [jnp.zeros((rows, wide - used), F32)] if wide > used else []
    gate_ref[0] = jnp.concatenate([both[:, :used]] + pad, 1)
    low = jnp.concatenate([both[:, used:]] + pad, 1).astype(BF)
    lin_ref[0] = low
    tail_ref[0] = low.astype(F32)[rows - 8 :, :]


def row_places(info, rows, nseq):
    i = pl.program_id(0)
    pos = info[i, 0] + lax.broadcasted_iota(jnp.int32, (rows, 1), 0)
    begin = jnp.zeros((rows, 1), jnp.int32) + info[i, 1]
    seg = jnp.zeros((rows, 1), jnp.int32)
    for s in range(1, nseq):
        begin = jnp.where(pos >= info[i, 1 + s], info[i, 1 + s], begin)
        seg = jnp.where(pos >= info[i, 1 + s], s, seg)
    return pos, begin, seg


def inputs_by_tap(ext, lin_ref, rim_ref, conv0_ref, begin_at, seg, taps):
    rows = lin_ref.shape[1]
    back = taps - 1
    ext[0:8, :] = rim_ref[0]
    ext[8 : 8 + rows, :] = lin_ref[0].astype(F32)
    slots = conv0_ref.shape[1]
    column = lax.broadcasted_iota(jnp.int32, (rows, slots), 1)
    found = [ext[8 : 8 + rows, :]]
    for k in range(1, taps):
        hot = (column == seg * back + begin_at - k + back) & (begin_at < k)
        stored = mdot(jnp.where(hot, 1.0, 0.0).astype(BF), conv0_ref[0])
        found.append(jnp.where(begin_at >= k, ext[8 - k : 8 - k + rows, :], stored))
    return found


def run_scan(a_s, b_s, p_ref, s_ref, rows, reverse):
    width = b_s.shape[1]
    groups = rows // 8
    row = lax.broadcasted_iota(jnp.int32, (8, width), 0)
    if reverse:
        row = 7 - row

    def step(i, carry):
        cp, cs = carry
        g = groups - 1 - i if reverse else i
        at = pl.ds(pl.multiple_of(g * 8, 8), 8)
        a, b = a_s[at, :], b_s[at, :]
        for d in (1, 2, 4):
            by = 8 - d if reverse else d
            inside = row >= d
            a_far = jnp.where(inside, pltpu.roll(a, by, 0), 1.0)
            b_far = jnp.where(inside, pltpu.roll(b, by, 0), 0.0)
            b = a * b_far + b
            a = a * a_far
        b = a * cs + b
        a = a * cp
        p_ref[0, at, :] = a
        s_ref[0, at, :] = b
        last = 0 if reverse else 7
        return a[last : last + 1], b[last : last + 1]

    start = (jnp.ones((1, width), F32), jnp.zeros((1, width), F32))
    lax.fori_loop(0, groups, step, start, unroll=4)


V_CBIAS, V_ABIAS, V_IBIAS, V_SOFT = 0, 1, 2, 3


def forward_kernel(
    nseq, taps, info, lin_ref, rim_ref, conv0_ref, state0_ref, wg_ref, vec_ref,
    conv_ref, retain_ref, admit_ref, p_ref, s_ref, pe_ref, se_ref, ext, a_s, b_s,
):
    i = pl.program_id(0)
    rows, wide = lin_ref.shape[1:]
    pos, begin, seg = row_places(info, rows, nseq)
    at = pos - begin

    def vec(k):
        return vec_ref[k : k + 1, :]

    by_tap = inputs_by_tap(ext, lin_ref, rim_ref, conv0_ref, at, seg, taps)
    total = vec(taps + V_CBIAS)
    for k in range(taps):
        total = total + vec(k) * by_tap[k]
    low = total.astype(BF)
    conv_ref[0] = low
    conv = low.astype(F32)
    both = mdot(low, wg_ref[...])
    retain = jax.nn.sigmoid(both[:, :wide] + vec(taps + V_ABIAS))
    admit = jax.nn.sigmoid(both[:, wide:] + vec(taps + V_IBIAS))
    retain_ref[0] = retain
    admit_ref[0] = admit
    a = jnp.exp(-8.0 * retain * vec(taps + V_SOFT))
    mult = jnp.sqrt(jnp.maximum((1.0 - a) * (1.0 + a), FLOOR))
    drive = mult * admit * conv
    for s in range(nseq):
        drive = drive + jnp.where(pos == info[i, 1 + s], a * state0_ref[0, s : s + 1, :], 0.0)
    a_s[...] = jnp.where(at == 0, 0.0, a)
    b_s[...] = drive
    run_scan(a_s, b_s, p_ref, s_ref, rows, False)
    pe_ref[0] = p_ref[0, rows - 8 : rows, :]
    se_ref[0] = s_ref[0, rows - 8 : rows, :]


def gelu_pair(x):
    root = 0.7978845608028654
    inner = root * (x + 0.044715 * (x * x * x))
    th = jnp.tanh(inner)
    cdf = 0.5 * (1.0 + th)
    slope = cdf + 0.5 * x * (1.0 - th * th) * (root * (1.0 + 3.0 * 0.044715 * (x * x)))
    return x * cdf, slope


def ffn_forward_kernel(info, n_ref, w_ref, inner_ref, by_gate_ref, by_up_ref):
    pair = mdot(n_ref[0], w_ref[...])
    hidden = inner_ref.shape[2]
    upward = pair[:, hidden:]
    active, slope = gelu_pair(pair[:, :hidden])
    inner_ref[0] = (active * upward).astype(BF)
    by_gate_ref[0] = (slope * upward).astype(BF)
    by_up_ref[0] = active.astype(BF)


def ffn_back_kernel(info, g_ref, w_ref, by_gate_ref, by_up_ref, *refs):
    out_ref = refs[-1]
    hidden = w_ref.shape[0]
    d_inner = ndot(g_ref[0], w_ref[...])
    out_ref[0, :, :hidden] = (d_inner * by_gate_ref[0].astype(F32)).astype(BF)
    out_ref[0, :, hidden:] = (d_inner * by_up_ref[0].astype(F32)).astype(BF)


def back_scan_kernel(
    nseq, taps, info, dres_ref, wo_ref, gate_ref, hidden_ref, retain_ref, vec_ref, *refs
):
    dgate_ref, p_ref, s_ref, pe_ref, se_ref, ext, a_s, b_s = refs[-8:]
    rows = gate_ref.shape[1]
    pos, begin, _ = row_places(info, rows, nseq)
    d_mixed = ndot(dres_ref[0], wo_ref[...])
    gelu, slope = gelu_pair(gate_ref[0])
    dgate_ref[0] = (d_mixed * hidden_ref[0] * slope).astype(BF)
    b_s[...] = d_mixed * gelu
    soft = vec_ref[taps + V_SOFT : taps + V_SOFT + 1, :]
    a = jnp.where(pos == begin, 0.0, jnp.exp(-8.0 * retain_ref[0] * soft))
    ext[0:rows, :] = a
    ext[rows : rows + 8, :] = jnp.ones((8, a.shape[1]), F32)
    a_s[...] = ext[1 : rows + 1, :]
    run_scan(a_s, b_s, p_ref, s_ref, rows, True)
    pe_ref[0] = ext[0:8, :] * p_ref[0, 0:8, :]
    se_ref[0] = ext[0:8, :] * s_ref[0, 0:8, :]


def back_kernel(
    nseq, taps, info, p_ref, s_ref, grad_in_ref, hidden_ref, state_in_ref, state0_ref, conv_ref,
    retain_ref, admit_ref, lin_ref, rim_ref, conv0_ref, wg_ref, vec_ref, *refs
):
    dconv_ref, head_ref, wgrad_ref, vgrad_ref, ext = refs[-5:]
    i = pl.program_id(0)
    rows, wide = lin_ref.shape[1:]
    pos, begin, seg = row_places(info, rows, nseq)
    at = pos - begin
    conv_low = conv_ref[0]
    conv = conv_low.astype(F32)
    retain, admit = retain_ref[0], admit_ref[0]
    soft = vec_ref[taps + V_SOFT : taps + V_SOFT + 1, :]
    e = p_ref[0] * grad_in_ref[0, 0:1, :] + s_ref[0]
    ext[0:8, :] = jnp.broadcast_to(state_in_ref[0], (8, wide))
    ext[8 : 8 + rows, :] = hidden_ref[0]
    previous = ext[7 : 7 + rows, :]
    for s in range(nseq):
        previous = jnp.where(pos == info[i, 1 + s], state0_ref[0, s : s + 1, :], previous)
    a = jnp.exp(-8.0 * retain * soft)
    spread = (1.0 - a) * (1.0 + a)
    mult = jnp.sqrt(jnp.maximum(spread, FLOOR))
    d_mult = e * admit * conv
    d_spread = jnp.where(spread > FLOOR, d_mult * 0.5 / mult, 0.0)
    d_log = e * previous * a - 2.0 * a * a * d_spread
    d_rate = (d_log * (-8.0 * soft) * retain * (1.0 - retain)).astype(BF)
    d_inflow = (e * mult * conv * admit * (1.0 - admit)).astype(BF)
    d_gates = jnp.concatenate([d_rate, d_inflow], 1)
    d_conv = e * mult * admit + ndot(d_gates, wg_ref[...])
    low = d_conv.astype(BF)
    dconv_ref[0] = low
    low = low.astype(F32)
    head_ref[0] = low[0:8, :]

    @pl.when(i == 0)
    def _():
        wgrad_ref[...] = jnp.zeros_like(wgrad_ref)
        vgrad_ref[...] = jnp.zeros_like(vgrad_ref)

    wgrad_ref[...] += tdot(conv_low, d_gates)
    sums = [low * v for v in inputs_by_tap(ext, lin_ref, rim_ref, conv0_ref, at, seg, taps)]
    sums += [low, d_rate.astype(F32), d_inflow.astype(F32), d_log * (-8.0 * retain)]
    for k, value in enumerate(sums):
        vgrad_ref[k : k + 1, :] += jnp.sum(value, axis=0, keepdims=True)


def back_conv_kernel(nseq, taps, info, dconv_ref, rim_ref, dgate_ref, vec_ref, *refs):
    out_ref, ext = refs[-2:]
    i = pl.program_id(0)
    rows, wide = dconv_ref.shape[1:]
    pos = info[i, 0] + lax.broadcasted_iota(jnp.int32, (rows, 1), 0)
    ext[0:rows, :] = dconv_ref[0].astype(F32)
    ext[rows : rows + 8, :] = rim_ref[0]
    total = vec_ref[0:1, :] * ext[0:rows, :]
    for k in range(1, taps):
        cut = jnp.zeros((rows, 1), jnp.int32)
        for s in range(nseq):
            start = info[i, 1 + s]
            cut = jnp.where((pos < start) & (pos + k >= start), 1, cut)
        total = total + vec_ref[k : k + 1, :] * jnp.where(cut == 0, ext[k : k + rows, :], 0.0)
    used = out_ref.shape[2] // 2
    both = [dgate_ref[0].astype(F32)[:, :used], total[:, :used]]
    out_ref[0] = jnp.concatenate(both, 1).astype(BF)


def by_block(body, info, ins, outs, scratch, done=(), name=None):
    blocks = info.shape[0]

    def spec(shape, blocked):
        zeros = (0,) * (len(shape) - 1)
        if blocked:
            return pl.BlockSpec((1,) + tuple(shape[1:]), lambda i, *_: (i,) + zeros)
        return pl.BlockSpec(tuple(shape), lambda i, *_: (0,) + zeros)

    hbm = pl.BlockSpec(memory_space=pl.ANY)
    return pl.pallas_call(
        body,
        grid_spec=pltpu.PrefetchScalarGridSpec(
            num_scalar_prefetch=1,
            grid=(blocks,),
            in_specs=[spec(v.shape, blocked) for v, blocked in ins] + [hbm] * len(done),
            out_specs=[spec(shape, blocked) for shape, _, blocked in outs],
            scratch_shapes=[pltpu.VMEM(shape, F32) for shape in scratch],
        ),
        out_shape=[jax.ShapeDtypeStruct(shape, kind) for shape, kind, _ in outs],
        compiler_params=pltpu.CompilerParams(vmem_limit_bytes=VMEM_LIMIT),
        cost_estimate=pl.CostEstimate(flops=0, bytes_accessed=1 << 20, transcendentals=0),
        name=name,
    )(info, *[v for v, _ in ins], *done)


def on_device(
    tokens,
    starts,
    init_state,
    init_conv,
    w_y,
    w_x,
    gate_a,
    gate_i,
    w_out,
    norm1_gain,
    conv_kernel,
    conv_bias,
    bias_a,
    bias_i,
    decay_param,
    w_gate,
    w_up,
    w_down,
    norm2_gain,
    cotangent,
):
    planes, count = lax.axis_size("a"), chips()
    a, b, n, c = (lax.axis_index(name) for name in ("a", "b", "n", "c"))
    u = chip()
    nn = count // 2
    rows, d_model = tokens.shape[1], tokens.shape[2]
    nseq = starts.shape[1]
    width = w_y.shape[1]
    head_w = gate_a.shape[1]
    half = gate_a.shape[0]
    taps = conv_kernel.shape[0]
    back = taps - 1
    heads_here = planes // 2
    wide_here = heads_here * head_w
    wp = -(-wide_here // 128) * 128
    hid = w_down.shape[0]
    drows = w_y.shape[0]
    nblocks = 2 * count

    def gather_a(value):
        return lax.all_gather(value, "a", axis=0, tiled=True)

    def scatter_a(value):
        return lax.psum_scatter(value, "a", scatter_dimension=0, tiled=True)

    def padded(v, axis=-1):
        pads = [(0, 0)] * v.ndim
        pads[axis] = (0, wp - wide_here)
        return jnp.pad(v, pads)

    vectors = jnp.concatenate(
        [conv_kernel, conv_bias[None], bias_a[None], bias_i[None], decay_param[None]], 0
    ).reshape(-1)
    vectors = jnp.concatenate([vectors, norm1_gain, norm2_gain]).astype(F32)
    lanes = -(-vectors.shape[0] // 1024) * 128
    vectors = jnp.pad(vectors, (0, 8 * lanes - vectors.shape[0])).reshape(8, lanes)
    at_start = jnp.concatenate([init_state[0][:, None], init_conv[0].astype(F32)], 1)
    at_start = at_start.reshape(nseq * taps, width)
    at_start = jnp.pad(at_start, ((0, 8), (0, 0)))
    at_start = at_start.at[nseq * taps, :nseq].set(starts[0].astype(F32))
    all_tokens, w_yx, w_gu, _, gate_rows, canon, at_start = start_exchange(
        tokens[0],
        w_y,
        w_x,
        w_gate,
        w_up,
        jnp.concatenate([gate_a, gate_i], 1),
        vectors,
        at_start,
    )
    w_yx = w_yx.reshape(d_model, 2 * wide_here)
    w_gu = gather_a(w_gu.reshape(-1, 2 * planes * hid))
    gate_rows = gate_rows.reshape(wide_here, -1)

    def join_halves(mine_all):
        away = swap_c(lax.dynamic_slice_in_dim(mine_all, (1 - c) * heads_here, heads_here, 0))
        own = lax.dynamic_slice_in_dim(mine_all, c * heads_here, heads_here, 0)
        first = jnp.where(c == 0, own, away)
        second = jnp.where(c == 0, away, own)
        return jnp.stack([first, second], 1).reshape((wide_here,) + mine_all.shape[2:])


    def part_halves(full):
        full = full.reshape((heads_here, 2, half) + full.shape[1:])
        own, away = pick(full, c, 1), swap_c(pick(full, 1 - c, 1))
        first = jnp.where(c == 0, own, away)
        second = jnp.where(c == 0, away, own)
        return jnp.concatenate([first, second], 0).reshape((planes * half,) + full.shape[3:])

    w_o = padded(join_halves(gather_a(w_out).reshape(planes, half, d_model)), 0)

    def block_diagonal(m):
        m = m.reshape(heads_here, head_w, head_w)
        eye = jnp.eye(heads_here, dtype=m.dtype)
        full = (m[:, :, None, :] * eye[:, None, :, None]).reshape(wide_here, wide_here)
        return padded(padded(full), 0)

    w_gates = jnp.concatenate(
        [
            block_diagonal(gate_rows[:, :head_w]),
            block_diagonal(gate_rows[:, head_w:]),
        ],
        1,
    )

    w_d = gather_a(w_down)
    f_here = planes * hid

    canon = canon.reshape(planes * nblocks, -1)
    nvec = (taps + 4) * half
    gain_one = canon[:, nvec : nvec + drows].reshape(-1)
    gain_two = canon[:, nvec + drows : nvec + 2 * drows].reshape(-1)
    mine = pick(canon[:, :nvec].reshape(2, heads_here, count, 2, taps + 4, half), c)
    mine = pick(mine, u, 1).transpose(2, 0, 1, 3).reshape(taps + 4, wide_here)
    decay_f = mine[taps + 3]
    vec = padded(jnp.concatenate([mine[: taps + 3], jax.nn.softplus(decay_f)[None]]))

    def my_channels(v):
        lead = v.shape[:-1]
        v = v.reshape(lead + (2, heads_here, count, head_w))
        v = pick(v, c, len(lead))
        return pick(v, u, len(lead) + 1).reshape(lead + (wide_here,))

    streams = 2 * nn
    at_start = at_start.reshape(streams, -1, width)
    offsets = at_start[:, nseq * taps, :nseq].astype(jnp.int32)
    at_start = my_channels(at_start[:, : nseq * taps].reshape(streams, nseq, taps, width))
    at_start = padded(at_start)
    state_0 = jnp.pad(at_start[:, :, 0], ((0, 0), (0, -nseq % 8), (0, 0)))
    conv_0 = at_start[:, :, 1:].reshape(streams, nseq * back, wp).astype(BF)
    conv_0 = jnp.pad(conv_0, ((0, 0), (0, -(nseq * back) % 16), (0, 0)))

    def per_block(v):
        v = v.reshape((2, 1, nn) + v.shape[1:])
        return jnp.broadcast_to(v, (2, 2, nn) + v.shape[3:]).reshape((nblocks,) + v.shape[3:])

    block_b = (jnp.arange(nblocks, dtype=jnp.int32) // nn) % 2
    first_row = (a * 2 + (b ^ block_b)) * rows
    position = first_row[:, None] + jnp.arange(rows, dtype=jnp.int32)[None]
    off_b = per_block(offsets)

    info = jnp.concatenate(
        [first_row[:, None], off_b, jnp.zeros((nblocks, -(nseq + 1) % 8), jnp.int32)], 1
    )

    grad_low = cotangent[0]
    grads = [grad_low] + [xor_u(grad_low, k) for k in range(1, count)]

    edge = ((nblocks, 8, wp), F32, True)
    normed, gate_in, linear, tail = by_block(
        norm_product_kernel,
        info,
        [(all_tokens, True), (w_yx, False), (gain_one[None], False)],
        [
            ((nblocks, rows, d_model), BF, True),
            ((nblocks, rows, wp), F32, True),
            ((nblocks, rows, wp), BF, True),
            edge,
        ],
        [],
        name="norm_product",
    )
    normed = normed.reshape(nblocks * rows, d_model)

    def two(v):
        return v.reshape((2, 2, nn) + v.shape[1:])

    rim = pass_along(6, "pass_rows", False, tail)
    conv_0b, state_0b = per_block(conv_0), per_block(state_0)
    full = (nblocks, rows, wp)
    conv_low, retain, admit, carry_mul, carry_add, end_mul, end_add = by_block(
        functools.partial(forward_kernel, nseq, taps),
        info,
        [
            (linear, True), (rim, True), (conv_0b, True), (state_0b, True),
            (w_gates, False), (vec, False),
        ],
        [
            (full, BF, True), (full, F32, True), (full, F32, True),
            (full, F32, True), (full, F32, True), edge, edge,
        ],
        [(rows + 8, wp), (rows, wp), (rows, wp)],
        name="mixer_forward",
    )

    (end_mul, end_add), grads = lax.optimization_barrier(((end_mul, end_add), grads))
    state_in = pass_along(7, "pass_state", False, end_mul, end_add)
    hidden = carry_mul * state_in + carry_add
    mixed_in = (hidden * jax.nn.gelu(gate_in)).astype(BF).reshape(-1, wp)
    resid, normed_two, grads = plane_reduce(
        2, "fwd", False, (mixed_in.reshape(2, count, rows, -1),), w_o, gain_two, tokens[0],
        tokens[0], grads,
    )
    normed_two = normed_two.reshape(nblocks * rows, d_model)
    grads = grads.reshape(nblocks * rows, d_model)

    hid_full = (nblocks, rows, f_here)
    inner, by_gate, by_up = by_block(
        ffn_forward_kernel,
        info,
        [(normed_two.reshape(nblocks, rows, d_model), True), (w_gu, False)],
        [(hid_full, BF, True)] * 3,
        [],
        name="ffn_forward",
    )
    inner = inner.reshape(nblocks * rows, f_here)
    cut = d_model // 2
    first_d = tdot(inner, grads[:, :cut]).astype(BF)
    second_d = tdot(inner, grads[:, cut:]).astype(BF)
    sent_d = scatter_a(first_d), scatter_a(second_d)
    d_pair = by_block(
        ffn_back_kernel,
        info,
        [
            (grads.reshape(nblocks, rows, d_model), True), (w_d, False), (by_gate, True),
            (by_up, True),
        ],
        [((nblocks, rows, 2 * f_here), BF, True)],
        [],
        (first_d, second_d),
        name="ffn_back",
    )[0]
    sums_gu = tdot(normed_two, d_pair.reshape(nblocks * rows, -1)).astype(BF)
    sent_gu = scatter_a(sums_gu)
    d_resid, d_resid_low, low = plane_reduce(
        3, "mid", True, (d_pair.reshape(2, count, rows, -1),), w_gu,
        gain_two, grad_low, resid, (inner.reshape(2, count, rows, f_here), w_d), (sent_d[0], sums_gu),
    )
    d_resid_low = d_resid_low.reshape(nblocks * rows, d_model)

    sums_o = tdot(mixed_in, d_resid_low)[:wide_here].astype(BF)
    grad_wo = scatter_a(part_halves(sums_o))
    low, sums_o = lax.optimization_barrier((low, sums_o))
    result = resid + low[0].astype(F32)
    for k in range(1, count):
        result = result + xor_u(low[k], k).astype(F32)
    result = result.astype(BF)

    d_gate_in, back_mul, back_add, end_mul, end_add = by_block(
        functools.partial(back_scan_kernel, nseq, taps),
        info,
        [
            (d_resid_low.reshape(nblocks, rows, d_model), True), (w_o, False), (gate_in, True),
            (hidden, True), (retain, True), (vec, False),
        ],
        [(full, BF, True), (full, F32, True), (full, F32, True), edge, edge],
        [(rows + 8, wp), (rows, wp), (rows, wp)],
        (sent_d[1], sums_o),
        name="mixer_back_scan",
    )
    grad_in = pass_along(8, "pass_state_back", True, end_mul, end_add)
    d_conv_low, head, sums_gates, vec_grads = by_block(
        functools.partial(back_kernel, nseq, taps),
        info,
        [
            (back_mul, True), (back_add, True), (grad_in, True), (hidden, True),
            (state_in, True), (state_0b, True), (conv_low, True), (retain, True),
            (admit, True), (linear, True), (rim, True), (conv_0b, True), (w_gates, False), (vec, False),
        ],
        [(full, BF, True), edge, ((wp, 2 * wp), F32, False), ((taps + 4, wp), F32, False)],
        [(rows + 8, wp)],
        (result, sent_gu),
        name="mixer_back",
    )

    def diagonal(m):
        m = m.reshape(heads_here, head_w, heads_here, head_w)
        return jnp.concatenate([m[h, :, h] for h in range(heads_here)], 0)

    grad_gates = jnp.concatenate(
        [
            diagonal(sums_gates[:wide_here, :wide_here]),
            diagonal(sums_gates[:wide_here, wp : wp + wide_here]),
        ],
        1,
    )
    rim_back = pass_along(9, "pass_rows_back", True, head)
    d_both = by_block(
        functools.partial(back_conv_kernel, nseq, taps),
        info,
        [(d_conv_low, True), (rim_back, True), (d_gate_in, True), (vec, False)],
        [((nblocks, rows, 2 * wide_here), BF, True)],
        [(rows + 8, wp)],
        (grad_wo,),
        name="mixer_back_conv",
    )[0]
    vec_grads = vec_grads[:, :wide_here].T
    vec_grads = jnp.concatenate(
        [vec_grads[:, :-1], vec_grads[:, -1:] * jax.nn.sigmoid(decay_f)[:, None]], 1
    )
    late = jnp.concatenate([grad_gates, vec_grads], 1).astype(BF)
    late = scatter_a(part_halves(late)).astype(F32)
    grad_wa, grad_wi = late[:, :head_w], late[:, head_w : 2 * head_w]
    vec_grads = late[:, 2 * head_w :].T

    sums_yx = tdot(normed, d_both.reshape(nblocks * rows, 2 * wide_here)).astype(BF)
    end = jnp.concatenate(
        [offsets[:, 1:], jnp.full((streams, 1), planes * 2 * rows, jnp.int32)], 1
    )
    end_b = per_block(end) - 1
    hot = (position[:, None, :] == end_b[:, :, None]).astype(BF)
    lasts = lax.dot_general(
        hot, hidden.astype(BF), (((2,), (1,)), ((0,), (0,))), preferred_element_type=F32
    )
    slots = jnp.arange(back, dtype=jnp.int32)
    where_conv = (end_b[:, :, None] - back + 1 + slots).reshape(nblocks, nseq * back)
    hot = (position[:, None, :] == where_conv[:, :, None]).astype(BF)
    conv_lasts = lax.dot_general(
        hot, linear, (((2,), (1,)), ((0,), (0,))), preferred_element_type=F32
    )
    lasts = two(jnp.concatenate([lasts, conv_lasts], 1)[..., :wide_here])
    lasts = (lasts[:, 0] + lasts[:, 1]).astype(BF)
    input_grad, grad_wg, grad_wu, found = plane_reduce(
        4, "last", True, (d_both.reshape(2, count, rows, -1),), w_yx, gain_one, tokens[0], d_resid,
        (sent_gu,), (sums_yx, result), hid, lasts,
    )
    grad_wy, grad_wx = finish(scatter_a(sums_yx), head_w)

    def gain_grad(gain, *pairs):
        total = sum(jnp.sum(w.astype(F32) * g, axis=1) for w, g in pairs)
        return total / gain.astype(F32)

    grad_gain_one = gain_grad(norm1_gain, (w_y, grad_wy), (w_x, grad_wx))
    grad_gain_two = gain_grad(norm2_gain, (w_gate, grad_wg), (w_up, grad_wu))

    found = found.reshape(2, count, nseq * taps, heads_here, head_w)
    found = found.transpose(2, 0, 3, 1, 4).reshape(nseq * taps, width)
    final_state = found[:nseq].astype(F32)
    final_conv = found[nseq:].reshape(nseq, back, width)

    return (
        result[None],
        input_grad[None],
        final_state[None],
        final_conv[None],
        grad_wy,
        grad_wx,
        grad_wa,
        grad_wi,
        grad_wo.astype(F32),
        grad_gain_one,
        vec_grads[:taps],
        vec_grads[taps],
        vec_grads[taps + 1],
        vec_grads[taps + 2],
        vec_grads[taps + 3],
        grad_wg,
        grad_wu,
        jnp.concatenate(sent_d, 1).astype(F32),
        grad_gain_two,
    )


WIDE = ("a", "b")
EVERY = ("a", "b", "n", "c")
HIGH = lax.Precision.HIGHEST


def passed_along(value, axis, by):
    size = lax.axis_size(axis)
    pairs = [(i, i + by) for i in range(size) if 0 <= i + by < size]
    return lax.ppermute(value, axis, pairs)


def entering(value, axis, combine, identity, reverse):
    size, place = (lax.axis_size(axis), lax.axis_index(axis))
    everything = jax.tree.map(lambda part: lax.all_gather(part, axis), value)
    start = jax.tree.map(
        lambda part, zero: jnp.broadcast_to(jnp.asarray(zero, part.dtype), part.shape),
        value,
        identity,
    )

    def hop(k, before):
        at = size - 1 - k if reverse else k
        reached = at > place if reverse else at < place
        new = combine(before, jax.tree.map(lambda part: part[at], everything))
        return jax.tree.map(lambda a, b: jnp.where(reached, a, b), new, before)

    return lax.fori_loop(0, size, hop, start)


def merged_2(value, axis, combine):
    everything = jax.tree.map(
        lambda part, kind: lax.all_gather(part.astype(kind), axis),
        value,
        jax.tree.map(lambda a: jnp.bfloat16 if a.dtype == jnp.float32 else a.dtype, value),
    )

    def take(k):
        return jax.tree.map(lambda part, own: part[k].astype(own.dtype), everything, value)

    return lax.fori_loop(
        1, lax.axis_size(axis), lambda k, so_far: combine(so_far, take(k)), take(0)
    )


def link(earlier, later):
    return (earlier[0] * later[0], later[0] * earlier[1] + later[1])


def norm_back(value, factor, gain, grad):
    weighted = grad * gain
    inner = jnp.mean(weighted * value, axis=-1, keepdims=True)
    return (
        factor * weighted - value * factor * factor * factor * inner,
        jnp.sum(grad * value * factor, axis=0),
    )


def later_one(first, second):
    pick = first[0] > second[0]
    return (
        jnp.where(pick, first[0], second[0]),
        jnp.where(pick[:, None], first[1], second[1]),
        jnp.where(pick[:, None, None], first[2], second[2]),
    )


def on_device_any(
    tokens,
    starts,
    init_state,
    init_conv,
    w_y,
    w_x,
    gate_a,
    gate_i,
    w_out,
    norm1_gain,
    conv_kernel,
    conv_bias,
    bias_a,
    bias_i,
    decay_param,
    w_gate,
    w_up,
    w_down,
    norm2_gain,
    cotangent,
):
    inputs = tokens[0].astype(jnp.float32)
    offsets = starts[0]
    nseqs = offsets.shape[0]
    rows_here = inputs.shape[0]
    width = w_y.shape[1]
    head_w = gate_a.shape[1]
    heads = width // head_w
    place = lax.axis_index(WIDE)
    mixer = (
        lax.all_gather(w_y, EVERY, axis=0, tiled=True),
        lax.all_gather(w_x, EVERY, axis=0, tiled=True),
        lax.all_gather(gate_a, EVERY, axis=0, tiled=True),
        lax.all_gather(gate_i, EVERY, axis=0, tiled=True),
        lax.all_gather(w_out, EVERY, axis=0, tiled=True),
        lax.all_gather(norm1_gain, EVERY, axis=0, tiled=True),
        lax.all_gather(conv_kernel, EVERY, axis=1, tiled=True),
        lax.all_gather(conv_bias, EVERY, axis=0, tiled=True),
        lax.all_gather(bias_a, EVERY, axis=0, tiled=True),
        lax.all_gather(bias_i, EVERY, axis=0, tiled=True),
        lax.all_gather(decay_param, EVERY, axis=0, tiled=True),
    )
    wy_full, wx_full, wa_full, wi_full, wo_full, gain_one, kernel, cbias, abias, ibias, decay = (
        mixer
    )
    gain_one = gain_one.astype(jnp.float32)
    kernel = kernel.astype(jnp.float32)
    taps = kernel.shape[0]
    back = taps - 1
    position = place * rows_here + jnp.arange(rows_here, dtype=jnp.int32)

    def segment_of(where_at):
        return jnp.sum((where_at[:, None] >= offsets[None, :]).astype(jnp.int32), axis=1) - 1

    segment = segment_of(position)
    member = segment[:, None] == jnp.arange(nseqs, dtype=jnp.int32)[None, :]
    begin = jnp.sum(jnp.where(member, offsets[None, :], 0), axis=1)
    opening = (position == begin)[:, None]
    scale_one = lax.rsqrt(jnp.mean(inputs * inputs, axis=-1, keepdims=True) + EPS)
    normed = (inputs * scale_one * gain_one).astype(jnp.bfloat16)
    gate_in = mdot(normed, wy_full)
    linear = mdot(normed, wx_full).astype(jnp.bfloat16)
    rim_rows = passed_along(linear[rows_here - back :], WIDE, 1)
    extended = jnp.concatenate([rim_rows, linear], 0)
    stored = mdot(member.astype(jnp.bfloat16), init_conv[0].reshape(nseqs, back * width)).reshape(
        rows_here, back, width
    )
    inputs_by_tap = [linear.astype(jnp.float32)]
    for shift_by in range(1, taps):
        earlier = extended[back - shift_by : back - shift_by + rows_here].astype(jnp.float32)
        offset = position - shift_by - begin
        from_start = jnp.zeros((rows_here, width), jnp.float32)
        for slot in range(back):
            from_start = from_start + jnp.where(
                (offset + back == slot)[:, None], stored[:, slot], 0.0
            )
        inputs_by_tap.append(jnp.where((offset >= 0)[:, None], earlier, from_start))
    conv_sum = cbias.astype(jnp.float32)
    for shift_by in range(taps):
        conv_sum = conv_sum + kernel[shift_by] * inputs_by_tap[shift_by]
    conv_low = conv_sum.astype(jnp.bfloat16)
    conv_val = conv_low.astype(jnp.float32)
    blocks = conv_low.reshape(rows_here, heads, head_w)
    wa_heads = wa_full.reshape(heads, head_w, head_w)
    wi_heads = wi_full.reshape(heads, head_w, head_w)
    rate = jnp.einsum("thi,hij->thj", blocks, wa_heads, preferred_element_type=jnp.float32).reshape(
        rows_here, width
    ) + abias.astype(jnp.float32)
    inflow = jnp.einsum(
        "thi,hij->thj", blocks, wi_heads, preferred_element_type=jnp.float32
    ).reshape(rows_here, width) + ibias.astype(jnp.float32)
    retain = jax.nn.sigmoid(rate)
    admit = jax.nn.sigmoid(inflow)
    decay_f = decay.astype(jnp.float32)
    soft_decay = jax.nn.softplus(decay_f)
    log_a = -8.0 * retain * soft_decay
    decay_now = jnp.exp(log_a)
    spread = -jnp.expm1(2.0 * log_a)
    mult = jnp.sqrt(jnp.maximum(spread, FLOOR))
    drive = mult * admit * conv_val
    state_rows = jnp.dot(member.astype(jnp.float32), init_state[0], precision=HIGH)
    a_used = jnp.where(opening, 0.0, decay_now)
    b_used = jnp.where(opening, decay_now * state_rows + drive, drive)
    carry_mul, carry_add = lax.associative_scan(link, (a_used, b_used), axis=0)
    identity = (jnp.ones((width,), jnp.float32), jnp.zeros((width,), jnp.float32))
    state_in = entering(
        (carry_mul[rows_here - 1], carry_add[rows_here - 1]), WIDE, link, identity, False
    )[1]
    hidden = carry_mul * state_in + carry_add
    gelu_y, gelu_y_back = jax.vjp(jax.nn.gelu, gate_in)
    mixed_in = (hidden * gelu_y).astype(jnp.bfloat16)
    resid = inputs + mdot(mixed_in, wo_full)
    wg_full, wu_full, wd_full, gain_two = (
        lax.all_gather(w_gate, EVERY, axis=0, tiled=True),
        lax.all_gather(w_up, EVERY, axis=0, tiled=True),
        lax.all_gather(w_down, EVERY, axis=0, tiled=True),
        lax.all_gather(norm2_gain, EVERY, axis=0, tiled=True),
    )
    gain_two = gain_two.astype(jnp.float32)
    scale_two = lax.rsqrt(jnp.mean(resid * resid, axis=-1, keepdims=True) + EPS)
    normed_two = (resid * scale_two * gain_two).astype(jnp.bfloat16)
    gate = mdot(normed_two, wg_full)
    upward = mdot(normed_two, wu_full)
    active, gate_back = jax.vjp(jax.nn.gelu, gate)
    inner = (active * upward).astype(jnp.bfloat16)
    result = (resid + mdot(inner, wd_full)).astype(jnp.bfloat16)
    local_rows = jnp.arange(rows_here, dtype=jnp.int32)
    last_row = jnp.max(jnp.where(member, local_rows[:, None], -1), axis=0)
    present = last_row >= 0
    safe_row = jnp.maximum(last_row, 0)
    marker = jnp.where(present, (place * rows_here + last_row).astype(jnp.float32), -1.0)
    state_last = jnp.where(present[:, None], hidden[safe_row], 0.0)
    conv_rows = extended[safe_row[:, None] + 1 + jnp.arange(back, dtype=jnp.int32)[None, :]].astype(
        jnp.float32
    )
    conv_last = jnp.where(present[:, None, None], conv_rows, 0.0)
    merged = merged_2((marker, state_last, conv_last), WIDE, later_one)
    wg_back, wu_back, wd_back = (
        lax.all_gather(w_gate, EVERY, axis=0, tiled=True),
        lax.all_gather(w_up, EVERY, axis=0, tiled=True),
        lax.all_gather(w_down, EVERY, axis=0, tiled=True),
    )
    grad_low = cotangent[0]
    grad_out = grad_low.astype(jnp.float32)
    d_inner = ndot(grad_low, wd_back)
    grad_wd = tdot(inner, grad_low)
    d_gate = gate_back(d_inner * upward)[0].astype(jnp.bfloat16)
    d_up = (d_inner * active).astype(jnp.bfloat16)
    grad_wg = tdot(normed_two, d_gate)
    grad_wu = tdot(normed_two, d_up)
    d_normed_two = ndot(d_gate, wg_back) + ndot(d_up, wu_back)
    d_resid_norm, grad_gain_two = norm_back(resid, scale_two, gain_two, d_normed_two)
    d_resid = grad_out + d_resid_norm
    wy_back, wx_back, wa_back, wi_back, wo_back = (
        lax.all_gather(w_y, EVERY, axis=0, tiled=True),
        lax.all_gather(w_x, EVERY, axis=0, tiled=True),
        lax.all_gather(gate_a, EVERY, axis=0, tiled=True),
        lax.all_gather(gate_i, EVERY, axis=0, tiled=True),
        lax.all_gather(w_out, EVERY, axis=0, tiled=True),
    )
    d_resid_low = d_resid.astype(jnp.bfloat16)
    d_mixed = ndot(d_resid_low, wo_back)
    grad_wo = tdot(mixed_in, d_resid_low)
    d_hidden = d_mixed * gelu_y
    d_gate_in = gelu_y_back(d_mixed * hidden)[0].astype(jnp.bfloat16)
    forward_mul = jnp.concatenate([a_used[1:], jnp.ones((1, width), jnp.float32)], 0)
    back_mul, back_add = lax.associative_scan(link, (forward_mul, d_hidden), reverse=True, axis=0)
    head_map = (a_used[0] * back_mul[0], a_used[0] * back_add[0])
    grad_in = entering(head_map, WIDE, link, identity, True)[1]
    total_grad = back_mul * grad_in + back_add
    previous = jnp.concatenate([state_in[None], hidden[:-1]], 0)
    previous = jnp.where(opening, state_rows, previous)
    d_decay = total_grad * previous
    d_mult = total_grad * admit * conv_val
    d_admit = total_grad * mult * conv_val
    d_conv = total_grad * mult * admit
    d_spread = jnp.where(spread > FLOOR, d_mult * 0.5 / mult, 0.0)
    d_log = d_decay * decay_now - 2.0 * decay_now * decay_now * d_spread
    d_retain = d_log * (-8.0 * soft_decay)
    grad_decay = jnp.sum(d_log * (-8.0 * retain), axis=0) * jax.nn.sigmoid(decay_f)
    d_rate = (d_retain * retain * (1.0 - retain)).astype(jnp.bfloat16)
    d_inflow = (d_admit * admit * (1.0 - admit)).astype(jnp.bfloat16)
    grad_abias = jnp.sum(d_rate.astype(jnp.float32), axis=0)
    grad_ibias = jnp.sum(d_inflow.astype(jnp.float32), axis=0)
    rate_heads = d_rate.reshape(rows_here, heads, head_w)
    inflow_heads = d_inflow.reshape(rows_here, heads, head_w)
    grad_wa = jnp.einsum(
        "thi,thj->hij", blocks, rate_heads, preferred_element_type=jnp.float32
    ).reshape(width, head_w)
    grad_wi = jnp.einsum(
        "thi,thj->hij", blocks, inflow_heads, preferred_element_type=jnp.float32
    ).reshape(width, head_w)
    d_conv = d_conv + jnp.einsum(
        "thj,hij->thi",
        rate_heads,
        wa_back.reshape(heads, head_w, head_w),
        preferred_element_type=jnp.float32,
    ).reshape(rows_here, width)
    d_conv = d_conv + jnp.einsum(
        "thj,hij->thi",
        inflow_heads,
        wi_back.reshape(heads, head_w, head_w),
        preferred_element_type=jnp.float32,
    ).reshape(rows_here, width)
    d_conv_low = d_conv.astype(jnp.bfloat16)
    d_conv_val = d_conv_low.astype(jnp.float32)
    rim_back = passed_along(d_conv_low[:back], WIDE, -1)
    ahead = jnp.concatenate([d_conv_low, rim_back], 0)
    d_linear = kernel[0] * d_conv_val
    kernel_grads = [jnp.sum(d_conv_val * inputs_by_tap[0], axis=0)]
    for shift_by in range(1, taps):
        later_rows = ahead[shift_by : shift_by + rows_here].astype(jnp.float32)
        same = (segment_of(position + shift_by) == segment)[:, None]
        d_linear = d_linear + kernel[shift_by] * jnp.where(same, later_rows, 0.0)
        kernel_grads.append(jnp.sum(d_conv_val * inputs_by_tap[shift_by], axis=0))
    grad_kernel = jnp.stack(kernel_grads, 0)
    grad_cbias = jnp.sum(d_conv_val, axis=0)
    d_linear_low = d_linear.astype(jnp.bfloat16)
    d_normed = ndot(d_gate_in, wy_back) + ndot(d_linear_low, wx_back)
    grad_wy = tdot(normed, d_gate_in)
    grad_wx = tdot(normed, d_linear_low)
    d_input_norm, grad_gain_one = norm_back(inputs, scale_one, gain_one, d_normed)
    input_grad = (d_resid + d_input_norm).astype(jnp.bfloat16)
    every_sum = (
        lax.psum_scatter(grad_wy, EVERY, scatter_dimension=0, tiled=True),
        lax.psum_scatter(grad_wx, EVERY, scatter_dimension=0, tiled=True),
        lax.psum_scatter(grad_wa, EVERY, scatter_dimension=0, tiled=True),
        lax.psum_scatter(grad_wi, EVERY, scatter_dimension=0, tiled=True),
        lax.psum_scatter(grad_wo, EVERY, scatter_dimension=0, tiled=True),
        lax.psum_scatter(grad_gain_one, EVERY, scatter_dimension=0, tiled=True),
        lax.psum_scatter(grad_kernel, EVERY, scatter_dimension=1, tiled=True),
        lax.psum_scatter(grad_cbias, EVERY, scatter_dimension=0, tiled=True),
        lax.psum_scatter(grad_abias, EVERY, scatter_dimension=0, tiled=True),
        lax.psum_scatter(grad_ibias, EVERY, scatter_dimension=0, tiled=True),
        lax.psum_scatter(grad_decay, EVERY, scatter_dimension=0, tiled=True),
        lax.psum_scatter(grad_wg, EVERY, scatter_dimension=0, tiled=True),
        lax.psum_scatter(grad_wu, EVERY, scatter_dimension=0, tiled=True),
        lax.psum_scatter(grad_wd, EVERY, scatter_dimension=0, tiled=True),
        lax.psum_scatter(grad_gain_two, EVERY, scatter_dimension=0, tiled=True),
    )
    mixer_sums = every_sum[:11]
    mlp_sums = every_sum[11:]
    return (
        result[None],
        input_grad[None],
        merged[1][None],
        merged[2].astype(jnp.bfloat16)[None],
        mixer_sums[0],
        mixer_sums[1],
        mixer_sums[2],
        mixer_sums[3],
        mixer_sums[4],
        mixer_sums[5],
        mixer_sums[6],
        mixer_sums[7],
        mixer_sums[8],
        mixer_sums[9],
        mixer_sums[10],
        mlp_sums[0],
        mlp_sums[1],
        mlp_sums[2],
        mlp_sums[3],
    )


def solution(mesh):
    wide, narrow = mesh.shape["wide"], mesh.shape["narrow"]
    def plan(*args):
        fits = args[6].shape[0] * 2 == args[6].shape[1] and narrow == 4
        return (on_device if fits else on_device_any)(*args)

    fine = Mesh(mesh.devices.reshape(wide // 2, 2, narrow // 2, 2), ("a", "b", "n", "c"))
    w, s = ("a", "b"), ("n", "c")
    everywhere = ("a", "b", "n", "c")
    acts, rows, vec = P(s, w, None), P(everywhere, None), P(everywhere)
    return jax.shard_map(
        plan,
        mesh=fine,
        in_specs=(
            acts,
            P(s, None),
            P(s, None, None),
            P(s, None, None, None),
            rows, rows, rows, rows, rows,
            vec,
            P(None, everywhere),
            vec, vec, vec, vec,
            rows, rows, rows,
            vec,
            acts,
        ),
        out_specs=(
            acts,
            acts,
            P(s, None, None),
            P(s, None, None, None),
            rows, rows, rows, rows, rows,
            vec,
            P(None, everywhere),
            vec, vec, vec, vec,
            rows, rows, rows,
            vec,
        ),
        check_vma=False,
    )
```

```python
import functools

import jax
import jax.numpy as jnp
from jax import lax
from jax.experimental import pallas as pl
from jax.experimental.pallas import tpu as pltpu
from jax.sharding import Mesh
from jax.sharding import PartitionSpec as P

EPS = 1e-06
FLOOR = 0.001
BF = jnp.bfloat16
F32 = jnp.float32


def tdot(left, right):
    return lax.dot_general(left, right, (((0,), (0,)), ((), ())), preferred_element_type=F32)


def ndot(left, right):
    return lax.dot_general(left, right, (((1,), (1,)), ((), ())), preferred_element_type=F32)


def mdot(left, right):
    return jnp.dot(left, right, preferred_element_type=F32)


def pick(stacked, index, axis=0):
    return lax.dynamic_index_in_dim(stacked, index, axis, keepdims=False)


def swap_c(value):
    return lax.ppermute(value, "c", [(0, 1), (1, 0)])


def xor_u(value, k):
    size = lax.axis_size("b") * lax.axis_size("n")
    return lax.ppermute(value, ("b", "n"), [(i, i ^ k) for i in range(size)])


def shift_a(value, by):
    size = lax.axis_size("a")
    return lax.ppermute(value, "a", [(i, i + by) for i in range(size) if 0 <= i + by < size])


def chips():
    return lax.axis_size("b") * lax.axis_size("n")


def chip():
    return lax.axis_index("b") * lax.axis_size("n") + lax.axis_index("n")


MESH = pl.DeviceIdType.MESH
VMEM_LIMIT = 60 * 1024 * 1024


def places():
    return tuple(lax.axis_index(name) for name in ("a", "b", "n", "c"))


def neighbours():
    a, b, n, c = places()
    return (a, 1 - b, n, c), (a, b, 1 - n, c), (a, b, n, 1 - c)


def greet(peers):
    barrier = pltpu.get_barrier_semaphore()
    for peer in peers:
        pl.semaphore_signal(barrier, inc=1, device_id=peer, device_id_type=MESH)
    pl.semaphore_wait(barrier, len(peers))


class Mover:
    def __init__(self, send, recv):
        self.send, self.recv, self.made = send, recv, {}
        self.names = []

    def copy(self, name, src, dst, peer):
        if name not in self.names:
            self.names.append(name)
        at = self.names.index(name)
        made = pltpu.make_async_remote_copy(
            src_ref=src,
            dst_ref=dst,
            send_sem=self.send.at[at],
            recv_sem=self.recv.at[at],
            device_id=peer,
            device_id_type=MESH,
        )
        self.made[name] = made
        return made

    def start(self, name, src, dst, peer):
        self.copy(name, src, dst, peer).start()

    def arrived(self, name):
        self.made[name].wait_recv()

    def sent(self):
        for made in self.made.values():
            made.wait_send()


def gather_plane_start(move, mine, everyone, h, half_rows):
    x, y, z = neighbours()
    at = pl.ds(h * half_rows, half_rows)
    move.start(f"gx{h}", mine.at[at], everyone.at[2, at], x)
    move.start(f"gy{h}", mine.at[at], everyone.at[1, at], y)
    move.start(f"gc{h}", mine.at[at], everyone.at[4, at], z)


def gather_plane_rest(move, everyone, half_rows, stage=None):
    x, y, z = neighbours()
    rows = [pl.ds(h * half_rows, half_rows) for h in range(2)]

    def on(name, k, h):
        move.start(name, everyone.at[k, rows[h]], everyone.at[4 + k, rows[h]], z)

    if stage in (None, 0):
        move.arrived("gx0")
        move.start("fy", everyone.at[2, rows[0]], everyone.at[3, rows[0]], y)
        on("cx0", 2, 0)
        move.arrived("gy1")
        move.start("fx", everyone.at[1, rows[1]], everyone.at[3, rows[1]], x)
        on("cy1", 1, 1)
    if stage in (None, 1):
        move.arrived("gx1")
        on("cx1", 2, 1)
        move.arrived("gy0")
        on("cy0", 1, 0)
    if stage in (None, 2):
        move.arrived("fy")
        on("cd0", 3, 0)
        move.arrived("fx")
        on("cd1", 3, 1)
        for name in ("gc0", "gc1", "cx0", "cx1", "cy0", "cy1", "cd0", "cd1"):
            move.arrived(name)


GATHER_COPIES = 14


def plane_peers_of():
    a, b, n, c = places()
    peers = {}
    for kc in range(2):
        for k in range(4):
            if (kc, k) != (0, 0):
                there = (a, 1 - b if k & 2 else b, 1 - n if k & 1 else n, 1 - c if kc else c)
                peers[kc, k] = there
    return peers


def peer_owner(kc, k):
    _, b, n, c = places()
    return ((b * 2 + n) ^ k) * 2 + (1 - c if kc else c)


def set_side_by_side(pieces, order, width):
    group = 1
    while group * width % 128 and group < len(order):
        group += 1
    for i in range(0, len(order), group):
        runs = [pieces[p, :, o : o + width].astype(F32) for p, o in order[i : i + group]]
        yield slice(i * width, (i + len(runs)) * width), jnp.concatenate(runs, 1)


def gain_sum(pairs, gain):
    total = sum(jnp.sum(w[...].astype(F32) * g[...], axis=-1, keepdims=True) for w, g in pairs)
    return total / gain[...]


def reduce_kernel(nt, post, nx, extra, waits, hid, head_w, *refs):
    x_hbm, refs = refs[:nx], refs[nx:]
    w_hbm, gain_ref, first_ref, second_ref = refs[:4]
    extra_in, refs = refs[4 : 4 + extra], refs[4 + extra :]
    if post == "last":
        lasts_ref, wg_ref, wu_ref, gain_two_ref = refs[:4]
        refs = refs[4:]
    refs = refs[waits:]
    out_ref, refs = refs[0], refs[1:]
    if post == "last":
        everyone = mine = None
        extra_out, lasts_out, gain_out = refs[:2], refs[2], refs[3]
        extra_buf, lasts_buf, lasts_mine, lasts_far, lasts_sent, lasts_sum = refs[4:10]
        refs = refs[10:]
    else:
        everyone, refs = refs[0], refs[1:]
        if extra:
            extra_out, refs = refs[0], refs[1:]
        mine, refs = refs[0], refs[1:]
        if post == "mid":
            (side_x, side_w, side_s, side_r), refs = refs[:4], refs[4:]
    x_v, w_v, away_s, away_r, acc, out_b, in_b, local, send, recv = refs
    rows, d_model = acc.shape[1:]
    half = rows // 2
    tile = min(512, d_model)
    px, py, pc = neighbours()
    move = Mover(send, recv)

    slots = iter(range(local.shape[0]))

    def keep(src, dst):
        made = pltpu.make_async_copy(src, dst, local.at[next(slots)])
        made.start()
        return made

    w_copy = keep(w_hbm, w_v)
    loads = {}
    each = x_v.shape[3] // nx
    for k in (3, 2, 1, 0):
        for kc in (1, 0):
            loads[kc, k] = [
                keep(x.at[kc, k], x_v.at[kc, k, :, pl.ds(i * each, each)])
                for i, x in enumerate(x_hbm)
            ]
    if post == "mid":
        side_loads = [keep(extra_in[0], side_x), keep(extra_in[1], side_w)]
    if post == "last":
        a, b, n, c = places()
        planes = lasts_far.shape[0] + 1
        columns = [(lax.rem(a + d, planes), b, n, c) for d in range(1, planes)]
        peers = plane_peers_of()
        greet([*peers.values(), *columns])
        for kc in range(2):
            for kn in range(2):
                lasts_sent[kc, kn] = (
                    lasts_ref[kc * 4 + kn].astype(F32) + lasts_ref[kc * 4 + 2 + kn].astype(F32)
                ).astype(BF)
        for (kc, k), peer in peers.items():
            move.start(f"l{kc}{k}", lasts_sent.at[kc, k % 2], lasts_buf.at[kc, k], peer)
    else:
        greet((px, py, pc))
    w_copy.wait()

    def product(kc, k, t):
        at = pl.ds(pl.multiple_of(t * tile, tile), tile)
        if nt:
            return at, ndot(x_v[kc, k], w_v[at, :])
        return at, mdot(x_v[kc, k], w_v[:, at])

    step = min(32, half)

    def by_rows(h, body):
        @pl.loop(0, half // step)
        def _(i):
            body(pl.ds(pl.multiple_of(i * step, step), step),
                 pl.ds(pl.multiple_of(h * half + i * step, step), step))

    def hand_on(name, slot, k, h, peer, extra=None):
        def body(inner, outer):
            value = acc[k, outer, :]
            if extra is not None:
                value = value + in_b[extra, inner, :].astype(F32)
            out_b[slot, inner, :] = value.astype(BF)

        by_rows(h, body)
        move.start(name, out_b.at[slot], in_b.at[slot], peer)

    for k in (3, 2, 1, 0):
        for load in loads[1, k]:
            load.wait()

        @pl.loop(0, d_model // tile)
        def _(t):
            at, value = product(1, k, t)
            away_s[k, :, at] = value.astype(BF)

        move.start(f"away{k}", away_s.at[k], away_r.at[k], pc)
        for load in loads[0, k]:
            load.wait()

        @pl.loop(0, d_model // tile)
        def _(t):
            at, value = product(0, k, t)
            acc[k, :, at] = value

        move.arrived(f"away{k}")
        for h in range(2):
            def add(inner, outer):
                acc[k, outer, :] += away_r[k, outer, :].astype(F32)

            by_rows(h, add)
        if k == 3:
            hand_on("d0", 0, 3, 0, px)
            hand_on("d1", 1, 3, 1, py)
        elif k == 2:
            hand_on("x0", 2, 2, 0, px)
        elif k == 1:
            hand_on("y1", 5, 1, 1, py)
    kept = []
    if extra and post == "fwd":
        for k in range(4):
            kept.append(keep(extra_in[k], extra_out.at[k]))
            move.start(f"e{k}", extra_in[k], extra_out.at[4 + k], pc)
    move.arrived("d0")
    hand_on("y0", 4, 1, 0, py, 0)
    move.arrived("d1")
    hand_on("x1", 3, 2, 1, px, 1)
    if post == "mid":
        for load in side_loads:
            load.wait()
        for k in range(4):

            @pl.loop(0, d_model // tile)
            def _(t):
                at = pl.ds(pl.multiple_of(t * tile, tile), tile)
                side_s[k, :, at] = mdot(side_x[1, k], side_w[:, at]).astype(BF)

            move.start(f"s{k}", side_s.at[k], side_r.at[k], pc)
        for k in range(4):
            move.arrived(f"s{k}")
            move.made.pop(f"s{k}").wait_send()

            @pl.loop(0, d_model // tile)
            def _(t):
                at = pl.ds(pl.multiple_of(t * tile, tile), tile)
                value = mdot(side_x[0, k], side_w[:, at]) + side_r[k, :, at].astype(F32)
                side_s[k, :, at] = value.astype(BF)

            kept.append(keep(side_s.at[k], extra_out.at[k]))
    if extra and post == "last":
        lasts_buf[0, 0] = lasts_sent[0, 0]
        for kc, k in peers:
            move.arrived(f"l{kc}{k}")
        u = b * 2 + n
        me = u * 2 + c
        for kc in range(2):
            for q in range(4):
                found = lasts_buf[kc, 0]
                for k in range(1, 4):
                    found = jnp.where((u ^ k) == q, lasts_buf[kc, k], found)
                lasts_mine[jnp.bitwise_xor(c, kc), q] = found
        for i, peer in enumerate(columns):
            move.start(f"z{i}", lasts_mine, lasts_far.at[i], peer)
        each_rows = extra_buf.shape[1]

        def part(owner):
            at = pl.multiple_of(owner * each_rows, each_rows)
            return extra_in[0].at[pl.ds(at, each_rows)]

        kept.append(keep(part(me), extra_buf.at[me]))
        for (kc, k), peer in peers.items():
            move.start(f"e{kc}{k}", part(peer_owner(kc, k)), extra_buf.at[me], peer)

    for h in range(2):
        move.arrived(f"x{h}")
        move.arrived(f"y{h}")

        def body(inner, outer):
            total = acc[0, outer, :]
            total = total + in_b[2 + h, inner, :].astype(F32)
            total = total + in_b[4 + h, inner, :].astype(F32)
            gain = gain_ref[...]
            if post == "fwd":
                value = first_ref[outer, :].astype(F32) + total
                out_ref[outer, :] = value
                factor = lax.rsqrt(jnp.mean(value * value, axis=-1, keepdims=True) + EPS)
                mine[outer, :] = (value * factor * gain).astype(BF)
                return
            value = second_ref[outer, :] if post == "mid" else first_ref[outer, :].astype(F32)
            base = first_ref[outer, :].astype(F32) if post == "mid" else second_ref[outer, :]
            factor = lax.rsqrt(jnp.mean(value * value, axis=-1, keepdims=True) + EPS)
            weighted = total * gain
            inner_mean = jnp.mean(weighted * value, axis=-1, keepdims=True)
            grad = base + factor * weighted - value * (factor * factor * factor * inner_mean)
            if post == "mid":
                out_ref[outer, :] = grad
                mine[outer, :] = grad.astype(BF)
            else:
                out_ref[outer, :] = grad.astype(BF)

        by_rows(h, body)
        if everyone is not None:
            gather_plane_start(move, mine, everyone, h, half)
    if everyone is not None:
        kept.append(keep(mine, everyone.at[0]))
        gather_plane_rest(move, everyone, half)
    if extra and post == "fwd":
        for k in range(4):
            move.arrived(f"e{k}")
    for made in kept:
        made.wait()
    if extra and post == "last":
        total = lasts_mine[...].astype(F32)
        for i in range(len(columns)):
            move.arrived(f"z{i}")
            total = total + lasts_far[i].astype(F32)
        lasts_sum[...] = total.reshape(lasts_sum.shape)
        heads = extra_buf.shape[2] // (2 * hid) // 2
        order = [
            (i * 4 + q, j * head_w) for i in range(2) for j in range(heads) for q in range(4)
        ]
        for at, value in set_side_by_side(lasts_sum, order, head_w):
            lasts_out[:, at] = value
        for kc, k in peers:
            move.arrived(f"e{kc}{k}")
        wide = extra_buf.shape[2] // 2
        for i in range(2):
            order = [(p, i * wide + z * hid) for z in range(wide // hid) for p in range(8)]
            for at, value in set_side_by_side(extra_buf, order, hid):
                extra_out[i][:, at] = value
        gain_out[...] = gain_sum(((wg_ref, extra_out[0]), (wu_ref, extra_out[1])), gain_two_ref)
    move.sent()


def plane_reduce(ident, post, nt, xs, w, gain, first, second, extra=(), done=(), hid=0, lasts=None, weights=(), head_w=0):
    rows, d_model = first.shape
    vmem = pl.BlockSpec(memory_space=pltpu.VMEM)
    hbm = pl.BlockSpec(memory_space=pl.ANY)
    out_type = BF if post == "last" else F32
    out_shape = [jax.ShapeDtypeStruct((rows, d_model), out_type)]
    out_specs = [vmem]
    scratch = []
    copies = 10
    if post != "last":
        out_shape.append(jax.ShapeDtypeStruct((8, rows, d_model), BF))
        out_specs.append(hbm)
        copies += GATHER_COPIES
        if extra:
            blocks = 8 if post == "fwd" else 4
            out_shape.append(jax.ShapeDtypeStruct((blocks, rows, d_model), BF))
            out_specs.append(hbm)
            copies += 4
        scratch.append(pltpu.VMEM((rows, d_model), BF))
        if post == "mid":
            scratch += [pltpu.VMEM(v.shape, BF) for v in extra]
            scratch += [pltpu.VMEM((4, rows, d_model), BF)] * 2
    else:
        each = extra[0].shape[0] // 8, extra[0].shape[1]
        for _ in range(2):
            out_shape.append(jax.ShapeDtypeStruct((each[0], 4 * each[1]), F32))
            out_specs.append(vmem)
        planes = lax.axis_size("a")
        copies += 7 * len(extra) + 7 + planes - 1
        block = (2, 4) + lasts.shape[1:]
        wide = lax.axis_size("a") * 4 * head_w
        out_shape.append(jax.ShapeDtypeStruct((lasts.shape[1], wide), F32))
        out_shape.append(jax.ShapeDtypeStruct((each[0], 1), F32))
        out_specs += [vmem, vmem]
        scratch.append(pltpu.VMEM((8,) + each, BF))
        scratch += [pltpu.VMEM(block, BF)] * 2 + [pltpu.VMEM((planes - 1,) + block, BF)]
        scratch += [pltpu.VMEM((2, 2) + block[2:], BF), pltpu.VMEM((8,) + block[2:], F32)]
    wide = sum(x.shape[3] for x in xs)
    scratch += [
        pltpu.VMEM((2, 4, rows, wide), BF),
        pltpu.VMEM(w.shape, BF),
        pltpu.VMEM((4, rows, d_model), BF),
        pltpu.VMEM((4, rows, d_model), BF),
        pltpu.VMEM((4, rows, d_model), F32),
        pltpu.VMEM((6, rows // 2, d_model), BF),
        pltpu.VMEM((6, rows // 2, d_model), BF),
        pltpu.SemaphoreType.DMA((8 + 8 * len(xs),)),
        pltpu.SemaphoreType.DMA((copies,)),
        pltpu.SemaphoreType.DMA((copies,)),
    ]
    last = []
    if post == "last":
        last = [lasts, *weights[:2], weights[2].astype(F32).reshape(-1, 1)]
    return pl.pallas_call(
        functools.partial(reduce_kernel, nt, post, len(xs), len(extra), len(done), hid, head_w),
        in_specs=[hbm] * (len(xs) + 1)
        + [vmem] * 3
        + [vmem if post == "fwd" else hbm] * len(extra)
        + [vmem] * (4 if post == "last" else 0)
        + [hbm] * len(done),
        out_specs=out_specs,
        out_shape=out_shape,
        scratch_shapes=scratch,
        compiler_params=pltpu.CompilerParams(
            collective_id=ident, has_side_effects=True, vmem_limit_bytes=VMEM_LIMIT
        ),
        cost_estimate=pl.CostEstimate(flops=0, bytes_accessed=8 << 20, transcendentals=0),
        name=f"plane_reduce_{post}",
    )(*xs, w, gain.reshape(1, -1), first, second, *extra, *last, *done)


def start_kernel(
    head_w, hid, tokens_ref, wy_ref, wx_ref, wg_ref, wu_ref, rows_ref, vec_ref, stream_ref,
    tok_out, yx_out, gu_out, rows_out, halves_out, vec_out, stream_out,
    yx_ref, gu_ref, local, send, recv,
):
    a, b, n, c = places()
    planes = yx_out.shape[0]
    p = (b * 2 + n) * 2 + c
    pc = neighbours()[2]
    plane_peers = plane_peers_of()
    up, down = (a + 1, b, n, c), (a - 1, b, n, c)
    each = planes // 2

    def pack(out, sources, columns, width):
        for owner in range(8):
            runs = [w[:, o : o + width] for w in sources for o in columns(owner)]
            out[owner] = jnp.concatenate(runs, 1)

    barrier = pltpu.get_barrier_semaphore()
    for peer in plane_peers.values():
        pl.semaphore_signal(barrier, inc=1, device_id=peer, device_id_type=MESH)

    @pl.when(a < planes - 1)
    def _():
        pl.semaphore_signal(barrier, inc=1, device_id=up, device_id_type=MESH)

    @pl.when(a > 0)
    def _():
        pl.semaphore_signal(barrier, inc=1, device_id=down, device_id_type=MESH)

    def head_columns(owner):
        return [((owner % 2 * each + j) * 4 + owner // 2) * head_w for j in range(each)]

    pack(yx_ref, (wy_ref, wx_ref), head_columns, head_w)
    others = len(plane_peers) + jnp.minimum(planes - 1 - a, 1) + jnp.minimum(a, 1)
    pl.semaphore_wait(barrier, others)

    move = Mover(send, recv)
    half = tokens_ref.shape[0] // 2

    def keep(i, src, dst):
        made = pltpu.make_async_copy(src, dst, local.at[i])
        made.start()
        return made

    def to_owners(name, pieces, out):
        for (kc, k), peer in plane_peers.items():
            move.start(f"{name}{kc}{k}", pieces.at[peer_owner(kc, k)], out.at[a, p], peer)

    chains = {}

    def chain_step(name, out, s):
        def up_copy(block):
            return move.copy(f"{name}u{s}", out.at[block], out.at[block], up)

        def down_copy(block):
            return move.copy(f"{name}d{s}", out.at[block], out.at[block], down)

        sends_up, sends_down = (a < planes - 1) & (a >= s), (a > 0) & (a + s < planes)

        @pl.when(sends_up)
        def _():
            up_copy(a - s).start()

        @pl.when(sends_down)
        def _():
            down_copy(a + s).start()

        chains[name, s] = (up_copy, down_copy, sends_up, sends_down)

    def chain_arrived(name, s):
        up_copy, down_copy, _, _ = chains[name, s]

        @pl.when(a - 1 >= s)
        def _():
            up_copy(a - 1 - s).wait_recv()

        @pl.when(a + 1 + s < planes)
        def _():
            down_copy(a + 1 + s).wait_recv()

    def chain_sent(name, s):
        up_copy, down_copy, sends_up, sends_down = chains[name, s]

        @pl.when(sends_up)
        def _():
            up_copy(a - s).wait_send()

        @pl.when(sends_down)
        def _():
            down_copy(a + s).wait_send()

    to_owners("yx", yx_ref, yx_out)
    for (kc, k), peer in plane_peers.items():
        move.start(f"vec{kc}{k}", vec_ref, vec_out.at[a, p], peer)
    own_yx = keep(1, yx_ref.at[p], yx_out.at[a, p])
    own_vec = keep(2, vec_ref, vec_out.at[a, p])
    own_rows = keep(0, rows_ref, rows_out.at[a])
    own_tok = keep(4, tokens_ref, tok_out.at[0])
    own_stream = keep(5, stream_ref, stream_out.at[0, 0])
    own_yx.wait()
    own_vec.wait()
    for kc, k in plane_peers:
        move.arrived(f"yx{kc}{k}")
        move.arrived(f"vec{kc}{k}")
    own_rows.wait()
    outs = (("yx", yx_out), ("vec", vec_out), ("rows", rows_out))
    for name, out in outs:
        chain_step(name, out, 0)
    for h in range(2):
        gather_plane_start(move, tokens_ref, tok_out, h, half)
    pack(gu_ref, (wg_ref, wu_ref), lambda o: [(z * 8 + o) * hid for z in range(planes)], hid)
    own_gu = keep(3, gu_ref.at[p], gu_out.at[p])
    gather_plane_rest(move, tok_out, half, 0)
    for kc in range(2):
        for kn in range(2):
            if (kc, kn) != (0, 0):
                move.start(f"st{kc}{kn}", stream_ref, stream_out.at[kc, kn], plane_peers[kc, kn])
    for name, out in outs:
        chain_arrived(name, 0)
        chain_step(name, out, 1)
    gather_plane_rest(move, tok_out, half, 1)
    for (kc, k), peer in plane_peers.items():
        move.start(f"gu{kc}{k}", gu_ref.at[peer_owner(kc, k)], gu_out.at[p], peer)
    for s in range(1, planes - 1):
        for name, out in outs:
            chain_arrived(name, s)
            if s + 1 < planes - 1:
                chain_step(name, out, s + 1)
    gather_plane_rest(move, tok_out, half, 2)
    swap = pltpu.make_async_remote_copy(
        src_ref=rows_out.at[pl.ds((1 - c) * each, each)],
        dst_ref=halves_out.at[:, c],
        send_sem=send.at[send.shape[0] - 1],
        recv_sem=recv.at[recv.shape[0] - 1],
        device_id=pc,
        device_id_type=MESH,
    )
    swap.start()
    own_halves = keep(6, rows_out.at[pl.ds(c * each, each)], halves_out.at[:, c])
    for kc, k in plane_peers:
        move.arrived(f"gu{kc}{k}")
    for kc in range(2):
        for kn in range(2):
            if (kc, kn) != (0, 0):
                move.arrived(f"st{kc}{kn}")
    for made in (own_gu, own_tok, own_stream, own_halves):
        made.wait()
    swap.wait()
    for name, s in chains:
        chain_sent(name, s)
    for name in [n for n in move.names if not any(n == f"{w}{d}{s}" for w, s in chains for d in "ud")]:
        move.made[name].wait_send()


def start_exchange(tokens, w_y, w_x, w_gate, w_up, gate_rows, vec, stream):
    planes = lax.axis_size("a")
    head_w, hid = gate_rows.shape[1] // 2, w_gate.shape[1] // (planes * 8)
    vmem = pl.BlockSpec(memory_space=pltpu.VMEM)
    hbm = pl.BlockSpec(memory_space=pl.ANY)
    yx = (8, w_y.shape[0], 2 * w_y.shape[1] // 8)
    gu = (8, w_gate.shape[0], 2 * w_gate.shape[1] // 8)
    shapes = [
        ((8,) + tokens.shape, BF),
        ((planes,) + yx, BF),
        (gu, BF),
        ((planes,) + gate_rows.shape, BF),
        ((planes // 2, 2) + gate_rows.shape, BF),
        ((planes, 8) + vec.shape, F32),
        ((2, 2) + stream.shape, F32),
    ]
    copies = 7 * 3 + 3 + GATHER_COPIES + 6 * (planes - 1) + 1
    return pl.pallas_call(
        functools.partial(start_kernel, head_w, hid),
        in_specs=[vmem] * 8,
        out_specs=[hbm] * 7,
        out_shape=[jax.ShapeDtypeStruct(*shape) for shape in shapes],
        scratch_shapes=[
            pltpu.VMEM(yx, BF),
            pltpu.VMEM(gu, BF),
            pltpu.SemaphoreType.DMA((7,)),
            pltpu.SemaphoreType.DMA((copies,)),
            pltpu.SemaphoreType.DMA((copies,)),
        ],
        compiler_params=pltpu.CompilerParams(
            collective_id=1, has_side_effects=True, vmem_limit_bytes=VMEM_LIMIT
        ),
        cost_estimate=pl.CostEstimate(flops=0, bytes_accessed=8 << 20, transcendentals=0),
        name="start_exchange",
    )(tokens, w_y, w_x, w_gate, w_up, gate_rows, vec, stream)


def finish_kernel(
    head_w, sums_ref, wy_ref, wx_ref, gain_ref, y_ref, x_ref, gain_out, buf, local, send, recv
):
    _, b, n, c = places()
    me = (b * 2 + n) * 2 + c
    peers = plane_peers_of()
    greet(list(peers.values()))
    move = Mover(send, recv)
    each_rows = buf.shape[1]

    def part(owner):
        return sums_ref.at[pl.ds(pl.multiple_of(owner * each_rows, each_rows), each_rows)]

    for (kc, k), peer in peers.items():
        move.start(f"e{kc}{k}", part(peer_owner(kc, k)), buf.at[me], peer)
    own = pltpu.make_async_copy(part(me), buf.at[me], local.at[0])
    own.start()
    own.wait()
    for kc, k in peers:
        move.arrived(f"e{kc}{k}")
    wide = buf.shape[2] // 2
    each = wide // head_w
    order = [(q * 2 + i, j * head_w) for i in range(2) for j in range(each) for q in range(4)]
    for first, out in ((0, y_ref), (wide, x_ref)):
        for at, value in set_side_by_side(buf, [(p, o + first) for p, o in order], head_w):
            out[:, at] = value
    gain_out[...] = gain_sum(((wy_ref, y_ref), (wx_ref, x_ref)), gain_ref)
    move.sent()


def finish(sums, w_y, w_x, gain, head_w):
    each = sums.shape[0] // 8, sums.shape[1]
    vmem = pl.BlockSpec(memory_space=pltpu.VMEM)
    return pl.pallas_call(
        functools.partial(finish_kernel, head_w),
        in_specs=[pl.BlockSpec(memory_space=pl.ANY), vmem, vmem, vmem],
        out_specs=[vmem] * 3,
        out_shape=[jax.ShapeDtypeStruct((each[0], 4 * each[1]), F32)] * 2
        + [jax.ShapeDtypeStruct((each[0], 1), F32)],
        scratch_shapes=[
            pltpu.VMEM((8,) + each, BF),
            pltpu.SemaphoreType.DMA((1,)),
            pltpu.SemaphoreType.DMA((7,)),
            pltpu.SemaphoreType.DMA((7,)),
        ],
        compiler_params=pltpu.CompilerParams(
            collective_id=5, has_side_effects=True, vmem_limit_bytes=VMEM_LIMIT
        ),
        name="finish",
    )(sums, w_y, w_x, gain.astype(F32).reshape(-1, 1))


def column_peers(planes):
    a, b, n, c = places()
    return [(lax.rem(a + d, planes), b, n, c) for d in range(1, planes)]


def earlier_blocks(ref, want, row=0, count=1):
    _, b, _, _ = places()
    return [
        jnp.where(
            b == want,
            ref[kc * 4 + kn, row : row + count, :],
            ref[kc * 4 + 2 + kn, row : row + count, :],
        )
        for kc in range(2)
        for kn in range(2)
    ]


def split_refs(refs):
    if len(refs) == 5:
        return None, refs[:1], refs[1:], None
    return refs[0], refs[1:3], refs[3:7], refs[7:]


def swap_halves(rows_ref, out_ref, local, send, recv):
    _, _, _, c = places()
    planes, half = out_ref.shape[:2]
    each = planes // 2
    made = []
    for j in range(each):
        away = pl.multiple_of((2 * j + 1 - c) * half, half)
        own = pl.multiple_of((2 * j + c) * half, half)
        made.append(
            pltpu.make_async_remote_copy(
                src_ref=rows_ref.at[pl.ds(away, half)],
                dst_ref=out_ref.at[c * each + j],
                send_sem=send.at[j],
                recv_sem=recv.at[j],
                device_id=neighbours()[2],
                device_id_type=MESH,
            )
        )
        made.append(
            pltpu.make_async_copy(
                rows_ref.at[pl.ds(own, half)], out_ref.at[c * each + j], local.at[j]
            )
        )
    for copy in made:
        copy.start()
    return made


def pass_state_kernel(reverse, mul_ref, add_ref, *refs):
    rows_ref, (out_ref, *halves), (whole, came, send, recv), swaps = split_refs(refs)
    a, b, n, c = places()
    planes = came.shape[0] + 1
    row = 0 if reverse else 7
    near_at, far_at = (1, 0) if reverse else (0, 1)
    came[...] = jnp.zeros_like(came)
    near_mul, near_add = earlier_blocks(mul_ref, near_at, row), earlier_blocks(add_ref, near_at, row)
    far_mul, far_add = earlier_blocks(mul_ref, far_at, row), earlier_blocks(add_ref, far_at, row)
    for i in range(4):
        whole[0, i : i + 1, :] = near_mul[i] * far_mul[i]
        whole[1, i : i + 1, :] = far_mul[i] * near_add[i] + far_add[i]
    greet(column_peers(planes) + ([neighbours()[2]] if swaps else []))
    swapped = swap_halves(rows_ref, halves[0], *swaps) if swaps else []

    def copy(d):
        return pltpu.make_async_remote_copy(
            src_ref=whole,
            dst_ref=came.at[d - 1],
            send_sem=send.at[d - 1],
            recv_sem=recv.at[d - 1],
            device_id=(a - d if reverse else a + d, b, n, c),
            device_id_type=MESH,
        )

    def sends(d):
        return a >= d if reverse else a + d < planes

    def receives(d):
        return a + d < planes if reverse else a >= d

    for d in range(1, planes):
        @pl.when(sends(d))
        def _():
            copy(d).start()

    for d in range(1, planes):
        @pl.when(receives(d))
        def _():
            copy(d).wait_recv()

    for i in range(4):
        at = slice(i, i + 1)
        value = came[planes - 2, 1, at, :]
        for d in range(planes - 2, 0, -1):
            value = came[d - 1, 0, at, :] * value + came[d - 1, 1, at, :]
        to_far = near_mul[i] * value + near_add[i]
        for kb in range(2):
            is_far = (b if kb == 0 else 1 - b) == far_at
            at = (i // 2) * 4 + kb * 2 + i % 2
            out_ref[at] = jnp.where(is_far, to_far, value)

    for d in range(1, planes):
        @pl.when(sends(d))
        def _():
            copy(d).wait_send()

    for made in swapped:
        made.wait()


def pass_rows_kernel(reverse, edge_ref, *refs):
    rows_ref, (out_ref, *halves), (leaving, came, send, recv), swaps = split_refs(refs)
    a, b, n, c = places()
    planes = lax.axis_size("a")
    near_at, far_at = (1, 0) if reverse else (0, 1)
    came[...] = jnp.zeros_like(came)
    out_ref[...] = jnp.zeros_like(out_ref)
    first = 0 if reverse else 4
    for i, value in enumerate(earlier_blocks(edge_ref, far_at, first, 4)):
        leaving[i * 4 : i * 4 + 4, :] = value
    greet(column_peers(planes) + ([neighbours()[2]] if swaps else []))
    swapped = swap_halves(rows_ref, halves[0], *swaps) if swaps else []
    copy = pltpu.make_async_remote_copy(
        src_ref=leaving,
        dst_ref=came,
        send_sem=send.at[0],
        recv_sem=recv.at[0],
        device_id=(a - 1 if reverse else a + 1, b, n, c),
        device_id_type=MESH,
    )
    sends = a >= 1 if reverse else a + 1 < planes
    receives = a + 1 < planes if reverse else a >= 1

    @pl.when(sends)
    def _():
        copy.start()

    @pl.when(receives)
    def _():
        copy.wait_recv()

    for i in range(4):
        for kb in range(2):
            is_far = (b if kb == 0 else 1 - b) == far_at
            at = (i // 2) * 4 + kb * 2 + i % 2
            other = (i // 2) * 4 + (1 - kb) * 2 + i % 2
            out_ref[at, first : first + 4, :] = jnp.where(
                is_far, edge_ref[other, first : first + 4, :], came[i * 4 : i * 4 + 4, :]
            )

    @pl.when(sends)
    def _():
        copy.wait_send()

    for made in swapped:
        made.wait()


def pass_along(ident, name, reverse, *edges, halves=None):
    shape = edges[0].shape
    planes = lax.axis_size("a")
    vmem = pl.BlockSpec(memory_space=pltpu.VMEM)
    if len(edges) == 2:
        body, out = pass_state_kernel, (shape[0], 1, shape[2])
        buffers = [(2, 4) + shape[2:], (planes - 1, 2, 4) + shape[2:]]
    else:
        body, out = pass_rows_kernel, shape
        buffers = [(16,) + shape[2:]] * 2
    given, out_shape = list(edges), [jax.ShapeDtypeStruct(out, F32)]
    scratch = [pltpu.VMEM(shape, F32) for shape in buffers]
    scratch += [pltpu.SemaphoreType.DMA((planes - 1,))] * 2
    if halves is not None:
        given.append(halves[0])
        to = (planes, halves[1], halves[0].shape[1])
        out_shape.append(jax.ShapeDtypeStruct(to, BF))
        scratch += [pltpu.SemaphoreType.DMA((planes // 2,))] * 3
    return pl.pallas_call(
        functools.partial(body, reverse),
        in_specs=[vmem] * len(given),
        out_specs=[vmem] * len(out_shape),
        out_shape=out_shape,
        scratch_shapes=scratch,
        compiler_params=pltpu.CompilerParams(
            collective_id=ident, has_side_effects=True, vmem_limit_bytes=VMEM_LIMIT
        ),
        cost_estimate=pl.CostEstimate(flops=0, bytes_accessed=1 << 20, transcendentals=0),
        name=name,
    )(*given)


def norm_product_kernel(info, tok_ref, w_ref, gain_ref, n_ref, gate_ref, lin_ref, tail_ref):
    rows, d_model = tok_ref.shape[1:]
    step = min(64, rows)

    @pl.loop(0, rows // step)
    def _(i):
        at = pl.ds(pl.multiple_of(i * step, step), step)
        value = tok_ref[0, at, :].astype(F32)
        factor = lax.rsqrt(jnp.mean(value * value, axis=-1, keepdims=True) + EPS)
        n_ref[0, at, :] = (value * factor * gain_ref[...]).astype(BF)

    wide = gate_ref.shape[2]
    both = mdot(n_ref[0], w_ref[...])
    used = both.shape[1] // 2
    pad = [jnp.zeros((rows, wide - used), F32)] if wide > used else []
    gate_ref[0] = jnp.concatenate([both[:, :used]] + pad, 1)
    low = jnp.concatenate([both[:, used:]] + pad, 1).astype(BF)
    lin_ref[0] = low
    tail_ref[0] = low.astype(F32)[rows - 8 :, :]


def row_places(info, rows, nseq):
    i = pl.program_id(0)
    pos = info[i, 0] + lax.broadcasted_iota(jnp.int32, (rows, 1), 0)
    begin = jnp.zeros((rows, 1), jnp.int32) + info[i, 1]
    seg = jnp.zeros((rows, 1), jnp.int32)
    for s in range(1, nseq):
        begin = jnp.where(pos >= info[i, 1 + s], info[i, 1 + s], begin)
        seg = jnp.where(pos >= info[i, 1 + s], s, seg)
    return pos, begin, seg


def inputs_by_tap(ext, lin_ref, rim_ref, conv0_ref, begin_at, seg, taps):
    rows = lin_ref.shape[1]
    back = taps - 1
    ext[0:8, :] = rim_ref[0]
    ext[8 : 8 + rows, :] = lin_ref[0].astype(F32)
    slots = conv0_ref.shape[1]
    column = lax.broadcasted_iota(jnp.int32, (rows, slots), 1)
    found = [ext[8 : 8 + rows, :]]
    for k in range(1, taps):
        hot = (column == seg * back + begin_at - k + back) & (begin_at < k)
        stored = mdot(jnp.where(hot, 1.0, 0.0).astype(BF), conv0_ref[0])
        found.append(jnp.where(begin_at >= k, ext[8 - k : 8 - k + rows, :], stored))
    return found


def run_scan(a_s, b_s, p_ref, s_ref, rows, reverse):
    width = b_s.shape[1]
    groups = rows // 8
    row = lax.broadcasted_iota(jnp.int32, (8, width), 0)
    if reverse:
        row = 7 - row

    def step(i, carry):
        cp, cs = carry
        g = groups - 1 - i if reverse else i
        at = pl.ds(pl.multiple_of(g * 8, 8), 8)
        a, b = a_s[at, :], b_s[at, :]
        for d in (1, 2, 4):
            by = 8 - d if reverse else d
            inside = row >= d
            a_far = jnp.where(inside, pltpu.roll(a, by, 0), 1.0)
            b_far = jnp.where(inside, pltpu.roll(b, by, 0), 0.0)
            b = a * b_far + b
            a = a * a_far
        b = a * cs + b
        a = a * cp
        p_ref[0, at, :] = a
        s_ref[0, at, :] = b
        last = 0 if reverse else 7
        return a[last : last + 1], b[last : last + 1]

    start = (jnp.ones((1, width), F32), jnp.zeros((1, width), F32))
    lax.fori_loop(0, groups, step, start, unroll=4)


V_CBIAS, V_ABIAS, V_IBIAS, V_SOFT = 0, 1, 2, 3


def forward_kernel(
    nseq, taps, info, lin_ref, rim_ref, conv0_ref, state0_ref, wg_ref, vec_ref,
    conv_ref, retain_ref, admit_ref, p_ref, s_ref, pe_ref, se_ref, ext, a_s, b_s,
):
    i = pl.program_id(0)
    rows, wide = lin_ref.shape[1:]
    pos, begin, seg = row_places(info, rows, nseq)
    at = pos - begin

    def vec(k):
        return vec_ref[k : k + 1, :]

    by_tap = inputs_by_tap(ext, lin_ref, rim_ref, conv0_ref, at, seg, taps)
    total = vec(taps + V_CBIAS)
    for k in range(taps):
        total = total + vec(k) * by_tap[k]
    low = total.astype(BF)
    conv_ref[0] = low
    conv = low.astype(F32)
    both = mdot(low, wg_ref[...])
    retain = jax.nn.sigmoid(both[:, :wide] + vec(taps + V_ABIAS))
    admit = jax.nn.sigmoid(both[:, wide:] + vec(taps + V_IBIAS))
    retain_ref[0] = retain
    admit_ref[0] = admit
    a = jnp.exp(-8.0 * retain * vec(taps + V_SOFT))
    mult = jnp.sqrt(jnp.maximum((1.0 - a) * (1.0 + a), FLOOR))
    drive = mult * admit * conv
    for s in range(nseq):
        drive = drive + jnp.where(pos == info[i, 1 + s], a * state0_ref[0, s : s + 1, :], 0.0)
    a_s[...] = jnp.where(at == 0, 0.0, a)
    b_s[...] = drive
    run_scan(a_s, b_s, p_ref, s_ref, rows, False)
    pe_ref[0] = p_ref[0, rows - 8 : rows, :]
    se_ref[0] = s_ref[0, rows - 8 : rows, :]


def gelu_pair(x):
    root = 0.7978845608028654
    inner = root * (x + 0.044715 * (x * x * x))
    th = jnp.tanh(inner)
    cdf = 0.5 * (1.0 + th)
    slope = cdf + 0.5 * x * (1.0 - th * th) * (root * (1.0 + 3.0 * 0.044715 * (x * x)))
    return x * cdf, slope


def ffn_forward_kernel(info, n_ref, w_ref, inner_ref, by_gate_ref, by_up_ref):
    pair = mdot(n_ref[0], w_ref[...])
    hidden = inner_ref.shape[2]
    upward = pair[:, hidden:]
    active, slope = gelu_pair(pair[:, :hidden])
    inner_ref[0] = (active * upward).astype(BF)
    by_gate_ref[0] = (slope * upward).astype(BF)
    by_up_ref[0] = active.astype(BF)


def ffn_back_kernel(info, g_ref, w_ref, by_gate_ref, by_up_ref, *refs):
    out_ref = refs[-1]
    hidden = w_ref.shape[0]
    d_inner = ndot(g_ref[0], w_ref[...])
    out_ref[0, :, :hidden] = (d_inner * by_gate_ref[0].astype(F32)).astype(BF)
    out_ref[0, :, hidden:] = (d_inner * by_up_ref[0].astype(F32)).astype(BF)


def back_scan_kernel(
    nseq, taps, info, dres_ref, wo_ref, gate_ref, hidden_ref, retain_ref, vec_ref, mixed_ref, *refs
):
    dgate_ref, p_ref, s_ref, pe_ref, se_ref, wgrad_ref, ext, a_s, b_s, wgrad = refs[-10:]
    rows = gate_ref.shape[1]
    i = pl.program_id(0)

    @pl.when(i == 0)
    def _():
        wgrad[...] = jnp.zeros_like(wgrad)

    wgrad[...] += tdot(mixed_ref[0], dres_ref[0])

    @pl.when(i == pl.num_programs(0) - 1)
    def _():
        wgrad_ref[...] = wgrad[...].astype(BF)

    pos, begin, _ = row_places(info, rows, nseq)
    d_mixed = ndot(dres_ref[0], wo_ref[...])
    gelu, slope = gelu_pair(gate_ref[0])
    dgate_ref[0] = (d_mixed * hidden_ref[0] * slope).astype(BF)
    b_s[...] = d_mixed * gelu
    soft = vec_ref[taps + V_SOFT : taps + V_SOFT + 1, :]
    a = jnp.where(pos == begin, 0.0, jnp.exp(-8.0 * retain_ref[0] * soft))
    ext[0:rows, :] = a
    ext[rows : rows + 8, :] = jnp.ones((8, a.shape[1]), F32)
    a_s[...] = ext[1 : rows + 1, :]
    run_scan(a_s, b_s, p_ref, s_ref, rows, True)
    pe_ref[0] = ext[0:8, :] * p_ref[0, 0:8, :]
    se_ref[0] = ext[0:8, :] * s_ref[0, 0:8, :]


def back_kernel(
    nseq, taps, length, info, p_ref, s_ref, grad_in_ref, hidden_ref, state_in_ref, state0_ref, conv_ref,
    retain_ref, admit_ref, lin_ref, rim_ref, conv0_ref, wg_ref, vec_ref, sums_o_ref, *refs
):
    dconv_ref, head_ref, late_ref, lasts_ref, ext, wgrad_ref, vgrad_ref = refs[-7:]
    i = pl.program_id(0)
    rows, wide = lin_ref.shape[1:]
    pos, begin, seg = row_places(info, rows, nseq)
    at = pos - begin
    conv_low = conv_ref[0]
    conv = conv_low.astype(F32)
    retain, admit = retain_ref[0], admit_ref[0]
    soft = vec_ref[taps + V_SOFT : taps + V_SOFT + 1, :]
    e = p_ref[0] * grad_in_ref[0, 0:1, :] + s_ref[0]
    ext[0:8, :] = jnp.broadcast_to(state_in_ref[0], (8, wide))
    ext[8 : 8 + rows, :] = hidden_ref[0]
    previous = ext[7 : 7 + rows, :]
    for s in range(nseq):
        previous = jnp.where(pos == info[i, 1 + s], state0_ref[0, s : s + 1, :], previous)
    a = jnp.exp(-8.0 * retain * soft)
    spread = (1.0 - a) * (1.0 + a)
    mult = jnp.sqrt(jnp.maximum(spread, FLOOR))
    d_mult = e * admit * conv
    d_spread = jnp.where(spread > FLOOR, d_mult * 0.5 / mult, 0.0)
    d_log = e * previous * a - 2.0 * a * a * d_spread
    d_rate = (d_log * (-8.0 * soft) * retain * (1.0 - retain)).astype(BF)
    d_inflow = (e * mult * conv * admit * (1.0 - admit)).astype(BF)
    d_gates = jnp.concatenate([d_rate, d_inflow], 1)
    d_conv = e * mult * admit + ndot(d_gates, wg_ref[...])
    low = d_conv.astype(BF)
    dconv_ref[0] = low
    low = low.astype(F32)
    head_ref[0] = low[0:8, :]

    @pl.when(i == 0)
    def _():
        wgrad_ref[...] = jnp.zeros_like(wgrad_ref)
        vgrad_ref[...] = jnp.zeros_like(vgrad_ref)

    wgrad_ref[...] += tdot(conv_low, d_gates)
    sums = [low * v for v in inputs_by_tap(ext, lin_ref, rim_ref, conv0_ref, at, seg, taps)]
    sums += [low, d_rate.astype(F32), d_inflow.astype(F32), d_log * (-8.0 * retain)]
    for k, value in enumerate(sums):
        vgrad_ref[k : k + 1, :] += jnp.sum(value, axis=0, keepdims=True)

    slots = lasts_ref.shape[1]
    column = lax.broadcasted_iota(jnp.int32, (1, slots), 1)
    wanted = jnp.full((1, slots), -1, jnp.int32)
    for q in range(nseq):
        end = (info[i, 2 + q] if q + 1 < nseq else length) - 1
        wanted = jnp.where(column == q, end, wanted)
        for j in range(taps - 1):
            wanted = jnp.where(column == nseq + q * (taps - 1) + j, end - (taps - 2) + j, wanted)
    hot = jnp.where(pos == wanted, 1.0, 0.0).astype(BF)
    states, convs = tdot(hot, hidden_ref[0].astype(BF)), tdot(hot, lin_ref[0])
    row = lax.broadcasted_iota(jnp.int32, states.shape, 0)
    lasts_ref[0] = jnp.where(row < nseq, states, convs).astype(BF)

    @pl.when(i == pl.num_programs(0) - 1)
    def _():
        used = late_ref.shape[0]
        before = sums_o_ref.shape[1]
        late_ref[:, :before] = sums_o_ref[:used, :]
        head_w = (late_ref.shape[1] - before - len(sums)) // 2
        last = len(sums) - 1
        vgrad_ref[last : last + 1, :] *= vec_ref[last + 1 : last + 2, :]
        count = vgrad_ref.shape[0]
        row = lax.broadcasted_iota(jnp.int32, (count, count), 0)
        column = lax.broadcasted_iota(jnp.int32, (count, count), 1)
        eye = jnp.where(row == column, 1.0, 0.0).astype(BF)
        turned = tdot(vgrad_ref[...].astype(BF), eye)
        for h in range(used // head_w):
            at = slice(h * head_w, (h + 1) * head_w)
            parts = [wgrad_ref[at, o + h * head_w : o + (h + 1) * head_w] for o in (0, wide)]
            parts.append(turned[at, : len(sums)])
            late_ref[at, before:] = jnp.concatenate(parts, 1).astype(BF)


def back_conv_kernel(nseq, taps, info, dconv_ref, rim_ref, dgate_ref, vec_ref, *refs):
    out_ref, ext = refs[-2:]
    i = pl.program_id(0)
    rows, wide = dconv_ref.shape[1:]
    pos = info[i, 0] + lax.broadcasted_iota(jnp.int32, (rows, 1), 0)
    ext[0:rows, :] = dconv_ref[0].astype(F32)
    ext[rows : rows + 8, :] = rim_ref[0]
    total = vec_ref[0:1, :] * ext[0:rows, :]
    for k in range(1, taps):
        cut = jnp.zeros((rows, 1), jnp.int32)
        for s in range(nseq):
            start = info[i, 1 + s]
            cut = jnp.where((pos < start) & (pos + k >= start), 1, cut)
        total = total + vec_ref[k : k + 1, :] * jnp.where(cut == 0, ext[k : k + rows, :], 0.0)
    used = out_ref.shape[2] // 2
    both = [dgate_ref[0].astype(F32)[:, :used], total[:, :used]]
    out_ref[0] = jnp.concatenate(both, 1).astype(BF)


def by_block(body, info, ins, outs, scratch, done=(), name=None):
    blocks = info.shape[0]

    def spec(shape, blocked):
        zeros = (0,) * (len(shape) - 1)
        if blocked:
            return pl.BlockSpec((1,) + tuple(shape[1:]), lambda i, *_: (i,) + zeros)
        return pl.BlockSpec(tuple(shape), lambda i, *_: (0,) + zeros)

    hbm = pl.BlockSpec(memory_space=pl.ANY)
    return pl.pallas_call(
        body,
        grid_spec=pltpu.PrefetchScalarGridSpec(
            num_scalar_prefetch=1,
            grid=(blocks,),
            in_specs=[spec(v.shape, blocked) for v, blocked in ins] + [hbm] * len(done),
            out_specs=[spec(shape, blocked) for shape, _, blocked in outs],
            scratch_shapes=[pltpu.VMEM(shape, F32) for shape in scratch],
        ),
        out_shape=[jax.ShapeDtypeStruct(shape, kind) for shape, kind, _ in outs],
        compiler_params=pltpu.CompilerParams(vmem_limit_bytes=VMEM_LIMIT),
        cost_estimate=pl.CostEstimate(flops=0, bytes_accessed=1 << 20, transcendentals=0),
        name=name,
    )(info, *[v for v, _ in ins], *done)


def on_device(
    tokens,
    starts,
    init_state,
    init_conv,
    w_y,
    w_x,
    gate_a,
    gate_i,
    w_out,
    norm1_gain,
    conv_kernel,
    conv_bias,
    bias_a,
    bias_i,
    decay_param,
    w_gate,
    w_up,
    w_down,
    norm2_gain,
    cotangent,
):
    planes, count = lax.axis_size("a"), chips()
    a, b, n, c = (lax.axis_index(name) for name in ("a", "b", "n", "c"))
    u = chip()
    nn = count // 2
    rows, d_model = tokens.shape[1], tokens.shape[2]
    nseq = starts.shape[1]
    width = w_y.shape[1]
    head_w = gate_a.shape[1]
    half = gate_a.shape[0]
    taps = conv_kernel.shape[0]
    back = taps - 1
    heads_here = planes // 2
    wide_here = heads_here * head_w
    wp = -(-wide_here // 128) * 128
    hid = w_down.shape[0]
    drows = w_y.shape[0]
    nblocks = 2 * count

    def gather_a(value):
        return lax.all_gather(value, "a", axis=0, tiled=True)

    def scatter_a(value):
        return lax.psum_scatter(value, "a", scatter_dimension=0, tiled=True)

    def padded(v, axis=-1):
        pads = [(0, 0)] * v.ndim
        pads[axis] = (0, wp - wide_here)
        return jnp.pad(v, pads)

    vectors = jnp.concatenate(
        [conv_kernel, conv_bias[None], bias_a[None], bias_i[None], decay_param[None]], 0
    ).reshape(-1)
    vectors = jnp.concatenate([vectors, norm1_gain, norm2_gain]).astype(F32)
    lanes = -(-vectors.shape[0] // 1024) * 128
    vectors = jnp.pad(vectors, (0, 8 * lanes - vectors.shape[0])).reshape(8, lanes)
    at_start = jnp.concatenate([init_state[0][:, None], init_conv[0].astype(F32)], 1)
    at_start = at_start.reshape(nseq * taps, width)
    at_start = jnp.pad(at_start, ((0, 8), (0, 0)))
    at_start = at_start.at[nseq * taps, :nseq].set(starts[0].astype(F32))
    all_tokens, w_yx, w_gu, _, gate_rows, canon, at_start = start_exchange(
        tokens[0],
        w_y,
        w_x,
        w_gate,
        w_up,
        jnp.concatenate([gate_a, gate_i], 1),
        vectors,
        at_start,
    )
    w_yx = w_yx.reshape(d_model, 2 * wide_here)
    w_gu = gather_a(w_gu.reshape(-1, 2 * planes * hid))
    gate_rows = gate_rows.reshape(wide_here, -1)

    def join_halves(mine_all):
        away = swap_c(lax.dynamic_slice_in_dim(mine_all, (1 - c) * heads_here, heads_here, 0))
        own = lax.dynamic_slice_in_dim(mine_all, c * heads_here, heads_here, 0)
        first = jnp.where(c == 0, own, away)
        second = jnp.where(c == 0, away, own)
        return jnp.stack([first, second], 1).reshape((wide_here,) + mine_all.shape[2:])


    w_o = padded(join_halves(gather_a(w_out).reshape(planes, half, d_model)), 0)

    def block_diagonal(m):
        m = m.reshape(heads_here, head_w, head_w)
        eye = jnp.eye(heads_here, dtype=m.dtype)
        full = (m[:, :, None, :] * eye[:, None, :, None]).reshape(wide_here, wide_here)
        return padded(padded(full), 0)

    w_gates = jnp.concatenate(
        [
            block_diagonal(gate_rows[:, :head_w]),
            block_diagonal(gate_rows[:, head_w:]),
        ],
        1,
    )

    w_d = gather_a(w_down)
    f_here = planes * hid

    canon = canon.reshape(planes * nblocks, -1)
    nvec = (taps + 4) * half
    gain_one = canon[:, nvec : nvec + drows].reshape(-1)
    gain_two = canon[:, nvec + drows : nvec + 2 * drows].reshape(-1)
    mine = pick(canon[:, :nvec].reshape(2, heads_here, count, 2, taps + 4, half), c)
    mine = pick(mine, u, 1).transpose(2, 0, 1, 3).reshape(taps + 4, wide_here)
    decay_f = mine[taps + 3]
    vec = [mine[: taps + 3], jax.nn.softplus(decay_f)[None], jax.nn.sigmoid(decay_f)[None]]
    vec = padded(jnp.concatenate(vec))

    def my_channels(v):
        lead = v.shape[:-1]
        v = v.reshape(lead + (2, heads_here, count, head_w))
        v = pick(v, c, len(lead))
        return pick(v, u, len(lead) + 1).reshape(lead + (wide_here,))

    streams = 2 * nn
    at_start = at_start.reshape(streams, -1, width)
    offsets = at_start[:, nseq * taps, :nseq].astype(jnp.int32)
    at_start = my_channels(at_start[:, : nseq * taps].reshape(streams, nseq, taps, width))
    at_start = padded(at_start)
    state_0 = jnp.pad(at_start[:, :, 0], ((0, 0), (0, -nseq % 8), (0, 0)))
    conv_0 = at_start[:, :, 1:].reshape(streams, nseq * back, wp).astype(BF)
    conv_0 = jnp.pad(conv_0, ((0, 0), (0, -(nseq * back) % 16), (0, 0)))

    def per_block(v):
        v = v.reshape((2, 1, nn) + v.shape[1:])
        return jnp.broadcast_to(v, (2, 2, nn) + v.shape[3:]).reshape((nblocks,) + v.shape[3:])

    block_b = (jnp.arange(nblocks, dtype=jnp.int32) // nn) % 2
    first_row = (a * 2 + (b ^ block_b)) * rows
    position = first_row[:, None] + jnp.arange(rows, dtype=jnp.int32)[None]
    off_b = per_block(offsets)

    info = jnp.concatenate(
        [first_row[:, None], off_b, jnp.zeros((nblocks, -(nseq + 1) % 8), jnp.int32)], 1
    )

    grad_low = cotangent[0]
    grads = [grad_low] + [xor_u(grad_low, k) for k in range(1, count)]

    edge = ((nblocks, 8, wp), F32, True)
    normed, gate_in, linear, tail = by_block(
        norm_product_kernel,
        info,
        [(all_tokens, True), (w_yx, False), (gain_one[None], False)],
        [
            ((nblocks, rows, d_model), BF, True),
            ((nblocks, rows, wp), F32, True),
            ((nblocks, rows, wp), BF, True),
            edge,
        ],
        [],
        name="norm_product",
    )
    normed = normed.reshape(nblocks * rows, d_model)

    def two(v):
        return v.reshape((2, 2, nn) + v.shape[1:])

    rim = pass_along(6, "pass_rows", False, tail)[0]
    conv_0b, state_0b = per_block(conv_0), per_block(state_0)
    full = (nblocks, rows, wp)
    conv_low, retain, admit, carry_mul, carry_add, end_mul, end_add = by_block(
        functools.partial(forward_kernel, nseq, taps),
        info,
        [
            (linear, True), (rim, True), (conv_0b, True), (state_0b, True),
            (w_gates, False), (vec, False),
        ],
        [
            (full, BF, True), (full, F32, True), (full, F32, True),
            (full, F32, True), (full, F32, True), edge, edge,
        ],
        [(rows + 8, wp), (rows, wp), (rows, wp)],
        name="mixer_forward",
    )

    (end_mul, end_add), grads = lax.optimization_barrier(((end_mul, end_add), grads))
    state_in = pass_along(7, "pass_state", False, end_mul, end_add)[0]
    hidden = carry_mul * state_in + carry_add
    mixed_in = (hidden * jax.nn.gelu(gate_in)).astype(BF).reshape(-1, wp)
    resid, normed_two, grads = plane_reduce(
        2, "fwd", False, (mixed_in.reshape(2, count, rows, -1),), w_o, gain_two, tokens[0],
        tokens[0], grads,
    )
    normed_two = normed_two.reshape(nblocks * rows, d_model)
    grads = grads.reshape(nblocks * rows, d_model)

    hid_full = (nblocks, rows, f_here)
    inner, by_gate, by_up = by_block(
        ffn_forward_kernel,
        info,
        [(normed_two.reshape(nblocks, rows, d_model), True), (w_gu, False)],
        [(hid_full, BF, True)] * 3,
        [],
        name="ffn_forward",
    )
    inner = inner.reshape(nblocks * rows, f_here)
    cut = d_model // 2
    first_d = tdot(inner, grads[:, :cut]).astype(BF)
    second_d = tdot(inner, grads[:, cut:]).astype(BF)
    sent_d = scatter_a(first_d), scatter_a(second_d)
    d_pair = by_block(
        ffn_back_kernel,
        info,
        [
            (grads.reshape(nblocks, rows, d_model), True), (w_d, False), (by_gate, True),
            (by_up, True),
        ],
        [((nblocks, rows, 2 * f_here), BF, True)],
        [],
        (first_d, second_d),
        name="ffn_back",
    )[0]
    sums_gu = tdot(normed_two, d_pair.reshape(nblocks * rows, -1)).astype(BF)
    sent_gu = scatter_a(sums_gu)
    d_resid, d_resid_low, low = plane_reduce(
        3, "mid", True, (d_pair.reshape(2, count, rows, -1),), w_gu,
        gain_two, grad_low, resid, (inner.reshape(2, count, rows, f_here), w_d), (sent_d[0], sums_gu),
    )
    d_resid_low = d_resid_low.reshape(nblocks * rows, d_model)

    result = resid + low[0].astype(F32)
    for k in range(1, count):
        result = result + xor_u(low[k], k).astype(F32)
    result = result.astype(BF)

    d_gate_in, back_mul, back_add, end_mul, end_add, sums_o = by_block(
        functools.partial(back_scan_kernel, nseq, taps),
        info,
        [
            (d_resid_low.reshape(nblocks, rows, d_model), True), (w_o, False), (gate_in, True),
            (hidden, True), (retain, True), (vec, False), (mixed_in.reshape(full), True),
        ],
        [
            (full, BF, True), (full, F32, True), (full, F32, True), edge, edge,
            ((wp, d_model), BF, False),
        ],
        [(rows + 8, wp), (rows, wp), (rows, wp), (wp, d_model)],
        (sent_d[1],),
        name="mixer_back_scan",
    )
    grad_in = pass_along(8, "pass_state_back", True, end_mul, end_add)[0]
    d_conv_low, head, late, lasts = by_block(
        functools.partial(back_kernel, nseq, taps, planes * 2 * rows),
        info,
        [
            (back_mul, True), (back_add, True), (grad_in, True), (hidden, True),
            (state_in, True), (state_0b, True), (conv_low, True), (retain, True),
            (admit, True), (linear, True), (rim, True), (conv_0b, True), (w_gates, False), (vec, False),
            (sums_o, False),
        ],
        [
            (full, BF, True), edge, ((wide_here, d_model + 2 * head_w + taps + 4), BF, False),
            ((nblocks, nseq * taps, wp), BF, True),
        ],
        [(rows + 8, wp), (wp, 2 * wp), (taps + 4, wp)],
        (),
        name="mixer_back",
    )

    rim_back, late = pass_along(9, "pass_rows_back", True, head, halves=(late, half))
    d_both = by_block(
        functools.partial(back_conv_kernel, nseq, taps),
        info,
        [(d_conv_low, True), (rim_back, True), (d_gate_in, True), (vec, False)],
        [((nblocks, rows, 2 * wide_here), BF, True)],
        [(rows + 8, wp)],
        (result, sent_gu),
        name="mixer_back_conv",
    )[0]
    late = scatter_a(late.reshape(planes * half, -1))
    sums_yx = tdot(normed, d_both.reshape(nblocks * rows, 2 * wide_here)).astype(BF)
    input_grad, grad_wg, grad_wu, found, grad_gain_two = plane_reduce(
        4, "last", True, (d_both.reshape(2, count, rows, -1),), w_yx, gain_one, tokens[0], d_resid,
        (sent_gu,), (sums_yx,), hid, lasts, (w_gate, w_up, norm2_gain), head_w,
    )
    late, input_grad = lax.optimization_barrier((late, input_grad))
    late = late.astype(F32)
    grad_wo, grad_gates, vec_grads = jnp.split(late, [d_model, d_model + 2 * head_w], 1)
    grad_wa, grad_wi, vec_grads = grad_gates[:, :head_w], grad_gates[:, head_w:], vec_grads.T
    grad_wy, grad_wx, grad_gain_one = finish(scatter_a(sums_yx), w_y, w_x, norm1_gain, head_w)
    grad_gain_one, grad_gain_two = grad_gain_one[:, 0], grad_gain_two[:, 0]

    final_state = found[:nseq]
    final_conv = found[nseq:].astype(BF).reshape(nseq, back, width)

    return (
        result[None],
        input_grad[None],
        final_state[None],
        final_conv[None],
        grad_wy,
        grad_wx,
        grad_wa,
        grad_wi,
        grad_wo,
        grad_gain_one,
        vec_grads[:taps],
        vec_grads[taps],
        vec_grads[taps + 1],
        vec_grads[taps + 2],
        vec_grads[taps + 3],
        grad_wg,
        grad_wu,
        jnp.concatenate(sent_d, 1).astype(F32),
        grad_gain_two,
    )


WIDE = ("a", "b")
EVERY = ("a", "b", "n", "c")
HIGH = lax.Precision.HIGHEST


def passed_along(value, axis, by):
    size = lax.axis_size(axis)
    pairs = [(i, i + by) for i in range(size) if 0 <= i + by < size]
    return lax.ppermute(value, axis, pairs)


def entering(value, axis, combine, identity, reverse):
    size, place = (lax.axis_size(axis), lax.axis_index(axis))
    everything = jax.tree.map(lambda part: lax.all_gather(part, axis), value)
    start = jax.tree.map(
        lambda part, zero: jnp.broadcast_to(jnp.asarray(zero, part.dtype), part.shape),
        value,
        identity,
    )

    def hop(k, before):
        at = size - 1 - k if reverse else k
        reached = at > place if reverse else at < place
        new = combine(before, jax.tree.map(lambda part: part[at], everything))
        return jax.tree.map(lambda a, b: jnp.where(reached, a, b), new, before)

    return lax.fori_loop(0, size, hop, start)


def merged_2(value, axis, combine):
    everything = jax.tree.map(
        lambda part, kind: lax.all_gather(part.astype(kind), axis),
        value,
        jax.tree.map(lambda a: jnp.bfloat16 if a.dtype == jnp.float32 else a.dtype, value),
    )

    def take(k):
        return jax.tree.map(lambda part, own: part[k].astype(own.dtype), everything, value)

    return lax.fori_loop(
        1, lax.axis_size(axis), lambda k, so_far: combine(so_far, take(k)), take(0)
    )


def link(earlier, later):
    return (earlier[0] * later[0], later[0] * earlier[1] + later[1])


def norm_back(value, factor, gain, grad):
    weighted = grad * gain
    inner = jnp.mean(weighted * value, axis=-1, keepdims=True)
    return (
        factor * weighted - value * factor * factor * factor * inner,
        jnp.sum(grad * value * factor, axis=0),
    )


def later_one(first, second):
    pick = first[0] > second[0]
    return (
        jnp.where(pick, first[0], second[0]),
        jnp.where(pick[:, None], first[1], second[1]),
        jnp.where(pick[:, None, None], first[2], second[2]),
    )


def on_device_any(
    tokens,
    starts,
    init_state,
    init_conv,
    w_y,
    w_x,
    gate_a,
    gate_i,
    w_out,
    norm1_gain,
    conv_kernel,
    conv_bias,
    bias_a,
    bias_i,
    decay_param,
    w_gate,
    w_up,
    w_down,
    norm2_gain,
    cotangent,
):
    inputs = tokens[0].astype(jnp.float32)
    offsets = starts[0]
    nseqs = offsets.shape[0]
    rows_here = inputs.shape[0]
    width = w_y.shape[1]
    head_w = gate_a.shape[1]
    heads = width // head_w
    place = lax.axis_index(WIDE)
    mixer = (
        lax.all_gather(w_y, EVERY, axis=0, tiled=True),
        lax.all_gather(w_x, EVERY, axis=0, tiled=True),
        lax.all_gather(gate_a, EVERY, axis=0, tiled=True),
        lax.all_gather(gate_i, EVERY, axis=0, tiled=True),
        lax.all_gather(w_out, EVERY, axis=0, tiled=True),
        lax.all_gather(norm1_gain, EVERY, axis=0, tiled=True),
        lax.all_gather(conv_kernel, EVERY, axis=1, tiled=True),
        lax.all_gather(conv_bias, EVERY, axis=0, tiled=True),
        lax.all_gather(bias_a, EVERY, axis=0, tiled=True),
        lax.all_gather(bias_i, EVERY, axis=0, tiled=True),
        lax.all_gather(decay_param, EVERY, axis=0, tiled=True),
    )
    wy_full, wx_full, wa_full, wi_full, wo_full, gain_one, kernel, cbias, abias, ibias, decay = (
        mixer
    )
    gain_one = gain_one.astype(jnp.float32)
    kernel = kernel.astype(jnp.float32)
    taps = kernel.shape[0]
    back = taps - 1
    position = place * rows_here + jnp.arange(rows_here, dtype=jnp.int32)

    def segment_of(where_at):
        return jnp.sum((where_at[:, None] >= offsets[None, :]).astype(jnp.int32), axis=1) - 1

    segment = segment_of(position)
    member = segment[:, None] == jnp.arange(nseqs, dtype=jnp.int32)[None, :]
    begin = jnp.sum(jnp.where(member, offsets[None, :], 0), axis=1)
    opening = (position == begin)[:, None]
    scale_one = lax.rsqrt(jnp.mean(inputs * inputs, axis=-1, keepdims=True) + EPS)
    normed = (inputs * scale_one * gain_one).astype(jnp.bfloat16)
    gate_in = mdot(normed, wy_full)
    linear = mdot(normed, wx_full).astype(jnp.bfloat16)
    rim_rows = passed_along(linear[rows_here - back :], WIDE, 1)
    extended = jnp.concatenate([rim_rows, linear], 0)
    stored = mdot(member.astype(jnp.bfloat16), init_conv[0].reshape(nseqs, back * width)).reshape(
        rows_here, back, width
    )
    inputs_by_tap = [linear.astype(jnp.float32)]
    for shift_by in range(1, taps):
        earlier = extended[back - shift_by : back - shift_by + rows_here].astype(jnp.float32)
        offset = position - shift_by - begin
        from_start = jnp.zeros((rows_here, width), jnp.float32)
        for slot in range(back):
            from_start = from_start + jnp.where(
                (offset + back == slot)[:, None], stored[:, slot], 0.0
            )
        inputs_by_tap.append(jnp.where((offset >= 0)[:, None], earlier, from_start))
    conv_sum = cbias.astype(jnp.float32)
    for shift_by in range(taps):
        conv_sum = conv_sum + kernel[shift_by] * inputs_by_tap[shift_by]
    conv_low = conv_sum.astype(jnp.bfloat16)
    conv_val = conv_low.astype(jnp.float32)
    blocks = conv_low.reshape(rows_here, heads, head_w)
    wa_heads = wa_full.reshape(heads, head_w, head_w)
    wi_heads = wi_full.reshape(heads, head_w, head_w)
    rate = jnp.einsum("thi,hij->thj", blocks, wa_heads, preferred_element_type=jnp.float32).reshape(
        rows_here, width
    ) + abias.astype(jnp.float32)
    inflow = jnp.einsum(
        "thi,hij->thj", blocks, wi_heads, preferred_element_type=jnp.float32
    ).reshape(rows_here, width) + ibias.astype(jnp.float32)
    retain = jax.nn.sigmoid(rate)
    admit = jax.nn.sigmoid(inflow)
    decay_f = decay.astype(jnp.float32)
    soft_decay = jax.nn.softplus(decay_f)
    log_a = -8.0 * retain * soft_decay
    decay_now = jnp.exp(log_a)
    spread = -jnp.expm1(2.0 * log_a)
    mult = jnp.sqrt(jnp.maximum(spread, FLOOR))
    drive = mult * admit * conv_val
    state_rows = jnp.dot(member.astype(jnp.float32), init_state[0], precision=HIGH)
    a_used = jnp.where(opening, 0.0, decay_now)
    b_used = jnp.where(opening, decay_now * state_rows + drive, drive)
    carry_mul, carry_add = lax.associative_scan(link, (a_used, b_used), axis=0)
    identity = (jnp.ones((width,), jnp.float32), jnp.zeros((width,), jnp.float32))
    state_in = entering(
        (carry_mul[rows_here - 1], carry_add[rows_here - 1]), WIDE, link, identity, False
    )[1]
    hidden = carry_mul * state_in + carry_add
    gelu_y, gelu_y_back = jax.vjp(jax.nn.gelu, gate_in)
    mixed_in = (hidden * gelu_y).astype(jnp.bfloat16)
    resid = inputs + mdot(mixed_in, wo_full)
    wg_full, wu_full, wd_full, gain_two = (
        lax.all_gather(w_gate, EVERY, axis=0, tiled=True),
        lax.all_gather(w_up, EVERY, axis=0, tiled=True),
        lax.all_gather(w_down, EVERY, axis=0, tiled=True),
        lax.all_gather(norm2_gain, EVERY, axis=0, tiled=True),
    )
    gain_two = gain_two.astype(jnp.float32)
    scale_two = lax.rsqrt(jnp.mean(resid * resid, axis=-1, keepdims=True) + EPS)
    normed_two = (resid * scale_two * gain_two).astype(jnp.bfloat16)
    gate = mdot(normed_two, wg_full)
    upward = mdot(normed_two, wu_full)
    active, gate_back = jax.vjp(jax.nn.gelu, gate)
    inner = (active * upward).astype(jnp.bfloat16)
    result = (resid + mdot(inner, wd_full)).astype(jnp.bfloat16)
    local_rows = jnp.arange(rows_here, dtype=jnp.int32)
    last_row = jnp.max(jnp.where(member, local_rows[:, None], -1), axis=0)
    present = last_row >= 0
    safe_row = jnp.maximum(last_row, 0)
    marker = jnp.where(present, (place * rows_here + last_row).astype(jnp.float32), -1.0)
    state_last = jnp.where(present[:, None], hidden[safe_row], 0.0)
    conv_rows = extended[safe_row[:, None] + 1 + jnp.arange(back, dtype=jnp.int32)[None, :]].astype(
        jnp.float32
    )
    conv_last = jnp.where(present[:, None, None], conv_rows, 0.0)
    merged = merged_2((marker, state_last, conv_last), WIDE, later_one)
    wg_back, wu_back, wd_back = (
        lax.all_gather(w_gate, EVERY, axis=0, tiled=True),
        lax.all_gather(w_up, EVERY, axis=0, tiled=True),
        lax.all_gather(w_down, EVERY, axis=0, tiled=True),
    )
    grad_low = cotangent[0]
    grad_out = grad_low.astype(jnp.float32)
    d_inner = ndot(grad_low, wd_back)
    grad_wd = tdot(inner, grad_low)
    d_gate = gate_back(d_inner * upward)[0].astype(jnp.bfloat16)
    d_up = (d_inner * active).astype(jnp.bfloat16)
    grad_wg = tdot(normed_two, d_gate)
    grad_wu = tdot(normed_two, d_up)
    d_normed_two = ndot(d_gate, wg_back) + ndot(d_up, wu_back)
    d_resid_norm, grad_gain_two = norm_back(resid, scale_two, gain_two, d_normed_two)
    d_resid = grad_out + d_resid_norm
    wy_back, wx_back, wa_back, wi_back, wo_back = (
        lax.all_gather(w_y, EVERY, axis=0, tiled=True),
        lax.all_gather(w_x, EVERY, axis=0, tiled=True),
        lax.all_gather(gate_a, EVERY, axis=0, tiled=True),
        lax.all_gather(gate_i, EVERY, axis=0, tiled=True),
        lax.all_gather(w_out, EVERY, axis=0, tiled=True),
    )
    d_resid_low = d_resid.astype(jnp.bfloat16)
    d_mixed = ndot(d_resid_low, wo_back)
    grad_wo = tdot(mixed_in, d_resid_low)
    d_hidden = d_mixed * gelu_y
    d_gate_in = gelu_y_back(d_mixed * hidden)[0].astype(jnp.bfloat16)
    forward_mul = jnp.concatenate([a_used[1:], jnp.ones((1, width), jnp.float32)], 0)
    back_mul, back_add = lax.associative_scan(link, (forward_mul, d_hidden), reverse=True, axis=0)
    head_map = (a_used[0] * back_mul[0], a_used[0] * back_add[0])
    grad_in = entering(head_map, WIDE, link, identity, True)[1]
    total_grad = back_mul * grad_in + back_add
    previous = jnp.concatenate([state_in[None], hidden[:-1]], 0)
    previous = jnp.where(opening, state_rows, previous)
    d_decay = total_grad * previous
    d_mult = total_grad * admit * conv_val
    d_admit = total_grad * mult * conv_val
    d_conv = total_grad * mult * admit
    d_spread = jnp.where(spread > FLOOR, d_mult * 0.5 / mult, 0.0)
    d_log = d_decay * decay_now - 2.0 * decay_now * decay_now * d_spread
    d_retain = d_log * (-8.0 * soft_decay)
    grad_decay = jnp.sum(d_log * (-8.0 * retain), axis=0) * jax.nn.sigmoid(decay_f)
    d_rate = (d_retain * retain * (1.0 - retain)).astype(jnp.bfloat16)
    d_inflow = (d_admit * admit * (1.0 - admit)).astype(jnp.bfloat16)
    grad_abias = jnp.sum(d_rate.astype(jnp.float32), axis=0)
    grad_ibias = jnp.sum(d_inflow.astype(jnp.float32), axis=0)
    rate_heads = d_rate.reshape(rows_here, heads, head_w)
    inflow_heads = d_inflow.reshape(rows_here, heads, head_w)
    grad_wa = jnp.einsum(
        "thi,thj->hij", blocks, rate_heads, preferred_element_type=jnp.float32
    ).reshape(width, head_w)
    grad_wi = jnp.einsum(
        "thi,thj->hij", blocks, inflow_heads, preferred_element_type=jnp.float32
    ).reshape(width, head_w)
    d_conv = d_conv + jnp.einsum(
        "thj,hij->thi",
        rate_heads,
        wa_back.reshape(heads, head_w, head_w),
        preferred_element_type=jnp.float32,
    ).reshape(rows_here, width)
    d_conv = d_conv + jnp.einsum(
        "thj,hij->thi",
        inflow_heads,
        wi_back.reshape(heads, head_w, head_w),
        preferred_element_type=jnp.float32,
    ).reshape(rows_here, width)
    d_conv_low = d_conv.astype(jnp.bfloat16)
    d_conv_val = d_conv_low.astype(jnp.float32)
    rim_back = passed_along(d_conv_low[:back], WIDE, -1)
    ahead = jnp.concatenate([d_conv_low, rim_back], 0)
    d_linear = kernel[0] * d_conv_val
    kernel_grads = [jnp.sum(d_conv_val * inputs_by_tap[0], axis=0)]
    for shift_by in range(1, taps):
        later_rows = ahead[shift_by : shift_by + rows_here].astype(jnp.float32)
        same = (segment_of(position + shift_by) == segment)[:, None]
        d_linear = d_linear + kernel[shift_by] * jnp.where(same, later_rows, 0.0)
        kernel_grads.append(jnp.sum(d_conv_val * inputs_by_tap[shift_by], axis=0))
    grad_kernel = jnp.stack(kernel_grads, 0)
    grad_cbias = jnp.sum(d_conv_val, axis=0)
    d_linear_low = d_linear.astype(jnp.bfloat16)
    d_normed = ndot(d_gate_in, wy_back) + ndot(d_linear_low, wx_back)
    grad_wy = tdot(normed, d_gate_in)
    grad_wx = tdot(normed, d_linear_low)
    d_input_norm, grad_gain_one = norm_back(inputs, scale_one, gain_one, d_normed)
    input_grad = (d_resid + d_input_norm).astype(jnp.bfloat16)
    every_sum = (
        lax.psum_scatter(grad_wy, EVERY, scatter_dimension=0, tiled=True),
        lax.psum_scatter(grad_wx, EVERY, scatter_dimension=0, tiled=True),
        lax.psum_scatter(grad_wa, EVERY, scatter_dimension=0, tiled=True),
        lax.psum_scatter(grad_wi, EVERY, scatter_dimension=0, tiled=True),
        lax.psum_scatter(grad_wo, EVERY, scatter_dimension=0, tiled=True),
        lax.psum_scatter(grad_gain_one, EVERY, scatter_dimension=0, tiled=True),
        lax.psum_scatter(grad_kernel, EVERY, scatter_dimension=1, tiled=True),
        lax.psum_scatter(grad_cbias, EVERY, scatter_dimension=0, tiled=True),
        lax.psum_scatter(grad_abias, EVERY, scatter_dimension=0, tiled=True),
        lax.psum_scatter(grad_ibias, EVERY, scatter_dimension=0, tiled=True),
        lax.psum_scatter(grad_decay, EVERY, scatter_dimension=0, tiled=True),
        lax.psum_scatter(grad_wg, EVERY, scatter_dimension=0, tiled=True),
        lax.psum_scatter(grad_wu, EVERY, scatter_dimension=0, tiled=True),
        lax.psum_scatter(grad_wd, EVERY, scatter_dimension=0, tiled=True),
        lax.psum_scatter(grad_gain_two, EVERY, scatter_dimension=0, tiled=True),
    )
    mixer_sums = every_sum[:11]
    mlp_sums = every_sum[11:]
    return (
        result[None],
        input_grad[None],
        merged[1][None],
        merged[2].astype(jnp.bfloat16)[None],
        mixer_sums[0],
        mixer_sums[1],
        mixer_sums[2],
        mixer_sums[3],
        mixer_sums[4],
        mixer_sums[5],
        mixer_sums[6],
        mixer_sums[7],
        mixer_sums[8],
        mixer_sums[9],
        mixer_sums[10],
        mlp_sums[0],
        mlp_sums[1],
        mlp_sums[2],
        mlp_sums[3],
    )


def solution(mesh):
    wide, narrow = mesh.shape["wide"], mesh.shape["narrow"]
    def plan(*args):
        fits = args[6].shape[0] * 2 == args[6].shape[1] and narrow == 4
        return (on_device if fits else on_device_any)(*args)

    fine = Mesh(mesh.devices.reshape(wide // 2, 2, narrow // 2, 2), ("a", "b", "n", "c"))
    w, s = ("a", "b"), ("n", "c")
    everywhere = ("a", "b", "n", "c")
    acts, rows, vec = P(s, w, None), P(everywhere, None), P(everywhere)
    return jax.shard_map(
        plan,
        mesh=fine,
        in_specs=(
            acts,
            P(s, None),
            P(s, None, None),
            P(s, None, None, None),
            rows, rows, rows, rows, rows,
            vec,
            P(None, everywhere),
            vec, vec, vec, vec,
            rows, rows, rows,
            vec,
            acts,
        ),
        out_specs=(
            acts,
            acts,
            P(s, None, None),
            P(s, None, None, None),
            rows, rows, rows, rows, rows,
            vec,
            P(None, everywhere),
            vec, vec, vec, vec,
            rows, rows, rows,
            vec,
        ),
        check_vma=False,
    )
```

```python
import functools

import jax
import jax.numpy as jnp
from jax import lax
from jax.experimental import pallas as pl
from jax.experimental.pallas import tpu as pltpu
from jax.sharding import Mesh
from jax.sharding import PartitionSpec as P

EPS = 1e-06
FLOOR = 0.001
BF = jnp.bfloat16
F32 = jnp.float32


def tdot(left, right):
    return lax.dot_general(left, right, (((0,), (0,)), ((), ())), preferred_element_type=F32)


def ndot(left, right):
    return lax.dot_general(left, right, (((1,), (1,)), ((), ())), preferred_element_type=F32)


def mdot(left, right):
    return jnp.dot(left, right, preferred_element_type=F32)


def pick(stacked, index, axis=0):
    return lax.dynamic_index_in_dim(stacked, index, axis, keepdims=False)


def swap_c(value):
    return lax.ppermute(value, "c", [(0, 1), (1, 0)])


def xor_u(value, k):
    size = lax.axis_size("b") * lax.axis_size("n")
    return lax.ppermute(value, ("b", "n"), [(i, i ^ k) for i in range(size)])


def shift_a(value, by):
    size = lax.axis_size("a")
    return lax.ppermute(value, "a", [(i, i + by) for i in range(size) if 0 <= i + by < size])


def chips():
    return lax.axis_size("b") * lax.axis_size("n")


def chip():
    return lax.axis_index("b") * lax.axis_size("n") + lax.axis_index("n")


MESH = pl.DeviceIdType.MESH
VMEM_LIMIT = 60 * 1024 * 1024


def places():
    return tuple(lax.axis_index(name) for name in ("a", "b", "n", "c"))


def neighbours():
    a, b, n, c = places()
    return (a, 1 - b, n, c), (a, b, 1 - n, c), (a, b, n, 1 - c)


def greet(peers):
    barrier = pltpu.get_barrier_semaphore()
    for peer in peers:
        pl.semaphore_signal(barrier, inc=1, device_id=peer, device_id_type=MESH)
    pl.semaphore_wait(barrier, len(peers))


class Mover:
    def __init__(self, send, recv):
        self.send, self.recv, self.made = send, recv, {}
        self.names = []

    def copy(self, name, src, dst, peer):
        if name not in self.names:
            self.names.append(name)
        at = self.names.index(name)
        made = pltpu.make_async_remote_copy(
            src_ref=src,
            dst_ref=dst,
            send_sem=self.send.at[at],
            recv_sem=self.recv.at[at],
            device_id=peer,
            device_id_type=MESH,
        )
        self.made[name] = made
        return made

    def start(self, name, src, dst, peer):
        self.copy(name, src, dst, peer).start()

    def arrived(self, name):
        self.made[name].wait_recv()

    def sent(self):
        for made in self.made.values():
            made.wait_send()


def gather_plane_start(move, mine, everyone, h, half_rows):
    x, y, z = neighbours()
    at = pl.ds(h * half_rows, half_rows)
    move.start(f"gx{h}", mine.at[at], everyone.at[2, at], x)
    move.start(f"gy{h}", mine.at[at], everyone.at[1, at], y)
    move.start(f"gc{h}", mine.at[at], everyone.at[4, at], z)


def gather_plane_rest(move, everyone, half_rows, stage=None):
    x, y, z = neighbours()
    rows = [pl.ds(h * half_rows, half_rows) for h in range(2)]

    def on(name, k, h):
        move.start(name, everyone.at[k, rows[h]], everyone.at[4 + k, rows[h]], z)

    if stage in (None, 0):
        move.arrived("gx0")
        move.start("fy", everyone.at[2, rows[0]], everyone.at[3, rows[0]], y)
        on("cx0", 2, 0)
        move.arrived("gy1")
        move.start("fx", everyone.at[1, rows[1]], everyone.at[3, rows[1]], x)
        on("cy1", 1, 1)
    if stage in (None, 1):
        move.arrived("gx1")
        on("cx1", 2, 1)
        move.arrived("gy0")
        on("cy0", 1, 0)
    if stage in (None, 2):
        move.arrived("fy")
        on("cd0", 3, 0)
        move.arrived("fx")
        on("cd1", 3, 1)
        for name in ("gc0", "gc1", "cx0", "cx1", "cy0", "cy1", "cd0", "cd1"):
            move.arrived(name)


GATHER_COPIES = 14


def plane_peers_of():
    a, b, n, c = places()
    peers = {}
    for kc in range(2):
        for k in range(4):
            if (kc, k) != (0, 0):
                there = (a, 1 - b if k & 2 else b, 1 - n if k & 1 else n, 1 - c if kc else c)
                peers[kc, k] = there
    return peers


def peer_owner(kc, k):
    _, b, n, c = places()
    return ((b * 2 + n) ^ k) * 2 + (1 - c if kc else c)


def set_side_by_side(pieces, order, width):
    group = 1
    while group * width % 128 and group < len(order):
        group += 1
    for i in range(0, len(order), group):
        runs = [pieces[p, :, o : o + width].astype(F32) for p, o in order[i : i + group]]
        yield slice(i * width, (i + len(runs)) * width), jnp.concatenate(runs, 1)


def gain_sum(pairs, gain):
    total = sum(jnp.sum(w[...].astype(F32) * g[...], axis=-1, keepdims=True) for w, g in pairs)
    size = total.shape[0]
    row = lax.broadcasted_iota(jnp.int32, (size, size), 0)
    column = lax.broadcasted_iota(jnp.int32, (size, size), 1)
    return jnp.sum(jnp.where(row == column, total, 0.0), axis=0, keepdims=True) / gain[...]


def reduce_kernel(nt, post, nx, extra, waits, *refs):
    x_hbm, refs = refs[:nx], refs[nx:]
    w_hbm, gain_ref, first_ref, second_ref = refs[:4]
    extra_in, refs = refs[4 : 4 + extra], refs[4 + extra :]
    if post == "last":
        lasts_ref, refs = refs[0], refs[1:]
    refs = refs[waits:]
    out_ref, refs = refs[0], refs[1:]
    if post == "last":
        everyone = mine = None
        extra_buf, lasts_sum = refs[:2]
        lasts_buf, lasts_mine, lasts_far, lasts_sent = refs[2:6]
        refs = refs[6:]
    else:
        everyone, refs = refs[0], refs[1:]
        if extra:
            extra_out, refs = refs[0], refs[1:]
        mine, refs = refs[0], refs[1:]
        if post == "mid":
            (side_x, side_w, side_s, side_r), refs = refs[:4], refs[4:]
    x_v, w_v, away_s, away_r, acc, out_b, in_b, local, send, recv = refs
    rows, d_model = acc.shape[1:]
    half = rows // 2
    tile = min(512, d_model)
    px, py, pc = neighbours()
    move = Mover(send, recv)

    slots = iter(range(local.shape[0]))

    def keep(src, dst):
        made = pltpu.make_async_copy(src, dst, local.at[next(slots)])
        made.start()
        return made

    w_copy = keep(w_hbm, w_v)
    loads = {}
    each = x_v.shape[3] // nx
    for k in (3, 2, 1, 0):
        for kc in (1, 0):
            loads[kc, k] = [
                keep(x.at[kc, k], x_v.at[kc, k, :, pl.ds(i * each, each)])
                for i, x in enumerate(x_hbm)
            ]
    if post == "mid":
        side_loads = [keep(extra_in[0], side_x), keep(extra_in[1], side_w)]
    if post == "last":
        a, b, n, c = places()
        planes = lasts_far.shape[0] + 1
        columns = [(lax.rem(a + d, planes), b, n, c) for d in range(1, planes)]
        peers = plane_peers_of()
        greet([*peers.values(), *columns])
        for kc in range(2):
            for kn in range(2):
                lasts_sent[kc, kn] = (
                    lasts_ref[kc * 4 + kn].astype(F32) + lasts_ref[kc * 4 + 2 + kn].astype(F32)
                ).astype(BF)
        for (kc, k), peer in peers.items():
            move.start(f"l{kc}{k}", lasts_sent.at[kc, k % 2], lasts_buf.at[kc, k], peer)
    else:
        greet((px, py, pc))
    w_copy.wait()

    def product(kc, k, t):
        at = pl.ds(pl.multiple_of(t * tile, tile), tile)
        if nt:
            return at, ndot(x_v[kc, k], w_v[at, :])
        return at, mdot(x_v[kc, k], w_v[:, at])

    step = min(32, half)

    def by_rows(h, body):
        @pl.loop(0, half // step)
        def _(i):
            body(pl.ds(pl.multiple_of(i * step, step), step),
                 pl.ds(pl.multiple_of(h * half + i * step, step), step))

    def hand_on(name, slot, k, h, peer, extra=None):
        def body(inner, outer):
            value = acc[k, outer, :]
            if extra is not None:
                value = value + in_b[extra, inner, :].astype(F32)
            out_b[slot, inner, :] = value.astype(BF)

        by_rows(h, body)
        move.start(name, out_b.at[slot], in_b.at[slot], peer)

    for k in (3, 2, 1, 0):
        for load in loads[1, k]:
            load.wait()

        @pl.loop(0, d_model // tile)
        def _(t):
            at, value = product(1, k, t)
            away_s[k, :, at] = value.astype(BF)

        move.start(f"away{k}", away_s.at[k], away_r.at[k], pc)
        for load in loads[0, k]:
            load.wait()

        @pl.loop(0, d_model // tile)
        def _(t):
            at, value = product(0, k, t)
            acc[k, :, at] = value

        move.arrived(f"away{k}")
        for h in range(2):
            def add(inner, outer):
                acc[k, outer, :] += away_r[k, outer, :].astype(F32)

            by_rows(h, add)
        if k == 3:
            hand_on("d0", 0, 3, 0, px)
            hand_on("d1", 1, 3, 1, py)
        elif k == 2:
            hand_on("x0", 2, 2, 0, px)
        elif k == 1:
            hand_on("y1", 5, 1, 1, py)
    kept = []
    if extra and post == "fwd":
        for k in range(4):
            kept.append(keep(extra_in[k], extra_out.at[k]))
            move.start(f"e{k}", extra_in[k], extra_out.at[4 + k], pc)
    move.arrived("d0")
    hand_on("y0", 4, 1, 0, py, 0)
    move.arrived("d1")
    hand_on("x1", 3, 2, 1, px, 1)
    if post == "mid":
        for load in side_loads:
            load.wait()
        for k in range(4):

            @pl.loop(0, d_model // tile)
            def _(t):
                at = pl.ds(pl.multiple_of(t * tile, tile), tile)
                side_s[k, :, at] = mdot(side_x[1, k], side_w[:, at]).astype(BF)

            move.start(f"s{k}", side_s.at[k], side_r.at[k], pc)
        for k in range(4):
            move.arrived(f"s{k}")
            move.made.pop(f"s{k}").wait_send()

            @pl.loop(0, d_model // tile)
            def _(t):
                at = pl.ds(pl.multiple_of(t * tile, tile), tile)
                value = mdot(side_x[0, k], side_w[:, at]) + side_r[k, :, at].astype(F32)
                side_s[k, :, at] = value.astype(BF)

            kept.append(keep(side_s.at[k], extra_out.at[k]))
    if extra and post == "last":
        lasts_buf[0, 0] = lasts_sent[0, 0]
        for kc, k in peers:
            move.arrived(f"l{kc}{k}")
        u = b * 2 + n
        me = u * 2 + c
        for kc in range(2):
            for q in range(4):
                found = lasts_buf[kc, 0]
                for k in range(1, 4):
                    found = jnp.where((u ^ k) == q, lasts_buf[kc, k], found)
                lasts_mine[jnp.bitwise_xor(c, kc), q] = found
        for i, peer in enumerate(columns):
            move.start(f"z{i}", lasts_mine, lasts_far.at[i], peer)
        each_rows = extra_buf.shape[1]

        def part(owner):
            at = pl.multiple_of(owner * each_rows, each_rows)
            return extra_in[0].at[pl.ds(at, each_rows)]

        kept.append(keep(part(me), extra_buf.at[me]))
        for (kc, k), peer in peers.items():
            move.start(f"e{kc}{k}", part(peer_owner(kc, k)), extra_buf.at[me], peer)

    for h in range(2):
        move.arrived(f"x{h}")
        move.arrived(f"y{h}")

        def body(inner, outer):
            total = acc[0, outer, :]
            total = total + in_b[2 + h, inner, :].astype(F32)
            total = total + in_b[4 + h, inner, :].astype(F32)
            gain = gain_ref[...]
            if post == "fwd":
                value = first_ref[outer, :].astype(F32) + total
                out_ref[outer, :] = value
                factor = lax.rsqrt(jnp.mean(value * value, axis=-1, keepdims=True) + EPS)
                mine[outer, :] = (value * factor * gain).astype(BF)
                return
            value = second_ref[outer, :] if post == "mid" else first_ref[outer, :].astype(F32)
            base = first_ref[outer, :].astype(F32) if post == "mid" else second_ref[outer, :]
            factor = lax.rsqrt(jnp.mean(value * value, axis=-1, keepdims=True) + EPS)
            weighted = total * gain
            inner_mean = jnp.mean(weighted * value, axis=-1, keepdims=True)
            grad = base + factor * weighted - value * (factor * factor * factor * inner_mean)
            if post == "mid":
                out_ref[outer, :] = grad
                mine[outer, :] = grad.astype(BF)
            else:
                out_ref[outer, :] = grad.astype(BF)

        by_rows(h, body)
        if everyone is not None:
            gather_plane_start(move, mine, everyone, h, half)
    if everyone is not None:
        kept.append(keep(mine, everyone.at[0]))
        gather_plane_rest(move, everyone, half)
    if extra and post == "fwd":
        for k in range(4):
            move.arrived(f"e{k}")
    for made in kept:
        made.wait()
    if extra and post == "last":
        total = lasts_mine[...].astype(F32)
        for i in range(len(columns)):
            move.arrived(f"z{i}")
            total = total + lasts_far[i].astype(F32)
        lasts_sum[...] = total.reshape(lasts_sum.shape)
        for kc, k in peers:
            move.arrived(f"e{kc}{k}")
    move.sent()


def plane_reduce(ident, post, nt, xs, w, gain, first, second, extra=(), done=(), lasts=None):
    rows, d_model = first.shape
    vmem = pl.BlockSpec(memory_space=pltpu.VMEM)
    hbm = pl.BlockSpec(memory_space=pl.ANY)
    out_type = BF if post == "last" else F32
    out_shape = [jax.ShapeDtypeStruct((rows, d_model), out_type)]
    out_specs = [vmem]
    scratch = []
    copies = 10
    if post != "last":
        out_shape.append(jax.ShapeDtypeStruct((8, rows, d_model), BF))
        out_specs.append(hbm)
        copies += GATHER_COPIES
        if extra:
            blocks = 8 if post == "fwd" else 4
            out_shape.append(jax.ShapeDtypeStruct((blocks, rows, d_model), BF))
            out_specs.append(hbm)
            copies += 4
        scratch.append(pltpu.VMEM((rows, d_model), BF))
        if post == "mid":
            scratch += [pltpu.VMEM(v.shape, BF) for v in extra]
            scratch += [pltpu.VMEM((4, rows, d_model), BF)] * 2
    else:
        each = extra[0].shape[0] // 8, extra[0].shape[1]
        planes = lax.axis_size("a")
        copies += 7 + 7 + planes - 1
        block = (2, 4) + lasts.shape[1:]
        out_shape.append(jax.ShapeDtypeStruct((8,) + each, BF))
        out_shape.append(jax.ShapeDtypeStruct((8,) + block[2:], F32))
        out_specs += [hbm, vmem]
        scratch += [pltpu.VMEM(block, BF)] * 2 + [pltpu.VMEM((planes - 1,) + block, BF)]
        scratch.append(pltpu.VMEM((2, 2) + block[2:], BF))
    wide = sum(x.shape[3] for x in xs)
    scratch += [
        pltpu.VMEM((2, 4, rows, wide), BF),
        pltpu.VMEM(w.shape, BF),
        pltpu.VMEM((4, rows, d_model), BF),
        pltpu.VMEM((4, rows, d_model), BF),
        pltpu.VMEM((4, rows, d_model), F32),
        pltpu.VMEM((6, rows // 2, d_model), BF),
        pltpu.VMEM((6, rows // 2, d_model), BF),
        pltpu.SemaphoreType.DMA((8 + 8 * len(xs),)),
        pltpu.SemaphoreType.DMA((copies,)),
        pltpu.SemaphoreType.DMA((copies,)),
    ]
    last = [] if lasts is None else [lasts]
    return pl.pallas_call(
        functools.partial(reduce_kernel, nt, post, len(xs), len(extra), len(done)),
        in_specs=[hbm] * (len(xs) + 1)
        + [vmem] * 3
        + [vmem if post == "fwd" else hbm] * len(extra)
        + [vmem] * (lasts is not None)
        + [hbm] * len(done),
        out_specs=out_specs,
        out_shape=out_shape,
        scratch_shapes=scratch,
        compiler_params=pltpu.CompilerParams(
            collective_id=ident, has_side_effects=True, vmem_limit_bytes=VMEM_LIMIT
        ),
        cost_estimate=pl.CostEstimate(flops=0, bytes_accessed=8 << 20, transcendentals=0),
        name=f"plane_reduce_{post}",
    )(*xs, w, gain.reshape(1, -1), first, second, *extra, *last, *done)


def start_kernel(
    head_w, hid, tokens_ref, wy_ref, wx_ref, wg_ref, wu_ref, rows_ref, vec_ref, stream_ref,
    tok_out, yx_out, gu_out, rows_out, halves_out, vec_out, stream_out,
    yx_ref, gu_ref, local, send, recv,
):
    a, b, n, c = places()
    planes = yx_out.shape[0]
    p = (b * 2 + n) * 2 + c
    pc = neighbours()[2]
    plane_peers = plane_peers_of()
    up, down = (a + 1, b, n, c), (a - 1, b, n, c)
    each = planes // 2

    def pack(out, sources, columns, width):
        for owner in range(8):
            runs = [w[:, o : o + width] for w in sources for o in columns(owner)]
            out[owner] = jnp.concatenate(runs, 1)

    barrier = pltpu.get_barrier_semaphore()
    for peer in plane_peers.values():
        pl.semaphore_signal(barrier, inc=1, device_id=peer, device_id_type=MESH)

    @pl.when(a < planes - 1)
    def _():
        pl.semaphore_signal(barrier, inc=1, device_id=up, device_id_type=MESH)

    @pl.when(a > 0)
    def _():
        pl.semaphore_signal(barrier, inc=1, device_id=down, device_id_type=MESH)

    def head_columns(owner):
        return [((owner % 2 * each + j) * 4 + owner // 2) * head_w for j in range(each)]

    pack(yx_ref, (wy_ref, wx_ref), head_columns, head_w)
    others = len(plane_peers) + jnp.minimum(planes - 1 - a, 1) + jnp.minimum(a, 1)
    pl.semaphore_wait(barrier, others)

    move = Mover(send, recv)
    half = tokens_ref.shape[0] // 2

    def keep(i, src, dst):
        made = pltpu.make_async_copy(src, dst, local.at[i])
        made.start()
        return made

    def to_owners(name, pieces, out):
        for (kc, k), peer in plane_peers.items():
            move.start(f"{name}{kc}{k}", pieces.at[peer_owner(kc, k)], out.at[a, p], peer)

    chains = {}

    def chain_step(name, out, s):
        def up_copy(block):
            return move.copy(f"{name}u{s}", out.at[block], out.at[block], up)

        def down_copy(block):
            return move.copy(f"{name}d{s}", out.at[block], out.at[block], down)

        sends_up, sends_down = (a < planes - 1) & (a >= s), (a > 0) & (a + s < planes)

        @pl.when(sends_up)
        def _():
            up_copy(a - s).start()

        @pl.when(sends_down)
        def _():
            down_copy(a + s).start()

        chains[name, s] = (up_copy, down_copy, sends_up, sends_down)

    def chain_arrived(name, s):
        up_copy, down_copy, _, _ = chains[name, s]

        @pl.when(a - 1 >= s)
        def _():
            up_copy(a - 1 - s).wait_recv()

        @pl.when(a + 1 + s < planes)
        def _():
            down_copy(a + 1 + s).wait_recv()

    def chain_sent(name, s):
        up_copy, down_copy, sends_up, sends_down = chains[name, s]

        @pl.when(sends_up)
        def _():
            up_copy(a - s).wait_send()

        @pl.when(sends_down)
        def _():
            down_copy(a + s).wait_send()

    to_owners("yx", yx_ref, yx_out)
    for (kc, k), peer in plane_peers.items():
        move.start(f"vec{kc}{k}", vec_ref, vec_out.at[a, p], peer)
    own_yx = keep(1, yx_ref.at[p], yx_out.at[a, p])
    own_vec = keep(2, vec_ref, vec_out.at[a, p])
    own_rows = keep(0, rows_ref, rows_out.at[a])
    own_tok = keep(4, tokens_ref, tok_out.at[0])
    own_stream = keep(5, stream_ref, stream_out.at[0, 0])
    own_yx.wait()
    own_vec.wait()
    for kc, k in plane_peers:
        move.arrived(f"yx{kc}{k}")
        move.arrived(f"vec{kc}{k}")
    own_rows.wait()
    outs = (("yx", yx_out), ("vec", vec_out), ("rows", rows_out))
    for name, out in outs:
        chain_step(name, out, 0)
    for h in range(2):
        gather_plane_start(move, tokens_ref, tok_out, h, half)
    pack(gu_ref, (wg_ref, wu_ref), lambda o: [(z * 8 + o) * hid for z in range(planes)], hid)
    own_gu = keep(3, gu_ref.at[p], gu_out.at[p])
    gather_plane_rest(move, tok_out, half, 0)
    for kc in range(2):
        for kn in range(2):
            if (kc, kn) != (0, 0):
                move.start(f"st{kc}{kn}", stream_ref, stream_out.at[kc, kn], plane_peers[kc, kn])
    for name, out in outs:
        chain_arrived(name, 0)
        chain_step(name, out, 1)
    gather_plane_rest(move, tok_out, half, 1)
    for (kc, k), peer in plane_peers.items():
        move.start(f"gu{kc}{k}", gu_ref.at[peer_owner(kc, k)], gu_out.at[p], peer)
    for s in range(1, planes - 1):
        for name, out in outs:
            chain_arrived(name, s)
            if s + 1 < planes - 1:
                chain_step(name, out, s + 1)
    gather_plane_rest(move, tok_out, half, 2)
    swap = pltpu.make_async_remote_copy(
        src_ref=rows_out.at[pl.ds((1 - c) * each, each)],
        dst_ref=halves_out.at[:, c],
        send_sem=send.at[send.shape[0] - 1],
        recv_sem=recv.at[recv.shape[0] - 1],
        device_id=pc,
        device_id_type=MESH,
    )
    swap.start()
    own_halves = keep(6, rows_out.at[pl.ds(c * each, each)], halves_out.at[:, c])
    for kc, k in plane_peers:
        move.arrived(f"gu{kc}{k}")
    for kc in range(2):
        for kn in range(2):
            if (kc, kn) != (0, 0):
                move.arrived(f"st{kc}{kn}")
    for made in (own_gu, own_tok, own_stream, own_halves):
        made.wait()
    swap.wait()
    for name, s in chains:
        chain_sent(name, s)
    for name in [n for n in move.names if not any(n == f"{w}{d}{s}" for w, s in chains for d in "ud")]:
        move.made[name].wait_send()


def start_exchange(tokens, w_y, w_x, w_gate, w_up, gate_rows, vec, stream):
    planes = lax.axis_size("a")
    head_w, hid = gate_rows.shape[1] // 2, w_gate.shape[1] // (planes * 8)
    vmem = pl.BlockSpec(memory_space=pltpu.VMEM)
    hbm = pl.BlockSpec(memory_space=pl.ANY)
    yx = (8, w_y.shape[0], 2 * w_y.shape[1] // 8)
    gu = (8, w_gate.shape[0], 2 * w_gate.shape[1] // 8)
    shapes = [
        ((8,) + tokens.shape, BF),
        ((planes,) + yx, BF),
        (gu, BF),
        ((planes,) + gate_rows.shape, BF),
        ((planes // 2, 2) + gate_rows.shape, BF),
        ((planes, 8) + vec.shape, F32),
        ((2, 2) + stream.shape, F32),
    ]
    copies = 7 * 3 + 3 + GATHER_COPIES + 6 * (planes - 1) + 1
    return pl.pallas_call(
        functools.partial(start_kernel, head_w, hid),
        in_specs=[vmem] * 8,
        out_specs=[hbm] * 7,
        out_shape=[jax.ShapeDtypeStruct(*shape) for shape in shapes],
        scratch_shapes=[
            pltpu.VMEM(yx, BF),
            pltpu.VMEM(gu, BF),
            pltpu.SemaphoreType.DMA((7,)),
            pltpu.SemaphoreType.DMA((copies,)),
            pltpu.SemaphoreType.DMA((copies,)),
        ],
        compiler_params=pltpu.CompilerParams(
            collective_id=1, has_side_effects=True, vmem_limit_bytes=VMEM_LIMIT
        ),
        cost_estimate=pl.CostEstimate(flops=0, bytes_accessed=8 << 20, transcendentals=0),
        name="start_exchange",
    )(tokens, w_y, w_x, w_gate, w_up, gate_rows, vec, stream)


def finish_kernel(sums_ref, buf, local, send, recv):
    _, b, n, c = places()
    me = (b * 2 + n) * 2 + c
    peers = plane_peers_of()
    greet(list(peers.values()))
    move = Mover(send, recv)
    each_rows = buf.shape[1]

    def part(owner):
        return sums_ref.at[pl.ds(pl.multiple_of(owner * each_rows, each_rows), each_rows)]

    for (kc, k), peer in peers.items():
        move.start(f"e{kc}{k}", part(peer_owner(kc, k)), buf.at[me], peer)
    own = pltpu.make_async_copy(part(me), buf.at[me], local.at[0])
    own.start()
    own.wait()
    for kc, k in peers:
        move.arrived(f"e{kc}{k}")
    move.sent()


def finish(sums, done):
    vmem = pl.BlockSpec(memory_space=pltpu.VMEM)

    def body(sums_ref, *refs):
        finish_kernel(sums_ref, *refs[len(done) :])

    return pl.pallas_call(
        body,
        in_specs=[vmem] + [pl.BlockSpec(memory_space=pl.ANY)] * len(done),
        out_specs=vmem,
        out_shape=jax.ShapeDtypeStruct((8, sums.shape[0] // 8, sums.shape[1]), BF),
        scratch_shapes=[
            pltpu.SemaphoreType.DMA((1,)),
            pltpu.SemaphoreType.DMA((7,)),
            pltpu.SemaphoreType.DMA((7,)),
        ],
        compiler_params=pltpu.CompilerParams(
            collective_id=5, has_side_effects=True, vmem_limit_bytes=VMEM_LIMIT
        ),
        cost_estimate=pl.CostEstimate(flops=0, bytes_accessed=1 << 20, transcendentals=0),
        name="finish",
    )(sums, *done)


def in_place(body, ins, outs, name):
    vmem = pl.BlockSpec(memory_space=pltpu.VMEM)
    return pl.pallas_call(
        body,
        in_specs=[vmem] * len(ins),
        out_specs=[vmem] * len(outs),
        out_shape=[jax.ShapeDtypeStruct(*out) for out in outs],
        compiler_params=pltpu.CompilerParams(vmem_limit_bytes=VMEM_LIMIT),
        cost_estimate=pl.CostEstimate(flops=0, bytes_accessed=1 << 20, transcendentals=0),
        name=name,
    )(*ins)


def order_hidden_kernel(
    hid, head_w, buf, wg_ref, wu_ref, gain_ref, late_ref, lasts_ref,
    g_ref, u_ref, gain_out, out_ref, a_ref, i_ref, state_ref, conv_ref, *vec_refs,
):
    wide = buf.shape[2] // 2
    for i, out in enumerate((g_ref, u_ref)):
        order = [(p, i * wide + z * hid) for z in range(wide // hid) for p in range(8)]
        for at, value in set_side_by_side(buf, order, hid):
            out[:, at] = value
    gain_out[...] = gain_sum(((wg_ref, g_ref), (wu_ref, u_ref)), gain_ref)
    heads = wide // hid // 2
    order = [(i * 4 + q, j * head_w) for i in range(2) for j in range(heads) for q in range(4)]
    for at, value in set_side_by_side(lasts_ref, order, head_w):
        nseq = state_ref.shape[0]
        state_ref[:, at] = value[:nseq]
        conv_ref[:, at] = value[nseq:].astype(BF)
    wide_out, half = out_ref.shape[1], late_ref.shape[0]
    out_ref[...] = late_ref[:, :wide_out].astype(F32)
    a_ref[...] = late_ref[:, wide_out : wide_out + head_w].astype(F32)
    i_ref[...] = late_ref[:, wide_out + head_w : wide_out + 2 * head_w].astype(F32)
    row = lax.broadcasted_iota(jnp.int32, (half, half), 0)
    column = lax.broadcasted_iota(jnp.int32, (half, half), 1)
    eye = jnp.where(row == column, 1.0, 0.0).astype(BF)
    turned = tdot(late_ref[:, wide_out + 2 * head_w :], eye)
    taps = vec_refs[0].shape[0]
    vec_refs[0][...] = turned[:taps]
    for i, vec_ref in enumerate(vec_refs[1:]):
        vec_ref[...] = turned[taps + i : taps + i + 1]


def order_heads_kernel(head_w, buf, wy_ref, wx_ref, gain_ref, y_ref, x_ref, gain_out):
    wide = buf.shape[2] // 2
    each = wide // head_w
    order = [(q * 2 + i, j * head_w) for i in range(2) for j in range(each) for q in range(4)]
    for first, out in ((0, y_ref), (wide, x_ref)):
        for at, value in set_side_by_side(buf, [(p, o + first) for p, o in order], head_w):
            out[:, at] = value
    gain_out[...] = gain_sum(((wy_ref, y_ref), (wx_ref, x_ref)), gain_ref)


def column_peers(planes):
    a, b, n, c = places()
    return [(lax.rem(a + d, planes), b, n, c) for d in range(1, planes)]


def earlier_blocks(ref, want, row=0, count=1):
    _, b, _, _ = places()
    return [
        jnp.where(
            b == want,
            ref[kc * 4 + kn, row : row + count, :],
            ref[kc * 4 + 2 + kn, row : row + count, :],
        )
        for kc in range(2)
        for kn in range(2)
    ]


def split_refs(refs):
    if len(refs) == 5:
        return None, refs[:1], refs[1:], None
    return refs[0], refs[1:3], refs[3:7], refs[7:]


def swap_halves(rows_ref, out_ref, local, send, recv):
    _, _, _, c = places()
    planes, half = out_ref.shape[:2]
    each = planes // 2
    made = []
    for j in range(each):
        away = pl.multiple_of((2 * j + 1 - c) * half, half)
        own = pl.multiple_of((2 * j + c) * half, half)
        made.append(
            pltpu.make_async_remote_copy(
                src_ref=rows_ref.at[pl.ds(away, half)],
                dst_ref=out_ref.at[c * each + j],
                send_sem=send.at[j],
                recv_sem=recv.at[j],
                device_id=neighbours()[2],
                device_id_type=MESH,
            )
        )
        made.append(
            pltpu.make_async_copy(
                rows_ref.at[pl.ds(own, half)], out_ref.at[c * each + j], local.at[j]
            )
        )
    for copy in made:
        copy.start()
    return made


def pass_state_kernel(reverse, mul_ref, add_ref, *refs):
    rows_ref, (out_ref, *halves), (whole, came, send, recv), swaps = split_refs(refs)
    a, b, n, c = places()
    planes = came.shape[0] + 1
    row = 0 if reverse else 7
    near_at, far_at = (1, 0) if reverse else (0, 1)
    came[...] = jnp.zeros_like(came)
    near_mul, near_add = earlier_blocks(mul_ref, near_at, row), earlier_blocks(add_ref, near_at, row)
    far_mul, far_add = earlier_blocks(mul_ref, far_at, row), earlier_blocks(add_ref, far_at, row)
    for i in range(4):
        whole[0, i : i + 1, :] = near_mul[i] * far_mul[i]
        whole[1, i : i + 1, :] = far_mul[i] * near_add[i] + far_add[i]
    greet(column_peers(planes) + ([neighbours()[2]] if swaps else []))
    swapped = swap_halves(rows_ref, halves[0], *swaps) if swaps else []

    def copy(d):
        return pltpu.make_async_remote_copy(
            src_ref=whole,
            dst_ref=came.at[d - 1],
            send_sem=send.at[d - 1],
            recv_sem=recv.at[d - 1],
            device_id=(a - d if reverse else a + d, b, n, c),
            device_id_type=MESH,
        )

    def sends(d):
        return a >= d if reverse else a + d < planes

    def receives(d):
        return a + d < planes if reverse else a >= d

    for d in range(1, planes):
        @pl.when(sends(d))
        def _():
            copy(d).start()

    for d in range(1, planes):
        @pl.when(receives(d))
        def _():
            copy(d).wait_recv()

    for i in range(4):
        at = slice(i, i + 1)
        value = came[planes - 2, 1, at, :]
        for d in range(planes - 2, 0, -1):
            value = came[d - 1, 0, at, :] * value + came[d - 1, 1, at, :]
        to_far = near_mul[i] * value + near_add[i]
        for kb in range(2):
            is_far = (b if kb == 0 else 1 - b) == far_at
            at = (i // 2) * 4 + kb * 2 + i % 2
            out_ref[at] = jnp.where(is_far, to_far, value)

    for d in range(1, planes):
        @pl.when(sends(d))
        def _():
            copy(d).wait_send()

    for made in swapped:
        made.wait()


def pass_rows_kernel(reverse, edge_ref, *refs):
    rows_ref, (out_ref, *halves), (leaving, came, send, recv), swaps = split_refs(refs)
    a, b, n, c = places()
    planes = lax.axis_size("a")
    near_at, far_at = (1, 0) if reverse else (0, 1)
    came[...] = jnp.zeros_like(came)
    out_ref[...] = jnp.zeros_like(out_ref)
    first = 0 if reverse else 4
    for i, value in enumerate(earlier_blocks(edge_ref, far_at, first, 4)):
        leaving[i * 4 : i * 4 + 4, :] = value
    greet(column_peers(planes) + ([neighbours()[2]] if swaps else []))
    swapped = swap_halves(rows_ref, halves[0], *swaps) if swaps else []
    copy = pltpu.make_async_remote_copy(
        src_ref=leaving,
        dst_ref=came,
        send_sem=send.at[0],
        recv_sem=recv.at[0],
        device_id=(a - 1 if reverse else a + 1, b, n, c),
        device_id_type=MESH,
    )
    sends = a >= 1 if reverse else a + 1 < planes
    receives = a + 1 < planes if reverse else a >= 1

    @pl.when(sends)
    def _():
        copy.start()

    @pl.when(receives)
    def _():
        copy.wait_recv()

    for i in range(4):
        for kb in range(2):
            is_far = (b if kb == 0 else 1 - b) == far_at
            at = (i // 2) * 4 + kb * 2 + i % 2
            other = (i // 2) * 4 + (1 - kb) * 2 + i % 2
            out_ref[at, first : first + 4, :] = jnp.where(
                is_far, edge_ref[other, first : first + 4, :], came[i * 4 : i * 4 + 4, :]
            )

    @pl.when(sends)
    def _():
        copy.wait_send()

    for made in swapped:
        made.wait()


def pass_along(ident, name, reverse, *edges, halves=None):
    shape = edges[0].shape
    planes = lax.axis_size("a")
    vmem = pl.BlockSpec(memory_space=pltpu.VMEM)
    if len(edges) == 2:
        body, out = pass_state_kernel, (shape[0], 1, shape[2])
        buffers = [(2, 4) + shape[2:], (planes - 1, 2, 4) + shape[2:]]
    else:
        body, out = pass_rows_kernel, shape
        buffers = [(16,) + shape[2:]] * 2
    given, out_shape = list(edges), [jax.ShapeDtypeStruct(out, F32)]
    scratch = [pltpu.VMEM(shape, F32) for shape in buffers]
    scratch += [pltpu.SemaphoreType.DMA((planes - 1,))] * 2
    if halves is not None:
        given.append(halves[0])
        to = (planes, halves[1], halves[0].shape[1])
        out_shape.append(jax.ShapeDtypeStruct(to, BF))
        scratch += [pltpu.SemaphoreType.DMA((planes // 2,))] * 3
    return pl.pallas_call(
        functools.partial(body, reverse),
        in_specs=[vmem] * len(given),
        out_specs=[vmem] * len(out_shape),
        out_shape=out_shape,
        scratch_shapes=scratch,
        compiler_params=pltpu.CompilerParams(
            collective_id=ident, has_side_effects=True, vmem_limit_bytes=VMEM_LIMIT
        ),
        cost_estimate=pl.CostEstimate(flops=0, bytes_accessed=1 << 20, transcendentals=0),
        name=name,
    )(*given)


def norm_product_kernel(info, tok_ref, w_ref, gain_ref, n_ref, gate_ref, lin_ref, tail_ref):
    rows, d_model = tok_ref.shape[1:]
    step = min(64, rows)

    @pl.loop(0, rows // step)
    def _(i):
        at = pl.ds(pl.multiple_of(i * step, step), step)
        value = tok_ref[0, at, :].astype(F32)
        factor = lax.rsqrt(jnp.mean(value * value, axis=-1, keepdims=True) + EPS)
        n_ref[0, at, :] = (value * factor * gain_ref[...]).astype(BF)

    wide = gate_ref.shape[2]
    both = mdot(n_ref[0], w_ref[...])
    used = both.shape[1] // 2
    pad = [jnp.zeros((rows, wide - used), F32)] if wide > used else []
    gate_ref[0] = jnp.concatenate([both[:, :used]] + pad, 1)
    low = jnp.concatenate([both[:, used:]] + pad, 1).astype(BF)
    lin_ref[0] = low
    tail_ref[0] = low.astype(F32)[rows - 8 :, :]


def row_places(info, rows, nseq):
    i = pl.program_id(0)
    pos = info[i, 0] + lax.broadcasted_iota(jnp.int32, (rows, 1), 0)
    begin = jnp.zeros((rows, 1), jnp.int32) + info[i, 1]
    seg = jnp.zeros((rows, 1), jnp.int32)
    for s in range(1, nseq):
        begin = jnp.where(pos >= info[i, 1 + s], info[i, 1 + s], begin)
        seg = jnp.where(pos >= info[i, 1 + s], s, seg)
    return pos, begin, seg


def inputs_by_tap(ext, lin_ref, rim_ref, conv0_ref, begin_at, seg, taps):
    rows = lin_ref.shape[1]
    back = taps - 1
    ext[0:8, :] = rim_ref[0]
    ext[8 : 8 + rows, :] = lin_ref[0].astype(F32)
    slots = conv0_ref.shape[1]
    column = lax.broadcasted_iota(jnp.int32, (rows, slots), 1)
    found = [ext[8 : 8 + rows, :]]
    for k in range(1, taps):
        hot = (column == seg * back + begin_at - k + back) & (begin_at < k)
        stored = mdot(jnp.where(hot, 1.0, 0.0).astype(BF), conv0_ref[0])
        found.append(jnp.where(begin_at >= k, ext[8 - k : 8 - k + rows, :], stored))
    return found


def run_scan(a_s, b_s, p_ref, s_ref, rows, reverse):
    width = b_s.shape[1]
    groups = rows // 8
    row = lax.broadcasted_iota(jnp.int32, (8, width), 0)
    if reverse:
        row = 7 - row

    def step(i, carry):
        cp, cs = carry
        g = groups - 1 - i if reverse else i
        at = pl.ds(pl.multiple_of(g * 8, 8), 8)
        a, b = a_s[at, :], b_s[at, :]
        for d in (1, 2, 4):
            by = 8 - d if reverse else d
            inside = row >= d
            a_far = jnp.where(inside, pltpu.roll(a, by, 0), 1.0)
            b_far = jnp.where(inside, pltpu.roll(b, by, 0), 0.0)
            b = a * b_far + b
            a = a * a_far
        b = a * cs + b
        a = a * cp
        p_ref[0, at, :] = a
        s_ref[0, at, :] = b
        last = 0 if reverse else 7
        return a[last : last + 1], b[last : last + 1]

    start = (jnp.ones((1, width), F32), jnp.zeros((1, width), F32))
    lax.fori_loop(0, groups, step, start, unroll=4)


V_CBIAS, V_ABIAS, V_IBIAS, V_SOFT = 0, 1, 2, 3


def forward_kernel(
    nseq, taps, info, lin_ref, rim_ref, conv0_ref, state0_ref, wg_ref, vec_ref,
    conv_ref, retain_ref, admit_ref, p_ref, s_ref, pe_ref, se_ref, ext, a_s, b_s,
):
    i = pl.program_id(0)
    rows, wide = lin_ref.shape[1:]
    pos, begin, seg = row_places(info, rows, nseq)
    at = pos - begin

    def vec(k):
        return vec_ref[k : k + 1, :]

    by_tap = inputs_by_tap(ext, lin_ref, rim_ref, conv0_ref, at, seg, taps)
    total = vec(taps + V_CBIAS)
    for k in range(taps):
        total = total + vec(k) * by_tap[k]
    low = total.astype(BF)
    conv_ref[0] = low
    conv = low.astype(F32)
    both = mdot(low, wg_ref[...])
    retain = jax.nn.sigmoid(both[:, :wide] + vec(taps + V_ABIAS))
    admit = jax.nn.sigmoid(both[:, wide:] + vec(taps + V_IBIAS))
    retain_ref[0] = retain
    admit_ref[0] = admit
    a = jnp.exp(-8.0 * retain * vec(taps + V_SOFT))
    mult = jnp.sqrt(jnp.maximum((1.0 - a) * (1.0 + a), FLOOR))
    drive = mult * admit * conv
    for s in range(nseq):
        drive = drive + jnp.where(pos == info[i, 1 + s], a * state0_ref[0, s : s + 1, :], 0.0)
    a_s[...] = jnp.where(at == 0, 0.0, a)
    b_s[...] = drive
    run_scan(a_s, b_s, p_ref, s_ref, rows, False)
    pe_ref[0] = p_ref[0, rows - 8 : rows, :]
    se_ref[0] = s_ref[0, rows - 8 : rows, :]


def gelu_pair(x):
    root = 0.7978845608028654
    inner = root * (x + 0.044715 * (x * x * x))
    th = jnp.tanh(inner)
    cdf = 0.5 * (1.0 + th)
    slope = cdf + 0.5 * x * (1.0 - th * th) * (root * (1.0 + 3.0 * 0.044715 * (x * x)))
    return x * cdf, slope


def ffn_forward_kernel(info, n_ref, w_ref, inner_ref, by_gate_ref, by_up_ref):
    pair = mdot(n_ref[0], w_ref[...])
    hidden = inner_ref.shape[2]
    upward = pair[:, hidden:]
    active, slope = gelu_pair(pair[:, :hidden])
    inner_ref[0] = (active * upward).astype(BF)
    by_gate_ref[0] = (slope * upward).astype(BF)
    by_up_ref[0] = active.astype(BF)


def ffn_back_kernel(info, g_ref, w_ref, by_gate_ref, by_up_ref, *refs):
    out_ref = refs[-1]
    hidden = w_ref.shape[0]
    d_inner = ndot(g_ref[0], w_ref[...])
    out_ref[0, :, :hidden] = (d_inner * by_gate_ref[0].astype(F32)).astype(BF)
    out_ref[0, :, hidden:] = (d_inner * by_up_ref[0].astype(F32)).astype(BF)


def back_scan_kernel(
    nseq, taps, info, dres_ref, wo_ref, gate_ref, hidden_ref, retain_ref, vec_ref, mixed_ref, *refs
):
    dgate_ref, p_ref, s_ref, pe_ref, se_ref, wgrad_ref, ext, a_s, b_s, wgrad = refs[-10:]
    rows = gate_ref.shape[1]
    i = pl.program_id(0)

    @pl.when(i == 0)
    def _():
        wgrad[...] = jnp.zeros_like(wgrad)

    wgrad[...] += tdot(mixed_ref[0], dres_ref[0])

    @pl.when(i == pl.num_programs(0) - 1)
    def _():
        wgrad_ref[...] = wgrad[...].astype(BF)

    pos, begin, _ = row_places(info, rows, nseq)
    d_mixed = ndot(dres_ref[0], wo_ref[...])
    gelu, slope = gelu_pair(gate_ref[0])
    dgate_ref[0] = (d_mixed * hidden_ref[0] * slope).astype(BF)
    b_s[...] = d_mixed * gelu
    soft = vec_ref[taps + V_SOFT : taps + V_SOFT + 1, :]
    a = jnp.where(pos == begin, 0.0, jnp.exp(-8.0 * retain_ref[0] * soft))
    ext[0:rows, :] = a
    ext[rows : rows + 8, :] = jnp.ones((8, a.shape[1]), F32)
    a_s[...] = ext[1 : rows + 1, :]
    run_scan(a_s, b_s, p_ref, s_ref, rows, True)
    pe_ref[0] = ext[0:8, :] * p_ref[0, 0:8, :]
    se_ref[0] = ext[0:8, :] * s_ref[0, 0:8, :]


def back_kernel(
    nseq, taps, length, info, p_ref, s_ref, grad_in_ref, hidden_ref, state_in_ref, state0_ref, conv_ref,
    retain_ref, admit_ref, lin_ref, rim_ref, conv0_ref, wg_ref, vec_ref, sums_o_ref, *refs
):
    dconv_ref, head_ref, late_ref, lasts_ref, ext, wgrad_ref, vgrad_ref = refs[-7:]
    i = pl.program_id(0)
    rows, wide = lin_ref.shape[1:]
    pos, begin, seg = row_places(info, rows, nseq)
    at = pos - begin
    conv_low = conv_ref[0]
    conv = conv_low.astype(F32)
    retain, admit = retain_ref[0], admit_ref[0]
    soft = vec_ref[taps + V_SOFT : taps + V_SOFT + 1, :]
    e = p_ref[0] * grad_in_ref[0, 0:1, :] + s_ref[0]
    ext[0:8, :] = jnp.broadcast_to(state_in_ref[0], (8, wide))
    ext[8 : 8 + rows, :] = hidden_ref[0]
    previous = ext[7 : 7 + rows, :]
    for s in range(nseq):
        previous = jnp.where(pos == info[i, 1 + s], state0_ref[0, s : s + 1, :], previous)
    a = jnp.exp(-8.0 * retain * soft)
    spread = (1.0 - a) * (1.0 + a)
    mult = jnp.sqrt(jnp.maximum(spread, FLOOR))
    d_mult = e * admit * conv
    d_spread = jnp.where(spread > FLOOR, d_mult * 0.5 / mult, 0.0)
    d_log = e * previous * a - 2.0 * a * a * d_spread
    d_rate = (d_log * (-8.0 * soft) * retain * (1.0 - retain)).astype(BF)
    d_inflow = (e * mult * conv * admit * (1.0 - admit)).astype(BF)
    d_gates = jnp.concatenate([d_rate, d_inflow], 1)
    d_conv = e * mult * admit + ndot(d_gates, wg_ref[...])
    low = d_conv.astype(BF)
    dconv_ref[0] = low
    low = low.astype(F32)
    head_ref[0] = low[0:8, :]

    @pl.when(i == 0)
    def _():
        wgrad_ref[...] = jnp.zeros_like(wgrad_ref)
        vgrad_ref[...] = jnp.zeros_like(vgrad_ref)

    wgrad_ref[...] += tdot(conv_low, d_gates)
    sums = [low * v for v in inputs_by_tap(ext, lin_ref, rim_ref, conv0_ref, at, seg, taps)]
    sums += [low, d_rate.astype(F32), d_inflow.astype(F32), d_log * (-8.0 * retain)]
    for k, value in enumerate(sums):
        vgrad_ref[k : k + 1, :] += jnp.sum(value, axis=0, keepdims=True)

    slots = lasts_ref.shape[1]
    column = lax.broadcasted_iota(jnp.int32, (1, slots), 1)
    wanted = jnp.full((1, slots), -1, jnp.int32)
    for q in range(nseq):
        end = (info[i, 2 + q] if q + 1 < nseq else length) - 1
        wanted = jnp.where(column == q, end, wanted)
        for j in range(taps - 1):
            wanted = jnp.where(column == nseq + q * (taps - 1) + j, end - (taps - 2) + j, wanted)
    hot = jnp.where(pos == wanted, 1.0, 0.0).astype(BF)
    states, convs = tdot(hot, hidden_ref[0].astype(BF)), tdot(hot, lin_ref[0])
    row = lax.broadcasted_iota(jnp.int32, states.shape, 0)
    lasts_ref[0] = jnp.where(row < nseq, states, convs).astype(BF)

    @pl.when(i == pl.num_programs(0) - 1)
    def _():
        used = late_ref.shape[0]
        before = sums_o_ref.shape[1]
        late_ref[:, :before] = sums_o_ref[:used, :]
        head_w = (late_ref.shape[1] - before - len(sums)) // 2
        last = len(sums) - 1
        vgrad_ref[last : last + 1, :] *= vec_ref[last + 1 : last + 2, :]
        count = vgrad_ref.shape[0]
        row = lax.broadcasted_iota(jnp.int32, (count, count), 0)
        column = lax.broadcasted_iota(jnp.int32, (count, count), 1)
        eye = jnp.where(row == column, 1.0, 0.0).astype(BF)
        turned = tdot(vgrad_ref[...].astype(BF), eye)
        for h in range(used // head_w):
            at = slice(h * head_w, (h + 1) * head_w)
            parts = [wgrad_ref[at, o + h * head_w : o + (h + 1) * head_w] for o in (0, wide)]
            parts.append(turned[at, : len(sums)])
            late_ref[at, before:] = jnp.concatenate(parts, 1).astype(BF)


def back_conv_kernel(nseq, taps, info, dconv_ref, rim_ref, dgate_ref, vec_ref, *refs):
    out_ref, ext = refs[-2:]
    i = pl.program_id(0)
    rows, wide = dconv_ref.shape[1:]
    pos = info[i, 0] + lax.broadcasted_iota(jnp.int32, (rows, 1), 0)
    ext[0:rows, :] = dconv_ref[0].astype(F32)
    ext[rows : rows + 8, :] = rim_ref[0]
    total = vec_ref[0:1, :] * ext[0:rows, :]
    for k in range(1, taps):
        cut = jnp.zeros((rows, 1), jnp.int32)
        for s in range(nseq):
            start = info[i, 1 + s]
            cut = jnp.where((pos < start) & (pos + k >= start), 1, cut)
        total = total + vec_ref[k : k + 1, :] * jnp.where(cut == 0, ext[k : k + rows, :], 0.0)
    used = out_ref.shape[2] // 2
    both = [dgate_ref[0].astype(F32)[:, :used], total[:, :used]]
    out_ref[0] = jnp.concatenate(both, 1).astype(BF)


def by_block(body, info, ins, outs, scratch, done=(), name=None):
    blocks = info.shape[0]

    def spec(shape, blocked):
        zeros = (0,) * (len(shape) - 1)
        if blocked:
            return pl.BlockSpec((1,) + tuple(shape[1:]), lambda i, *_: (i,) + zeros)
        return pl.BlockSpec(tuple(shape), lambda i, *_: (0,) + zeros)

    hbm = pl.BlockSpec(memory_space=pl.ANY)
    return pl.pallas_call(
        body,
        grid_spec=pltpu.PrefetchScalarGridSpec(
            num_scalar_prefetch=1,
            grid=(blocks,),
            in_specs=[spec(v.shape, blocked) for v, blocked in ins] + [hbm] * len(done),
            out_specs=[spec(shape, blocked) for shape, _, blocked in outs],
            scratch_shapes=[pltpu.VMEM(shape, F32) for shape in scratch],
        ),
        out_shape=[jax.ShapeDtypeStruct(shape, kind) for shape, kind, _ in outs],
        compiler_params=pltpu.CompilerParams(vmem_limit_bytes=VMEM_LIMIT),
        cost_estimate=pl.CostEstimate(flops=0, bytes_accessed=1 << 20, transcendentals=0),
        name=name,
    )(info, *[v for v, _ in ins], *done)


def on_device(
    tokens,
    starts,
    init_state,
    init_conv,
    w_y,
    w_x,
    gate_a,
    gate_i,
    w_out,
    norm1_gain,
    conv_kernel,
    conv_bias,
    bias_a,
    bias_i,
    decay_param,
    w_gate,
    w_up,
    w_down,
    norm2_gain,
    cotangent,
):
    planes, count = lax.axis_size("a"), chips()
    a, b, n, c = (lax.axis_index(name) for name in ("a", "b", "n", "c"))
    u = chip()
    nn = count // 2
    rows, d_model = tokens.shape[1], tokens.shape[2]
    nseq = starts.shape[1]
    width = w_y.shape[1]
    head_w = gate_a.shape[1]
    half = gate_a.shape[0]
    taps = conv_kernel.shape[0]
    back = taps - 1
    heads_here = planes // 2
    wide_here = heads_here * head_w
    wp = -(-wide_here // 128) * 128
    hid = w_down.shape[0]
    drows = w_y.shape[0]
    nblocks = 2 * count

    def gather_a(value):
        return lax.all_gather(value, "a", axis=0, tiled=True)

    def scatter_a(value):
        return lax.psum_scatter(value, "a", scatter_dimension=0, tiled=True)

    def padded(v, axis=-1):
        pads = [(0, 0)] * v.ndim
        pads[axis] = (0, wp - wide_here)
        return jnp.pad(v, pads)

    vectors = jnp.concatenate(
        [conv_kernel, conv_bias[None], bias_a[None], bias_i[None], decay_param[None]], 0
    ).reshape(-1)
    vectors = jnp.concatenate([vectors, norm1_gain, norm2_gain]).astype(F32)
    lanes = -(-vectors.shape[0] // 1024) * 128
    vectors = jnp.pad(vectors, (0, 8 * lanes - vectors.shape[0])).reshape(8, lanes)
    at_start = jnp.concatenate([init_state[0][:, None], init_conv[0].astype(F32)], 1)
    at_start = at_start.reshape(nseq * taps, width)
    at_start = jnp.pad(at_start, ((0, 8), (0, 0)))
    at_start = at_start.at[nseq * taps, :nseq].set(starts[0].astype(F32))
    all_tokens, w_yx, w_gu, _, gate_rows, canon, at_start = start_exchange(
        tokens[0],
        w_y,
        w_x,
        w_gate,
        w_up,
        jnp.concatenate([gate_a, gate_i], 1),
        vectors,
        at_start,
    )
    w_yx = w_yx.reshape(d_model, 2 * wide_here)
    w_gu = gather_a(w_gu.reshape(-1, 2 * planes * hid))
    gate_rows = gate_rows.reshape(wide_here, -1)

    def join_halves(mine_all):
        away = swap_c(lax.dynamic_slice_in_dim(mine_all, (1 - c) * heads_here, heads_here, 0))
        own = lax.dynamic_slice_in_dim(mine_all, c * heads_here, heads_here, 0)
        first = jnp.where(c == 0, own, away)
        second = jnp.where(c == 0, away, own)
        return jnp.stack([first, second], 1).reshape((wide_here,) + mine_all.shape[2:])


    w_o = padded(join_halves(gather_a(w_out).reshape(planes, half, d_model)), 0)

    def block_diagonal(m):
        m = m.reshape(heads_here, head_w, head_w)
        eye = jnp.eye(heads_here, dtype=m.dtype)
        full = (m[:, :, None, :] * eye[:, None, :, None]).reshape(wide_here, wide_here)
        return padded(padded(full), 0)

    w_gates = jnp.concatenate(
        [
            block_diagonal(gate_rows[:, :head_w]),
            block_diagonal(gate_rows[:, head_w:]),
        ],
        1,
    )

    w_d = gather_a(w_down)
    f_here = planes * hid

    canon = canon.reshape(planes * nblocks, -1)
    nvec = (taps + 4) * half
    gain_one = canon[:, nvec : nvec + drows].reshape(-1)
    gain_two = canon[:, nvec + drows : nvec + 2 * drows].reshape(-1)
    mine = pick(canon[:, :nvec].reshape(2, heads_here, count, 2, taps + 4, half), c)
    mine = pick(mine, u, 1).transpose(2, 0, 1, 3).reshape(taps + 4, wide_here)
    decay_f = mine[taps + 3]
    vec = [mine[: taps + 3], jax.nn.softplus(decay_f)[None], jax.nn.sigmoid(decay_f)[None]]
    vec = padded(jnp.concatenate(vec))

    def my_channels(v):
        lead = v.shape[:-1]
        v = v.reshape(lead + (2, heads_here, count, head_w))
        v = pick(v, c, len(lead))
        return pick(v, u, len(lead) + 1).reshape(lead + (wide_here,))

    streams = 2 * nn
    at_start = at_start.reshape(streams, -1, width)
    offsets = at_start[:, nseq * taps, :nseq].astype(jnp.int32)
    at_start = my_channels(at_start[:, : nseq * taps].reshape(streams, nseq, taps, width))
    at_start = padded(at_start)
    state_0 = jnp.pad(at_start[:, :, 0], ((0, 0), (0, -nseq % 8), (0, 0)))
    conv_0 = at_start[:, :, 1:].reshape(streams, nseq * back, wp).astype(BF)
    conv_0 = jnp.pad(conv_0, ((0, 0), (0, -(nseq * back) % 16), (0, 0)))

    def per_block(v):
        v = v.reshape((2, 1, nn) + v.shape[1:])
        return jnp.broadcast_to(v, (2, 2, nn) + v.shape[3:]).reshape((nblocks,) + v.shape[3:])

    block_b = (jnp.arange(nblocks, dtype=jnp.int32) // nn) % 2
    first_row = (a * 2 + (b ^ block_b)) * rows
    position = first_row[:, None] + jnp.arange(rows, dtype=jnp.int32)[None]
    off_b = per_block(offsets)

    info = jnp.concatenate(
        [first_row[:, None], off_b, jnp.zeros((nblocks, -(nseq + 1) % 8), jnp.int32)], 1
    )

    grad_low = cotangent[0]
    grads = [grad_low] + [xor_u(grad_low, k) for k in range(1, count)]

    edge = ((nblocks, 8, wp), F32, True)
    normed, gate_in, linear, tail = by_block(
        norm_product_kernel,
        info,
        [(all_tokens, True), (w_yx, False), (gain_one[None], False)],
        [
            ((nblocks, rows, d_model), BF, True),
            ((nblocks, rows, wp), F32, True),
            ((nblocks, rows, wp), BF, True),
            edge,
        ],
        [],
        name="norm_product",
    )
    normed = normed.reshape(nblocks * rows, d_model)

    def two(v):
        return v.reshape((2, 2, nn) + v.shape[1:])

    rim = pass_along(6, "pass_rows", False, tail)[0]
    conv_0b, state_0b = per_block(conv_0), per_block(state_0)
    full = (nblocks, rows, wp)
    conv_low, retain, admit, carry_mul, carry_add, end_mul, end_add = by_block(
        functools.partial(forward_kernel, nseq, taps),
        info,
        [
            (linear, True), (rim, True), (conv_0b, True), (state_0b, True),
            (w_gates, False), (vec, False),
        ],
        [
            (full, BF, True), (full, F32, True), (full, F32, True),
            (full, F32, True), (full, F32, True), edge, edge,
        ],
        [(rows + 8, wp), (rows, wp), (rows, wp)],
        name="mixer_forward",
    )

    (end_mul, end_add), grads = lax.optimization_barrier(((end_mul, end_add), grads))
    state_in = pass_along(7, "pass_state", False, end_mul, end_add)[0]
    hidden = carry_mul * state_in + carry_add
    mixed_in = (hidden * jax.nn.gelu(gate_in)).astype(BF).reshape(-1, wp)
    resid, normed_two, grads = plane_reduce(
        2, "fwd", False, (mixed_in.reshape(2, count, rows, -1),), w_o, gain_two, tokens[0],
        tokens[0], grads,
    )
    normed_two = normed_two.reshape(nblocks * rows, d_model)
    grads = grads.reshape(nblocks * rows, d_model)

    hid_full = (nblocks, rows, f_here)
    inner, by_gate, by_up = by_block(
        ffn_forward_kernel,
        info,
        [(normed_two.reshape(nblocks, rows, d_model), True), (w_gu, False)],
        [(hid_full, BF, True)] * 3,
        [],
        name="ffn_forward",
    )
    inner = inner.reshape(nblocks * rows, f_here)
    cut = d_model // 2
    first_d = tdot(inner, grads[:, :cut]).astype(BF)
    second_d = tdot(inner, grads[:, cut:]).astype(BF)
    sent_d = scatter_a(first_d), scatter_a(second_d)
    d_pair = by_block(
        ffn_back_kernel,
        info,
        [
            (grads.reshape(nblocks, rows, d_model), True), (w_d, False), (by_gate, True),
            (by_up, True),
        ],
        [((nblocks, rows, 2 * f_here), BF, True)],
        [],
        (first_d, second_d),
        name="ffn_back",
    )[0]
    sums_gu = tdot(normed_two, d_pair.reshape(nblocks * rows, -1)).astype(BF)
    sent_gu = scatter_a(sums_gu)
    d_resid, d_resid_low, low = plane_reduce(
        3, "mid", True, (d_pair.reshape(2, count, rows, -1),), w_gu,
        gain_two, grad_low, resid, (inner.reshape(2, count, rows, f_here), w_d), (sent_d[0], sums_gu),
    )
    d_resid_low = d_resid_low.reshape(nblocks * rows, d_model)

    result = resid + low[0].astype(F32)
    for k in range(1, count):
        result = result + xor_u(low[k], k).astype(F32)
    result = result.astype(BF)

    d_gate_in, back_mul, back_add, end_mul, end_add, sums_o = by_block(
        functools.partial(back_scan_kernel, nseq, taps),
        info,
        [
            (d_resid_low.reshape(nblocks, rows, d_model), True), (w_o, False), (gate_in, True),
            (hidden, True), (retain, True), (vec, False), (mixed_in.reshape(full), True),
        ],
        [
            (full, BF, True), (full, F32, True), (full, F32, True), edge, edge,
            ((wp, d_model), BF, False),
        ],
        [(rows + 8, wp), (rows, wp), (rows, wp), (wp, d_model)],
        (sent_d[1],),
        name="mixer_back_scan",
    )
    grad_in = pass_along(8, "pass_state_back", True, end_mul, end_add)[0]
    d_conv_low, head, late, lasts = by_block(
        functools.partial(back_kernel, nseq, taps, planes * 2 * rows),
        info,
        [
            (back_mul, True), (back_add, True), (grad_in, True), (hidden, True),
            (state_in, True), (state_0b, True), (conv_low, True), (retain, True),
            (admit, True), (linear, True), (rim, True), (conv_0b, True), (w_gates, False), (vec, False),
            (sums_o, False),
        ],
        [
            (full, BF, True), edge, ((wide_here, d_model + 2 * head_w + taps + 4), BF, False),
            ((nblocks, nseq * taps, wp), BF, True),
        ],
        [(rows + 8, wp), (wp, 2 * wp), (taps + 4, wp)],
        (),
        name="mixer_back",
    )

    rim_back, late = pass_along(9, "pass_rows_back", True, head, halves=(late, half))
    d_both = by_block(
        functools.partial(back_conv_kernel, nseq, taps),
        info,
        [(d_conv_low, True), (rim_back, True), (d_gate_in, True), (vec, False)],
        [((nblocks, rows, 2 * wide_here), BF, True)],
        [(rows + 8, wp)],
        (result, sent_gu),
        name="mixer_back_conv",
    )[0]
    late = scatter_a(late.reshape(planes * half, -1))
    sums_yx = tdot(normed, d_both.reshape(nblocks * rows, 2 * wide_here)).astype(BF)
    input_grad, pieces, lasts = plane_reduce(
        4, "last", True, (d_both.reshape(2, count, rows, -1),), w_yx, gain_one, tokens[0], d_resid,
        (sent_gu,), (sums_yx,), lasts,
    )
    gain_shape = ((1, drows), F32)
    (
        grad_wg, grad_wu, grad_gain_two, grad_wo, grad_wa, grad_wi, final_state, final_conv,
        grad_taps, *vec_grads,
    ) = in_place(
        functools.partial(order_hidden_kernel, hid, head_w),
        (pieces, w_gate, w_up, norm2_gain.astype(F32)[None], late, lasts),
        [
            (w_gate.shape, F32), (w_up.shape, F32), gain_shape, (w_out.shape, F32),
            (gate_a.shape, F32), (gate_i.shape, F32), ((nseq, width), F32),
            ((nseq * back, width), BF), ((taps, half), F32),
        ]
        + [((1, half), F32)] * 4,
        "order_hidden",
    )
    pieces = finish(scatter_a(sums_yx), (grad_wg,))
    grad_wy, grad_wx, grad_gain_one = in_place(
        functools.partial(order_heads_kernel, head_w),
        (pieces, w_y, w_x, norm1_gain.astype(F32)[None]),
        [(w_y.shape, F32), (w_x.shape, F32), gain_shape],
        "order_heads",
    )
    grad_gain_one, grad_gain_two = grad_gain_one[0], grad_gain_two[0]
    final_conv = final_conv.reshape(nseq, back, width)

    return (
        result[None],
        input_grad[None],
        final_state[None],
        final_conv[None],
        grad_wy,
        grad_wx,
        grad_wa,
        grad_wi,
        grad_wo,
        grad_gain_one,
        grad_taps,
        *[v[0] for v in vec_grads],
        grad_wg,
        grad_wu,
        jnp.concatenate(sent_d, 1).astype(F32),
        grad_gain_two,
    )


WIDE = ("a", "b")
EVERY = ("a", "b", "n", "c")
HIGH = lax.Precision.HIGHEST


def passed_along(value, axis, by):
    size = lax.axis_size(axis)
    pairs = [(i, i + by) for i in range(size) if 0 <= i + by < size]
    return lax.ppermute(value, axis, pairs)


def entering(value, axis, combine, identity, reverse):
    size, place = (lax.axis_size(axis), lax.axis_index(axis))
    everything = jax.tree.map(lambda part: lax.all_gather(part, axis), value)
    start = jax.tree.map(
        lambda part, zero: jnp.broadcast_to(jnp.asarray(zero, part.dtype), part.shape),
        value,
        identity,
    )

    def hop(k, before):
        at = size - 1 - k if reverse else k
        reached = at > place if reverse else at < place
        new = combine(before, jax.tree.map(lambda part: part[at], everything))
        return jax.tree.map(lambda a, b: jnp.where(reached, a, b), new, before)

    return lax.fori_loop(0, size, hop, start)


def merged_2(value, axis, combine):
    everything = jax.tree.map(
        lambda part, kind: lax.all_gather(part.astype(kind), axis),
        value,
        jax.tree.map(lambda a: jnp.bfloat16 if a.dtype == jnp.float32 else a.dtype, value),
    )

    def take(k):
        return jax.tree.map(lambda part, own: part[k].astype(own.dtype), everything, value)

    return lax.fori_loop(
        1, lax.axis_size(axis), lambda k, so_far: combine(so_far, take(k)), take(0)
    )


def link(earlier, later):
    return (earlier[0] * later[0], later[0] * earlier[1] + later[1])


def norm_back(value, factor, gain, grad):
    weighted = grad * gain
    inner = jnp.mean(weighted * value, axis=-1, keepdims=True)
    return (
        factor * weighted - value * factor * factor * factor * inner,
        jnp.sum(grad * value * factor, axis=0),
    )


def later_one(first, second):
    pick = first[0] > second[0]
    return (
        jnp.where(pick, first[0], second[0]),
        jnp.where(pick[:, None], first[1], second[1]),
        jnp.where(pick[:, None, None], first[2], second[2]),
    )


def on_device_any(
    tokens,
    starts,
    init_state,
    init_conv,
    w_y,
    w_x,
    gate_a,
    gate_i,
    w_out,
    norm1_gain,
    conv_kernel,
    conv_bias,
    bias_a,
    bias_i,
    decay_param,
    w_gate,
    w_up,
    w_down,
    norm2_gain,
    cotangent,
):
    inputs = tokens[0].astype(jnp.float32)
    offsets = starts[0]
    nseqs = offsets.shape[0]
    rows_here = inputs.shape[0]
    width = w_y.shape[1]
    head_w = gate_a.shape[1]
    heads = width // head_w
    place = lax.axis_index(WIDE)
    mixer = (
        lax.all_gather(w_y, EVERY, axis=0, tiled=True),
        lax.all_gather(w_x, EVERY, axis=0, tiled=True),
        lax.all_gather(gate_a, EVERY, axis=0, tiled=True),
        lax.all_gather(gate_i, EVERY, axis=0, tiled=True),
        lax.all_gather(w_out, EVERY, axis=0, tiled=True),
        lax.all_gather(norm1_gain, EVERY, axis=0, tiled=True),
        lax.all_gather(conv_kernel, EVERY, axis=1, tiled=True),
        lax.all_gather(conv_bias, EVERY, axis=0, tiled=True),
        lax.all_gather(bias_a, EVERY, axis=0, tiled=True),
        lax.all_gather(bias_i, EVERY, axis=0, tiled=True),
        lax.all_gather(decay_param, EVERY, axis=0, tiled=True),
    )
    wy_full, wx_full, wa_full, wi_full, wo_full, gain_one, kernel, cbias, abias, ibias, decay = (
        mixer
    )
    gain_one = gain_one.astype(jnp.float32)
    kernel = kernel.astype(jnp.float32)
    taps = kernel.shape[0]
    back = taps - 1
    position = place * rows_here + jnp.arange(rows_here, dtype=jnp.int32)

    def segment_of(where_at):
        return jnp.sum((where_at[:, None] >= offsets[None, :]).astype(jnp.int32), axis=1) - 1

    segment = segment_of(position)
    member = segment[:, None] == jnp.arange(nseqs, dtype=jnp.int32)[None, :]
    begin = jnp.sum(jnp.where(member, offsets[None, :], 0), axis=1)
    opening = (position == begin)[:, None]
    scale_one = lax.rsqrt(jnp.mean(inputs * inputs, axis=-1, keepdims=True) + EPS)
    normed = (inputs * scale_one * gain_one).astype(jnp.bfloat16)
    gate_in = mdot(normed, wy_full)
    linear = mdot(normed, wx_full).astype(jnp.bfloat16)
    rim_rows = passed_along(linear[rows_here - back :], WIDE, 1)
    extended = jnp.concatenate([rim_rows, linear], 0)
    stored = mdot(member.astype(jnp.bfloat16), init_conv[0].reshape(nseqs, back * width)).reshape(
        rows_here, back, width
    )
    inputs_by_tap = [linear.astype(jnp.float32)]
    for shift_by in range(1, taps):
        earlier = extended[back - shift_by : back - shift_by + rows_here].astype(jnp.float32)
        offset = position - shift_by - begin
        from_start = jnp.zeros((rows_here, width), jnp.float32)
        for slot in range(back):
            from_start = from_start + jnp.where(
                (offset + back == slot)[:, None], stored[:, slot], 0.0
            )
        inputs_by_tap.append(jnp.where((offset >= 0)[:, None], earlier, from_start))
    conv_sum = cbias.astype(jnp.float32)
    for shift_by in range(taps):
        conv_sum = conv_sum + kernel[shift_by] * inputs_by_tap[shift_by]
    conv_low = conv_sum.astype(jnp.bfloat16)
    conv_val = conv_low.astype(jnp.float32)
    blocks = conv_low.reshape(rows_here, heads, head_w)
    wa_heads = wa_full.reshape(heads, head_w, head_w)
    wi_heads = wi_full.reshape(heads, head_w, head_w)
    rate = jnp.einsum("thi,hij->thj", blocks, wa_heads, preferred_element_type=jnp.float32).reshape(
        rows_here, width
    ) + abias.astype(jnp.float32)
    inflow = jnp.einsum(
        "thi,hij->thj", blocks, wi_heads, preferred_element_type=jnp.float32
    ).reshape(rows_here, width) + ibias.astype(jnp.float32)
    retain = jax.nn.sigmoid(rate)
    admit = jax.nn.sigmoid(inflow)
    decay_f = decay.astype(jnp.float32)
    soft_decay = jax.nn.softplus(decay_f)
    log_a = -8.0 * retain * soft_decay
    decay_now = jnp.exp(log_a)
    spread = -jnp.expm1(2.0 * log_a)
    mult = jnp.sqrt(jnp.maximum(spread, FLOOR))
    drive = mult * admit * conv_val
    state_rows = jnp.dot(member.astype(jnp.float32), init_state[0], precision=HIGH)
    a_used = jnp.where(opening, 0.0, decay_now)
    b_used = jnp.where(opening, decay_now * state_rows + drive, drive)
    carry_mul, carry_add = lax.associative_scan(link, (a_used, b_used), axis=0)
    identity = (jnp.ones((width,), jnp.float32), jnp.zeros((width,), jnp.float32))
    state_in = entering(
        (carry_mul[rows_here - 1], carry_add[rows_here - 1]), WIDE, link, identity, False
    )[1]
    hidden = carry_mul * state_in + carry_add
    gelu_y, gelu_y_back = jax.vjp(jax.nn.gelu, gate_in)
    mixed_in = (hidden * gelu_y).astype(jnp.bfloat16)
    resid = inputs + mdot(mixed_in, wo_full)
    wg_full, wu_full, wd_full, gain_two = (
        lax.all_gather(w_gate, EVERY, axis=0, tiled=True),
        lax.all_gather(w_up, EVERY, axis=0, tiled=True),
        lax.all_gather(w_down, EVERY, axis=0, tiled=True),
        lax.all_gather(norm2_gain, EVERY, axis=0, tiled=True),
    )
    gain_two = gain_two.astype(jnp.float32)
    scale_two = lax.rsqrt(jnp.mean(resid * resid, axis=-1, keepdims=True) + EPS)
    normed_two = (resid * scale_two * gain_two).astype(jnp.bfloat16)
    gate = mdot(normed_two, wg_full)
    upward = mdot(normed_two, wu_full)
    active, gate_back = jax.vjp(jax.nn.gelu, gate)
    inner = (active * upward).astype(jnp.bfloat16)
    result = (resid + mdot(inner, wd_full)).astype(jnp.bfloat16)
    local_rows = jnp.arange(rows_here, dtype=jnp.int32)
    last_row = jnp.max(jnp.where(member, local_rows[:, None], -1), axis=0)
    present = last_row >= 0
    safe_row = jnp.maximum(last_row, 0)
    marker = jnp.where(present, (place * rows_here + last_row).astype(jnp.float32), -1.0)
    state_last = jnp.where(present[:, None], hidden[safe_row], 0.0)
    conv_rows = extended[safe_row[:, None] + 1 + jnp.arange(back, dtype=jnp.int32)[None, :]].astype(
        jnp.float32
    )
    conv_last = jnp.where(present[:, None, None], conv_rows, 0.0)
    merged = merged_2((marker, state_last, conv_last), WIDE, later_one)
    wg_back, wu_back, wd_back = (
        lax.all_gather(w_gate, EVERY, axis=0, tiled=True),
        lax.all_gather(w_up, EVERY, axis=0, tiled=True),
        lax.all_gather(w_down, EVERY, axis=0, tiled=True),
    )
    grad_low = cotangent[0]
    grad_out = grad_low.astype(jnp.float32)
    d_inner = ndot(grad_low, wd_back)
    grad_wd = tdot(inner, grad_low)
    d_gate = gate_back(d_inner * upward)[0].astype(jnp.bfloat16)
    d_up = (d_inner * active).astype(jnp.bfloat16)
    grad_wg = tdot(normed_two, d_gate)
    grad_wu = tdot(normed_two, d_up)
    d_normed_two = ndot(d_gate, wg_back) + ndot(d_up, wu_back)
    d_resid_norm, grad_gain_two = norm_back(resid, scale_two, gain_two, d_normed_two)
    d_resid = grad_out + d_resid_norm
    wy_back, wx_back, wa_back, wi_back, wo_back = (
        lax.all_gather(w_y, EVERY, axis=0, tiled=True),
        lax.all_gather(w_x, EVERY, axis=0, tiled=True),
        lax.all_gather(gate_a, EVERY, axis=0, tiled=True),
        lax.all_gather(gate_i, EVERY, axis=0, tiled=True),
        lax.all_gather(w_out, EVERY, axis=0, tiled=True),
    )
    d_resid_low = d_resid.astype(jnp.bfloat16)
    d_mixed = ndot(d_resid_low, wo_back)
    grad_wo = tdot(mixed_in, d_resid_low)
    d_hidden = d_mixed * gelu_y
    d_gate_in = gelu_y_back(d_mixed * hidden)[0].astype(jnp.bfloat16)
    forward_mul = jnp.concatenate([a_used[1:], jnp.ones((1, width), jnp.float32)], 0)
    back_mul, back_add = lax.associative_scan(link, (forward_mul, d_hidden), reverse=True, axis=0)
    head_map = (a_used[0] * back_mul[0], a_used[0] * back_add[0])
    grad_in = entering(head_map, WIDE, link, identity, True)[1]
    total_grad = back_mul * grad_in + back_add
    previous = jnp.concatenate([state_in[None], hidden[:-1]], 0)
    previous = jnp.where(opening, state_rows, previous)
    d_decay = total_grad * previous
    d_mult = total_grad * admit * conv_val
    d_admit = total_grad * mult * conv_val
    d_conv = total_grad * mult * admit
    d_spread = jnp.where(spread > FLOOR, d_mult * 0.5 / mult, 0.0)
    d_log = d_decay * decay_now - 2.0 * decay_now * decay_now * d_spread
    d_retain = d_log * (-8.0 * soft_decay)
    grad_decay = jnp.sum(d_log * (-8.0 * retain), axis=0) * jax.nn.sigmoid(decay_f)
    d_rate = (d_retain * retain * (1.0 - retain)).astype(jnp.bfloat16)
    d_inflow = (d_admit * admit * (1.0 - admit)).astype(jnp.bfloat16)
    grad_abias = jnp.sum(d_rate.astype(jnp.float32), axis=0)
    grad_ibias = jnp.sum(d_inflow.astype(jnp.float32), axis=0)
    rate_heads = d_rate.reshape(rows_here, heads, head_w)
    inflow_heads = d_inflow.reshape(rows_here, heads, head_w)
    grad_wa = jnp.einsum(
        "thi,thj->hij", blocks, rate_heads, preferred_element_type=jnp.float32
    ).reshape(width, head_w)
    grad_wi = jnp.einsum(
        "thi,thj->hij", blocks, inflow_heads, preferred_element_type=jnp.float32
    ).reshape(width, head_w)
    d_conv = d_conv + jnp.einsum(
        "thj,hij->thi",
        rate_heads,
        wa_back.reshape(heads, head_w, head_w),
        preferred_element_type=jnp.float32,
    ).reshape(rows_here, width)
    d_conv = d_conv + jnp.einsum(
        "thj,hij->thi",
        inflow_heads,
        wi_back.reshape(heads, head_w, head_w),
        preferred_element_type=jnp.float32,
    ).reshape(rows_here, width)
    d_conv_low = d_conv.astype(jnp.bfloat16)
    d_conv_val = d_conv_low.astype(jnp.float32)
    rim_back = passed_along(d_conv_low[:back], WIDE, -1)
    ahead = jnp.concatenate([d_conv_low, rim_back], 0)
    d_linear = kernel[0] * d_conv_val
    kernel_grads = [jnp.sum(d_conv_val * inputs_by_tap[0], axis=0)]
    for shift_by in range(1, taps):
        later_rows = ahead[shift_by : shift_by + rows_here].astype(jnp.float32)
        same = (segment_of(position + shift_by) == segment)[:, None]
        d_linear = d_linear + kernel[shift_by] * jnp.where(same, later_rows, 0.0)
        kernel_grads.append(jnp.sum(d_conv_val * inputs_by_tap[shift_by], axis=0))
    grad_kernel = jnp.stack(kernel_grads, 0)
    grad_cbias = jnp.sum(d_conv_val, axis=0)
    d_linear_low = d_linear.astype(jnp.bfloat16)
    d_normed = ndot(d_gate_in, wy_back) + ndot(d_linear_low, wx_back)
    grad_wy = tdot(normed, d_gate_in)
    grad_wx = tdot(normed, d_linear_low)
    d_input_norm, grad_gain_one = norm_back(inputs, scale_one, gain_one, d_normed)
    input_grad = (d_resid + d_input_norm).astype(jnp.bfloat16)
    every_sum = (
        lax.psum_scatter(grad_wy, EVERY, scatter_dimension=0, tiled=True),
        lax.psum_scatter(grad_wx, EVERY, scatter_dimension=0, tiled=True),
        lax.psum_scatter(grad_wa, EVERY, scatter_dimension=0, tiled=True),
        lax.psum_scatter(grad_wi, EVERY, scatter_dimension=0, tiled=True),
        lax.psum_scatter(grad_wo, EVERY, scatter_dimension=0, tiled=True),
        lax.psum_scatter(grad_gain_one, EVERY, scatter_dimension=0, tiled=True),
        lax.psum_scatter(grad_kernel, EVERY, scatter_dimension=1, tiled=True),
        lax.psum_scatter(grad_cbias, EVERY, scatter_dimension=0, tiled=True),
        lax.psum_scatter(grad_abias, EVERY, scatter_dimension=0, tiled=True),
        lax.psum_scatter(grad_ibias, EVERY, scatter_dimension=0, tiled=True),
        lax.psum_scatter(grad_decay, EVERY, scatter_dimension=0, tiled=True),
        lax.psum_scatter(grad_wg, EVERY, scatter_dimension=0, tiled=True),
        lax.psum_scatter(grad_wu, EVERY, scatter_dimension=0, tiled=True),
        lax.psum_scatter(grad_wd, EVERY, scatter_dimension=0, tiled=True),
        lax.psum_scatter(grad_gain_two, EVERY, scatter_dimension=0, tiled=True),
    )
    mixer_sums = every_sum[:11]
    mlp_sums = every_sum[11:]
    return (
        result[None],
        input_grad[None],
        merged[1][None],
        merged[2].astype(jnp.bfloat16)[None],
        mixer_sums[0],
        mixer_sums[1],
        mixer_sums[2],
        mixer_sums[3],
        mixer_sums[4],
        mixer_sums[5],
        mixer_sums[6],
        mixer_sums[7],
        mixer_sums[8],
        mixer_sums[9],
        mixer_sums[10],
        mlp_sums[0],
        mlp_sums[1],
        mlp_sums[2],
        mlp_sums[3],
    )


def solution(mesh):
    wide, narrow = mesh.shape["wide"], mesh.shape["narrow"]
    def plan(*args):
        fits = args[6].shape[0] * 2 == args[6].shape[1] and narrow == 4
        return (on_device if fits else on_device_any)(*args)

    fine = Mesh(mesh.devices.reshape(wide // 2, 2, narrow // 2, 2), ("a", "b", "n", "c"))
    w, s = ("a", "b"), ("n", "c")
    everywhere = ("a", "b", "n", "c")
    acts, rows, vec = P(s, w, None), P(everywhere, None), P(everywhere)
    return jax.shard_map(
        plan,
        mesh=fine,
        in_specs=(
            acts,
            P(s, None),
            P(s, None, None),
            P(s, None, None, None),
            rows, rows, rows, rows, rows,
            vec,
            P(None, everywhere),
            vec, vec, vec, vec,
            rows, rows, rows,
            vec,
            acts,
        ),
        out_specs=(
            acts,
            acts,
            P(s, None, None),
            P(s, None, None, None),
            rows, rows, rows, rows, rows,
            vec,
            P(None, everywhere),
            vec, vec, vec, vec,
            rows, rows, rows,
            vec,
        ),
        check_vma=False,
    )
```

```python
import functools

import jax
import jax.numpy as jnp
from jax import lax
from jax.experimental import pallas as pl
from jax.experimental.pallas import tpu as pltpu
from jax.sharding import Mesh
from jax.sharding import PartitionSpec as P

EPS = 1e-06
FLOOR = 0.001
BF = jnp.bfloat16
F32 = jnp.float32


def tdot(left, right):
    return lax.dot_general(left, right, (((0,), (0,)), ((), ())), preferred_element_type=F32)


def ndot(left, right):
    return lax.dot_general(left, right, (((1,), (1,)), ((), ())), preferred_element_type=F32)


def mdot(left, right):
    return jnp.dot(left, right, preferred_element_type=F32)


def pick(stacked, index, axis=0):
    return lax.dynamic_index_in_dim(stacked, index, axis, keepdims=False)


def swap_c(value):
    return lax.ppermute(value, "c", [(0, 1), (1, 0)])


def xor_u(value, k):
    size = lax.axis_size("b") * lax.axis_size("n")
    return lax.ppermute(value, ("b", "n"), [(i, i ^ k) for i in range(size)])


def shift_a(value, by):
    size = lax.axis_size("a")
    return lax.ppermute(value, "a", [(i, i + by) for i in range(size) if 0 <= i + by < size])


def chips():
    return lax.axis_size("b") * lax.axis_size("n")


def chip():
    return lax.axis_index("b") * lax.axis_size("n") + lax.axis_index("n")


MESH = pl.DeviceIdType.MESH
VMEM_LIMIT = 60 * 1024 * 1024


def places():
    return tuple(lax.axis_index(name) for name in ("a", "b", "n", "c"))


def neighbours():
    a, b, n, c = places()
    return (a, 1 - b, n, c), (a, b, 1 - n, c), (a, b, n, 1 - c)


def greet(peers):
    barrier = pltpu.get_barrier_semaphore()
    for peer in peers:
        pl.semaphore_signal(barrier, inc=1, device_id=peer, device_id_type=MESH)
    pl.semaphore_wait(barrier, len(peers))


class Mover:
    def __init__(self, send, recv):
        self.send, self.recv, self.made = send, recv, {}
        self.names = []

    def copy(self, name, src, dst, peer):
        if name not in self.names:
            self.names.append(name)
        at = self.names.index(name)
        made = pltpu.make_async_remote_copy(
            src_ref=src,
            dst_ref=dst,
            send_sem=self.send.at[at],
            recv_sem=self.recv.at[at],
            device_id=peer,
            device_id_type=MESH,
        )
        self.made[name] = made
        return made

    def start(self, name, src, dst, peer):
        self.copy(name, src, dst, peer).start()

    def arrived(self, name):
        self.made[name].wait_recv()

    def sent(self):
        for made in self.made.values():
            made.wait_send()


def gather_plane_start(move, mine, everyone, h, half_rows):
    x, y, z = neighbours()
    at = pl.ds(h * half_rows, half_rows)
    move.start(f"gx{h}", mine.at[at], everyone.at[2, at], x)
    move.start(f"gy{h}", mine.at[at], everyone.at[1, at], y)
    move.start(f"gc{h}", mine.at[at], everyone.at[4, at], z)


def gather_plane_rest(move, everyone, half_rows, stage=None):
    x, y, z = neighbours()
    rows = [pl.ds(h * half_rows, half_rows) for h in range(2)]

    def on(name, k, h):
        move.start(name, everyone.at[k, rows[h]], everyone.at[4 + k, rows[h]], z)

    if stage in (None, 0):
        move.arrived("gx0")
        move.start("fy", everyone.at[2, rows[0]], everyone.at[3, rows[0]], y)
        on("cx0", 2, 0)
        move.arrived("gy1")
        move.start("fx", everyone.at[1, rows[1]], everyone.at[3, rows[1]], x)
        on("cy1", 1, 1)
    if stage in (None, 1):
        move.arrived("gx1")
        on("cx1", 2, 1)
        move.arrived("gy0")
        on("cy0", 1, 0)
    if stage in (None, 2):
        move.arrived("fy")
        on("cd0", 3, 0)
        move.arrived("fx")
        on("cd1", 3, 1)
        for name in ("gc0", "gc1", "cx0", "cx1", "cy0", "cy1", "cd0", "cd1"):
            move.arrived(name)


GATHER_COPIES = 14


def plane_peers_of():
    a, b, n, c = places()
    peers = {}
    for kc in range(2):
        for k in range(4):
            if (kc, k) != (0, 0):
                there = (a, 1 - b if k & 2 else b, 1 - n if k & 1 else n, 1 - c if kc else c)
                peers[kc, k] = there
    return peers


def peer_owner(kc, k):
    _, b, n, c = places()
    return ((b * 2 + n) ^ k) * 2 + (1 - c if kc else c)


def set_side_by_side(pieces, order, width):
    group = 1
    while group * width % 128 and group < len(order):
        group += 1
    for i in range(0, len(order), group):
        runs = [pieces[p, :, o : o + width].astype(F32) for p, o in order[i : i + group]]
        yield slice(i * width, (i + len(runs)) * width), jnp.concatenate(runs, 1)


def gain_sum(pairs, gain):
    total = sum(jnp.sum(w[...].astype(F32) * g[...], axis=-1, keepdims=True) for w, g in pairs)
    size = total.shape[0]
    row = lax.broadcasted_iota(jnp.int32, (size, size), 0)
    column = lax.broadcasted_iota(jnp.int32, (size, size), 1)
    return jnp.sum(jnp.where(row == column, total, 0.0), axis=0, keepdims=True) / gain[...]


def reduce_kernel(nt, post, nx, extra, waits, *refs):
    x_hbm, refs = refs[:nx], refs[nx:]
    w_hbm, gain_ref, first_ref, second_ref = refs[:4]
    extra_in, refs = refs[4 : 4 + extra], refs[4 + extra :]
    if post == "last":
        lasts_ref, refs = refs[0], refs[1:]
    refs = refs[waits:]
    out_ref, refs = refs[0], refs[1:]
    if post == "last":
        everyone = mine = None
        extra_buf, lasts_sum = refs[:2]
        lasts_buf, lasts_mine, lasts_far, lasts_sent = refs[2:6]
        refs = refs[6:]
    else:
        everyone, refs = refs[0], refs[1:]
        if extra and post == "fwd":
            extra_out, refs = refs[0], refs[1:]
        elif extra:
            extra_out, refs = refs[:4], refs[4:]
        mine, refs = refs[0], refs[1:]
        if post == "mid":
            (side_x, side_w, side_s, side_r), refs = refs[:4], refs[4:]
    x_v, w_v, away_s, away_r, acc, out_b, in_b, local, send, recv = refs
    rows, d_model = acc.shape[1:]
    half = rows // 2
    tile = min(512, d_model)
    px, py, pc = neighbours()
    move = Mover(send, recv)

    slots = iter(range(local.shape[0]))

    def keep(src, dst):
        made = pltpu.make_async_copy(src, dst, local.at[next(slots)])
        made.start()
        return made

    w_copy = keep(w_hbm, w_v)
    loads = {}
    each = x_v.shape[3] // nx
    for k in (3, 2, 1, 0):
        for kc in (1, 0):
            loads[kc, k] = [
                keep(x.at[kc, k], x_v.at[kc, k, :, pl.ds(i * each, each)])
                for i, x in enumerate(x_hbm)
            ]
    if post == "mid":
        side_loads = [keep(extra_in[0], side_x), keep(extra_in[1], side_w)]
    if post == "last":
        a, b, n, c = places()
        planes = lasts_far.shape[0] + 1
        columns = [(lax.rem(a + d, planes), b, n, c) for d in range(1, planes)]
        peers = plane_peers_of()
        greet([*peers.values(), *columns])
        for kc in range(2):
            for kn in range(2):
                lasts_sent[kc, kn] = (
                    lasts_ref[kc * 4 + kn].astype(F32) + lasts_ref[kc * 4 + 2 + kn].astype(F32)
                ).astype(BF)
        for (kc, k), peer in peers.items():
            move.start(f"l{kc}{k}", lasts_sent.at[kc, k % 2], lasts_buf.at[kc, k], peer)
    else:
        greet((px, py, pc))
    w_copy.wait()

    def product(kc, k, t):
        at = pl.ds(pl.multiple_of(t * tile, tile), tile)
        if nt:
            return at, ndot(x_v[kc, k], w_v[at, :])
        return at, mdot(x_v[kc, k], w_v[:, at])

    step = min(32, half)

    def by_rows(h, body):
        @pl.loop(0, half // step)
        def _(i):
            body(pl.ds(pl.multiple_of(i * step, step), step),
                 pl.ds(pl.multiple_of(h * half + i * step, step), step))

    def hand_on(name, slot, k, h, peer, extra=None):
        def body(inner, outer):
            value = acc[k, outer, :]
            if extra is not None:
                value = value + in_b[extra, inner, :].astype(F32)
            out_b[slot, inner, :] = value.astype(BF)

        by_rows(h, body)
        move.start(name, out_b.at[slot], in_b.at[slot], peer)

    for k in (3, 2, 1, 0):
        for load in loads[1, k]:
            load.wait()

        @pl.loop(0, d_model // tile)
        def _(t):
            at, value = product(1, k, t)
            away_s[k, :, at] = value.astype(BF)

        move.start(f"away{k}", away_s.at[k], away_r.at[k], pc)
        for load in loads[0, k]:
            load.wait()

        @pl.loop(0, d_model // tile)
        def _(t):
            at, value = product(0, k, t)
            acc[k, :, at] = value

        move.arrived(f"away{k}")
        for h in range(2):
            def add(inner, outer):
                acc[k, outer, :] += away_r[k, outer, :].astype(F32)

            by_rows(h, add)
        if k == 3:
            hand_on("d0", 0, 3, 0, px)
            hand_on("d1", 1, 3, 1, py)
        elif k == 2:
            hand_on("x0", 2, 2, 0, px)
        elif k == 1:
            hand_on("y1", 5, 1, 1, py)
    kept = []
    if extra and post == "fwd":
        for k in range(4):
            kept.append(keep(extra_in[k], extra_out.at[k]))
            move.start(f"e{k}", extra_in[k], extra_out.at[4 + k], pc)
    move.arrived("d0")
    hand_on("y0", 4, 1, 0, py, 0)
    move.arrived("d1")
    hand_on("x1", 3, 2, 1, px, 1)
    if post == "mid":
        for load in side_loads:
            load.wait()
        for k in range(4):

            @pl.loop(0, d_model // tile)
            def _(t):
                at = pl.ds(pl.multiple_of(t * tile, tile), tile)
                side_s[k, :, at] = mdot(side_x[1, k], side_w[:, at]).astype(BF)

            move.start(f"s{k}", side_s.at[k], side_r.at[k], pc)
        for k in range(4):
            move.arrived(f"s{k}")
            move.made.pop(f"s{k}").wait_send()

            @pl.loop(0, d_model // tile)
            def _(t):
                at = pl.ds(pl.multiple_of(t * tile, tile), tile)
                value = mdot(side_x[0, k], side_w[:, at]) + side_r[k, :, at].astype(F32)
                side_s[k, :, at] = value.astype(BF)

            kept.append(keep(side_s.at[k], extra_out[k]))
    if extra and post == "last":
        lasts_buf[0, 0] = lasts_sent[0, 0]
        for kc, k in peers:
            move.arrived(f"l{kc}{k}")
        u = b * 2 + n
        me = u * 2 + c
        for kc in range(2):
            for q in range(4):
                found = lasts_buf[kc, 0]
                for k in range(1, 4):
                    found = jnp.where((u ^ k) == q, lasts_buf[kc, k], found)
                lasts_mine[jnp.bitwise_xor(c, kc), q] = found
        for i, peer in enumerate(columns):
            move.start(f"z{i}", lasts_mine, lasts_far.at[i], peer)
        each_rows = extra_buf.shape[1]

        def part(owner):
            at = pl.multiple_of(owner * each_rows, each_rows)
            return extra_in[0].at[pl.ds(at, each_rows)]

        kept.append(keep(part(me), extra_buf.at[me]))
        for (kc, k), peer in peers.items():
            move.start(f"e{kc}{k}", part(peer_owner(kc, k)), extra_buf.at[me], peer)

    for h in range(2):
        move.arrived(f"x{h}")
        move.arrived(f"y{h}")

        def body(inner, outer):
            total = acc[0, outer, :]
            total = total + in_b[2 + h, inner, :].astype(F32)
            total = total + in_b[4 + h, inner, :].astype(F32)
            gain = gain_ref[...]
            if post == "fwd":
                value = first_ref[outer, :].astype(F32) + total
                out_ref[outer, :] = value
                factor = lax.rsqrt(jnp.mean(value * value, axis=-1, keepdims=True) + EPS)
                mine[outer, :] = (value * factor * gain).astype(BF)
                return
            value = second_ref[outer, :] if post == "mid" else first_ref[outer, :].astype(F32)
            base = first_ref[outer, :].astype(F32) if post == "mid" else second_ref[outer, :]
            factor = lax.rsqrt(jnp.mean(value * value, axis=-1, keepdims=True) + EPS)
            weighted = total * gain
            inner_mean = jnp.mean(weighted * value, axis=-1, keepdims=True)
            grad = base + factor * weighted - value * (factor * factor * factor * inner_mean)
            if post == "mid":
                out_ref[outer, :] = grad
                mine[outer, :] = grad.astype(BF)
            else:
                out_ref[outer, :] = grad.astype(BF)

        by_rows(h, body)
        if everyone is not None:
            gather_plane_start(move, mine, everyone, h, half)
    if everyone is not None:
        kept.append(keep(mine, everyone.at[0]))
        gather_plane_rest(move, everyone, half)
    if extra and post == "fwd":
        for k in range(4):
            move.arrived(f"e{k}")
    for made in kept:
        made.wait()
    if extra and post == "last":
        total = lasts_mine[...].astype(F32)
        for i in range(len(columns)):
            move.arrived(f"z{i}")
            total = total + lasts_far[i].astype(F32)
        lasts_sum[...] = total.reshape(lasts_sum.shape)
        for kc, k in peers:
            move.arrived(f"e{kc}{k}")
    move.sent()


def plane_reduce(ident, post, nt, xs, w, gain, first, second, extra=(), done=(), lasts=None):
    rows, d_model = first.shape
    vmem = pl.BlockSpec(memory_space=pltpu.VMEM)
    hbm = pl.BlockSpec(memory_space=pl.ANY)
    out_type = BF if post == "last" else F32
    out_shape = [jax.ShapeDtypeStruct((rows, d_model), out_type)]
    out_specs = [vmem]
    scratch = []
    copies = 10
    if post != "last":
        out_shape.append(jax.ShapeDtypeStruct((8, rows, d_model), BF))
        out_specs.append(hbm)
        copies += GATHER_COPIES
        if extra:
            shapes = [(8, rows, d_model)] if post == "fwd" else [(rows, d_model)] * 4
            out_shape += [jax.ShapeDtypeStruct(shape, BF) for shape in shapes]
            out_specs += [hbm] * len(shapes)
            copies += 4
        scratch.append(pltpu.VMEM((rows, d_model), BF))
        if post == "mid":
            scratch += [pltpu.VMEM(v.shape, BF) for v in extra]
            scratch += [pltpu.VMEM((4, rows, d_model), BF)] * 2
    else:
        each = extra[0].shape[0] // 8, extra[0].shape[1]
        planes = lax.axis_size("a")
        copies += 7 + 7 + planes - 1
        block = (2, 4) + lasts.shape[1:]
        out_shape.append(jax.ShapeDtypeStruct((8,) + each, BF))
        out_shape.append(jax.ShapeDtypeStruct((8,) + block[2:], F32))
        out_specs += [hbm, vmem]
        scratch += [pltpu.VMEM(block, BF)] * 2 + [pltpu.VMEM((planes - 1,) + block, BF)]
        scratch.append(pltpu.VMEM((2, 2) + block[2:], BF))
    wide = sum(x.shape[3] for x in xs)
    scratch += [
        pltpu.VMEM((2, 4, rows, wide), BF),
        pltpu.VMEM(w.shape, BF),
        pltpu.VMEM((4, rows, d_model), BF),
        pltpu.VMEM((4, rows, d_model), BF),
        pltpu.VMEM((4, rows, d_model), F32),
        pltpu.VMEM((6, rows // 2, d_model), BF),
        pltpu.VMEM((6, rows // 2, d_model), BF),
        pltpu.SemaphoreType.DMA((8 + 8 * len(xs),)),
        pltpu.SemaphoreType.DMA((copies,)),
        pltpu.SemaphoreType.DMA((copies,)),
    ]
    last = [] if lasts is None else [lasts]
    return pl.pallas_call(
        functools.partial(reduce_kernel, nt, post, len(xs), len(extra), len(done)),
        in_specs=[hbm] * (len(xs) + 1)
        + [vmem] * 3
        + [vmem if post == "fwd" else hbm] * len(extra)
        + [vmem] * (lasts is not None)
        + [hbm] * len(done),
        out_specs=out_specs,
        out_shape=out_shape,
        scratch_shapes=scratch,
        compiler_params=pltpu.CompilerParams(
            collective_id=ident, has_side_effects=True, vmem_limit_bytes=VMEM_LIMIT
        ),
        cost_estimate=pl.CostEstimate(flops=0, bytes_accessed=8 << 20, transcendentals=0),
        name=f"plane_reduce_{post}",
    )(*xs, w, gain.reshape(1, -1), first, second, *extra, *last, *done)


def start_kernel(
    head_w, hid, tokens_ref, wy_ref, wx_ref, wg_ref, wu_ref, rows_ref, vec_ref, stream_ref,
    tok_out, yx_out, gu_out, rows_out, halves_out, vec_out, stream_out,
    yx_ref, gu_ref, local, send, recv,
):
    a, b, n, c = places()
    planes = yx_out.shape[0]
    p = (b * 2 + n) * 2 + c
    pc = neighbours()[2]
    plane_peers = plane_peers_of()
    up, down = (a + 1, b, n, c), (a - 1, b, n, c)
    each = planes // 2

    def pack(out, sources, columns, width):
        for owner in range(8):
            runs = [w[:, o : o + width] for w in sources for o in columns(owner)]
            out[owner] = jnp.concatenate(runs, 1)

    barrier = pltpu.get_barrier_semaphore()
    for peer in plane_peers.values():
        pl.semaphore_signal(barrier, inc=1, device_id=peer, device_id_type=MESH)

    @pl.when(a < planes - 1)
    def _():
        pl.semaphore_signal(barrier, inc=1, device_id=up, device_id_type=MESH)

    @pl.when(a > 0)
    def _():
        pl.semaphore_signal(barrier, inc=1, device_id=down, device_id_type=MESH)

    def head_columns(owner):
        return [((owner % 2 * each + j) * 4 + owner // 2) * head_w for j in range(each)]

    pack(yx_ref, (wy_ref, wx_ref), head_columns, head_w)
    others = len(plane_peers) + jnp.minimum(planes - 1 - a, 1) + jnp.minimum(a, 1)
    pl.semaphore_wait(barrier, others)

    move = Mover(send, recv)
    half = tokens_ref.shape[0] // 2

    def keep(i, src, dst):
        made = pltpu.make_async_copy(src, dst, local.at[i])
        made.start()
        return made

    def to_owners(name, pieces, out):
        for (kc, k), peer in plane_peers.items():
            move.start(f"{name}{kc}{k}", pieces.at[peer_owner(kc, k)], out.at[a, p], peer)

    chains = {}

    def chain_step(name, out, s):
        def up_copy(block):
            return move.copy(f"{name}u{s}", out.at[block], out.at[block], up)

        def down_copy(block):
            return move.copy(f"{name}d{s}", out.at[block], out.at[block], down)

        sends_up, sends_down = (a < planes - 1) & (a >= s), (a > 0) & (a + s < planes)

        @pl.when(sends_up)
        def _():
            up_copy(a - s).start()

        @pl.when(sends_down)
        def _():
            down_copy(a + s).start()

        chains[name, s] = (up_copy, down_copy, sends_up, sends_down)

    def chain_arrived(name, s):
        up_copy, down_copy, _, _ = chains[name, s]

        @pl.when(a - 1 >= s)
        def _():
            up_copy(a - 1 - s).wait_recv()

        @pl.when(a + 1 + s < planes)
        def _():
            down_copy(a + 1 + s).wait_recv()

    def chain_sent(name, s):
        up_copy, down_copy, sends_up, sends_down = chains[name, s]

        @pl.when(sends_up)
        def _():
            up_copy(a - s).wait_send()

        @pl.when(sends_down)
        def _():
            down_copy(a + s).wait_send()

    to_owners("yx", yx_ref, yx_out)
    for (kc, k), peer in plane_peers.items():
        move.start(f"vec{kc}{k}", vec_ref, vec_out.at[a, p], peer)
    own_yx = keep(1, yx_ref.at[p], yx_out.at[a, p])
    own_vec = keep(2, vec_ref, vec_out.at[a, p])
    own_rows = keep(0, rows_ref, rows_out.at[a])
    own_tok = keep(4, tokens_ref, tok_out.at[0])
    own_stream = keep(5, stream_ref, stream_out.at[0, 0])
    own_yx.wait()
    own_vec.wait()
    for kc, k in plane_peers:
        move.arrived(f"yx{kc}{k}")
        move.arrived(f"vec{kc}{k}")
    own_rows.wait()
    outs = (("yx", yx_out), ("vec", vec_out), ("rows", rows_out))
    for name, out in outs:
        chain_step(name, out, 0)
    for h in range(2):
        gather_plane_start(move, tokens_ref, tok_out, h, half)
    pack(gu_ref, (wg_ref, wu_ref), lambda o: [(z * 8 + o) * hid for z in range(planes)], hid)
    own_gu = keep(3, gu_ref.at[p], gu_out.at[p])
    gather_plane_rest(move, tok_out, half, 0)
    for kc in range(2):
        for kn in range(2):
            if (kc, kn) != (0, 0):
                move.start(f"st{kc}{kn}", stream_ref, stream_out.at[kc, kn], plane_peers[kc, kn])
    for name, out in outs:
        chain_arrived(name, 0)
        chain_step(name, out, 1)
    gather_plane_rest(move, tok_out, half, 1)
    for (kc, k), peer in plane_peers.items():
        move.start(f"gu{kc}{k}", gu_ref.at[peer_owner(kc, k)], gu_out.at[p], peer)
    for s in range(1, planes - 1):
        for name, out in outs:
            chain_arrived(name, s)
            if s + 1 < planes - 1:
                chain_step(name, out, s + 1)
    gather_plane_rest(move, tok_out, half, 2)
    swap = pltpu.make_async_remote_copy(
        src_ref=rows_out.at[pl.ds((1 - c) * each, each)],
        dst_ref=halves_out.at[:, c],
        send_sem=send.at[send.shape[0] - 1],
        recv_sem=recv.at[recv.shape[0] - 1],
        device_id=pc,
        device_id_type=MESH,
    )
    swap.start()
    own_halves = keep(6, rows_out.at[pl.ds(c * each, each)], halves_out.at[:, c])
    for kc, k in plane_peers:
        move.arrived(f"gu{kc}{k}")
    for kc in range(2):
        for kn in range(2):
            if (kc, kn) != (0, 0):
                move.arrived(f"st{kc}{kn}")
    for made in (own_gu, own_tok, own_stream, own_halves):
        made.wait()
    swap.wait()
    for name, s in chains:
        chain_sent(name, s)
    for name in [n for n in move.names if not any(n == f"{w}{d}{s}" for w, s in chains for d in "ud")]:
        move.made[name].wait_send()


def start_exchange(tokens, w_y, w_x, w_gate, w_up, gate_rows, vec, stream):
    planes = lax.axis_size("a")
    head_w, hid = gate_rows.shape[1] // 2, w_gate.shape[1] // (planes * 8)
    vmem = pl.BlockSpec(memory_space=pltpu.VMEM)
    hbm = pl.BlockSpec(memory_space=pl.ANY)
    yx = (8, w_y.shape[0], 2 * w_y.shape[1] // 8)
    gu = (8, w_gate.shape[0], 2 * w_gate.shape[1] // 8)
    shapes = [
        ((8,) + tokens.shape, BF),
        ((planes,) + yx, BF),
        (gu, BF),
        ((planes,) + gate_rows.shape, BF),
        ((planes // 2, 2) + gate_rows.shape, BF),
        ((planes, 8) + vec.shape, F32),
        ((2, 2) + stream.shape, F32),
    ]
    copies = 7 * 3 + 3 + GATHER_COPIES + 6 * (planes - 1) + 1
    return pl.pallas_call(
        functools.partial(start_kernel, head_w, hid),
        in_specs=[vmem] * 8,
        out_specs=[hbm] * 7,
        out_shape=[jax.ShapeDtypeStruct(*shape) for shape in shapes],
        scratch_shapes=[
            pltpu.VMEM(yx, BF),
            pltpu.VMEM(gu, BF),
            pltpu.SemaphoreType.DMA((7,)),
            pltpu.SemaphoreType.DMA((copies,)),
            pltpu.SemaphoreType.DMA((copies,)),
        ],
        compiler_params=pltpu.CompilerParams(
            collective_id=1, has_side_effects=True, vmem_limit_bytes=VMEM_LIMIT
        ),
        cost_estimate=pl.CostEstimate(flops=0, bytes_accessed=8 << 20, transcendentals=0),
        name="start_exchange",
    )(tokens, w_y, w_x, w_gate, w_up, gate_rows, vec, stream)


def finish_kernel(sums_ref, buf, local, send, recv):
    _, b, n, c = places()
    me = (b * 2 + n) * 2 + c
    peers = plane_peers_of()
    greet(list(peers.values()))
    move = Mover(send, recv)
    each_rows = buf.shape[1]

    def part(owner):
        return sums_ref.at[pl.ds(pl.multiple_of(owner * each_rows, each_rows), each_rows)]

    for (kc, k), peer in peers.items():
        move.start(f"e{kc}{k}", part(peer_owner(kc, k)), buf.at[me], peer)
    own = pltpu.make_async_copy(part(me), buf.at[me], local.at[0])
    own.start()
    own.wait()
    for kc, k in peers:
        move.arrived(f"e{kc}{k}")
    move.sent()


def finish(sums, done):
    vmem = pl.BlockSpec(memory_space=pltpu.VMEM)

    def body(sums_ref, *refs):
        finish_kernel(sums_ref, *refs[len(done) :])

    return pl.pallas_call(
        body,
        in_specs=[vmem] + [pl.BlockSpec(memory_space=pl.ANY)] * len(done),
        out_specs=vmem,
        out_shape=jax.ShapeDtypeStruct((8, sums.shape[0] // 8, sums.shape[1]), BF),
        scratch_shapes=[
            pltpu.SemaphoreType.DMA((1,)),
            pltpu.SemaphoreType.DMA((7,)),
            pltpu.SemaphoreType.DMA((7,)),
        ],
        compiler_params=pltpu.CompilerParams(
            collective_id=5, has_side_effects=True, vmem_limit_bytes=VMEM_LIMIT
        ),
        cost_estimate=pl.CostEstimate(flops=0, bytes_accessed=1 << 20, transcendentals=0),
        name="finish",
    )(sums, *done)


def in_place(body, ins, outs, name):
    vmem = pl.BlockSpec(memory_space=pltpu.VMEM)
    return pl.pallas_call(
        body,
        in_specs=[vmem] * len(ins),
        out_specs=[vmem] * len(outs),
        out_shape=[jax.ShapeDtypeStruct(*out) for out in outs],
        compiler_params=pltpu.CompilerParams(vmem_limit_bytes=VMEM_LIMIT),
        cost_estimate=pl.CostEstimate(flops=0, bytes_accessed=1 << 20, transcendentals=0),
        name=name,
    )(*ins)


def order_hidden_kernel(
    hid, head_w, buf, wg_ref, wu_ref, gain_ref, late_ref, lasts_ref,
    g_ref, u_ref, gain_out, out_ref, a_ref, i_ref, state_ref, conv_ref, *vec_refs,
):
    wide = buf.shape[2] // 2
    for i, out in enumerate((g_ref, u_ref)):
        order = [(p, i * wide + z * hid) for z in range(wide // hid) for p in range(8)]
        for at, value in set_side_by_side(buf, order, hid):
            out[:, at] = value
    gain_out[...] = gain_sum(((wg_ref, g_ref), (wu_ref, u_ref)), gain_ref)
    heads = wide // hid // 2
    order = [(i * 4 + q, j * head_w) for i in range(2) for j in range(heads) for q in range(4)]
    for at, value in set_side_by_side(lasts_ref, order, head_w):
        nseq = state_ref.shape[0]
        state_ref[:, at] = value[:nseq]
        conv_ref[:, at] = value[nseq:].astype(BF)
    wide_out, half = out_ref.shape[1], late_ref.shape[0]
    out_ref[...] = late_ref[:, :wide_out].astype(F32)
    a_ref[...] = late_ref[:, wide_out : wide_out + head_w].astype(F32)
    i_ref[...] = late_ref[:, wide_out + head_w : wide_out + 2 * head_w].astype(F32)
    row = lax.broadcasted_iota(jnp.int32, (half, half), 0)
    column = lax.broadcasted_iota(jnp.int32, (half, half), 1)
    eye = jnp.where(row == column, 1.0, 0.0).astype(BF)
    turned = tdot(late_ref[:, wide_out + 2 * head_w :], eye)
    taps = vec_refs[0].shape[0]
    vec_refs[0][...] = turned[:taps]
    for i, vec_ref in enumerate(vec_refs[1:]):
        vec_ref[...] = turned[taps + i : taps + i + 1]


def order_heads_kernel(head_w, buf, wy_ref, wx_ref, gain_ref, y_ref, x_ref, gain_out):
    wide = buf.shape[2] // 2
    each = wide // head_w
    order = [(q * 2 + i, j * head_w) for i in range(2) for j in range(each) for q in range(4)]
    for first, out in ((0, y_ref), (wide, x_ref)):
        for at, value in set_side_by_side(buf, [(p, o + first) for p, o in order], head_w):
            out[:, at] = value
    gain_out[...] = gain_sum(((wy_ref, y_ref), (wx_ref, x_ref)), gain_ref)


def column_peers(planes):
    a, b, n, c = places()
    return [(lax.rem(a + d, planes), b, n, c) for d in range(1, planes)]


def earlier_blocks(ref, want, row=0, count=1):
    _, b, _, _ = places()
    return [
        jnp.where(
            b == want,
            ref[kc * 4 + kn, row : row + count, :],
            ref[kc * 4 + 2 + kn, row : row + count, :],
        )
        for kc in range(2)
        for kn in range(2)
    ]


def split_refs(refs):
    if len(refs) == 5:
        return None, refs[:1], refs[1:], None
    return refs[0], refs[1:3], refs[3:7], refs[7:]


def swap_halves(rows_ref, out_ref, local, send, recv):
    _, _, _, c = places()
    planes, half = out_ref.shape[:2]
    each = planes // 2
    made = []
    for j in range(each):
        away = pl.multiple_of((2 * j + 1 - c) * half, half)
        own = pl.multiple_of((2 * j + c) * half, half)
        made.append(
            pltpu.make_async_remote_copy(
                src_ref=rows_ref.at[pl.ds(away, half)],
                dst_ref=out_ref.at[c * each + j],
                send_sem=send.at[j],
                recv_sem=recv.at[j],
                device_id=neighbours()[2],
                device_id_type=MESH,
            )
        )
        made.append(
            pltpu.make_async_copy(
                rows_ref.at[pl.ds(own, half)], out_ref.at[c * each + j], local.at[j]
            )
        )
    for copy in made:
        copy.start()
    return made


def pass_state_kernel(reverse, mul_ref, add_ref, *refs):
    rows_ref, (out_ref, *halves), (whole, came, send, recv), swaps = split_refs(refs)
    a, b, n, c = places()
    planes = came.shape[0] + 1
    row = 0 if reverse else 7
    near_at, far_at = (1, 0) if reverse else (0, 1)
    came[...] = jnp.zeros_like(came)
    near_mul, near_add = earlier_blocks(mul_ref, near_at, row), earlier_blocks(add_ref, near_at, row)
    far_mul, far_add = earlier_blocks(mul_ref, far_at, row), earlier_blocks(add_ref, far_at, row)
    for i in range(4):
        whole[0, i : i + 1, :] = near_mul[i] * far_mul[i]
        whole[1, i : i + 1, :] = far_mul[i] * near_add[i] + far_add[i]
    greet(column_peers(planes) + ([neighbours()[2]] if swaps else []))
    swapped = swap_halves(rows_ref, halves[0], *swaps) if swaps else []

    def copy(d):
        return pltpu.make_async_remote_copy(
            src_ref=whole,
            dst_ref=came.at[d - 1],
            send_sem=send.at[d - 1],
            recv_sem=recv.at[d - 1],
            device_id=(a - d if reverse else a + d, b, n, c),
            device_id_type=MESH,
        )

    def sends(d):
        return a >= d if reverse else a + d < planes

    def receives(d):
        return a + d < planes if reverse else a >= d

    for d in range(1, planes):
        @pl.when(sends(d))
        def _():
            copy(d).start()

    for d in range(1, planes):
        @pl.when(receives(d))
        def _():
            copy(d).wait_recv()

    for i in range(4):
        at = slice(i, i + 1)
        value = came[planes - 2, 1, at, :]
        for d in range(planes - 2, 0, -1):
            value = came[d - 1, 0, at, :] * value + came[d - 1, 1, at, :]
        to_far = near_mul[i] * value + near_add[i]
        for kb in range(2):
            is_far = (b if kb == 0 else 1 - b) == far_at
            at = (i // 2) * 4 + kb * 2 + i % 2
            out_ref[at] = jnp.where(is_far, to_far, value)

    for d in range(1, planes):
        @pl.when(sends(d))
        def _():
            copy(d).wait_send()

    for made in swapped:
        made.wait()


def pass_rows_kernel(reverse, edge_ref, *refs):
    rows_ref, (out_ref, *halves), (leaving, came, send, recv), swaps = split_refs(refs)
    a, b, n, c = places()
    planes = lax.axis_size("a")
    near_at, far_at = (1, 0) if reverse else (0, 1)
    came[...] = jnp.zeros_like(came)
    out_ref[...] = jnp.zeros_like(out_ref)
    first = 0 if reverse else 4
    for i, value in enumerate(earlier_blocks(edge_ref, far_at, first, 4)):
        leaving[i * 4 : i * 4 + 4, :] = value
    greet(column_peers(planes) + ([neighbours()[2]] if swaps else []))
    swapped = swap_halves(rows_ref, halves[0], *swaps) if swaps else []
    copy = pltpu.make_async_remote_copy(
        src_ref=leaving,
        dst_ref=came,
        send_sem=send.at[0],
        recv_sem=recv.at[0],
        device_id=(a - 1 if reverse else a + 1, b, n, c),
        device_id_type=MESH,
    )
    sends = a >= 1 if reverse else a + 1 < planes
    receives = a + 1 < planes if reverse else a >= 1

    @pl.when(sends)
    def _():
        copy.start()

    @pl.when(receives)
    def _():
        copy.wait_recv()

    for i in range(4):
        for kb in range(2):
            is_far = (b if kb == 0 else 1 - b) == far_at
            at = (i // 2) * 4 + kb * 2 + i % 2
            other = (i // 2) * 4 + (1 - kb) * 2 + i % 2
            out_ref[at, first : first + 4, :] = jnp.where(
                is_far, edge_ref[other, first : first + 4, :], came[i * 4 : i * 4 + 4, :]
            )

    @pl.when(sends)
    def _():
        copy.wait_send()

    for made in swapped:
        made.wait()


def pass_along(ident, name, reverse, *edges, halves=None):
    shape = edges[0].shape
    planes = lax.axis_size("a")
    vmem = pl.BlockSpec(memory_space=pltpu.VMEM)
    if len(edges) == 2:
        body, out = pass_state_kernel, (shape[0], 1, shape[2])
        buffers = [(2, 4) + shape[2:], (planes - 1, 2, 4) + shape[2:]]
    else:
        body, out = pass_rows_kernel, shape
        buffers = [(16,) + shape[2:]] * 2
    given, out_shape = list(edges), [jax.ShapeDtypeStruct(out, F32)]
    scratch = [pltpu.VMEM(shape, F32) for shape in buffers]
    scratch += [pltpu.SemaphoreType.DMA((planes - 1,))] * 2
    if halves is not None:
        given.append(halves[0])
        to = (planes, halves[1], halves[0].shape[1])
        out_shape.append(jax.ShapeDtypeStruct(to, BF))
        scratch += [pltpu.SemaphoreType.DMA((planes // 2,))] * 3
    return pl.pallas_call(
        functools.partial(body, reverse),
        in_specs=[vmem] * len(given),
        out_specs=[vmem] * len(out_shape),
        out_shape=out_shape,
        scratch_shapes=scratch,
        compiler_params=pltpu.CompilerParams(
            collective_id=ident, has_side_effects=True, vmem_limit_bytes=VMEM_LIMIT
        ),
        cost_estimate=pl.CostEstimate(flops=0, bytes_accessed=1 << 20, transcendentals=0),
        name=name,
    )(*given)


def norm_product_kernel(tok_ref, w_ref, gain_ref, n_ref, gate_ref, lin_ref, tail_ref, held):
    i = pl.program_id(0)
    rows = tok_ref.shape[1]
    wide = gate_ref.shape[2]
    both = mdot(held[(i + 1) % 2], w_ref[...])
    used = both.shape[1] // 2
    pad = [jnp.zeros((rows, wide - used), F32)] if wide > used else []
    gate_ref[0] = jnp.concatenate([both[:, :used]] + pad, 1)
    low = jnp.concatenate([both[:, used:]] + pad, 1).astype(BF)
    lin_ref[0] = low
    tail_ref[0] = low.astype(F32)[rows - 8 :, :]
    step = min(64, rows)
    for k in range(rows // step):
        at = slice(k * step, (k + 1) * step)
        value = tok_ref[0, at, :].astype(F32)
        factor = lax.rsqrt(jnp.mean(value * value, axis=-1, keepdims=True) + EPS)
        low = (value * factor * gain_ref[...]).astype(BF)
        n_ref[0, at, :] = low
        held[i % 2, at, :] = low


def norm_product(tokens, w, gain, wide):
    blocks, rows, d_model = tokens.shape

    def now(i):
        return (jnp.minimum(i, blocks - 1), 0, 0)

    def last(i):
        return (jnp.maximum(i - 1, 0), 0, 0)

    shapes = [(rows, d_model, BF), (rows, wide, F32), (rows, wide, BF), (8, wide, F32)]
    return pl.pallas_call(
        norm_product_kernel,
        grid=(blocks + 1,),
        in_specs=[
            pl.BlockSpec((1, rows, d_model), now),
            pl.BlockSpec(w.shape, lambda i: (0, 0)),
            pl.BlockSpec(gain.shape, lambda i: (0, 0)),
        ],
        out_specs=[
            pl.BlockSpec((1,) + shape[:2], last if k else now) for k, shape in enumerate(shapes)
        ],
        out_shape=[jax.ShapeDtypeStruct((blocks,) + s[:2], s[2]) for s in shapes],
        scratch_shapes=[pltpu.VMEM((2, rows, d_model), BF)],
        compiler_params=pltpu.CompilerParams(vmem_limit_bytes=VMEM_LIMIT),
        cost_estimate=pl.CostEstimate(flops=0, bytes_accessed=1 << 20, transcendentals=0),
        name="norm_product",
    )(tokens, w, gain)


def row_places(info, rows, nseq):
    i = pl.program_id(0)
    pos = info[i, 0] + lax.broadcasted_iota(jnp.int32, (rows, 1), 0)
    begin = jnp.zeros((rows, 1), jnp.int32) + info[i, 1]
    seg = jnp.zeros((rows, 1), jnp.int32)
    for s in range(1, nseq):
        begin = jnp.where(pos >= info[i, 1 + s], info[i, 1 + s], begin)
        seg = jnp.where(pos >= info[i, 1 + s], s, seg)
    return pos, begin, seg


def inputs_by_tap(ext, lin_ref, rim_ref, conv0_ref, begin_at, seg, taps):
    rows = lin_ref.shape[1]
    back = taps - 1
    ext[0:8, :] = rim_ref[0]
    ext[8 : 8 + rows, :] = lin_ref[0].astype(F32)
    slots = conv0_ref.shape[1]
    column = lax.broadcasted_iota(jnp.int32, (rows, slots), 1)
    found = [ext[8 : 8 + rows, :]]
    for k in range(1, taps):
        hot = (column == seg * back + begin_at - k + back) & (begin_at < k)
        stored = mdot(jnp.where(hot, 1.0, 0.0).astype(BF), conv0_ref[0])
        found.append(jnp.where(begin_at >= k, ext[8 - k : 8 - k + rows, :], stored))
    return found


def run_scan(a_s, b_s, p_ref, s_ref, rows, reverse):
    width = b_s.shape[1]
    groups = rows // 8
    row = lax.broadcasted_iota(jnp.int32, (8, width), 0)
    if reverse:
        row = 7 - row

    def step(i, carry):
        cp, cs = carry
        g = groups - 1 - i if reverse else i
        at = pl.ds(pl.multiple_of(g * 8, 8), 8)
        a, b = a_s[at, :], b_s[at, :]
        for d in (1, 2, 4):
            by = 8 - d if reverse else d
            inside = row >= d
            a_far = jnp.where(inside, pltpu.roll(a, by, 0), 1.0)
            b_far = jnp.where(inside, pltpu.roll(b, by, 0), 0.0)
            b = a * b_far + b
            a = a * a_far
        b = a * cs + b
        a = a * cp
        p_ref[0, at, :] = a
        s_ref[0, at, :] = b
        last = 0 if reverse else 7
        return a[last : last + 1], b[last : last + 1]

    start = (jnp.ones((1, width), F32), jnp.zeros((1, width), F32))
    lax.fori_loop(0, groups, step, start, unroll=4)


V_CBIAS, V_ABIAS, V_IBIAS, V_SOFT = 0, 1, 2, 3


def forward_kernel(
    nseq, taps, info, lin_ref, rim_ref, conv0_ref, state0_ref, wg_ref, vec_ref,
    conv_ref, retain_ref, admit_ref, p_ref, s_ref, pe_ref, se_ref, ext, a_s, b_s,
):
    i = pl.program_id(0)
    rows, wide = lin_ref.shape[1:]
    pos, begin, seg = row_places(info, rows, nseq)
    at = pos - begin

    def vec(k):
        return vec_ref[k : k + 1, :]

    by_tap = inputs_by_tap(ext, lin_ref, rim_ref, conv0_ref, at, seg, taps)
    total = vec(taps + V_CBIAS)
    for k in range(taps):
        total = total + vec(k) * by_tap[k]
    low = total.astype(BF)
    conv_ref[0] = low
    conv = low.astype(F32)
    both = mdot(low, wg_ref[...])
    retain = jax.nn.sigmoid(both[:, :wide] + vec(taps + V_ABIAS))
    admit = jax.nn.sigmoid(both[:, wide:] + vec(taps + V_IBIAS))
    retain_ref[0] = retain
    admit_ref[0] = admit
    a = jnp.exp(-8.0 * retain * vec(taps + V_SOFT))
    mult = jnp.sqrt(jnp.maximum((1.0 - a) * (1.0 + a), FLOOR))
    drive = mult * admit * conv
    for s in range(nseq):
        drive = drive + jnp.where(pos == info[i, 1 + s], a * state0_ref[0, s : s + 1, :], 0.0)
    a_s[...] = jnp.where(at == 0, 0.0, a)
    b_s[...] = drive
    run_scan(a_s, b_s, p_ref, s_ref, rows, False)
    pe_ref[0] = p_ref[0, rows - 8 : rows, :]
    se_ref[0] = s_ref[0, rows - 8 : rows, :]


def gelu_pair(x):
    root = 0.7978845608028654
    inner = root * (x + 0.044715 * (x * x * x))
    th = jnp.tanh(inner)
    cdf = 0.5 * (1.0 + th)
    slope = cdf + 0.5 * x * (1.0 - th * th) * (root * (1.0 + 3.0 * 0.044715 * (x * x)))
    return x * cdf, slope


def ffn_forward_kernel(info, n_ref, w_ref, inner_ref, by_gate_ref, by_up_ref):
    pair = mdot(n_ref[0], w_ref[...])
    hidden = inner_ref.shape[2]
    upward = pair[:, hidden:]
    active, slope = gelu_pair(pair[:, :hidden])
    inner_ref[0] = (active * upward).astype(BF)
    by_gate_ref[0] = (slope * upward).astype(BF)
    by_up_ref[0] = active.astype(BF)


def ffn_back_kernel(info, g_ref, w_ref, by_gate_ref, by_up_ref, *refs):
    out_ref = refs[-1]
    hidden = w_ref.shape[0]
    d_inner = ndot(g_ref[0], w_ref[...])
    out_ref[0, :, :hidden] = (d_inner * by_gate_ref[0].astype(F32)).astype(BF)
    out_ref[0, :, hidden:] = (d_inner * by_up_ref[0].astype(F32)).astype(BF)


def back_scan_kernel(
    nseq, taps, info, dres_ref, wo_ref, gate_ref, hidden_ref, retain_ref, vec_ref, mixed_ref, *refs
):
    dgate_ref, p_ref, s_ref, pe_ref, se_ref, wgrad_ref, ext, a_s, b_s, wgrad = refs[-10:]
    rows = gate_ref.shape[1]
    i = pl.program_id(0)

    @pl.when(i == 0)
    def _():
        wgrad[...] = jnp.zeros_like(wgrad)

    wgrad[...] += tdot(mixed_ref[0], dres_ref[0])

    @pl.when(i == pl.num_programs(0) - 1)
    def _():
        wgrad_ref[...] = wgrad[...].astype(BF)

    pos, begin, _ = row_places(info, rows, nseq)
    d_mixed = ndot(dres_ref[0], wo_ref[...])
    gelu, slope = gelu_pair(gate_ref[0])
    dgate_ref[0] = (d_mixed * hidden_ref[0] * slope).astype(BF)
    b_s[...] = d_mixed * gelu
    soft = vec_ref[taps + V_SOFT : taps + V_SOFT + 1, :]
    a = jnp.where(pos == begin, 0.0, jnp.exp(-8.0 * retain_ref[0] * soft))
    ext[0:rows, :] = a
    ext[rows : rows + 8, :] = jnp.ones((8, a.shape[1]), F32)
    a_s[...] = ext[1 : rows + 1, :]
    run_scan(a_s, b_s, p_ref, s_ref, rows, True)
    pe_ref[0] = ext[0:8, :] * p_ref[0, 0:8, :]
    se_ref[0] = ext[0:8, :] * s_ref[0, 0:8, :]


def back_kernel(
    nseq, taps, length, info, p_ref, s_ref, grad_in_ref, hidden_ref, state_in_ref, state0_ref, conv_ref,
    retain_ref, admit_ref, lin_ref, rim_ref, conv0_ref, wg_ref, vec_ref, sums_o_ref, *refs
):
    dconv_ref, head_ref, late_ref, lasts_ref, ext, wgrad_ref, vgrad_ref = refs[-7:]
    i = pl.program_id(0)
    rows, wide = lin_ref.shape[1:]
    pos, begin, seg = row_places(info, rows, nseq)
    at = pos - begin
    conv_low = conv_ref[0]
    conv = conv_low.astype(F32)
    retain, admit = retain_ref[0], admit_ref[0]
    soft = vec_ref[taps + V_SOFT : taps + V_SOFT + 1, :]
    e = p_ref[0] * grad_in_ref[0, 0:1, :] + s_ref[0]
    ext[0:8, :] = jnp.broadcast_to(state_in_ref[0], (8, wide))
    ext[8 : 8 + rows, :] = hidden_ref[0]
    previous = ext[7 : 7 + rows, :]
    for s in range(nseq):
        previous = jnp.where(pos == info[i, 1 + s], state0_ref[0, s : s + 1, :], previous)
    a = jnp.exp(-8.0 * retain * soft)
    spread = (1.0 - a) * (1.0 + a)
    mult = jnp.sqrt(jnp.maximum(spread, FLOOR))
    d_mult = e * admit * conv
    d_spread = jnp.where(spread > FLOOR, d_mult * 0.5 / mult, 0.0)
    d_log = e * previous * a - 2.0 * a * a * d_spread
    d_rate = (d_log * (-8.0 * soft) * retain * (1.0 - retain)).astype(BF)
    d_inflow = (e * mult * conv * admit * (1.0 - admit)).astype(BF)
    d_gates = jnp.concatenate([d_rate, d_inflow], 1)
    d_conv = e * mult * admit + ndot(d_gates, wg_ref[...])
    low = d_conv.astype(BF)
    dconv_ref[0] = low
    low = low.astype(F32)
    head_ref[0] = low[0:8, :]

    @pl.when(i == 0)
    def _():
        wgrad_ref[...] = jnp.zeros_like(wgrad_ref)
        vgrad_ref[...] = jnp.zeros_like(vgrad_ref)

    wgrad_ref[...] += tdot(conv_low, d_gates)
    sums = [low * v for v in inputs_by_tap(ext, lin_ref, rim_ref, conv0_ref, at, seg, taps)]
    sums += [low, d_rate.astype(F32), d_inflow.astype(F32), d_log * (-8.0 * retain)]
    for k, value in enumerate(sums):
        vgrad_ref[k : k + 1, :] += jnp.sum(value, axis=0, keepdims=True)

    slots = lasts_ref.shape[1]
    column = lax.broadcasted_iota(jnp.int32, (1, slots), 1)
    wanted = jnp.full((1, slots), -1, jnp.int32)
    for q in range(nseq):
        end = (info[i, 2 + q] if q + 1 < nseq else length) - 1
        wanted = jnp.where(column == q, end, wanted)
        for j in range(taps - 1):
            wanted = jnp.where(column == nseq + q * (taps - 1) + j, end - (taps - 2) + j, wanted)
    hot = jnp.where(pos == wanted, 1.0, 0.0).astype(BF)
    states, convs = tdot(hot, hidden_ref[0].astype(BF)), tdot(hot, lin_ref[0])
    row = lax.broadcasted_iota(jnp.int32, states.shape, 0)
    lasts_ref[0] = jnp.where(row < nseq, states, convs).astype(BF)

    @pl.when(i == pl.num_programs(0) - 1)
    def _():
        used = late_ref.shape[0]
        before = sums_o_ref.shape[1]
        late_ref[:, :before] = sums_o_ref[:used, :]
        head_w = (late_ref.shape[1] - before - len(sums)) // 2
        last = len(sums) - 1
        vgrad_ref[last : last + 1, :] *= vec_ref[last + 1 : last + 2, :]
        count = vgrad_ref.shape[0]
        row = lax.broadcasted_iota(jnp.int32, (count, count), 0)
        column = lax.broadcasted_iota(jnp.int32, (count, count), 1)
        eye = jnp.where(row == column, 1.0, 0.0).astype(BF)
        turned = tdot(vgrad_ref[...].astype(BF), eye)
        for h in range(used // head_w):
            at = slice(h * head_w, (h + 1) * head_w)
            parts = [wgrad_ref[at, o + h * head_w : o + (h + 1) * head_w] for o in (0, wide)]
            parts.append(turned[at, : len(sums)])
            late_ref[at, before:] = jnp.concatenate(parts, 1).astype(BF)


def back_conv_kernel(nseq, taps, info, dconv_ref, rim_ref, dgate_ref, vec_ref, *refs):
    out_ref, ext = refs[-2:]
    i = pl.program_id(0)
    rows, wide = dconv_ref.shape[1:]
    pos = info[i, 0] + lax.broadcasted_iota(jnp.int32, (rows, 1), 0)
    ext[0:rows, :] = dconv_ref[0].astype(F32)
    ext[rows : rows + 8, :] = rim_ref[0]
    total = vec_ref[0:1, :] * ext[0:rows, :]
    for k in range(1, taps):
        cut = jnp.zeros((rows, 1), jnp.int32)
        for s in range(nseq):
            start = info[i, 1 + s]
            cut = jnp.where((pos < start) & (pos + k >= start), 1, cut)
        total = total + vec_ref[k : k + 1, :] * jnp.where(cut == 0, ext[k : k + rows, :], 0.0)
    used = out_ref.shape[2] // 2
    both = [dgate_ref[0].astype(F32)[:, :used], total[:, :used]]
    out_ref[0] = jnp.concatenate(both, 1).astype(BF)


def by_block(body, info, ins, outs, scratch, done=(), name=None):
    blocks = info.shape[0]

    def spec(shape, blocked):
        zeros = (0,) * (len(shape) - 1)
        if blocked:
            return pl.BlockSpec((1,) + tuple(shape[1:]), lambda i, *_: (i,) + zeros)
        return pl.BlockSpec(tuple(shape), lambda i, *_: (0,) + zeros)

    hbm = pl.BlockSpec(memory_space=pl.ANY)
    return pl.pallas_call(
        body,
        grid_spec=pltpu.PrefetchScalarGridSpec(
            num_scalar_prefetch=1,
            grid=(blocks,),
            in_specs=[spec(v.shape, blocked) for v, blocked in ins] + [hbm] * len(done),
            out_specs=[spec(shape, blocked) for shape, _, blocked in outs],
            scratch_shapes=[pltpu.VMEM(shape, F32) for shape in scratch],
        ),
        out_shape=[jax.ShapeDtypeStruct(shape, kind) for shape, kind, _ in outs],
        compiler_params=pltpu.CompilerParams(vmem_limit_bytes=VMEM_LIMIT),
        cost_estimate=pl.CostEstimate(flops=0, bytes_accessed=1 << 20, transcendentals=0),
        name=name,
    )(info, *[v for v, _ in ins], *done)


def on_device(
    tokens,
    starts,
    init_state,
    init_conv,
    w_y,
    w_x,
    gate_a,
    gate_i,
    w_out,
    norm1_gain,
    conv_kernel,
    conv_bias,
    bias_a,
    bias_i,
    decay_param,
    w_gate,
    w_up,
    w_down,
    norm2_gain,
    cotangent,
):
    planes, count = lax.axis_size("a"), chips()
    a, b, n, c = (lax.axis_index(name) for name in ("a", "b", "n", "c"))
    u = chip()
    nn = count // 2
    rows, d_model = tokens.shape[1], tokens.shape[2]
    nseq = starts.shape[1]
    width = w_y.shape[1]
    head_w = gate_a.shape[1]
    half = gate_a.shape[0]
    taps = conv_kernel.shape[0]
    back = taps - 1
    heads_here = planes // 2
    wide_here = heads_here * head_w
    wp = -(-wide_here // 128) * 128
    hid = w_down.shape[0]
    drows = w_y.shape[0]
    nblocks = 2 * count

    def gather_a(value):
        return lax.all_gather(value, "a", axis=0, tiled=True)

    def scatter_a(value):
        return lax.psum_scatter(value, "a", scatter_dimension=0, tiled=True)

    def padded(v, axis=-1):
        pads = [(0, 0)] * v.ndim
        pads[axis] = (0, wp - wide_here)
        return jnp.pad(v, pads)

    vectors = jnp.concatenate(
        [conv_kernel, conv_bias[None], bias_a[None], bias_i[None], decay_param[None]], 0
    ).reshape(-1)
    vectors = jnp.concatenate([vectors, norm1_gain, norm2_gain]).astype(F32)
    lanes = -(-vectors.shape[0] // 1024) * 128
    vectors = jnp.pad(vectors, (0, 8 * lanes - vectors.shape[0])).reshape(8, lanes)
    at_start = jnp.concatenate([init_state[0][:, None], init_conv[0].astype(F32)], 1)
    at_start = at_start.reshape(nseq * taps, width)
    at_start = jnp.pad(at_start, ((0, 8), (0, 0)))
    at_start = at_start.at[nseq * taps, :nseq].set(starts[0].astype(F32))
    all_tokens, w_yx, w_gu, _, gate_rows, canon, at_start = start_exchange(
        tokens[0],
        w_y,
        w_x,
        w_gate,
        w_up,
        jnp.concatenate([gate_a, gate_i], 1),
        vectors,
        at_start,
    )
    w_yx = w_yx.reshape(d_model, 2 * wide_here)
    w_gu = gather_a(w_gu.reshape(-1, 2 * planes * hid))
    gate_rows = gate_rows.reshape(wide_here, -1)

    def join_halves(mine_all):
        away = swap_c(lax.dynamic_slice_in_dim(mine_all, (1 - c) * heads_here, heads_here, 0))
        own = lax.dynamic_slice_in_dim(mine_all, c * heads_here, heads_here, 0)
        first = jnp.where(c == 0, own, away)
        second = jnp.where(c == 0, away, own)
        return jnp.stack([first, second], 1).reshape((wide_here,) + mine_all.shape[2:])


    w_o = padded(join_halves(gather_a(w_out).reshape(planes, half, d_model)), 0)

    def block_diagonal(m):
        m = m.reshape(heads_here, head_w, head_w)
        eye = jnp.eye(heads_here, dtype=m.dtype)
        full = (m[:, :, None, :] * eye[:, None, :, None]).reshape(wide_here, wide_here)
        return padded(padded(full), 0)

    w_gates = jnp.concatenate(
        [
            block_diagonal(gate_rows[:, :head_w]),
            block_diagonal(gate_rows[:, head_w:]),
        ],
        1,
    )

    w_d = gather_a(w_down)
    f_here = planes * hid

    canon = canon.reshape(planes * nblocks, -1)
    nvec = (taps + 4) * half
    gain_one = canon[:, nvec : nvec + drows].reshape(-1)
    gain_two = canon[:, nvec + drows : nvec + 2 * drows].reshape(-1)
    mine = pick(canon[:, :nvec].reshape(2, heads_here, count, 2, taps + 4, half), c)
    mine = pick(mine, u, 1).transpose(2, 0, 1, 3).reshape(taps + 4, wide_here)
    decay_f = mine[taps + 3]
    vec = [mine[: taps + 3], jax.nn.softplus(decay_f)[None], jax.nn.sigmoid(decay_f)[None]]
    vec = padded(jnp.concatenate(vec))

    def my_channels(v):
        lead = v.shape[:-1]
        v = v.reshape(lead + (2, heads_here, count, head_w))
        v = pick(v, c, len(lead))
        return pick(v, u, len(lead) + 1).reshape(lead + (wide_here,))

    streams = 2 * nn
    at_start = at_start.reshape(streams, -1, width)
    offsets = at_start[:, nseq * taps, :nseq].astype(jnp.int32)
    at_start = my_channels(at_start[:, : nseq * taps].reshape(streams, nseq, taps, width))
    at_start = padded(at_start)
    state_0 = jnp.pad(at_start[:, :, 0], ((0, 0), (0, -nseq % 8), (0, 0)))
    conv_0 = at_start[:, :, 1:].reshape(streams, nseq * back, wp).astype(BF)
    conv_0 = jnp.pad(conv_0, ((0, 0), (0, -(nseq * back) % 16), (0, 0)))

    def per_block(v):
        v = v.reshape((2, 1, nn) + v.shape[1:])
        return jnp.broadcast_to(v, (2, 2, nn) + v.shape[3:]).reshape((nblocks,) + v.shape[3:])

    block_b = (jnp.arange(nblocks, dtype=jnp.int32) // nn) % 2
    first_row = (a * 2 + (b ^ block_b)) * rows
    position = first_row[:, None] + jnp.arange(rows, dtype=jnp.int32)[None]
    off_b = per_block(offsets)

    info = jnp.concatenate(
        [first_row[:, None], off_b, jnp.zeros((nblocks, -(nseq + 1) % 8), jnp.int32)], 1
    )

    grad_low = cotangent[0]
    grads = [grad_low] + [xor_u(grad_low, k) for k in range(1, count)]

    edge = ((nblocks, 8, wp), F32, True)
    normed, gate_in, linear, tail = norm_product(all_tokens, w_yx, gain_one[None], wp)
    normed = normed.reshape(nblocks * rows, d_model)

    def two(v):
        return v.reshape((2, 2, nn) + v.shape[1:])

    rim = pass_along(6, "pass_rows", False, tail)[0]
    conv_0b, state_0b = per_block(conv_0), per_block(state_0)
    full = (nblocks, rows, wp)
    conv_low, retain, admit, carry_mul, carry_add, end_mul, end_add = by_block(
        functools.partial(forward_kernel, nseq, taps),
        info,
        [
            (linear, True), (rim, True), (conv_0b, True), (state_0b, True),
            (w_gates, False), (vec, False),
        ],
        [
            (full, BF, True), (full, F32, True), (full, F32, True),
            (full, F32, True), (full, F32, True), edge, edge,
        ],
        [(rows + 8, wp), (rows, wp), (rows, wp)],
        name="mixer_forward",
    )

    (end_mul, end_add), grads = lax.optimization_barrier(((end_mul, end_add), grads))
    state_in = pass_along(7, "pass_state", False, end_mul, end_add)[0]
    hidden = carry_mul * state_in + carry_add
    mixed_in = (hidden * jax.nn.gelu(gate_in)).astype(BF).reshape(-1, wp)
    resid, normed_two, grads = plane_reduce(
        2, "fwd", False, (mixed_in.reshape(2, count, rows, -1),), w_o, gain_two, tokens[0],
        tokens[0], grads,
    )
    normed_two = normed_two.reshape(nblocks * rows, d_model)
    grads = grads.reshape(nblocks * rows, d_model)

    hid_full = (nblocks, rows, f_here)
    inner, by_gate, by_up = by_block(
        ffn_forward_kernel,
        info,
        [(normed_two.reshape(nblocks, rows, d_model), True), (w_gu, False)],
        [(hid_full, BF, True)] * 3,
        [],
        name="ffn_forward",
    )
    inner = inner.reshape(nblocks * rows, f_here)
    cut = d_model * 3 // 8
    sums_d = tdot(inner, grads).astype(BF)
    first_d, second_d = sums_d[:, :cut], sums_d[:, cut:]
    sent_d = scatter_a(first_d), scatter_a(second_d)
    d_pair = by_block(
        ffn_back_kernel,
        info,
        [
            (grads.reshape(nblocks, rows, d_model), True), (w_d, False), (by_gate, True),
            (by_up, True),
        ],
        [((nblocks, rows, 2 * f_here), BF, True)],
        [],
        (sums_d,),
        name="ffn_back",
    )[0]
    sums_gu = tdot(normed_two, d_pair.reshape(nblocks * rows, -1)).astype(BF)
    sent_gu = scatter_a(sums_gu)
    d_resid, d_resid_low, *low = plane_reduce(
        3, "mid", True, (d_pair.reshape(2, count, rows, -1),), w_gu,
        gain_two, grad_low, resid, (inner.reshape(2, count, rows, f_here), w_d), (sent_d[0], sums_gu),
    )
    d_resid_low = d_resid_low.reshape(nblocks * rows, d_model)

    result = resid + low[0].astype(F32)
    for k in range(1, count):
        result = result + xor_u(low[k], k).astype(F32)
    result = result.astype(BF)

    d_gate_in, back_mul, back_add, end_mul, end_add, sums_o = by_block(
        functools.partial(back_scan_kernel, nseq, taps),
        info,
        [
            (d_resid_low.reshape(nblocks, rows, d_model), True), (w_o, False), (gate_in, True),
            (hidden, True), (retain, True), (vec, False), (mixed_in.reshape(full), True),
        ],
        [
            (full, BF, True), (full, F32, True), (full, F32, True), edge, edge,
            ((wp, d_model), BF, False),
        ],
        [(rows + 8, wp), (rows, wp), (rows, wp), (wp, d_model)],
        (sent_d[1],),
        name="mixer_back_scan",
    )
    grad_in = pass_along(8, "pass_state_back", True, end_mul, end_add)[0]
    d_conv_low, head, late, lasts = by_block(
        functools.partial(back_kernel, nseq, taps, planes * 2 * rows),
        info,
        [
            (back_mul, True), (back_add, True), (grad_in, True), (hidden, True),
            (state_in, True), (state_0b, True), (conv_low, True), (retain, True),
            (admit, True), (linear, True), (rim, True), (conv_0b, True), (w_gates, False), (vec, False),
            (sums_o, False),
        ],
        [
            (full, BF, True), edge, ((wide_here, d_model + 2 * head_w + taps + 4), BF, False),
            ((nblocks, nseq * taps, wp), BF, True),
        ],
        [(rows + 8, wp), (wp, 2 * wp), (taps + 4, wp)],
        (),
        name="mixer_back",
    )

    rim_back, late = pass_along(9, "pass_rows_back", True, head, halves=(late, half))
    d_both = by_block(
        functools.partial(back_conv_kernel, nseq, taps),
        info,
        [(d_conv_low, True), (rim_back, True), (d_gate_in, True), (vec, False)],
        [((nblocks, rows, 2 * wide_here), BF, True)],
        [(rows + 8, wp)],
        (result, sent_gu),
        name="mixer_back_conv",
    )[0]
    late = scatter_a(late.reshape(planes * half, -1))
    sums_yx = tdot(normed, d_both.reshape(nblocks * rows, 2 * wide_here)).astype(BF)
    input_grad, pieces, lasts = plane_reduce(
        4, "last", True, (d_both.reshape(2, count, rows, -1),), w_yx, gain_one, tokens[0], d_resid,
        (sent_gu,), (sums_yx,), lasts,
    )
    gain_shape = ((1, drows), F32)
    (
        grad_wg, grad_wu, grad_gain_two, grad_wo, grad_wa, grad_wi, final_state, final_conv,
        grad_taps, *vec_grads,
    ) = in_place(
        functools.partial(order_hidden_kernel, hid, head_w),
        (pieces, w_gate, w_up, norm2_gain.astype(F32)[None], late, lasts),
        [
            (w_gate.shape, F32), (w_up.shape, F32), gain_shape, (w_out.shape, F32),
            (gate_a.shape, F32), (gate_i.shape, F32), ((nseq, width), F32),
            ((nseq * back, width), BF), ((taps, half), F32),
        ]
        + [((1, half), F32)] * 4,
        "order_hidden",
    )
    pieces = finish(scatter_a(sums_yx), (grad_wg,))
    grad_wy, grad_wx, grad_gain_one = in_place(
        functools.partial(order_heads_kernel, head_w),
        (pieces, w_y, w_x, norm1_gain.astype(F32)[None]),
        [(w_y.shape, F32), (w_x.shape, F32), gain_shape],
        "order_heads",
    )
    grad_gain_one, grad_gain_two = grad_gain_one[0], grad_gain_two[0]
    final_conv = final_conv.reshape(nseq, back, width)

    return (
        result[None],
        input_grad[None],
        final_state[None],
        final_conv[None],
        grad_wy,
        grad_wx,
        grad_wa,
        grad_wi,
        grad_wo,
        grad_gain_one,
        grad_taps,
        *[v[0] for v in vec_grads],
        grad_wg,
        grad_wu,
        jnp.concatenate(sent_d, 1).astype(F32),
        grad_gain_two,
    )


WIDE = ("a", "b")
EVERY = ("a", "b", "n", "c")
HIGH = lax.Precision.HIGHEST


def passed_along(value, axis, by):
    size = lax.axis_size(axis)
    pairs = [(i, i + by) for i in range(size) if 0 <= i + by < size]
    return lax.ppermute(value, axis, pairs)


def entering(value, axis, combine, identity, reverse):
    size, place = (lax.axis_size(axis), lax.axis_index(axis))
    everything = jax.tree.map(lambda part: lax.all_gather(part, axis), value)
    start = jax.tree.map(
        lambda part, zero: jnp.broadcast_to(jnp.asarray(zero, part.dtype), part.shape),
        value,
        identity,
    )

    def hop(k, before):
        at = size - 1 - k if reverse else k
        reached = at > place if reverse else at < place
        new = combine(before, jax.tree.map(lambda part: part[at], everything))
        return jax.tree.map(lambda a, b: jnp.where(reached, a, b), new, before)

    return lax.fori_loop(0, size, hop, start)


def merged_2(value, axis, combine):
    everything = jax.tree.map(
        lambda part, kind: lax.all_gather(part.astype(kind), axis),
        value,
        jax.tree.map(lambda a: jnp.bfloat16 if a.dtype == jnp.float32 else a.dtype, value),
    )

    def take(k):
        return jax.tree.map(lambda part, own: part[k].astype(own.dtype), everything, value)

    return lax.fori_loop(
        1, lax.axis_size(axis), lambda k, so_far: combine(so_far, take(k)), take(0)
    )


def link(earlier, later):
    return (earlier[0] * later[0], later[0] * earlier[1] + later[1])


def norm_back(value, factor, gain, grad):
    weighted = grad * gain
    inner = jnp.mean(weighted * value, axis=-1, keepdims=True)
    return (
        factor * weighted - value * factor * factor * factor * inner,
        jnp.sum(grad * value * factor, axis=0),
    )


def later_one(first, second):
    pick = first[0] > second[0]
    return (
        jnp.where(pick, first[0], second[0]),
        jnp.where(pick[:, None], first[1], second[1]),
        jnp.where(pick[:, None, None], first[2], second[2]),
    )


def on_device_any(
    tokens,
    starts,
    init_state,
    init_conv,
    w_y,
    w_x,
    gate_a,
    gate_i,
    w_out,
    norm1_gain,
    conv_kernel,
    conv_bias,
    bias_a,
    bias_i,
    decay_param,
    w_gate,
    w_up,
    w_down,
    norm2_gain,
    cotangent,
):
    inputs = tokens[0].astype(jnp.float32)
    offsets = starts[0]
    nseqs = offsets.shape[0]
    rows_here = inputs.shape[0]
    width = w_y.shape[1]
    head_w = gate_a.shape[1]
    heads = width // head_w
    place = lax.axis_index(WIDE)
    mixer = (
        lax.all_gather(w_y, EVERY, axis=0, tiled=True),
        lax.all_gather(w_x, EVERY, axis=0, tiled=True),
        lax.all_gather(gate_a, EVERY, axis=0, tiled=True),
        lax.all_gather(gate_i, EVERY, axis=0, tiled=True),
        lax.all_gather(w_out, EVERY, axis=0, tiled=True),
        lax.all_gather(norm1_gain, EVERY, axis=0, tiled=True),
        lax.all_gather(conv_kernel, EVERY, axis=1, tiled=True),
        lax.all_gather(conv_bias, EVERY, axis=0, tiled=True),
        lax.all_gather(bias_a, EVERY, axis=0, tiled=True),
        lax.all_gather(bias_i, EVERY, axis=0, tiled=True),
        lax.all_gather(decay_param, EVERY, axis=0, tiled=True),
    )
    wy_full, wx_full, wa_full, wi_full, wo_full, gain_one, kernel, cbias, abias, ibias, decay = (
        mixer
    )
    gain_one = gain_one.astype(jnp.float32)
    kernel = kernel.astype(jnp.float32)
    taps = kernel.shape[0]
    back = taps - 1
    position = place * rows_here + jnp.arange(rows_here, dtype=jnp.int32)

    def segment_of(where_at):
        return jnp.sum((where_at[:, None] >= offsets[None, :]).astype(jnp.int32), axis=1) - 1

    segment = segment_of(position)
    member = segment[:, None] == jnp.arange(nseqs, dtype=jnp.int32)[None, :]
    begin = jnp.sum(jnp.where(member, offsets[None, :], 0), axis=1)
    opening = (position == begin)[:, None]
    scale_one = lax.rsqrt(jnp.mean(inputs * inputs, axis=-1, keepdims=True) + EPS)
    normed = (inputs * scale_one * gain_one).astype(jnp.bfloat16)
    gate_in = mdot(normed, wy_full)
    linear = mdot(normed, wx_full).astype(jnp.bfloat16)
    rim_rows = passed_along(linear[rows_here - back :], WIDE, 1)
    extended = jnp.concatenate([rim_rows, linear], 0)
    stored = mdot(member.astype(jnp.bfloat16), init_conv[0].reshape(nseqs, back * width)).reshape(
        rows_here, back, width
    )
    inputs_by_tap = [linear.astype(jnp.float32)]
    for shift_by in range(1, taps):
        earlier = extended[back - shift_by : back - shift_by + rows_here].astype(jnp.float32)
        offset = position - shift_by - begin
        from_start = jnp.zeros((rows_here, width), jnp.float32)
        for slot in range(back):
            from_start = from_start + jnp.where(
                (offset + back == slot)[:, None], stored[:, slot], 0.0
            )
        inputs_by_tap.append(jnp.where((offset >= 0)[:, None], earlier, from_start))
    conv_sum = cbias.astype(jnp.float32)
    for shift_by in range(taps):
        conv_sum = conv_sum + kernel[shift_by] * inputs_by_tap[shift_by]
    conv_low = conv_sum.astype(jnp.bfloat16)
    conv_val = conv_low.astype(jnp.float32)
    blocks = conv_low.reshape(rows_here, heads, head_w)
    wa_heads = wa_full.reshape(heads, head_w, head_w)
    wi_heads = wi_full.reshape(heads, head_w, head_w)
    rate = jnp.einsum("thi,hij->thj", blocks, wa_heads, preferred_element_type=jnp.float32).reshape(
        rows_here, width
    ) + abias.astype(jnp.float32)
    inflow = jnp.einsum(
        "thi,hij->thj", blocks, wi_heads, preferred_element_type=jnp.float32
    ).reshape(rows_here, width) + ibias.astype(jnp.float32)
    retain = jax.nn.sigmoid(rate)
    admit = jax.nn.sigmoid(inflow)
    decay_f = decay.astype(jnp.float32)
    soft_decay = jax.nn.softplus(decay_f)
    log_a = -8.0 * retain * soft_decay
    decay_now = jnp.exp(log_a)
    spread = -jnp.expm1(2.0 * log_a)
    mult = jnp.sqrt(jnp.maximum(spread, FLOOR))
    drive = mult * admit * conv_val
    state_rows = jnp.dot(member.astype(jnp.float32), init_state[0], precision=HIGH)
    a_used = jnp.where(opening, 0.0, decay_now)
    b_used = jnp.where(opening, decay_now * state_rows + drive, drive)
    carry_mul, carry_add = lax.associative_scan(link, (a_used, b_used), axis=0)
    identity = (jnp.ones((width,), jnp.float32), jnp.zeros((width,), jnp.float32))
    state_in = entering(
        (carry_mul[rows_here - 1], carry_add[rows_here - 1]), WIDE, link, identity, False
    )[1]
    hidden = carry_mul * state_in + carry_add
    gelu_y, gelu_y_back = jax.vjp(jax.nn.gelu, gate_in)
    mixed_in = (hidden * gelu_y).astype(jnp.bfloat16)
    resid = inputs + mdot(mixed_in, wo_full)
    wg_full, wu_full, wd_full, gain_two = (
        lax.all_gather(w_gate, EVERY, axis=0, tiled=True),
        lax.all_gather(w_up, EVERY, axis=0, tiled=True),
        lax.all_gather(w_down, EVERY, axis=0, tiled=True),
        lax.all_gather(norm2_gain, EVERY, axis=0, tiled=True),
    )
    gain_two = gain_two.astype(jnp.float32)
    scale_two = lax.rsqrt(jnp.mean(resid * resid, axis=-1, keepdims=True) + EPS)
    normed_two = (resid * scale_two * gain_two).astype(jnp.bfloat16)
    gate = mdot(normed_two, wg_full)
    upward = mdot(normed_two, wu_full)
    active, gate_back = jax.vjp(jax.nn.gelu, gate)
    inner = (active * upward).astype(jnp.bfloat16)
    result = (resid + mdot(inner, wd_full)).astype(jnp.bfloat16)
    local_rows = jnp.arange(rows_here, dtype=jnp.int32)
    last_row = jnp.max(jnp.where(member, local_rows[:, None], -1), axis=0)
    present = last_row >= 0
    safe_row = jnp.maximum(last_row, 0)
    marker = jnp.where(present, (place * rows_here + last_row).astype(jnp.float32), -1.0)
    state_last = jnp.where(present[:, None], hidden[safe_row], 0.0)
    conv_rows = extended[safe_row[:, None] + 1 + jnp.arange(back, dtype=jnp.int32)[None, :]].astype(
        jnp.float32
    )
    conv_last = jnp.where(present[:, None, None], conv_rows, 0.0)
    merged = merged_2((marker, state_last, conv_last), WIDE, later_one)
    wg_back, wu_back, wd_back = (
        lax.all_gather(w_gate, EVERY, axis=0, tiled=True),
        lax.all_gather(w_up, EVERY, axis=0, tiled=True),
        lax.all_gather(w_down, EVERY, axis=0, tiled=True),
    )
    grad_low = cotangent[0]
    grad_out = grad_low.astype(jnp.float32)
    d_inner = ndot(grad_low, wd_back)
    grad_wd = tdot(inner, grad_low)
    d_gate = gate_back(d_inner * upward)[0].astype(jnp.bfloat16)
    d_up = (d_inner * active).astype(jnp.bfloat16)
    grad_wg = tdot(normed_two, d_gate)
    grad_wu = tdot(normed_two, d_up)
    d_normed_two = ndot(d_gate, wg_back) + ndot(d_up, wu_back)
    d_resid_norm, grad_gain_two = norm_back(resid, scale_two, gain_two, d_normed_two)
    d_resid = grad_out + d_resid_norm
    wy_back, wx_back, wa_back, wi_back, wo_back = (
        lax.all_gather(w_y, EVERY, axis=0, tiled=True),
        lax.all_gather(w_x, EVERY, axis=0, tiled=True),
        lax.all_gather(gate_a, EVERY, axis=0, tiled=True),
        lax.all_gather(gate_i, EVERY, axis=0, tiled=True),
        lax.all_gather(w_out, EVERY, axis=0, tiled=True),
    )
    d_resid_low = d_resid.astype(jnp.bfloat16)
    d_mixed = ndot(d_resid_low, wo_back)
    grad_wo = tdot(mixed_in, d_resid_low)
    d_hidden = d_mixed * gelu_y
    d_gate_in = gelu_y_back(d_mixed * hidden)[0].astype(jnp.bfloat16)
    forward_mul = jnp.concatenate([a_used[1:], jnp.ones((1, width), jnp.float32)], 0)
    back_mul, back_add = lax.associative_scan(link, (forward_mul, d_hidden), reverse=True, axis=0)
    head_map = (a_used[0] * back_mul[0], a_used[0] * back_add[0])
    grad_in = entering(head_map, WIDE, link, identity, True)[1]
    total_grad = back_mul * grad_in + back_add
    previous = jnp.concatenate([state_in[None], hidden[:-1]], 0)
    previous = jnp.where(opening, state_rows, previous)
    d_decay = total_grad * previous
    d_mult = total_grad * admit * conv_val
    d_admit = total_grad * mult * conv_val
    d_conv = total_grad * mult * admit
    d_spread = jnp.where(spread > FLOOR, d_mult * 0.5 / mult, 0.0)
    d_log = d_decay * decay_now - 2.0 * decay_now * decay_now * d_spread
    d_retain = d_log * (-8.0 * soft_decay)
    grad_decay = jnp.sum(d_log * (-8.0 * retain), axis=0) * jax.nn.sigmoid(decay_f)
    d_rate = (d_retain * retain * (1.0 - retain)).astype(jnp.bfloat16)
    d_inflow = (d_admit * admit * (1.0 - admit)).astype(jnp.bfloat16)
    grad_abias = jnp.sum(d_rate.astype(jnp.float32), axis=0)
    grad_ibias = jnp.sum(d_inflow.astype(jnp.float32), axis=0)
    rate_heads = d_rate.reshape(rows_here, heads, head_w)
    inflow_heads = d_inflow.reshape(rows_here, heads, head_w)
    grad_wa = jnp.einsum(
        "thi,thj->hij", blocks, rate_heads, preferred_element_type=jnp.float32
    ).reshape(width, head_w)
    grad_wi = jnp.einsum(
        "thi,thj->hij", blocks, inflow_heads, preferred_element_type=jnp.float32
    ).reshape(width, head_w)
    d_conv = d_conv + jnp.einsum(
        "thj,hij->thi",
        rate_heads,
        wa_back.reshape(heads, head_w, head_w),
        preferred_element_type=jnp.float32,
    ).reshape(rows_here, width)
    d_conv = d_conv + jnp.einsum(
        "thj,hij->thi",
        inflow_heads,
        wi_back.reshape(heads, head_w, head_w),
        preferred_element_type=jnp.float32,
    ).reshape(rows_here, width)
    d_conv_low = d_conv.astype(jnp.bfloat16)
    d_conv_val = d_conv_low.astype(jnp.float32)
    rim_back = passed_along(d_conv_low[:back], WIDE, -1)
    ahead = jnp.concatenate([d_conv_low, rim_back], 0)
    d_linear = kernel[0] * d_conv_val
    kernel_grads = [jnp.sum(d_conv_val * inputs_by_tap[0], axis=0)]
    for shift_by in range(1, taps):
        later_rows = ahead[shift_by : shift_by + rows_here].astype(jnp.float32)
        same = (segment_of(position + shift_by) == segment)[:, None]
        d_linear = d_linear + kernel[shift_by] * jnp.where(same, later_rows, 0.0)
        kernel_grads.append(jnp.sum(d_conv_val * inputs_by_tap[shift_by], axis=0))
    grad_kernel = jnp.stack(kernel_grads, 0)
    grad_cbias = jnp.sum(d_conv_val, axis=0)
    d_linear_low = d_linear.astype(jnp.bfloat16)
    d_normed = ndot(d_gate_in, wy_back) + ndot(d_linear_low, wx_back)
    grad_wy = tdot(normed, d_gate_in)
    grad_wx = tdot(normed, d_linear_low)
    d_input_norm, grad_gain_one = norm_back(inputs, scale_one, gain_one, d_normed)
    input_grad = (d_resid + d_input_norm).astype(jnp.bfloat16)
    every_sum = (
        lax.psum_scatter(grad_wy, EVERY, scatter_dimension=0, tiled=True),
        lax.psum_scatter(grad_wx, EVERY, scatter_dimension=0, tiled=True),
        lax.psum_scatter(grad_wa, EVERY, scatter_dimension=0, tiled=True),
        lax.psum_scatter(grad_wi, EVERY, scatter_dimension=0, tiled=True),
        lax.psum_scatter(grad_wo, EVERY, scatter_dimension=0, tiled=True),
        lax.psum_scatter(grad_gain_one, EVERY, scatter_dimension=0, tiled=True),
        lax.psum_scatter(grad_kernel, EVERY, scatter_dimension=1, tiled=True),
        lax.psum_scatter(grad_cbias, EVERY, scatter_dimension=0, tiled=True),
        lax.psum_scatter(grad_abias, EVERY, scatter_dimension=0, tiled=True),
        lax.psum_scatter(grad_ibias, EVERY, scatter_dimension=0, tiled=True),
        lax.psum_scatter(grad_decay, EVERY, scatter_dimension=0, tiled=True),
        lax.psum_scatter(grad_wg, EVERY, scatter_dimension=0, tiled=True),
        lax.psum_scatter(grad_wu, EVERY, scatter_dimension=0, tiled=True),
        lax.psum_scatter(grad_wd, EVERY, scatter_dimension=0, tiled=True),
        lax.psum_scatter(grad_gain_two, EVERY, scatter_dimension=0, tiled=True),
    )
    mixer_sums = every_sum[:11]
    mlp_sums = every_sum[11:]
    return (
        result[None],
        input_grad[None],
        merged[1][None],
        merged[2].astype(jnp.bfloat16)[None],
        mixer_sums[0],
        mixer_sums[1],
        mixer_sums[2],
        mixer_sums[3],
        mixer_sums[4],
        mixer_sums[5],
        mixer_sums[6],
        mixer_sums[7],
        mixer_sums[8],
        mixer_sums[9],
        mixer_sums[10],
        mlp_sums[0],
        mlp_sums[1],
        mlp_sums[2],
        mlp_sums[3],
    )


def solution(mesh):
    wide, narrow = mesh.shape["wide"], mesh.shape["narrow"]
    def plan(*args):
        fits = args[6].shape[0] * 2 == args[6].shape[1] and narrow == 4
        return (on_device if fits else on_device_any)(*args)

    fine = Mesh(mesh.devices.reshape(wide // 2, 2, narrow // 2, 2), ("a", "b", "n", "c"))
    w, s = ("a", "b"), ("n", "c")
    everywhere = ("a", "b", "n", "c")
    acts, rows, vec = P(s, w, None), P(everywhere, None), P(everywhere)
    return jax.shard_map(
        plan,
        mesh=fine,
        in_specs=(
            acts,
            P(s, None),
            P(s, None, None),
            P(s, None, None, None),
            rows, rows, rows, rows, rows,
            vec,
            P(None, everywhere),
            vec, vec, vec, vec,
            rows, rows, rows,
            vec,
            acts,
        ),
        out_specs=(
            acts,
            acts,
            P(s, None, None),
            P(s, None, None, None),
            rows, rows, rows, rows, rows,
            vec,
            P(None, everywhere),
            vec, vec, vec, vec,
            rows, rows, rows,
            vec,
        ),
        check_vma=False,
    )
```

```python
import functools

import jax
import jax.numpy as jnp
from jax import lax
from jax.experimental import pallas as pl
from jax.experimental.pallas import tpu as pltpu
from jax.sharding import Mesh
from jax.sharding import PartitionSpec as P

EPS = 1e-06
FLOOR = 0.001
BF = jnp.bfloat16
F32 = jnp.float32


def tdot(left, right):
    return lax.dot_general(left, right, (((0,), (0,)), ((), ())), preferred_element_type=F32)


def ndot(left, right):
    return lax.dot_general(left, right, (((1,), (1,)), ((), ())), preferred_element_type=F32)


def mdot(left, right):
    return jnp.dot(left, right, preferred_element_type=F32)


def pick(stacked, index, axis=0):
    return lax.dynamic_index_in_dim(stacked, index, axis, keepdims=False)


def swap_c(value):
    return lax.ppermute(value, "c", [(0, 1), (1, 0)])


def xor_u(value, k):
    size = lax.axis_size("b") * lax.axis_size("n")
    return lax.ppermute(value, ("b", "n"), [(i, i ^ k) for i in range(size)])


def shift_a(value, by):
    size = lax.axis_size("a")
    return lax.ppermute(value, "a", [(i, i + by) for i in range(size) if 0 <= i + by < size])


def chips():
    return lax.axis_size("b") * lax.axis_size("n")


def chip():
    return lax.axis_index("b") * lax.axis_size("n") + lax.axis_index("n")


MESH = pl.DeviceIdType.MESH
VMEM_LIMIT = 60 * 1024 * 1024


def places():
    return tuple(lax.axis_index(name) for name in ("a", "b", "n", "c"))


def neighbours():
    a, b, n, c = places()
    return (a, 1 - b, n, c), (a, b, 1 - n, c), (a, b, n, 1 - c)


def greet(peers):
    barrier = pltpu.get_barrier_semaphore()
    for peer in peers:
        pl.semaphore_signal(barrier, inc=1, device_id=peer, device_id_type=MESH)
    pl.semaphore_wait(barrier, len(peers))


PARTS = 2
IN_PARTS = frozenset("d0 d1 x0 x1 y0 y1 gx0 gx1 gy0 gy1 fx fy".split(" "))


class Mover:
    def __init__(self, send, recv):
        self.send, self.recv, self.made = send, recv, {}
        self.names = []

    def copy(self, name, src, dst, peer):
        if name not in self.names:
            self.names.append(name)
        at = self.names.index(name)
        made = pltpu.make_async_remote_copy(
            src_ref=src,
            dst_ref=dst,
            send_sem=self.send.at[at],
            recv_sem=self.recv.at[at],
            device_id=peer,
            device_id_type=MESH,
        )
        self.made[name] = made
        return made

    def start(self, name, src, dst, peer):
        if name not in IN_PARTS:
            self.copy(name, src, dst, peer).start()
            return
        rows = src.shape[0] // PARTS
        for i in range(PARTS):
            at = pl.ds(i * rows, rows)
            self.copy(f"{name}.{i}", src.at[at], dst.at[at], peer).start()

    def arrived(self, name):
        for part in [f"{name}.{i}" for i in range(PARTS)] if name in IN_PARTS else [name]:
            self.made[part].wait_recv()

    def sent(self):
        for made in self.made.values():
            made.wait_send()


def gather_plane_start(move, mine, everyone, h, half_rows):
    x, y, z = neighbours()
    at = pl.ds(h * half_rows, half_rows)
    move.start(f"gx{h}", mine.at[at], everyone.at[2, at], x)
    move.start(f"gy{h}", mine.at[at], everyone.at[1, at], y)
    move.start(f"gc{h}", mine.at[at], everyone.at[4, at], z)


def gather_plane_rest(move, everyone, half_rows, stage=None):
    x, y, z = neighbours()
    rows = [pl.ds(h * half_rows, half_rows) for h in range(2)]

    def on(name, k, h):
        move.start(name, everyone.at[k, rows[h]], everyone.at[4 + k, rows[h]], z)

    if stage in (None, 0):
        move.arrived("gx0")
        move.start("fy", everyone.at[2, rows[0]], everyone.at[3, rows[0]], y)
        on("cx0", 2, 0)
        move.arrived("gy1")
        move.start("fx", everyone.at[1, rows[1]], everyone.at[3, rows[1]], x)
        on("cy1", 1, 1)
    if stage in (None, 1):
        move.arrived("gx1")
        on("cx1", 2, 1)
        move.arrived("gy0")
        on("cy0", 1, 0)
    if stage in (None, 2):
        move.arrived("fy")
        on("cd0", 3, 0)
        move.arrived("fx")
        on("cd1", 3, 1)
        for name in ("gc0", "gc1", "cx0", "cx1", "cy0", "cy1", "cd0", "cd1"):
            move.arrived(name)


GATHER_COPIES = 14 + 6 * (PARTS - 1)


def plane_peers_of():
    a, b, n, c = places()
    peers = {}
    for kc in range(2):
        for k in range(4):
            if (kc, k) != (0, 0):
                there = (a, 1 - b if k & 2 else b, 1 - n if k & 1 else n, 1 - c if kc else c)
                peers[kc, k] = there
    return peers


def peer_owner(kc, k):
    _, b, n, c = places()
    return ((b * 2 + n) ^ k) * 2 + (1 - c if kc else c)


def set_side_by_side(pieces, order, width):
    group = 1
    while group * width % 128 and group < len(order):
        group += 1
    for i in range(0, len(order), group):
        runs = [pieces[p, :, o : o + width].astype(F32) for p, o in order[i : i + group]]
        yield slice(i * width, (i + len(runs)) * width), jnp.concatenate(runs, 1)


def gain_sum(pairs, gain):
    total = sum(jnp.sum(w[...].astype(F32) * g[...], axis=-1, keepdims=True) for w, g in pairs)
    size = total.shape[0]
    row = lax.broadcasted_iota(jnp.int32, (size, size), 0)
    column = lax.broadcasted_iota(jnp.int32, (size, size), 1)
    return jnp.sum(jnp.where(row == column, total, 0.0), axis=0, keepdims=True) / gain[...]


def reduce_kernel(nt, post, nx, extra, waits, *refs):
    x_hbm, refs = refs[:nx], refs[nx:]
    w_hbm, gain_ref, first_ref, second_ref = refs[:4]
    extra_in, refs = refs[4 : 4 + extra], refs[4 + extra :]
    if post == "last":
        lasts_ref, refs = refs[0], refs[1:]
    refs = refs[waits:]
    out_ref, refs = refs[0], refs[1:]
    if post == "last":
        everyone = mine = None
        extra_buf, lasts_sum = refs[:2]
        lasts_buf, lasts_mine, lasts_far, lasts_sent = refs[2:6]
        refs = refs[6:]
    else:
        everyone, refs = refs[0], refs[1:]
        if extra and post == "fwd":
            extra_out, refs = refs[0], refs[1:]
        elif extra:
            extra_out, refs = refs[:4], refs[4:]
        mine, refs = refs[0], refs[1:]
        if post == "mid":
            (side_x, side_w, side_s, side_r), refs = refs[:4], refs[4:]
    x_v, w_v, away_s, away_r, acc, out_b, in_b, local, send, recv = refs
    rows, d_model = acc.shape[1:]
    half = rows // 2
    tile = min(512, d_model)
    px, py, pc = neighbours()
    move = Mover(send, recv)

    slots = iter(range(local.shape[0]))

    def keep(src, dst):
        made = pltpu.make_async_copy(src, dst, local.at[next(slots)])
        made.start()
        return made

    w_copy = keep(w_hbm, w_v)
    loads = {}
    each = x_v.shape[3] // nx
    for k in (3, 2, 1, 0):
        for kc in (1, 0):
            loads[kc, k] = [
                keep(x.at[kc, k], x_v.at[kc, k, :, pl.ds(i * each, each)])
                for i, x in enumerate(x_hbm)
            ]
    if post == "mid":
        side_loads = [keep(extra_in[0], side_x), keep(extra_in[1], side_w)]
    if post == "last":
        a, b, n, c = places()
        planes = lasts_far.shape[0] + 1
        columns = [(lax.rem(a + d, planes), b, n, c) for d in range(1, planes)]
        peers = plane_peers_of()
        greet([*peers.values(), *columns])
        for kc in range(2):
            for kn in range(2):
                lasts_sent[kc, kn] = (
                    lasts_ref[kc * 4 + kn].astype(F32) + lasts_ref[kc * 4 + 2 + kn].astype(F32)
                ).astype(BF)
        for (kc, k), peer in peers.items():
            move.start(f"l{kc}{k}", lasts_sent.at[kc, k % 2], lasts_buf.at[kc, k], peer)
    else:
        greet((px, py, pc))
    w_copy.wait()

    def product(kc, k, t):
        at = pl.ds(pl.multiple_of(t * tile, tile), tile)
        if nt:
            return at, ndot(x_v[kc, k], w_v[at, :])
        return at, mdot(x_v[kc, k], w_v[:, at])

    step = min(32, half)

    def by_rows(h, body):
        @pl.loop(0, half // step)
        def _(i):
            body(pl.ds(pl.multiple_of(i * step, step), step),
                 pl.ds(pl.multiple_of(h * half + i * step, step), step))

    def hand_on(name, slot, k, h, peer, extra=None):
        def body(inner, outer):
            value = acc[k, outer, :]
            if extra is not None:
                value = value + in_b[extra, inner, :].astype(F32)
            out_b[slot, inner, :] = value.astype(BF)

        by_rows(h, body)
        move.start(name, out_b.at[slot], in_b.at[slot], peer)

    for k in (3, 2, 1, 0):
        for load in loads[1, k]:
            load.wait()

        @pl.loop(0, d_model // tile)
        def _(t):
            at, value = product(1, k, t)
            away_s[k, :, at] = value.astype(BF)

        move.start(f"away{k}", away_s.at[k], away_r.at[k], pc)
        for load in loads[0, k]:
            load.wait()

        @pl.loop(0, d_model // tile)
        def _(t):
            at, value = product(0, k, t)
            acc[k, :, at] = value

        move.arrived(f"away{k}")
        for h in range(2):
            def add(inner, outer):
                acc[k, outer, :] += away_r[k, outer, :].astype(F32)

            by_rows(h, add)
        if k == 3:
            hand_on("d0", 0, 3, 0, px)
            hand_on("d1", 1, 3, 1, py)
        elif k == 2:
            hand_on("x0", 2, 2, 0, px)
        elif k == 1:
            hand_on("y1", 5, 1, 1, py)
    kept = []
    if extra and post == "fwd":
        for k in range(4):
            kept.append(keep(extra_in[k], extra_out.at[k]))
            move.start(f"e{k}", extra_in[k], extra_out.at[4 + k], pc)
    move.arrived("d0")
    hand_on("y0", 4, 1, 0, py, 0)
    move.arrived("d1")
    hand_on("x1", 3, 2, 1, px, 1)
    if post == "mid":
        for load in side_loads:
            load.wait()
        for k in range(4):

            @pl.loop(0, d_model // tile)
            def _(t):
                at = pl.ds(pl.multiple_of(t * tile, tile), tile)
                side_s[k, :, at] = mdot(side_x[1, k], side_w[:, at]).astype(BF)

            move.start(f"s{k}", side_s.at[k], side_r.at[k], pc)
        for k in range(4):
            move.arrived(f"s{k}")
            move.made.pop(f"s{k}").wait_send()

            @pl.loop(0, d_model // tile)
            def _(t):
                at = pl.ds(pl.multiple_of(t * tile, tile), tile)
                value = mdot(side_x[0, k], side_w[:, at]) + side_r[k, :, at].astype(F32)
                side_s[k, :, at] = value.astype(BF)

            kept.append(keep(side_s.at[k], extra_out[k]))
    if extra and post == "last":
        lasts_buf[0, 0] = lasts_sent[0, 0]
        for kc, k in peers:
            move.arrived(f"l{kc}{k}")
        u = b * 2 + n
        me = u * 2 + c
        for kc in range(2):
            for q in range(4):
                found = lasts_buf[kc, 0]
                for k in range(1, 4):
                    found = jnp.where((u ^ k) == q, lasts_buf[kc, k], found)
                lasts_mine[jnp.bitwise_xor(c, kc), q] = found
        for i, peer in enumerate(columns):
            move.start(f"z{i}", lasts_mine, lasts_far.at[i], peer)
        each_rows = extra_buf.shape[1]

        def part(owner):
            at = pl.multiple_of(owner * each_rows, each_rows)
            return extra_in[0].at[pl.ds(at, each_rows)]

        kept.append(keep(part(me), extra_buf.at[me]))
        for (kc, k), peer in peers.items():
            move.start(f"e{kc}{k}", part(peer_owner(kc, k)), extra_buf.at[me], peer)

    for h in range(2):
        move.arrived(f"x{h}")
        move.arrived(f"y{h}")

        def body(inner, outer):
            total = acc[0, outer, :]
            total = total + in_b[2 + h, inner, :].astype(F32)
            total = total + in_b[4 + h, inner, :].astype(F32)
            gain = gain_ref[...]
            if post == "fwd":
                value = first_ref[outer, :].astype(F32) + total
                out_ref[outer, :] = value
                factor = lax.rsqrt(jnp.mean(value * value, axis=-1, keepdims=True) + EPS)
                mine[outer, :] = (value * factor * gain).astype(BF)
                return
            value = second_ref[outer, :] if post == "mid" else first_ref[outer, :].astype(F32)
            base = first_ref[outer, :].astype(F32) if post == "mid" else second_ref[outer, :]
            factor = lax.rsqrt(jnp.mean(value * value, axis=-1, keepdims=True) + EPS)
            weighted = total * gain
            inner_mean = jnp.mean(weighted * value, axis=-1, keepdims=True)
            grad = base + factor * weighted - value * (factor * factor * factor * inner_mean)
            if post == "mid":
                out_ref[outer, :] = grad
                mine[outer, :] = grad.astype(BF)
            else:
                out_ref[outer, :] = grad.astype(BF)

        by_rows(h, body)
        if everyone is not None:
            gather_plane_start(move, mine, everyone, h, half)
    if everyone is not None:
        kept.append(keep(mine, everyone.at[0]))
        gather_plane_rest(move, everyone, half)
    if extra and post == "fwd":
        for k in range(4):
            move.arrived(f"e{k}")
    for made in kept:
        made.wait()
    if extra and post == "last":
        total = lasts_mine[...].astype(F32)
        for i in range(len(columns)):
            move.arrived(f"z{i}")
            total = total + lasts_far[i].astype(F32)
        lasts_sum[...] = total.reshape(lasts_sum.shape)
        for kc, k in peers:
            move.arrived(f"e{kc}{k}")
    move.sent()


def plane_reduce(ident, post, nt, xs, w, gain, first, second, extra=(), done=(), lasts=None):
    rows, d_model = first.shape
    vmem = pl.BlockSpec(memory_space=pltpu.VMEM)
    hbm = pl.BlockSpec(memory_space=pl.ANY)
    out_type = BF if post == "last" else F32
    out_shape = [jax.ShapeDtypeStruct((rows, d_model), out_type)]
    out_specs = [vmem]
    scratch = []
    copies = 10 + 6 * (PARTS - 1)
    if post != "last":
        out_shape.append(jax.ShapeDtypeStruct((8, rows, d_model), BF))
        out_specs.append(hbm)
        copies += GATHER_COPIES
        if extra:
            shapes = [(8, rows, d_model)] if post == "fwd" else [(rows, d_model)] * 4
            out_shape += [jax.ShapeDtypeStruct(shape, BF) for shape in shapes]
            out_specs += [hbm] * len(shapes)
            copies += 4
        scratch.append(pltpu.VMEM((rows, d_model), BF))
        if post == "mid":
            scratch += [pltpu.VMEM(v.shape, BF) for v in extra]
            scratch += [pltpu.VMEM((4, rows, d_model), BF)] * 2
    else:
        each = extra[0].shape[0] // 8, extra[0].shape[1]
        planes = lax.axis_size("a")
        copies += 7 + 7 + planes - 1
        block = (2, 4) + lasts.shape[1:]
        out_shape.append(jax.ShapeDtypeStruct((8,) + each, BF))
        out_shape.append(jax.ShapeDtypeStruct((8,) + block[2:], F32))
        out_specs += [hbm, vmem]
        scratch += [pltpu.VMEM(block, BF)] * 2 + [pltpu.VMEM((planes - 1,) + block, BF)]
        scratch.append(pltpu.VMEM((2, 2) + block[2:], BF))
    wide = sum(x.shape[3] for x in xs)
    scratch += [
        pltpu.VMEM((2, 4, rows, wide), BF),
        pltpu.VMEM(w.shape, BF),
        pltpu.VMEM((4, rows, d_model), BF),
        pltpu.VMEM((4, rows, d_model), BF),
        pltpu.VMEM((4, rows, d_model), F32),
        pltpu.VMEM((6, rows // 2, d_model), BF),
        pltpu.VMEM((6, rows // 2, d_model), BF),
        pltpu.SemaphoreType.DMA((8 + 8 * len(xs),)),
        pltpu.SemaphoreType.DMA((copies,)),
        pltpu.SemaphoreType.DMA((copies,)),
    ]
    last = [] if lasts is None else [lasts]
    return pl.pallas_call(
        functools.partial(reduce_kernel, nt, post, len(xs), len(extra), len(done)),
        in_specs=[hbm] * (len(xs) + 1)
        + [vmem] * 3
        + [vmem if post == "fwd" else hbm] * len(extra)
        + [vmem] * (lasts is not None)
        + [hbm] * len(done),
        out_specs=out_specs,
        out_shape=out_shape,
        scratch_shapes=scratch,
        compiler_params=pltpu.CompilerParams(
            collective_id=ident, has_side_effects=True, vmem_limit_bytes=VMEM_LIMIT
        ),
        cost_estimate=pl.CostEstimate(flops=0, bytes_accessed=8 << 20, transcendentals=0),
        name=f"plane_reduce_{post}",
    )(*xs, w, gain.reshape(1, -1), first, second, *extra, *last, *done)


def start_kernel(
    head_w, hid, tokens_ref, wy_ref, wx_ref, wg_ref, wu_ref, rows_ref, vec_ref, stream_ref,
    tok_out, yx_out, gu_out, rows_out, halves_out, vec_out, stream_out,
    yx_ref, gu_ref, local, send, recv,
):
    a, b, n, c = places()
    planes = yx_out.shape[0]
    p = (b * 2 + n) * 2 + c
    pc = neighbours()[2]
    plane_peers = plane_peers_of()
    up, down = (a + 1, b, n, c), (a - 1, b, n, c)
    each = planes // 2

    def pack(out, sources, columns, width):
        for owner in range(8):
            runs = [w[:, o : o + width] for w in sources for o in columns(owner)]
            out[owner] = jnp.concatenate(runs, 1)

    barrier = pltpu.get_barrier_semaphore()
    for peer in plane_peers.values():
        pl.semaphore_signal(barrier, inc=1, device_id=peer, device_id_type=MESH)

    @pl.when(a < planes - 1)
    def _():
        pl.semaphore_signal(barrier, inc=1, device_id=up, device_id_type=MESH)

    @pl.when(a > 0)
    def _():
        pl.semaphore_signal(barrier, inc=1, device_id=down, device_id_type=MESH)

    def head_columns(owner):
        return [((owner % 2 * each + j) * 4 + owner // 2) * head_w for j in range(each)]

    pack(yx_ref, (wy_ref, wx_ref), head_columns, head_w)
    others = len(plane_peers) + jnp.minimum(planes - 1 - a, 1) + jnp.minimum(a, 1)
    pl.semaphore_wait(barrier, others)

    move = Mover(send, recv)
    half = tokens_ref.shape[0] // 2

    def keep(i, src, dst):
        made = pltpu.make_async_copy(src, dst, local.at[i])
        made.start()
        return made

    def to_owners(name, pieces, out):
        for (kc, k), peer in plane_peers.items():
            move.start(f"{name}{kc}{k}", pieces.at[peer_owner(kc, k)], out.at[a, p], peer)

    chains = {}

    def chain_step(name, out, s):
        def up_copy(block):
            return move.copy(f"{name}u{s}", out.at[block], out.at[block], up)

        def down_copy(block):
            return move.copy(f"{name}d{s}", out.at[block], out.at[block], down)

        sends_up, sends_down = (a < planes - 1) & (a >= s), (a > 0) & (a + s < planes)

        @pl.when(sends_up)
        def _():
            up_copy(a - s).start()

        @pl.when(sends_down)
        def _():
            down_copy(a + s).start()

        chains[name, s] = (up_copy, down_copy, sends_up, sends_down)

    def chain_arrived(name, s):
        up_copy, down_copy, _, _ = chains[name, s]

        @pl.when(a - 1 >= s)
        def _():
            up_copy(a - 1 - s).wait_recv()

        @pl.when(a + 1 + s < planes)
        def _():
            down_copy(a + 1 + s).wait_recv()

    def chain_sent(name, s):
        up_copy, down_copy, sends_up, sends_down = chains[name, s]

        @pl.when(sends_up)
        def _():
            up_copy(a - s).wait_send()

        @pl.when(sends_down)
        def _():
            down_copy(a + s).wait_send()

    to_owners("yx", yx_ref, yx_out)
    for (kc, k), peer in plane_peers.items():
        move.start(f"vec{kc}{k}", vec_ref, vec_out.at[a, p], peer)
    own_yx = keep(1, yx_ref.at[p], yx_out.at[a, p])
    own_vec = keep(2, vec_ref, vec_out.at[a, p])
    own_rows = keep(0, rows_ref, rows_out.at[a])
    own_tok = keep(4, tokens_ref, tok_out.at[0])
    own_stream = keep(5, stream_ref, stream_out.at[0, 0])
    own_yx.wait()
    own_vec.wait()
    for kc, k in plane_peers:
        move.arrived(f"yx{kc}{k}")
        move.arrived(f"vec{kc}{k}")
    own_rows.wait()
    outs = (("yx", yx_out), ("vec", vec_out), ("rows", rows_out))
    for name, out in outs:
        chain_step(name, out, 0)
    for h in range(2):
        gather_plane_start(move, tokens_ref, tok_out, h, half)
    pack(gu_ref, (wg_ref, wu_ref), lambda o: [(z * 8 + o) * hid for z in range(planes)], hid)
    own_gu = keep(3, gu_ref.at[p], gu_out.at[p])
    gather_plane_rest(move, tok_out, half, 0)
    for kc in range(2):
        for kn in range(2):
            if (kc, kn) != (0, 0):
                move.start(f"st{kc}{kn}", stream_ref, stream_out.at[kc, kn], plane_peers[kc, kn])
    for name, out in outs:
        chain_arrived(name, 0)
        chain_step(name, out, 1)
    gather_plane_rest(move, tok_out, half, 1)
    for (kc, k), peer in plane_peers.items():
        move.start(f"gu{kc}{k}", gu_ref.at[peer_owner(kc, k)], gu_out.at[p], peer)
    for s in range(1, planes - 1):
        for name, out in outs:
            chain_arrived(name, s)
            if s + 1 < planes - 1:
                chain_step(name, out, s + 1)
    gather_plane_rest(move, tok_out, half, 2)
    swap = pltpu.make_async_remote_copy(
        src_ref=rows_out.at[pl.ds((1 - c) * each, each)],
        dst_ref=halves_out.at[:, c],
        send_sem=send.at[send.shape[0] - 1],
        recv_sem=recv.at[recv.shape[0] - 1],
        device_id=pc,
        device_id_type=MESH,
    )
    swap.start()
    own_halves = keep(6, rows_out.at[pl.ds(c * each, each)], halves_out.at[:, c])
    for kc, k in plane_peers:
        move.arrived(f"gu{kc}{k}")
    for kc in range(2):
        for kn in range(2):
            if (kc, kn) != (0, 0):
                move.arrived(f"st{kc}{kn}")
    for made in (own_gu, own_tok, own_stream, own_halves):
        made.wait()
    swap.wait()
    for name, s in chains:
        chain_sent(name, s)
    for name in [n for n in move.names if not any(n == f"{w}{d}{s}" for w, s in chains for d in "ud")]:
        move.made[name].wait_send()


def start_exchange(tokens, w_y, w_x, w_gate, w_up, gate_rows, vec, stream):
    planes = lax.axis_size("a")
    head_w, hid = gate_rows.shape[1] // 2, w_gate.shape[1] // (planes * 8)
    vmem = pl.BlockSpec(memory_space=pltpu.VMEM)
    hbm = pl.BlockSpec(memory_space=pl.ANY)
    yx = (8, w_y.shape[0], 2 * w_y.shape[1] // 8)
    gu = (8, w_gate.shape[0], 2 * w_gate.shape[1] // 8)
    shapes = [
        ((8,) + tokens.shape, BF),
        ((planes,) + yx, BF),
        (gu, BF),
        ((planes,) + gate_rows.shape, BF),
        ((planes // 2, 2) + gate_rows.shape, BF),
        ((planes, 8) + vec.shape, F32),
        ((2, 2) + stream.shape, F32),
    ]
    copies = 7 * 3 + 3 + GATHER_COPIES + 6 * (planes - 1) + 1
    return pl.pallas_call(
        functools.partial(start_kernel, head_w, hid),
        in_specs=[vmem] * 8,
        out_specs=[hbm] * 7,
        out_shape=[jax.ShapeDtypeStruct(*shape) for shape in shapes],
        scratch_shapes=[
            pltpu.VMEM(yx, BF),
            pltpu.VMEM(gu, BF),
            pltpu.SemaphoreType.DMA((7,)),
            pltpu.SemaphoreType.DMA((copies,)),
            pltpu.SemaphoreType.DMA((copies,)),
        ],
        compiler_params=pltpu.CompilerParams(
            collective_id=1, has_side_effects=True, vmem_limit_bytes=VMEM_LIMIT
        ),
        cost_estimate=pl.CostEstimate(flops=0, bytes_accessed=8 << 20, transcendentals=0),
        name="start_exchange",
    )(tokens, w_y, w_x, w_gate, w_up, gate_rows, vec, stream)


def finish_kernel(sums_ref, buf, local, send, recv):
    _, b, n, c = places()
    me = (b * 2 + n) * 2 + c
    peers = plane_peers_of()
    greet(list(peers.values()))
    move = Mover(send, recv)
    each_rows = buf.shape[1]

    def part(owner):
        return sums_ref.at[pl.ds(pl.multiple_of(owner * each_rows, each_rows), each_rows)]

    for (kc, k), peer in peers.items():
        move.start(f"e{kc}{k}", part(peer_owner(kc, k)), buf.at[me], peer)
    own = pltpu.make_async_copy(part(me), buf.at[me], local.at[0])
    own.start()
    own.wait()
    for kc, k in peers:
        move.arrived(f"e{kc}{k}")
    move.sent()


def finish(sums, done):
    vmem = pl.BlockSpec(memory_space=pltpu.VMEM)

    def body(sums_ref, *refs):
        finish_kernel(sums_ref, *refs[len(done) :])

    return pl.pallas_call(
        body,
        in_specs=[vmem] + [pl.BlockSpec(memory_space=pl.ANY)] * len(done),
        out_specs=vmem,
        out_shape=jax.ShapeDtypeStruct((8, sums.shape[0] // 8, sums.shape[1]), BF),
        scratch_shapes=[
            pltpu.SemaphoreType.DMA((1,)),
            pltpu.SemaphoreType.DMA((7,)),
            pltpu.SemaphoreType.DMA((7,)),
        ],
        compiler_params=pltpu.CompilerParams(
            collective_id=5, has_side_effects=True, vmem_limit_bytes=VMEM_LIMIT
        ),
        cost_estimate=pl.CostEstimate(flops=0, bytes_accessed=1 << 20, transcendentals=0),
        name="finish",
    )(sums, *done)


def in_place(body, ins, outs, name):
    vmem = pl.BlockSpec(memory_space=pltpu.VMEM)
    return pl.pallas_call(
        body,
        in_specs=[vmem] * len(ins),
        out_specs=[vmem] * len(outs),
        out_shape=[jax.ShapeDtypeStruct(*out) for out in outs],
        compiler_params=pltpu.CompilerParams(vmem_limit_bytes=VMEM_LIMIT),
        cost_estimate=pl.CostEstimate(flops=0, bytes_accessed=1 << 20, transcendentals=0),
        name=name,
    )(*ins)


def order_hidden_kernel(
    hid, head_w, buf, wg_ref, wu_ref, gain_ref, late_ref, lasts_ref,
    g_ref, u_ref, gain_out, out_ref, a_ref, i_ref, state_ref, conv_ref, *vec_refs,
):
    wide = buf.shape[2] // 2
    for i, out in enumerate((g_ref, u_ref)):
        order = [(p, i * wide + z * hid) for z in range(wide // hid) for p in range(8)]
        for at, value in set_side_by_side(buf, order, hid):
            out[:, at] = value
    gain_out[...] = gain_sum(((wg_ref, g_ref), (wu_ref, u_ref)), gain_ref)
    heads = wide // hid // 2
    order = [(i * 4 + q, j * head_w) for i in range(2) for j in range(heads) for q in range(4)]
    for at, value in set_side_by_side(lasts_ref, order, head_w):
        nseq = state_ref.shape[0]
        state_ref[:, at] = value[:nseq]
        conv_ref[:, at] = value[nseq:].astype(BF)
    wide_out, half = out_ref.shape[1], late_ref.shape[0]
    out_ref[...] = late_ref[:, :wide_out].astype(F32)
    a_ref[...] = late_ref[:, wide_out : wide_out + head_w].astype(F32)
    i_ref[...] = late_ref[:, wide_out + head_w : wide_out + 2 * head_w].astype(F32)
    row = lax.broadcasted_iota(jnp.int32, (half, half), 0)
    column = lax.broadcasted_iota(jnp.int32, (half, half), 1)
    eye = jnp.where(row == column, 1.0, 0.0).astype(BF)
    turned = tdot(late_ref[:, wide_out + 2 * head_w :], eye)
    taps = vec_refs[0].shape[0]
    vec_refs[0][...] = turned[:taps]
    for i, vec_ref in enumerate(vec_refs[1:]):
        vec_ref[...] = turned[taps + i : taps + i + 1]


def order_heads_kernel(head_w, buf, wy_ref, wx_ref, gain_ref, y_ref, x_ref, gain_out):
    wide = buf.shape[2] // 2
    each = wide // head_w
    order = [(q * 2 + i, j * head_w) for i in range(2) for j in range(each) for q in range(4)]
    for first, out in ((0, y_ref), (wide, x_ref)):
        for at, value in set_side_by_side(buf, [(p, o + first) for p, o in order], head_w):
            out[:, at] = value
    gain_out[...] = gain_sum(((wy_ref, y_ref), (wx_ref, x_ref)), gain_ref)


def column_peers(planes):
    a, b, n, c = places()
    return [(lax.rem(a + d, planes), b, n, c) for d in range(1, planes)]


def earlier_blocks(ref, want, row=0, count=1):
    _, b, _, _ = places()
    return [
        jnp.where(
            b == want,
            ref[kc * 4 + kn, row : row + count, :],
            ref[kc * 4 + 2 + kn, row : row + count, :],
        )
        for kc in range(2)
        for kn in range(2)
    ]


def split_refs(refs):
    if len(refs) == 5:
        return None, refs[:1], refs[1:], None
    return refs[0], refs[1:3], refs[3:7], refs[7:]


def swap_halves(rows_ref, out_ref, local, send, recv):
    _, _, _, c = places()
    planes, half = out_ref.shape[:2]
    each = planes // 2
    made = []
    for j in range(each):
        away = pl.multiple_of((2 * j + 1 - c) * half, half)
        own = pl.multiple_of((2 * j + c) * half, half)
        made.append(
            pltpu.make_async_remote_copy(
                src_ref=rows_ref.at[pl.ds(away, half)],
                dst_ref=out_ref.at[c * each + j],
                send_sem=send.at[j],
                recv_sem=recv.at[j],
                device_id=neighbours()[2],
                device_id_type=MESH,
            )
        )
        made.append(
            pltpu.make_async_copy(
                rows_ref.at[pl.ds(own, half)], out_ref.at[c * each + j], local.at[j]
            )
        )
    for copy in made:
        copy.start()
    return made


def pass_state_kernel(reverse, mul_ref, add_ref, *refs):
    rows_ref, (out_ref, *halves), (whole, came, send, recv), swaps = split_refs(refs)
    a, b, n, c = places()
    planes = came.shape[0] + 1
    row = 0 if reverse else 7
    near_at, far_at = (1, 0) if reverse else (0, 1)
    came[...] = jnp.zeros_like(came)
    near_mul, near_add = earlier_blocks(mul_ref, near_at, row), earlier_blocks(add_ref, near_at, row)
    far_mul, far_add = earlier_blocks(mul_ref, far_at, row), earlier_blocks(add_ref, far_at, row)
    for i in range(4):
        whole[0, i : i + 1, :] = near_mul[i] * far_mul[i]
        whole[1, i : i + 1, :] = far_mul[i] * near_add[i] + far_add[i]
    greet(column_peers(planes) + ([neighbours()[2]] if swaps else []))
    swapped = swap_halves(rows_ref, halves[0], *swaps) if swaps else []

    def copy(d):
        return pltpu.make_async_remote_copy(
            src_ref=whole,
            dst_ref=came.at[d - 1],
            send_sem=send.at[d - 1],
            recv_sem=recv.at[d - 1],
            device_id=(a - d if reverse else a + d, b, n, c),
            device_id_type=MESH,
        )

    def sends(d):
        return a >= d if reverse else a + d < planes

    def receives(d):
        return a + d < planes if reverse else a >= d

    for d in range(1, planes):
        @pl.when(sends(d))
        def _():
            copy(d).start()

    for d in range(1, planes):
        @pl.when(receives(d))
        def _():
            copy(d).wait_recv()

    for i in range(4):
        at = slice(i, i + 1)
        value = came[planes - 2, 1, at, :]
        for d in range(planes - 2, 0, -1):
            value = came[d - 1, 0, at, :] * value + came[d - 1, 1, at, :]
        to_far = near_mul[i] * value + near_add[i]
        for kb in range(2):
            is_far = (b if kb == 0 else 1 - b) == far_at
            at = (i // 2) * 4 + kb * 2 + i % 2
            out_ref[at] = jnp.where(is_far, to_far, value)

    for d in range(1, planes):
        @pl.when(sends(d))
        def _():
            copy(d).wait_send()

    for made in swapped:
        made.wait()


def pass_rows_kernel(reverse, edge_ref, *refs):
    rows_ref, (out_ref, *halves), (leaving, came, send, recv), swaps = split_refs(refs)
    a, b, n, c = places()
    planes = lax.axis_size("a")
    near_at, far_at = (1, 0) if reverse else (0, 1)
    came[...] = jnp.zeros_like(came)
    out_ref[...] = jnp.zeros_like(out_ref)
    first = 0 if reverse else 4
    for i, value in enumerate(earlier_blocks(edge_ref, far_at, first, 4)):
        leaving[i * 4 : i * 4 + 4, :] = value
    greet(column_peers(planes) + ([neighbours()[2]] if swaps else []))
    swapped = swap_halves(rows_ref, halves[0], *swaps) if swaps else []
    copy = pltpu.make_async_remote_copy(
        src_ref=leaving,
        dst_ref=came,
        send_sem=send.at[0],
        recv_sem=recv.at[0],
        device_id=(a - 1 if reverse else a + 1, b, n, c),
        device_id_type=MESH,
    )
    sends = a >= 1 if reverse else a + 1 < planes
    receives = a + 1 < planes if reverse else a >= 1

    @pl.when(sends)
    def _():
        copy.start()

    @pl.when(receives)
    def _():
        copy.wait_recv()

    for i in range(4):
        for kb in range(2):
            is_far = (b if kb == 0 else 1 - b) == far_at
            at = (i // 2) * 4 + kb * 2 + i % 2
            other = (i // 2) * 4 + (1 - kb) * 2 + i % 2
            out_ref[at, first : first + 4, :] = jnp.where(
                is_far, edge_ref[other, first : first + 4, :], came[i * 4 : i * 4 + 4, :]
            )

    @pl.when(sends)
    def _():
        copy.wait_send()

    for made in swapped:
        made.wait()


def pass_along(ident, name, reverse, *edges, halves=None):
    shape = edges[0].shape
    planes = lax.axis_size("a")
    vmem = pl.BlockSpec(memory_space=pltpu.VMEM)
    if len(edges) == 2:
        body, out = pass_state_kernel, (shape[0], 1, shape[2])
        buffers = [(2, 4) + shape[2:], (planes - 1, 2, 4) + shape[2:]]
    else:
        body, out = pass_rows_kernel, shape
        buffers = [(16,) + shape[2:]] * 2
    given, out_shape = list(edges), [jax.ShapeDtypeStruct(out, F32)]
    scratch = [pltpu.VMEM(shape, F32) for shape in buffers]
    scratch += [pltpu.SemaphoreType.DMA((planes - 1,))] * 2
    if halves is not None:
        given.append(halves[0])
        to = (planes, halves[1], halves[0].shape[1])
        out_shape.append(jax.ShapeDtypeStruct(to, BF))
        scratch += [pltpu.SemaphoreType.DMA((planes // 2,))] * 3
    return pl.pallas_call(
        functools.partial(body, reverse),
        in_specs=[vmem] * len(given),
        out_specs=[vmem] * len(out_shape),
        out_shape=out_shape,
        scratch_shapes=scratch,
        compiler_params=pltpu.CompilerParams(
            collective_id=ident, has_side_effects=True, vmem_limit_bytes=VMEM_LIMIT
        ),
        cost_estimate=pl.CostEstimate(flops=0, bytes_accessed=1 << 20, transcendentals=0),
        name=name,
    )(*given)


def norm_product_kernel(tok_ref, w_ref, gain_ref, n_ref, gate_ref, lin_ref, tail_ref, held):
    i = pl.program_id(0)
    rows = tok_ref.shape[1]
    wide = gate_ref.shape[2]
    both = mdot(held[(i + 1) % 2], w_ref[...])
    used = both.shape[1] // 2
    pad = [jnp.zeros((rows, wide - used), F32)] if wide > used else []
    gate_ref[0] = jnp.concatenate([both[:, :used]] + pad, 1)
    low = jnp.concatenate([both[:, used:]] + pad, 1).astype(BF)
    lin_ref[0] = low
    tail_ref[0] = low.astype(F32)[rows - 8 :, :]
    step = min(64, rows)
    for k in range(rows // step):
        at = slice(k * step, (k + 1) * step)
        value = tok_ref[0, at, :].astype(F32)
        factor = lax.rsqrt(jnp.mean(value * value, axis=-1, keepdims=True) + EPS)
        low = (value * factor * gain_ref[...]).astype(BF)
        n_ref[0, at, :] = low
        held[i % 2, at, :] = low


def norm_product(tokens, w, gain, wide):
    blocks, rows, d_model = tokens.shape

    def now(i):
        return (jnp.minimum(i, blocks - 1), 0, 0)

    def last(i):
        return (jnp.maximum(i - 1, 0), 0, 0)

    shapes = [(rows, d_model, BF), (rows, wide, F32), (rows, wide, BF), (8, wide, F32)]
    return pl.pallas_call(
        norm_product_kernel,
        grid=(blocks + 1,),
        in_specs=[
            pl.BlockSpec((1, rows, d_model), now),
            pl.BlockSpec(w.shape, lambda i: (0, 0)),
            pl.BlockSpec(gain.shape, lambda i: (0, 0)),
        ],
        out_specs=[
            pl.BlockSpec((1,) + shape[:2], last if k else now) for k, shape in enumerate(shapes)
        ],
        out_shape=[jax.ShapeDtypeStruct((blocks,) + s[:2], s[2]) for s in shapes],
        scratch_shapes=[pltpu.VMEM((2, rows, d_model), BF)],
        compiler_params=pltpu.CompilerParams(vmem_limit_bytes=VMEM_LIMIT),
        cost_estimate=pl.CostEstimate(flops=0, bytes_accessed=1 << 20, transcendentals=0),
        name="norm_product",
    )(tokens, w, gain)


def row_places(info, rows, nseq):
    i = pl.program_id(0)
    pos = info[i, 0] + lax.broadcasted_iota(jnp.int32, (rows, 1), 0)
    begin = jnp.zeros((rows, 1), jnp.int32) + info[i, 1]
    seg = jnp.zeros((rows, 1), jnp.int32)
    for s in range(1, nseq):
        begin = jnp.where(pos >= info[i, 1 + s], info[i, 1 + s], begin)
        seg = jnp.where(pos >= info[i, 1 + s], s, seg)
    return pos, begin, seg


def inputs_by_tap(ext, lin_ref, rim_ref, conv0_ref, begin_at, seg, taps):
    rows = lin_ref.shape[1]
    back = taps - 1
    ext[0:8, :] = rim_ref[0]
    ext[8 : 8 + rows, :] = lin_ref[0].astype(F32)
    slots = conv0_ref.shape[1]
    column = lax.broadcasted_iota(jnp.int32, (rows, slots), 1)
    found = [ext[8 : 8 + rows, :]]
    for k in range(1, taps):
        hot = (column == seg * back + begin_at - k + back) & (begin_at < k)
        stored = mdot(jnp.where(hot, 1.0, 0.0).astype(BF), conv0_ref[0])
        found.append(jnp.where(begin_at >= k, ext[8 - k : 8 - k + rows, :], stored))
    return found


def run_scan(a_s, b_s, p_ref, s_ref, rows, reverse):
    width = b_s.shape[1]
    groups = rows // 8
    row = lax.broadcasted_iota(jnp.int32, (8, width), 0)
    if reverse:
        row = 7 - row

    def step(i, carry):
        cp, cs = carry
        g = groups - 1 - i if reverse else i
        at = pl.ds(pl.multiple_of(g * 8, 8), 8)
        a, b = a_s[at, :], b_s[at, :]
        for d in (1, 2, 4):
            by = 8 - d if reverse else d
            inside = row >= d
            a_far = jnp.where(inside, pltpu.roll(a, by, 0), 1.0)
            b_far = jnp.where(inside, pltpu.roll(b, by, 0), 0.0)
            b = a * b_far + b
            a = a * a_far
        b = a * cs + b
        a = a * cp
        p_ref[0, at, :] = a
        s_ref[0, at, :] = b
        last = 0 if reverse else 7
        return a[last : last + 1], b[last : last + 1]

    start = (jnp.ones((1, width), F32), jnp.zeros((1, width), F32))
    lax.fori_loop(0, groups, step, start, unroll=4)


V_CBIAS, V_ABIAS, V_IBIAS, V_SOFT = 0, 1, 2, 3


def forward_kernel(
    nseq, taps, info, lin_ref, rim_ref, conv0_ref, state0_ref, wg_ref, vec_ref,
    conv_ref, retain_ref, admit_ref, p_ref, s_ref, pe_ref, se_ref, ext, a_s, b_s,
):
    i = pl.program_id(0)
    rows, wide = lin_ref.shape[1:]
    pos, begin, seg = row_places(info, rows, nseq)
    at = pos - begin

    def vec(k):
        return vec_ref[k : k + 1, :]

    by_tap = inputs_by_tap(ext, lin_ref, rim_ref, conv0_ref, at, seg, taps)
    total = vec(taps + V_CBIAS)
    for k in range(taps):
        total = total + vec(k) * by_tap[k]
    low = total.astype(BF)
    conv_ref[0] = low
    conv = low.astype(F32)
    both = mdot(low, wg_ref[...])
    retain = jax.nn.sigmoid(both[:, :wide] + vec(taps + V_ABIAS))
    admit = jax.nn.sigmoid(both[:, wide:] + vec(taps + V_IBIAS))
    retain_ref[0] = retain
    admit_ref[0] = admit
    a = jnp.exp(-8.0 * retain * vec(taps + V_SOFT))
    mult = jnp.sqrt(jnp.maximum((1.0 - a) * (1.0 + a), FLOOR))
    drive = mult * admit * conv
    for s in range(nseq):
        drive = drive + jnp.where(pos == info[i, 1 + s], a * state0_ref[0, s : s + 1, :], 0.0)
    a_s[...] = jnp.where(at == 0, 0.0, a)
    b_s[...] = drive
    run_scan(a_s, b_s, p_ref, s_ref, rows, False)
    pe_ref[0] = p_ref[0, rows - 8 : rows, :]
    se_ref[0] = s_ref[0, rows - 8 : rows, :]


def gelu_pair(x):
    root = 0.7978845608028654
    inner = root * (x + 0.044715 * (x * x * x))
    th = jnp.tanh(inner)
    cdf = 0.5 * (1.0 + th)
    slope = cdf + 0.5 * x * (1.0 - th * th) * (root * (1.0 + 3.0 * 0.044715 * (x * x)))
    return x * cdf, slope


def ffn_forward_kernel(info, n_ref, w_ref, inner_ref, by_gate_ref, by_up_ref):
    pair = mdot(n_ref[0], w_ref[...])
    hidden = inner_ref.shape[2]
    upward = pair[:, hidden:]
    active, slope = gelu_pair(pair[:, :hidden])
    inner_ref[0] = (active * upward).astype(BF)
    by_gate_ref[0] = (slope * upward).astype(BF)
    by_up_ref[0] = active.astype(BF)


def ffn_back_kernel(info, g_ref, w_ref, by_gate_ref, by_up_ref, *refs):
    out_ref = refs[-1]
    hidden = w_ref.shape[0]
    d_inner = ndot(g_ref[0], w_ref[...])
    out_ref[0, :, :hidden] = (d_inner * by_gate_ref[0].astype(F32)).astype(BF)
    out_ref[0, :, hidden:] = (d_inner * by_up_ref[0].astype(F32)).astype(BF)


def back_scan_kernel(
    nseq, taps, info, dres_ref, wo_ref, gate_ref, hidden_ref, retain_ref, vec_ref, mixed_ref, *refs
):
    dgate_ref, p_ref, s_ref, pe_ref, se_ref, wgrad_ref, ext, a_s, b_s, wgrad = refs[-10:]
    rows = gate_ref.shape[1]
    i = pl.program_id(0)

    @pl.when(i == 0)
    def _():
        wgrad[...] = jnp.zeros_like(wgrad)

    wgrad[...] += tdot(mixed_ref[0], dres_ref[0])

    @pl.when(i == pl.num_programs(0) - 1)
    def _():
        wgrad_ref[...] = wgrad[...].astype(BF)

    pos, begin, _ = row_places(info, rows, nseq)
    d_mixed = ndot(dres_ref[0], wo_ref[...])
    gelu, slope = gelu_pair(gate_ref[0])
    dgate_ref[0] = (d_mixed * hidden_ref[0] * slope).astype(BF)
    b_s[...] = d_mixed * gelu
    soft = vec_ref[taps + V_SOFT : taps + V_SOFT + 1, :]
    a = jnp.where(pos == begin, 0.0, jnp.exp(-8.0 * retain_ref[0] * soft))
    ext[0:rows, :] = a
    ext[rows : rows + 8, :] = jnp.ones((8, a.shape[1]), F32)
    a_s[...] = ext[1 : rows + 1, :]
    run_scan(a_s, b_s, p_ref, s_ref, rows, True)
    pe_ref[0] = ext[0:8, :] * p_ref[0, 0:8, :]
    se_ref[0] = ext[0:8, :] * s_ref[0, 0:8, :]


def back_kernel(
    nseq, taps, length, info, p_ref, s_ref, grad_in_ref, hidden_ref, state_in_ref, state0_ref, conv_ref,
    retain_ref, admit_ref, lin_ref, rim_ref, conv0_ref, wg_ref, vec_ref, sums_o_ref, *refs
):
    dconv_ref, head_ref, late_ref, lasts_ref, ext, wgrad_ref, vgrad_ref = refs[-7:]
    i = pl.program_id(0)
    rows, wide = lin_ref.shape[1:]
    pos, begin, seg = row_places(info, rows, nseq)
    at = pos - begin
    conv_low = conv_ref[0]
    conv = conv_low.astype(F32)
    retain, admit = retain_ref[0], admit_ref[0]
    soft = vec_ref[taps + V_SOFT : taps + V_SOFT + 1, :]
    e = p_ref[0] * grad_in_ref[0, 0:1, :] + s_ref[0]
    ext[0:8, :] = jnp.broadcast_to(state_in_ref[0], (8, wide))
    ext[8 : 8 + rows, :] = hidden_ref[0]
    previous = ext[7 : 7 + rows, :]
    for s in range(nseq):
        previous = jnp.where(pos == info[i, 1 + s], state0_ref[0, s : s + 1, :], previous)
    a = jnp.exp(-8.0 * retain * soft)
    spread = (1.0 - a) * (1.0 + a)
    mult = jnp.sqrt(jnp.maximum(spread, FLOOR))
    d_mult = e * admit * conv
    d_spread = jnp.where(spread > FLOOR, d_mult * 0.5 / mult, 0.0)
    d_log = e * previous * a - 2.0 * a * a * d_spread
    d_rate = (d_log * (-8.0 * soft) * retain * (1.0 - retain)).astype(BF)
    d_inflow = (e * mult * conv * admit * (1.0 - admit)).astype(BF)
    d_gates = jnp.concatenate([d_rate, d_inflow], 1)
    d_conv = e * mult * admit + ndot(d_gates, wg_ref[...])
    low = d_conv.astype(BF)
    dconv_ref[0] = low
    low = low.astype(F32)
    head_ref[0] = low[0:8, :]

    @pl.when(i == 0)
    def _():
        wgrad_ref[...] = jnp.zeros_like(wgrad_ref)
        vgrad_ref[...] = jnp.zeros_like(vgrad_ref)

    wgrad_ref[...] += tdot(conv_low, d_gates)
    sums = [low * v for v in inputs_by_tap(ext, lin_ref, rim_ref, conv0_ref, at, seg, taps)]
    sums += [low, d_rate.astype(F32), d_inflow.astype(F32), d_log * (-8.0 * retain)]
    for k, value in enumerate(sums):
        vgrad_ref[k : k + 1, :] += jnp.sum(value, axis=0, keepdims=True)

    slots = lasts_ref.shape[1]
    column = lax.broadcasted_iota(jnp.int32, (1, slots), 1)
    wanted = jnp.full((1, slots), -1, jnp.int32)
    for q in range(nseq):
        end = (info[i, 2 + q] if q + 1 < nseq else length) - 1
        wanted = jnp.where(column == q, end, wanted)
        for j in range(taps - 1):
            wanted = jnp.where(column == nseq + q * (taps - 1) + j, end - (taps - 2) + j, wanted)
    hot = jnp.where(pos == wanted, 1.0, 0.0).astype(BF)
    states, convs = tdot(hot, hidden_ref[0].astype(BF)), tdot(hot, lin_ref[0])
    row = lax.broadcasted_iota(jnp.int32, states.shape, 0)
    lasts_ref[0] = jnp.where(row < nseq, states, convs).astype(BF)

    @pl.when(i == pl.num_programs(0) - 1)
    def _():
        used = late_ref.shape[0]
        before = sums_o_ref.shape[1]
        late_ref[:, :before] = sums_o_ref[:used, :]
        head_w = (late_ref.shape[1] - before - len(sums)) // 2
        last = len(sums) - 1
        vgrad_ref[last : last + 1, :] *= vec_ref[last + 1 : last + 2, :]
        count = vgrad_ref.shape[0]
        row = lax.broadcasted_iota(jnp.int32, (count, count), 0)
        column = lax.broadcasted_iota(jnp.int32, (count, count), 1)
        eye = jnp.where(row == column, 1.0, 0.0).astype(BF)
        turned = tdot(vgrad_ref[...].astype(BF), eye)
        for h in range(used // head_w):
            at = slice(h * head_w, (h + 1) * head_w)
            parts = [wgrad_ref[at, o + h * head_w : o + (h + 1) * head_w] for o in (0, wide)]
            parts.append(turned[at, : len(sums)])
            late_ref[at, before:] = jnp.concatenate(parts, 1).astype(BF)


def back_conv_kernel(nseq, taps, info, dconv_ref, rim_ref, dgate_ref, vec_ref, *refs):
    out_ref, ext = refs[-2:]
    i = pl.program_id(0)
    rows, wide = dconv_ref.shape[1:]
    pos = info[i, 0] + lax.broadcasted_iota(jnp.int32, (rows, 1), 0)
    ext[0:rows, :] = dconv_ref[0].astype(F32)
    ext[rows : rows + 8, :] = rim_ref[0]
    total = vec_ref[0:1, :] * ext[0:rows, :]
    for k in range(1, taps):
        cut = jnp.zeros((rows, 1), jnp.int32)
        for s in range(nseq):
            start = info[i, 1 + s]
            cut = jnp.where((pos < start) & (pos + k >= start), 1, cut)
        total = total + vec_ref[k : k + 1, :] * jnp.where(cut == 0, ext[k : k + rows, :], 0.0)
    used = out_ref.shape[2] // 2
    both = [dgate_ref[0].astype(F32)[:, :used], total[:, :used]]
    out_ref[0] = jnp.concatenate(both, 1).astype(BF)


def by_block(body, info, ins, outs, scratch, done=(), name=None):
    blocks = info.shape[0]

    def spec(shape, blocked):
        zeros = (0,) * (len(shape) - 1)
        if blocked:
            return pl.BlockSpec((1,) + tuple(shape[1:]), lambda i, *_: (i,) + zeros)
        return pl.BlockSpec(tuple(shape), lambda i, *_: (0,) + zeros)

    hbm = pl.BlockSpec(memory_space=pl.ANY)
    return pl.pallas_call(
        body,
        grid_spec=pltpu.PrefetchScalarGridSpec(
            num_scalar_prefetch=1,
            grid=(blocks,),
            in_specs=[spec(v.shape, blocked) for v, blocked in ins] + [hbm] * len(done),
            out_specs=[spec(shape, blocked) for shape, _, blocked in outs],
            scratch_shapes=[pltpu.VMEM(shape, F32) for shape in scratch],
        ),
        out_shape=[jax.ShapeDtypeStruct(shape, kind) for shape, kind, _ in outs],
        compiler_params=pltpu.CompilerParams(vmem_limit_bytes=VMEM_LIMIT),
        cost_estimate=pl.CostEstimate(flops=0, bytes_accessed=1 << 20, transcendentals=0),
        name=name,
    )(info, *[v for v, _ in ins], *done)


def on_device(
    tokens,
    starts,
    init_state,
    init_conv,
    w_y,
    w_x,
    gate_a,
    gate_i,
    w_out,
    norm1_gain,
    conv_kernel,
    conv_bias,
    bias_a,
    bias_i,
    decay_param,
    w_gate,
    w_up,
    w_down,
    norm2_gain,
    cotangent,
):
    planes, count = lax.axis_size("a"), chips()
    a, b, n, c = (lax.axis_index(name) for name in ("a", "b", "n", "c"))
    u = chip()
    nn = count // 2
    rows, d_model = tokens.shape[1], tokens.shape[2]
    nseq = starts.shape[1]
    width = w_y.shape[1]
    head_w = gate_a.shape[1]
    half = gate_a.shape[0]
    taps = conv_kernel.shape[0]
    back = taps - 1
    heads_here = planes // 2
    wide_here = heads_here * head_w
    wp = -(-wide_here // 128) * 128
    hid = w_down.shape[0]
    drows = w_y.shape[0]
    nblocks = 2 * count

    def gather_a(value):
        return lax.all_gather(value, "a", axis=0, tiled=True)

    def scatter_a(value):
        return lax.psum_scatter(value, "a", scatter_dimension=0, tiled=True)

    def padded(v, axis=-1):
        pads = [(0, 0)] * v.ndim
        pads[axis] = (0, wp - wide_here)
        return jnp.pad(v, pads)

    vectors = jnp.concatenate(
        [conv_kernel, conv_bias[None], bias_a[None], bias_i[None], decay_param[None]], 0
    ).reshape(-1)
    vectors = jnp.concatenate([vectors, norm1_gain, norm2_gain]).astype(F32)
    lanes = -(-vectors.shape[0] // 1024) * 128
    vectors = jnp.pad(vectors, (0, 8 * lanes - vectors.shape[0])).reshape(8, lanes)
    at_start = jnp.concatenate([init_state[0][:, None], init_conv[0].astype(F32)], 1)
    at_start = at_start.reshape(nseq * taps, width)
    at_start = jnp.pad(at_start, ((0, 8), (0, 0)))
    at_start = at_start.at[nseq * taps, :nseq].set(starts[0].astype(F32))
    all_tokens, w_yx, w_gu, _, gate_rows, canon, at_start = start_exchange(
        tokens[0],
        w_y,
        w_x,
        w_gate,
        w_up,
        jnp.concatenate([gate_a, gate_i], 1),
        vectors,
        at_start,
    )
    w_yx = w_yx.reshape(d_model, 2 * wide_here)
    w_gu = gather_a(w_gu.reshape(-1, 2 * planes * hid))
    gate_rows = gate_rows.reshape(wide_here, -1)

    def join_halves(mine_all):
        away = swap_c(lax.dynamic_slice_in_dim(mine_all, (1 - c) * heads_here, heads_here, 0))
        own = lax.dynamic_slice_in_dim(mine_all, c * heads_here, heads_here, 0)
        first = jnp.where(c == 0, own, away)
        second = jnp.where(c == 0, away, own)
        return jnp.stack([first, second], 1).reshape((wide_here,) + mine_all.shape[2:])


    w_o = padded(join_halves(gather_a(w_out).reshape(planes, half, d_model)), 0)

    def block_diagonal(m):
        m = m.reshape(heads_here, head_w, head_w)
        eye = jnp.eye(heads_here, dtype=m.dtype)
        full = (m[:, :, None, :] * eye[:, None, :, None]).reshape(wide_here, wide_here)
        return padded(padded(full), 0)

    w_gates = jnp.concatenate(
        [
            block_diagonal(gate_rows[:, :head_w]),
            block_diagonal(gate_rows[:, head_w:]),
        ],
        1,
    )

    w_d = gather_a(w_down)
    f_here = planes * hid

    canon = canon.reshape(planes * nblocks, -1)
    nvec = (taps + 4) * half
    gain_one = canon[:, nvec : nvec + drows].reshape(-1)
    gain_two = canon[:, nvec + drows : nvec + 2 * drows].reshape(-1)
    mine = pick(canon[:, :nvec].reshape(2, heads_here, count, 2, taps + 4, half), c)
    mine = pick(mine, u, 1).transpose(2, 0, 1, 3).reshape(taps + 4, wide_here)
    decay_f = mine[taps + 3]
    vec = [mine[: taps + 3], jax.nn.softplus(decay_f)[None], jax.nn.sigmoid(decay_f)[None]]
    vec = padded(jnp.concatenate(vec))

    def my_channels(v):
        lead = v.shape[:-1]
        v = v.reshape(lead + (2, heads_here, count, head_w))
        v = pick(v, c, len(lead))
        return pick(v, u, len(lead) + 1).reshape(lead + (wide_here,))

    streams = 2 * nn
    at_start = at_start.reshape(streams, -1, width)
    offsets = at_start[:, nseq * taps, :nseq].astype(jnp.int32)
    at_start = my_channels(at_start[:, : nseq * taps].reshape(streams, nseq, taps, width))
    at_start = padded(at_start)
    state_0 = jnp.pad(at_start[:, :, 0], ((0, 0), (0, -nseq % 8), (0, 0)))
    conv_0 = at_start[:, :, 1:].reshape(streams, nseq * back, wp).astype(BF)
    conv_0 = jnp.pad(conv_0, ((0, 0), (0, -(nseq * back) % 16), (0, 0)))

    def per_block(v):
        v = v.reshape((2, 1, nn) + v.shape[1:])
        return jnp.broadcast_to(v, (2, 2, nn) + v.shape[3:]).reshape((nblocks,) + v.shape[3:])

    block_b = (jnp.arange(nblocks, dtype=jnp.int32) // nn) % 2
    first_row = (a * 2 + (b ^ block_b)) * rows
    position = first_row[:, None] + jnp.arange(rows, dtype=jnp.int32)[None]
    off_b = per_block(offsets)

    info = jnp.concatenate(
        [first_row[:, None], off_b, jnp.zeros((nblocks, -(nseq + 1) % 8), jnp.int32)], 1
    )

    grad_low = cotangent[0]
    grads = [grad_low] + [xor_u(grad_low, k) for k in range(1, count)]

    edge = ((nblocks, 8, wp), F32, True)
    normed, gate_in, linear, tail = norm_product(all_tokens, w_yx, gain_one[None], wp)
    normed = normed.reshape(nblocks * rows, d_model)

    def two(v):
        return v.reshape((2, 2, nn) + v.shape[1:])

    rim = pass_along(6, "pass_rows", False, tail)[0]
    conv_0b, state_0b = per_block(conv_0), per_block(state_0)
    full = (nblocks, rows, wp)
    conv_low, retain, admit, carry_mul, carry_add, end_mul, end_add = by_block(
        functools.partial(forward_kernel, nseq, taps),
        info,
        [
            (linear, True), (rim, True), (conv_0b, True), (state_0b, True),
            (w_gates, False), (vec, False),
        ],
        [
            (full, BF, True), (full, F32, True), (full, F32, True),
            (full, F32, True), (full, F32, True), edge, edge,
        ],
        [(rows + 8, wp), (rows, wp), (rows, wp)],
        name="mixer_forward",
    )

    (end_mul, end_add), grads = lax.optimization_barrier(((end_mul, end_add), grads))
    state_in = pass_along(7, "pass_state", False, end_mul, end_add)[0]
    hidden = carry_mul * state_in + carry_add
    mixed_in = (hidden * jax.nn.gelu(gate_in)).astype(BF).reshape(-1, wp)
    resid, normed_two, grads = plane_reduce(
        2, "fwd", False, (mixed_in.reshape(2, count, rows, -1),), w_o, gain_two, tokens[0],
        tokens[0], grads,
    )
    normed_two = normed_two.reshape(nblocks * rows, d_model)
    grads = grads.reshape(nblocks * rows, d_model)

    hid_full = (nblocks, rows, f_here)
    inner, by_gate, by_up = by_block(
        ffn_forward_kernel,
        info,
        [(normed_two.reshape(nblocks, rows, d_model), True), (w_gu, False)],
        [(hid_full, BF, True)] * 3,
        [],
        name="ffn_forward",
    )
    inner = inner.reshape(nblocks * rows, f_here)
    cut = d_model // 2
    first_d = tdot(inner, grads[:, :cut]).astype(BF)
    second_d = tdot(inner, grads[:, cut:]).astype(BF)
    sent_d = scatter_a(first_d), scatter_a(second_d)
    d_pair = by_block(
        ffn_back_kernel,
        info,
        [
            (grads.reshape(nblocks, rows, d_model), True), (w_d, False), (by_gate, True),
            (by_up, True),
        ],
        [((nblocks, rows, 2 * f_here), BF, True)],
        [],
        (first_d, second_d),
        name="ffn_back",
    )[0]
    sums_gu = tdot(normed_two, d_pair.reshape(nblocks * rows, -1)).astype(BF)
    sent_gu = scatter_a(sums_gu)
    d_resid, d_resid_low, *low = plane_reduce(
        3, "mid", True, (d_pair.reshape(2, count, rows, -1),), w_gu,
        gain_two, grad_low, resid, (inner.reshape(2, count, rows, f_here), w_d), (sent_d[0], sums_gu),
    )
    d_resid_low = d_resid_low.reshape(nblocks * rows, d_model)

    result = resid + low[0].astype(F32)
    for k in range(1, count):
        result = result + xor_u(low[k], k).astype(F32)
    result = result.astype(BF)

    d_gate_in, back_mul, back_add, end_mul, end_add, sums_o = by_block(
        functools.partial(back_scan_kernel, nseq, taps),
        info,
        [
            (d_resid_low.reshape(nblocks, rows, d_model), True), (w_o, False), (gate_in, True),
            (hidden, True), (retain, True), (vec, False), (mixed_in.reshape(full), True),
        ],
        [
            (full, BF, True), (full, F32, True), (full, F32, True), edge, edge,
            ((wp, d_model), BF, False),
        ],
        [(rows + 8, wp), (rows, wp), (rows, wp), (wp, d_model)],
        (sent_d[1],),
        name="mixer_back_scan",
    )
    grad_in = pass_along(8, "pass_state_back", True, end_mul, end_add)[0]
    d_conv_low, head, late, lasts = by_block(
        functools.partial(back_kernel, nseq, taps, planes * 2 * rows),
        info,
        [
            (back_mul, True), (back_add, True), (grad_in, True), (hidden, True),
            (state_in, True), (state_0b, True), (conv_low, True), (retain, True),
            (admit, True), (linear, True), (rim, True), (conv_0b, True), (w_gates, False), (vec, False),
            (sums_o, False),
        ],
        [
            (full, BF, True), edge, ((wide_here, d_model + 2 * head_w + taps + 4), BF, False),
            ((nblocks, nseq * taps, wp), BF, True),
        ],
        [(rows + 8, wp), (wp, 2 * wp), (taps + 4, wp)],
        (),
        name="mixer_back",
    )

    rim_back, late = pass_along(9, "pass_rows_back", True, head, halves=(late, half))
    d_both = by_block(
        functools.partial(back_conv_kernel, nseq, taps),
        info,
        [(d_conv_low, True), (rim_back, True), (d_gate_in, True), (vec, False)],
        [((nblocks, rows, 2 * wide_here), BF, True)],
        [(rows + 8, wp)],
        (result, sent_gu),
        name="mixer_back_conv",
    )[0]
    late = scatter_a(late.reshape(planes * half, -1))
    sums_yx = tdot(normed, d_both.reshape(nblocks * rows, 2 * wide_here)).astype(BF)
    input_grad, pieces, lasts = plane_reduce(
        4, "last", True, (d_both.reshape(2, count, rows, -1),), w_yx, gain_one, tokens[0], d_resid,
        (sent_gu,), (sums_yx,), lasts,
    )
    gain_shape = ((1, drows), F32)
    (
        grad_wg, grad_wu, grad_gain_two, grad_wo, grad_wa, grad_wi, final_state, final_conv,
        grad_taps, *vec_grads,
    ) = in_place(
        functools.partial(order_hidden_kernel, hid, head_w),
        (pieces, w_gate, w_up, norm2_gain.astype(F32)[None], late, lasts),
        [
            (w_gate.shape, F32), (w_up.shape, F32), gain_shape, (w_out.shape, F32),
            (gate_a.shape, F32), (gate_i.shape, F32), ((nseq, width), F32),
            ((nseq * back, width), BF), ((taps, half), F32),
        ]
        + [((1, half), F32)] * 4,
        "order_hidden",
    )
    pieces = finish(scatter_a(sums_yx), (grad_wg,))
    grad_wy, grad_wx, grad_gain_one = in_place(
        functools.partial(order_heads_kernel, head_w),
        (pieces, w_y, w_x, norm1_gain.astype(F32)[None]),
        [(w_y.shape, F32), (w_x.shape, F32), gain_shape],
        "order_heads",
    )
    grad_gain_one, grad_gain_two = grad_gain_one[0], grad_gain_two[0]
    final_conv = final_conv.reshape(nseq, back, width)

    return (
        result[None],
        input_grad[None],
        final_state[None],
        final_conv[None],
        grad_wy,
        grad_wx,
        grad_wa,
        grad_wi,
        grad_wo,
        grad_gain_one,
        grad_taps,
        *[v[0] for v in vec_grads],
        grad_wg,
        grad_wu,
        jnp.concatenate(sent_d, 1).astype(F32),
        grad_gain_two,
    )


WIDE = ("a", "b")
EVERY = ("a", "b", "n", "c")
HIGH = lax.Precision.HIGHEST


def passed_along(value, axis, by):
    size = lax.axis_size(axis)
    pairs = [(i, i + by) for i in range(size) if 0 <= i + by < size]
    return lax.ppermute(value, axis, pairs)


def entering(value, axis, combine, identity, reverse):
    size, place = (lax.axis_size(axis), lax.axis_index(axis))
    everything = jax.tree.map(lambda part: lax.all_gather(part, axis), value)
    start = jax.tree.map(
        lambda part, zero: jnp.broadcast_to(jnp.asarray(zero, part.dtype), part.shape),
        value,
        identity,
    )

    def hop(k, before):
        at = size - 1 - k if reverse else k
        reached = at > place if reverse else at < place
        new = combine(before, jax.tree.map(lambda part: part[at], everything))
        return jax.tree.map(lambda a, b: jnp.where(reached, a, b), new, before)

    return lax.fori_loop(0, size, hop, start)


def merged_2(value, axis, combine):
    everything = jax.tree.map(
        lambda part, kind: lax.all_gather(part.astype(kind), axis),
        value,
        jax.tree.map(lambda a: jnp.bfloat16 if a.dtype == jnp.float32 else a.dtype, value),
    )

    def take(k):
        return jax.tree.map(lambda part, own: part[k].astype(own.dtype), everything, value)

    return lax.fori_loop(
        1, lax.axis_size(axis), lambda k, so_far: combine(so_far, take(k)), take(0)
    )


def link(earlier, later):
    return (earlier[0] * later[0], later[0] * earlier[1] + later[1])


def norm_back(value, factor, gain, grad):
    weighted = grad * gain
    inner = jnp.mean(weighted * value, axis=-1, keepdims=True)
    return (
        factor * weighted - value * factor * factor * factor * inner,
        jnp.sum(grad * value * factor, axis=0),
    )


def later_one(first, second):
    pick = first[0] > second[0]
    return (
        jnp.where(pick, first[0], second[0]),
        jnp.where(pick[:, None], first[1], second[1]),
        jnp.where(pick[:, None, None], first[2], second[2]),
    )


def on_device_any(
    tokens,
    starts,
    init_state,
    init_conv,
    w_y,
    w_x,
    gate_a,
    gate_i,
    w_out,
    norm1_gain,
    conv_kernel,
    conv_bias,
    bias_a,
    bias_i,
    decay_param,
    w_gate,
    w_up,
    w_down,
    norm2_gain,
    cotangent,
):
    inputs = tokens[0].astype(jnp.float32)
    offsets = starts[0]
    nseqs = offsets.shape[0]
    rows_here = inputs.shape[0]
    width = w_y.shape[1]
    head_w = gate_a.shape[1]
    heads = width // head_w
    place = lax.axis_index(WIDE)
    mixer = (
        lax.all_gather(w_y, EVERY, axis=0, tiled=True),
        lax.all_gather(w_x, EVERY, axis=0, tiled=True),
        lax.all_gather(gate_a, EVERY, axis=0, tiled=True),
        lax.all_gather(gate_i, EVERY, axis=0, tiled=True),
        lax.all_gather(w_out, EVERY, axis=0, tiled=True),
        lax.all_gather(norm1_gain, EVERY, axis=0, tiled=True),
        lax.all_gather(conv_kernel, EVERY, axis=1, tiled=True),
        lax.all_gather(conv_bias, EVERY, axis=0, tiled=True),
        lax.all_gather(bias_a, EVERY, axis=0, tiled=True),
        lax.all_gather(bias_i, EVERY, axis=0, tiled=True),
        lax.all_gather(decay_param, EVERY, axis=0, tiled=True),
    )
    wy_full, wx_full, wa_full, wi_full, wo_full, gain_one, kernel, cbias, abias, ibias, decay = (
        mixer
    )
    gain_one = gain_one.astype(jnp.float32)
    kernel = kernel.astype(jnp.float32)
    taps = kernel.shape[0]
    back = taps - 1
    position = place * rows_here + jnp.arange(rows_here, dtype=jnp.int32)

    def segment_of(where_at):
        return jnp.sum((where_at[:, None] >= offsets[None, :]).astype(jnp.int32), axis=1) - 1

    segment = segment_of(position)
    member = segment[:, None] == jnp.arange(nseqs, dtype=jnp.int32)[None, :]
    begin = jnp.sum(jnp.where(member, offsets[None, :], 0), axis=1)
    opening = (position == begin)[:, None]
    scale_one = lax.rsqrt(jnp.mean(inputs * inputs, axis=-1, keepdims=True) + EPS)
    normed = (inputs * scale_one * gain_one).astype(jnp.bfloat16)
    gate_in = mdot(normed, wy_full)
    linear = mdot(normed, wx_full).astype(jnp.bfloat16)
    rim_rows = passed_along(linear[rows_here - back :], WIDE, 1)
    extended = jnp.concatenate([rim_rows, linear], 0)
    stored = mdot(member.astype(jnp.bfloat16), init_conv[0].reshape(nseqs, back * width)).reshape(
        rows_here, back, width
    )
    inputs_by_tap = [linear.astype(jnp.float32)]
    for shift_by in range(1, taps):
        earlier = extended[back - shift_by : back - shift_by + rows_here].astype(jnp.float32)
        offset = position - shift_by - begin
        from_start = jnp.zeros((rows_here, width), jnp.float32)
        for slot in range(back):
            from_start = from_start + jnp.where(
                (offset + back == slot)[:, None], stored[:, slot], 0.0
            )
        inputs_by_tap.append(jnp.where((offset >= 0)[:, None], earlier, from_start))
    conv_sum = cbias.astype(jnp.float32)
    for shift_by in range(taps):
        conv_sum = conv_sum + kernel[shift_by] * inputs_by_tap[shift_by]
    conv_low = conv_sum.astype(jnp.bfloat16)
    conv_val = conv_low.astype(jnp.float32)
    blocks = conv_low.reshape(rows_here, heads, head_w)
    wa_heads = wa_full.reshape(heads, head_w, head_w)
    wi_heads = wi_full.reshape(heads, head_w, head_w)
    rate = jnp.einsum("thi,hij->thj", blocks, wa_heads, preferred_element_type=jnp.float32).reshape(
        rows_here, width
    ) + abias.astype(jnp.float32)
    inflow = jnp.einsum(
        "thi,hij->thj", blocks, wi_heads, preferred_element_type=jnp.float32
    ).reshape(rows_here, width) + ibias.astype(jnp.float32)
    retain = jax.nn.sigmoid(rate)
    admit = jax.nn.sigmoid(inflow)
    decay_f = decay.astype(jnp.float32)
    soft_decay = jax.nn.softplus(decay_f)
    log_a = -8.0 * retain * soft_decay
    decay_now = jnp.exp(log_a)
    spread = -jnp.expm1(2.0 * log_a)
    mult = jnp.sqrt(jnp.maximum(spread, FLOOR))
    drive = mult * admit * conv_val
    state_rows = jnp.dot(member.astype(jnp.float32), init_state[0], precision=HIGH)
    a_used = jnp.where(opening, 0.0, decay_now)
    b_used = jnp.where(opening, decay_now * state_rows + drive, drive)
    carry_mul, carry_add = lax.associative_scan(link, (a_used, b_used), axis=0)
    identity = (jnp.ones((width,), jnp.float32), jnp.zeros((width,), jnp.float32))
    state_in = entering(
        (carry_mul[rows_here - 1], carry_add[rows_here - 1]), WIDE, link, identity, False
    )[1]
    hidden = carry_mul * state_in + carry_add
    gelu_y, gelu_y_back = jax.vjp(jax.nn.gelu, gate_in)
    mixed_in = (hidden * gelu_y).astype(jnp.bfloat16)
    resid = inputs + mdot(mixed_in, wo_full)
    wg_full, wu_full, wd_full, gain_two = (
        lax.all_gather(w_gate, EVERY, axis=0, tiled=True),
        lax.all_gather(w_up, EVERY, axis=0, tiled=True),
        lax.all_gather(w_down, EVERY, axis=0, tiled=True),
        lax.all_gather(norm2_gain, EVERY, axis=0, tiled=True),
    )
    gain_two = gain_two.astype(jnp.float32)
    scale_two = lax.rsqrt(jnp.mean(resid * resid, axis=-1, keepdims=True) + EPS)
    normed_two = (resid * scale_two * gain_two).astype(jnp.bfloat16)
    gate = mdot(normed_two, wg_full)
    upward = mdot(normed_two, wu_full)
    active, gate_back = jax.vjp(jax.nn.gelu, gate)
    inner = (active * upward).astype(jnp.bfloat16)
    result = (resid + mdot(inner, wd_full)).astype(jnp.bfloat16)
    local_rows = jnp.arange(rows_here, dtype=jnp.int32)
    last_row = jnp.max(jnp.where(member, local_rows[:, None], -1), axis=0)
    present = last_row >= 0
    safe_row = jnp.maximum(last_row, 0)
    marker = jnp.where(present, (place * rows_here + last_row).astype(jnp.float32), -1.0)
    state_last = jnp.where(present[:, None], hidden[safe_row], 0.0)
    conv_rows = extended[safe_row[:, None] + 1 + jnp.arange(back, dtype=jnp.int32)[None, :]].astype(
        jnp.float32
    )
    conv_last = jnp.where(present[:, None, None], conv_rows, 0.0)
    merged = merged_2((marker, state_last, conv_last), WIDE, later_one)
    wg_back, wu_back, wd_back = (
        lax.all_gather(w_gate, EVERY, axis=0, tiled=True),
        lax.all_gather(w_up, EVERY, axis=0, tiled=True),
        lax.all_gather(w_down, EVERY, axis=0, tiled=True),
    )
    grad_low = cotangent[0]
    grad_out = grad_low.astype(jnp.float32)
    d_inner = ndot(grad_low, wd_back)
    grad_wd = tdot(inner, grad_low)
    d_gate = gate_back(d_inner * upward)[0].astype(jnp.bfloat16)
    d_up = (d_inner * active).astype(jnp.bfloat16)
    grad_wg = tdot(normed_two, d_gate)
    grad_wu = tdot(normed_two, d_up)
    d_normed_two = ndot(d_gate, wg_back) + ndot(d_up, wu_back)
    d_resid_norm, grad_gain_two = norm_back(resid, scale_two, gain_two, d_normed_two)
    d_resid = grad_out + d_resid_norm
    wy_back, wx_back, wa_back, wi_back, wo_back = (
        lax.all_gather(w_y, EVERY, axis=0, tiled=True),
        lax.all_gather(w_x, EVERY, axis=0, tiled=True),
        lax.all_gather(gate_a, EVERY, axis=0, tiled=True),
        lax.all_gather(gate_i, EVERY, axis=0, tiled=True),
        lax.all_gather(w_out, EVERY, axis=0, tiled=True),
    )
    d_resid_low = d_resid.astype(jnp.bfloat16)
    d_mixed = ndot(d_resid_low, wo_back)
    grad_wo = tdot(mixed_in, d_resid_low)
    d_hidden = d_mixed * gelu_y
    d_gate_in = gelu_y_back(d_mixed * hidden)[0].astype(jnp.bfloat16)
    forward_mul = jnp.concatenate([a_used[1:], jnp.ones((1, width), jnp.float32)], 0)
    back_mul, back_add = lax.associative_scan(link, (forward_mul, d_hidden), reverse=True, axis=0)
    head_map = (a_used[0] * back_mul[0], a_used[0] * back_add[0])
    grad_in = entering(head_map, WIDE, link, identity, True)[1]
    total_grad = back_mul * grad_in + back_add
    previous = jnp.concatenate([state_in[None], hidden[:-1]], 0)
    previous = jnp.where(opening, state_rows, previous)
    d_decay = total_grad * previous
    d_mult = total_grad * admit * conv_val
    d_admit = total_grad * mult * conv_val
    d_conv = total_grad * mult * admit
    d_spread = jnp.where(spread > FLOOR, d_mult * 0.5 / mult, 0.0)
    d_log = d_decay * decay_now - 2.0 * decay_now * decay_now * d_spread
    d_retain = d_log * (-8.0 * soft_decay)
    grad_decay = jnp.sum(d_log * (-8.0 * retain), axis=0) * jax.nn.sigmoid(decay_f)
    d_rate = (d_retain * retain * (1.0 - retain)).astype(jnp.bfloat16)
    d_inflow = (d_admit * admit * (1.0 - admit)).astype(jnp.bfloat16)
    grad_abias = jnp.sum(d_rate.astype(jnp.float32), axis=0)
    grad_ibias = jnp.sum(d_inflow.astype(jnp.float32), axis=0)
    rate_heads = d_rate.reshape(rows_here, heads, head_w)
    inflow_heads = d_inflow.reshape(rows_here, heads, head_w)
    grad_wa = jnp.einsum(
        "thi,thj->hij", blocks, rate_heads, preferred_element_type=jnp.float32
    ).reshape(width, head_w)
    grad_wi = jnp.einsum(
        "thi,thj->hij", blocks, inflow_heads, preferred_element_type=jnp.float32
    ).reshape(width, head_w)
    d_conv = d_conv + jnp.einsum(
        "thj,hij->thi",
        rate_heads,
        wa_back.reshape(heads, head_w, head_w),
        preferred_element_type=jnp.float32,
    ).reshape(rows_here, width)
    d_conv = d_conv + jnp.einsum(
        "thj,hij->thi",
        inflow_heads,
        wi_back.reshape(heads, head_w, head_w),
        preferred_element_type=jnp.float32,
    ).reshape(rows_here, width)
    d_conv_low = d_conv.astype(jnp.bfloat16)
    d_conv_val = d_conv_low.astype(jnp.float32)
    rim_back = passed_along(d_conv_low[:back], WIDE, -1)
    ahead = jnp.concatenate([d_conv_low, rim_back], 0)
    d_linear = kernel[0] * d_conv_val
    kernel_grads = [jnp.sum(d_conv_val * inputs_by_tap[0], axis=0)]
    for shift_by in range(1, taps):
        later_rows = ahead[shift_by : shift_by + rows_here].astype(jnp.float32)
        same = (segment_of(position + shift_by) == segment)[:, None]
        d_linear = d_linear + kernel[shift_by] * jnp.where(same, later_rows, 0.0)
        kernel_grads.append(jnp.sum(d_conv_val * inputs_by_tap[shift_by], axis=0))
    grad_kernel = jnp.stack(kernel_grads, 0)
    grad_cbias = jnp.sum(d_conv_val, axis=0)
    d_linear_low = d_linear.astype(jnp.bfloat16)
    d_normed = ndot(d_gate_in, wy_back) + ndot(d_linear_low, wx_back)
    grad_wy = tdot(normed, d_gate_in)
    grad_wx = tdot(normed, d_linear_low)
    d_input_norm, grad_gain_one = norm_back(inputs, scale_one, gain_one, d_normed)
    input_grad = (d_resid + d_input_norm).astype(jnp.bfloat16)
    every_sum = (
        lax.psum_scatter(grad_wy, EVERY, scatter_dimension=0, tiled=True),
        lax.psum_scatter(grad_wx, EVERY, scatter_dimension=0, tiled=True),
        lax.psum_scatter(grad_wa, EVERY, scatter_dimension=0, tiled=True),
        lax.psum_scatter(grad_wi, EVERY, scatter_dimension=0, tiled=True),
        lax.psum_scatter(grad_wo, EVERY, scatter_dimension=0, tiled=True),
        lax.psum_scatter(grad_gain_one, EVERY, scatter_dimension=0, tiled=True),
        lax.psum_scatter(grad_kernel, EVERY, scatter_dimension=1, tiled=True),
        lax.psum_scatter(grad_cbias, EVERY, scatter_dimension=0, tiled=True),
        lax.psum_scatter(grad_abias, EVERY, scatter_dimension=0, tiled=True),
        lax.psum_scatter(grad_ibias, EVERY, scatter_dimension=0, tiled=True),
        lax.psum_scatter(grad_decay, EVERY, scatter_dimension=0, tiled=True),
        lax.psum_scatter(grad_wg, EVERY, scatter_dimension=0, tiled=True),
        lax.psum_scatter(grad_wu, EVERY, scatter_dimension=0, tiled=True),
        lax.psum_scatter(grad_wd, EVERY, scatter_dimension=0, tiled=True),
        lax.psum_scatter(grad_gain_two, EVERY, scatter_dimension=0, tiled=True),
    )
    mixer_sums = every_sum[:11]
    mlp_sums = every_sum[11:]
    return (
        result[None],
        input_grad[None],
        merged[1][None],
        merged[2].astype(jnp.bfloat16)[None],
        mixer_sums[0],
        mixer_sums[1],
        mixer_sums[2],
        mixer_sums[3],
        mixer_sums[4],
        mixer_sums[5],
        mixer_sums[6],
        mixer_sums[7],
        mixer_sums[8],
        mixer_sums[9],
        mixer_sums[10],
        mlp_sums[0],
        mlp_sums[1],
        mlp_sums[2],
        mlp_sums[3],
    )


def solution(mesh):
    wide, narrow = mesh.shape["wide"], mesh.shape["narrow"]
    def plan(*args):
        fits = args[6].shape[0] * 2 == args[6].shape[1] and narrow == 4
        return (on_device if fits else on_device_any)(*args)

    fine = Mesh(mesh.devices.reshape(wide // 2, 2, narrow // 2, 2), ("a", "b", "n", "c"))
    w, s = ("a", "b"), ("n", "c")
    everywhere = ("a", "b", "n", "c")
    acts, rows, vec = P(s, w, None), P(everywhere, None), P(everywhere)
    return jax.shard_map(
        plan,
        mesh=fine,
        in_specs=(
            acts,
            P(s, None),
            P(s, None, None),
            P(s, None, None, None),
            rows, rows, rows, rows, rows,
            vec,
            P(None, everywhere),
            vec, vec, vec, vec,
            rows, rows, rows,
            vec,
            acts,
        ),
        out_specs=(
            acts,
            acts,
            P(s, None, None),
            P(s, None, None, None),
            rows, rows, rows, rows, rows,
            vec,
            P(None, everywhere),
            vec, vec, vec, vec,
            rows, rows, rows,
            vec,
        ),
        check_vma=False,
    )
```
